32 devices in a mesh: groups: 2 (over y), wide: 4 (over z), narrow: 4 (over x, core).
Axes of the slice: x: 2, y: 2, z: 4, core: 2. Of those that a mesh axis runs over, the one named last changes fastest.
Arguments:
- operators: float32 [32, 1024, 1024], P(('groups', 'wide', 'narrow')), parts along dimension 0
- coarse_inverse: float32 [2048, 1024], P(('groups', 'wide'), 'narrow'), parts along dimension 0
- modes: float32 [32, 64, 1024], P(('groups', 'wide', 'narrow')), parts along dimension 0, may hold values from -0.1875 to 0.1875
- gap: float32 [32, 1024, 128], P(('groups', 'wide', 'narrow')), parts along dimension 0, may hold values from -6 to 6
- start_mult: float32 [32, 1024, 128], P(('groups', 'wide', 'narrow')), parts along dimension 0, may hold values from -3 to 3
- peer_list: int32 [32, 256, 1], P(('groups', 'wide', 'narrow')), parts along dimension 0, may hold values from 0 to 3; in each aligned block of 256 rows (0 to 255, 256 to 511, ..., all dimensions but the last counted through in order) at most 128 rows name the same one
- partner_row: int32 [32, 256], P(('groups', 'wide', 'narrow')), parts along dimension 0, may hold values from 0 to 255
- interface_size: int32 [32], P(('groups', 'wide', 'narrow')), parts along dimension 0, may hold values from 512 to 1024, as said below
- contact_rows: int32 [32, 1024], P(('groups', 'wide', 'narrow')), parts along dimension 0, may hold values 0 or 1
Outputs:
- mult: float32 [32, 1024, 128], P(('groups', 'wide', 'narrow')), parts along dimension 0
- residual: float32 [32, 1024, 128], P(('groups', 'wide', 'narrow')), parts along dimension 0
The draws below stay inside these ranges and needn't reach their ends.
There are 2 independent parts, one for each index of `groups`. The reference program is written for one: setup_inputs(seed, part) draws one part's arguments, and reference() takes and returns one part's arrays. A program takes and returns all parts, laid end to end along the dimension named above; each array names one. Nothing has to cross between parts.
Inputs may be any that keep to these rules, and one draw needn't show every extreme that they name: `peer_list`: among the 256 shared rows of one subdomain at most 128 name the same neighbour, and exactly 128 do in some subdomain. `interface_size`: some subdomain has all 1024 rows live.
All inputs are finite; a program needn't handle non-finite values. No bound on the sum of `contact_rows` on one device may be relied on, other than what follows from the above.
Results may differ from the reference program's by a relative error of at most 0.0002.
Values sent between devices are 32-bit elements; how exact they have to be, the bound alone decides.
No kernel may reach another device: no remote copies, remote signals or barrier semaphores. Data moves between devices by JAX's collectives and lax.ppermute only.
A program may use at most 64 MiB of HBM per device.

```python
import math
import jax
import jax.numpy as jnp
import numpy as np
from jax import lax

M = 1024
SHARED = 256
MODES = 64
LOADS = 128
OUTER = 2
INNER = 3
WIDE_SUBS = 4
NARROW_SUBS = 4
SUBS = 16
CAP = 128


def draw_operators(key, part):
    first, second = jax.random.split(jax.random.fold_in(key, 11), 2)
    subs = WIDE_SUBS * NARROW_SUBS
    diag = jax.random.uniform(first, (subs, M), jnp.float32, 1.0, 3.0)
    noise = jax.random.normal(second, (subs, M, M), jnp.float32)
    sym = (noise + jnp.swapaxes(noise, 1, 2)) * (0.42 / math.sqrt(M))
    ident = jnp.eye(M, dtype=jnp.float32)
    return sym + ident[None, :, :] * diag[:, :, None]


def draw_coarse_inverse(key, part):
    first, second = jax.random.split(jax.random.fold_in(key, 23), 2)
    size = MODES * WIDE_SUBS * NARROW_SUBS
    rows = jnp.arange(size, dtype=jnp.int32)
    wide_of = rows // (NARROW_SUBS * MODES)
    narrow_of = rows // MODES % NARROW_SUBS
    matched = (narrow_of * WIDE_SUBS + wide_of) * MODES + rows % MODES
    base = (rows[None, :] == matched[:, None]).astype(jnp.float32)
    scales = jax.random.uniform(first, (size, 1), jnp.float32, 0.5, 1.5)
    noise = jax.random.normal(second, (size, size), jnp.float32) * (0.5 / math.sqrt(size))
    return base * scales + noise


def draw_interface_size(key, part):
    first, second = jax.random.split(jax.random.fold_in(key, 37), 2)
    subs = WIDE_SUBS * NARROW_SUBS
    sizes = jax.random.randint(first, (subs,), M // 2, M + 1, dtype=jnp.int32)
    spot = jax.random.randint(second, (), 0, subs, dtype=jnp.int32)
    return jnp.where(jnp.arange(subs, dtype=jnp.int32) == spot, M, sizes).astype(jnp.int32)


def set_ends(entries, rng, smallest, largest):
    place = [jax.random.randint(jax.random.fold_in(rng, axis), (), 0, length) for axis, length in enumerate(entries.shape)]
    widest = entries.shape.index(max(entries.shape))
    neighbour = place[:widest] + [(place[widest] + 1) % entries.shape[widest]] + place[widest + 1:]
    return entries.at[tuple(place)].set(smallest).at[tuple(neighbour)].set(largest)


def level_of(rng, shape, cuts, smallest, largest):
    loudness = 1.0
    for axis_at, shards_of in cuts:
        draws = jax.random.uniform(jax.random.fold_in(jax.random.fold_in(rng, 6), axis_at), (shards_of,), jnp.float32, smallest / len(cuts), largest / len(cuts))
        loudness = loudness * jnp.repeat(jnp.exp(draws), shape[axis_at] // shards_of).reshape((-1,) + (1,) * (len(shape) - 1 - axis_at))
    return loudness


def shared_out(rng, own, number, rows, number_of, top, reach, skew):
    order = jax.random.permutation(rng, number_of)
    heavy_load, ordinary = portions_of(number_of, rows * top, reach, skew, True), portions_of(number_of, rows * top, reach, skew, False)
    places = jnp.arange(number_of)

    def named(lengths, rotation):
        used = int((lengths > 0).sum())
        fixed = max(1, used // 4)
        passed = fixed + (places - fixed + rotation * (used - fixed)) % max(1, number_of - fixed)
        return jnp.zeros((number_of,), jnp.int32).at[order[jnp.where(places < fixed, places, passed)]].set(jnp.asarray(lengths, jnp.int32))

    lengths = jnp.where(number % 4 == 0, named(heavy_load, number // 4), named(ordinary, number - number // 4 - 1))
    mixed = jax.random.permutation(jax.random.fold_in(own, 3), number_of)
    donor, receiver = mixed[0:number_of // 2 * 2:2], mixed[1:number_of // 2 * 2:2]
    slack = jnp.minimum(lengths[donor] - 1, reach - lengths[receiver]) // 2
    slack = jnp.where((donor == order[0]) | (receiver == order[0]) | (lengths[receiver] == 0), 0, jnp.maximum(slack, 0))
    passed = jax.random.randint(jax.random.fold_in(own, 4), (number_of // 2,), 0, 1 << 20) % (slack + 1)
    lengths = lengths.at[donor].add(-passed).at[receiver].add(passed)
    items = jnp.searchsorted(jnp.cumsum(lengths), jnp.arange(rows * top), side="right").astype(jnp.int32)
    grid = items.reshape(top, rows).T
    grid = grid[jax.random.permutation(jax.random.fold_in(own, 1), rows)]
    rotation = jax.random.randint(jax.random.fold_in(own, 2), (rows, 1), 0, top)
    return jnp.take_along_axis(grid, (jnp.arange(top)[None, :] + rotation) % top, axis=1)


def portions_of(count, total, most, lean, full):
    portions = [(1 << 20) // math.isqrt(rank ** lean) + 1 for rank in range(1, count + 1)]
    largest = most if full else min(most, max(-(-total // count), total * portions[0] // sum(portions)))
    least = 1 if total - largest >= count - 1 else 0
    counts, rest = [largest] + [least] * (count - 1), total - largest - least * (count - 1)
    while rest > 0:
        candidates = [i for i in range(1, count) if counts[i] < largest] or [i for i in range(1, count) if counts[i] < most]
        mass, left = sum([portions[i] for i in candidates]), rest
        for i in candidates:
            extra = min(most - counts[i], max(1, left * portions[i] // mass), rest)
            counts[i] = counts[i] + extra
            rest = rest - extra
    return np.array(counts)


def gaussian(own_key, extent, scale, limit, shards=(), held_as=jnp.bfloat16):
    entries = scale * jax.random.normal(own_key, extent, jnp.float32)
    if shards:
        entries = entries * level_of(own_key, extent, shards, -0.22, 0.18)
    return jnp.clip(entries, -limit, limit).astype(held_as)


def setup_inputs(seed: int = 0, part: int = 0) -> dict:
    key_of = jax.random.split(jax.random.key(seed), 10)
    part_keys = jax.random.split(jax.random.fold_in(key_of[9], part), 10)
    operators = draw_operators(jax.random.fold_in(jax.random.fold_in(key_of[9], part), 71), part)
    coarse_inverse = draw_coarse_inverse(jax.random.fold_in(jax.random.fold_in(key_of[9], part), 71), part)
    modes = gaussian(part_keys[2], (SUBS, MODES, M), M ** -0.5, 0.1875, ((0, 16),), jnp.float32)
    gap = gaussian(part_keys[3], (SUBS, M, LOADS), 1.0, 6.0, ((0, 16),), jnp.float32)
    start_mult = gaussian(part_keys[4], (SUBS, M, LOADS), 0.5, 3.0, ((0, 16),), jnp.float32)
    peer_list_keys = jax.random.split(jax.random.fold_in(part_keys[5], 1), SUBS * SHARED // SHARED)
    peer_list_turns = jax.random.permutation(jax.random.fold_in(part_keys[5], 3), SUBS * SHARED // SHARED)
    peer_list = jax.vmap(lambda own, number: shared_out(jax.random.fold_in(part_keys[5], 2), own, number, SHARED, WIDE_SUBS, 1, CAP, 2))(peer_list_keys, peer_list_turns).reshape((SUBS, SHARED, 1))
    partner_row = set_ends(jax.random.randint(part_keys[6], (SUBS, SHARED), 0, SHARED), jax.random.fold_in(part_keys[6], 1), 0, SHARED - 1).astype(jnp.int32)
    interface_size = draw_interface_size(jax.random.fold_in(jax.random.fold_in(key_of[9], part), 71), part)
    contact_rows = set_ends((jax.random.randint(part_keys[8], (SUBS, M), 0, 2) < 1).astype(jnp.int32), jax.random.fold_in(part_keys[8], 1), 0, 1)
    return {"operators": operators, "coarse_inverse": coarse_inverse, "modes": modes, "gap": gap, "start_mult": start_mult, "peer_list": peer_list, "partner_row": partner_row, "interface_size": interface_size, "contact_rows": contact_rows}


def reference(operators, coarse_inverse, modes, gap, start_mult, peer_list, partner_row, interface_size, contact_rows):
    subs = WIDE_SUBS * NARROW_SUBS
    highest = lax.Precision.HIGHEST
    active = (jnp.arange(M, dtype=jnp.int32)[None, :] < interface_size[:, None])[:, :, None]
    contact = (contact_rows == 1)[:, :, None]
    owner = peer_list[:, :, 0] * NARROW_SUBS + (jnp.arange(subs, dtype=jnp.int32) % NARROW_SUBS)[:, None]
    flat_index = (owner * M + partner_row).astype(jnp.int32)
    mult = start_mult
    residual = jnp.zeros_like(gap)
    for outer in range(OUTER):
        for inner in range(INNER):
            image = jnp.einsum("smn,snk->smk", operators, mult, precision=highest)
            across = image.reshape(subs * M, LOADS)[flat_index]
            jump = jnp.concatenate([image[:, :SHARED] - across, image[:, SHARED:]], axis=1)
            residual = jnp.where(active, gap - jump, 0.0)
            update = 0.3 * residual
            if inner == 0:
                coarse = jnp.einsum("scm,smk->sck", modes, residual, precision=highest)
                ordered = coarse.reshape(WIDE_SUBS, NARROW_SUBS, MODES, LOADS).transpose(1, 0, 2, 3).reshape(subs * MODES, LOADS)
                solved = jnp.dot(coarse_inverse, ordered, precision=highest, preferred_element_type=jnp.float32).reshape(subs, MODES, LOADS)
                update = update + jnp.einsum("scm,sck->smk", modes, solved, precision=highest)
            trial = mult + update
            mult = jnp.where(active, jnp.where(contact, jnp.maximum(trial, 0.0), trial), 0.0)
    return mult, residual
```

```python
import jax
import jax.numpy as jnp
from jax import lax
from jax.sharding import PartitionSpec as P

OUTER = 2
INNER = 3


def shifted(block, axis, count, step):
    return lax.ppermute(block, axis, [(i, (i + step) % count) for i in range(count)])


def local(
    wide,
    narrow,
    operators,
    coarse_inverse,
    modes,
    gap,
    start_mult,
    peer_list,
    partner_row,
    interface_size,
    contact_rows,
):
    highest = lax.Precision.HIGHEST
    high = lax.Precision.HIGH
    operator = operators[0]
    basis = modes[0]
    target = gap[0]
    mult = start_mult[0]
    peers = peer_list[0, :, 0]
    rows_wanted = partner_row[0]
    order = operator.shape[0]
    shared = peers.shape[0]
    count = basis.shape[0]
    my_wide = lax.axis_index("wide")
    my_narrow = lax.axis_index("narrow")
    place = lax.rem(my_wide - peers + wide, wide) * shared + rows_wanted
    active = (lax.iota(jnp.int32, order) < interface_size[0])[:, None]
    contact = (contact_rows[0] == 1)[:, None]
    tile = coarse_inverse.reshape(coarse_inverse.shape[0], wide, count)
    tile = jnp.take(tile, lax.rem(my_wide - jnp.arange(wide) + wide, wide), axis=1)
    tile = tile.reshape(coarse_inverse.shape)
    residual = jnp.zeros_like(target)
    for outer in range(OUTER):
        for inner in range(INNER):
            image = jnp.dot(operator, mult, precision=high, preferred_element_type=jnp.float32)
            head = image[:shared]
            whole = jnp.concatenate(
                [head] + [shifted(head, "wide", wide, d) for d in range(1, wide)], axis=0
            )
            across = whole[place]
            jump = jnp.concatenate([head - across, image[shared:]], axis=0)
            residual = jnp.where(active, target - jump, 0.0)
            update = 0.3 * residual
            if inner == 0:
                coarse = jnp.dot(
                    basis, residual, precision=high, preferred_element_type=jnp.float32
                )
                gathered = jnp.concatenate(
                    [coarse] + [shifted(coarse, "wide", wide, d) for d in range(1, wide)], axis=0
                )
                parts = jnp.dot(
                    tile, gathered, precision=high, preferred_element_type=jnp.float32
                )

                def part(d):
                    start = lax.rem(my_narrow + d, narrow) * count
                    return lax.dynamic_slice_in_dim(parts, start, count, axis=0)

                solved = part(0)
                for d in range(1, narrow):
                    solved = solved + shifted(part(d), "narrow", narrow, d)
                update = update + lax.dot_general(
                    basis,
                    solved,
                    (((0,), (0,)), ((), ())),
                    precision=high,
                    preferred_element_type=jnp.float32,
                )
            trial = mult + update
            mult = jnp.where(active, jnp.where(contact, jnp.maximum(trial, 0.0), trial), 0.0)
    return (mult[None], residual[None])


def solution(mesh):
    wide = mesh.shape["wide"]
    narrow = mesh.shape["narrow"]

    def body(*args):
        return local(wide, narrow, *args)

    return jax.shard_map(
        body,
        mesh=mesh,
        in_specs=(
            P(("groups", "wide", "narrow"), None, None),
            P(("groups", "wide"), "narrow"),
            P(("groups", "wide", "narrow"), None, None),
            P(("groups", "wide", "narrow"), None, None),
            P(("groups", "wide", "narrow"), None, None),
            P(("groups", "wide", "narrow"), None, None),
            P(("groups", "wide", "narrow"), None),
            P(("groups", "wide", "narrow")),
            P(("groups", "wide", "narrow"), None),
        ),
        out_specs=(
            P(("groups", "wide", "narrow"), None, None),
            P(("groups", "wide", "narrow"), None, None),
        ),
        check_vma=False,
    )
```

```python
import jax
import jax.numpy as jnp
from jax import lax
from jax.sharding import PartitionSpec as P

OUTER = 2
INNER = 3


def local(
    wide,
    narrow,
    operators,
    coarse_inverse,
    modes,
    gap,
    start_mult,
    peer_list,
    partner_row,
    interface_size,
    contact_rows,
):
    highest = lax.Precision.HIGHEST
    high = lax.Precision.HIGH
    operator = operators[0]
    basis = modes[0]
    target = gap[0]
    mult = start_mult[0]
    peers = peer_list[0, :, 0]
    rows_wanted = partner_row[0]
    order = operator.shape[0]
    shared = peers.shape[0]
    count = basis.shape[0]
    cap = 2 * shared // wide
    same = peers[:, None] == peers[None, :]
    earlier = lax.iota(jnp.int32, shared)[None, :] < lax.iota(jnp.int32, shared)[:, None]
    slot = jnp.sum((same & earlier).astype(jnp.int32), axis=1)
    place = peers * cap + slot
    hit = lax.iota(jnp.int32, wide * cap)[:, None] == place[None, :]
    asked = jnp.sum(jnp.where(hit, rows_wanted[None, :], 0), axis=1).reshape(wide, cap)
    given = lax.all_to_all(asked, "wide", 0, 0, tiled=True).reshape(-1)
    active = (lax.iota(jnp.int32, order) < interface_size[0])[:, None]
    contact = (contact_rows[0] == 1)[:, None]
    residual = jnp.zeros_like(target)
    for outer in range(OUTER):
        for inner in range(INNER):
            image = jnp.dot(operator, mult, precision=high, preferred_element_type=jnp.float32)
            head = image[:shared]
            sent = head[given].reshape(wide, cap, -1)
            came = lax.all_to_all(sent, "wide", 0, 0, tiled=True).reshape(wide * cap, -1)
            across = came[place]
            jump = jnp.concatenate([head - across, image[shared:]], axis=0)
            residual = jnp.where(active, target - jump, 0.0)
            update = 0.3 * residual
            if inner == 0:
                coarse = jnp.dot(
                    basis, residual, precision=high, preferred_element_type=jnp.float32
                )
                gathered = lax.all_to_all(
                    jnp.broadcast_to(coarse[None], (wide,) + coarse.shape),
                    "wide", 0, 0, tiled=True,
                ).reshape(wide * count, -1)
                parts = jnp.dot(
                    coarse_inverse, gathered, precision=high, preferred_element_type=jnp.float32
                )

                solved = jnp.sum(
                    lax.all_to_all(
                        parts.reshape(narrow, count, -1), "narrow", 0, 0, tiled=True
                    ),
                    axis=0,
                )
                update = update + lax.dot_general(
                    basis,
                    solved,
                    (((0,), (0,)), ((), ())),
                    precision=high,
                    preferred_element_type=jnp.float32,
                )
            trial = mult + update
            mult = jnp.where(active, jnp.where(contact, jnp.maximum(trial, 0.0), trial), 0.0)
    return (mult[None], residual[None])


def solution(mesh):
    wide = mesh.shape["wide"]
    narrow = mesh.shape["narrow"]

    def body(*args):
        return local(wide, narrow, *args)

    return jax.shard_map(
        body,
        mesh=mesh,
        in_specs=(
            P(("groups", "wide", "narrow"), None, None),
            P(("groups", "wide"), "narrow"),
            P(("groups", "wide", "narrow"), None, None),
            P(("groups", "wide", "narrow"), None, None),
            P(("groups", "wide", "narrow"), None, None),
            P(("groups", "wide", "narrow"), None, None),
            P(("groups", "wide", "narrow"), None),
            P(("groups", "wide", "narrow")),
            P(("groups", "wide", "narrow"), None),
        ),
        out_specs=(
            P(("groups", "wide", "narrow"), None, None),
            P(("groups", "wide", "narrow"), None, None),
        ),
        check_vma=False,
    )
```

```python
import functools

import jax
import jax.numpy as jnp
from jax import lax
from jax.experimental import pallas as pl
from jax.experimental.pallas import tpu as pltpu
from jax.sharding import PartitionSpec as P

OUTER = 2
INNER = 3
STEP = 0.3
F32 = jnp.float32
BF16 = jnp.bfloat16
PARAMS = pltpu.CompilerParams(vmem_limit_bytes=24 * 1024 * 1024)


def split(value):
    high = value.astype(BF16)
    return high, (value - high.astype(F32)).astype(BF16)


def mm(left, right):
    return jnp.dot(left, right, preferred_element_type=F32)


def product(left, right):
    (left_high, left_low), (right_high, right_low) = left, right
    width = right_high.shape[1]
    both = mm(left_high, jnp.concatenate([right_high, right_low], axis=1))
    return both[:, :width] + (both[:, width:] + mm(left_low, right_high))


def pick(chosen, value):
    width = value.shape[1]
    high, rest = value.astype(BF16), None
    rest = value - high.astype(F32)
    middle = rest.astype(BF16)
    low = (rest - middle.astype(F32)).astype(BF16)
    parts = mm(chosen, jnp.concatenate([high, middle, low], axis=1))
    return (parts[:, :width] + parts[:, width:2 * width]) + parts[:, 2 * width:]


def live(size, start, rows, width):
    return lax.broadcasted_iota(jnp.int32, (rows, width), 0) + start < size


def call(body, ins, in_specs, outs, out_specs, scratch=(), grid=(1,), flops=0, moved=0, alias=None, name=None):
    return pl.pallas_call(
        body,
        out_shape=outs,
        grid_spec=pl.GridSpec(grid=grid, in_specs=in_specs, out_specs=out_specs, scratch_shapes=list(scratch)),
        compiler_params=PARAMS,
        cost_estimate=pl.CostEstimate(flops=flops, bytes_accessed=moved, transcendentals=0),
        input_output_aliases=alias or {},
        name=name,
    )(*ins)


def whole(shape):
    return pl.BlockSpec(shape, lambda *i: (0,) * len(shape))


def block(shape, at=0, across=False):
    if across:
        return pl.BlockSpec(shape, lambda i: (0, i + at))
    return pl.BlockSpec(shape, lambda i: (i + at, 0))


SMEM = pl.BlockSpec(memory_space=pltpu.SMEM)


def shape(rows, columns, dtype=F32):
    return jax.ShapeDtypeStruct((rows, columns), dtype)


def lists_kernel(cap, me, peers, rows, unpack, asked):
    shared = peers.shape[1]
    asked_width = asked.shape[1]
    across = jnp.broadcast_to(peers[...], (shared, shared))
    down = across.T
    first = lax.broadcasted_iota(jnp.int32, (shared, shared), 0)
    second = lax.broadcasted_iota(jnp.int32, (shared, shared), 1)
    slot = jnp.sum(
        jnp.where((across == down) & (second < first), 1.0, 0.0), axis=1, keepdims=True
    ).astype(jnp.int32)
    rows_down = jnp.broadcast_to(rows[...], (shared, shared)).T[:, :1]
    far = down[:, :1] ^ me[0]
    key = jnp.where(far == 0, rows_down, shared + (far - 1) * cap + slot)
    hit = key == lax.broadcasted_iota(jnp.int32, unpack.shape, 1)
    unpack[...] = jnp.where(hit, 1.0, 0.0).astype(BF16)
    asked[...] = jnp.sum(
        jnp.where(hit[:, shared:], rows_down.astype(F32), 0.0), axis=0, keepdims=True
    )[:, :asked_width]


def first_kernel(operator, mult, high, low, image):
    parts = split(operator[...])
    high[...], low[...] = parts
    image[...] = product(parts, split(mult[...]))


def pack_kernel(cap, given, image, pack, *sends):
    shared = image.shape[0]
    wanted = jnp.broadcast_to(given[...], (shared, given.shape[1])).T
    chosen = jnp.where(
        wanted == lax.broadcasted_iota(jnp.int32, pack.shape, 1).astype(F32), 1.0, 0.0
    ).astype(BF16)
    pack[...] = chosen
    send(cap, chosen, image[...], sends)


def send(cap, chosen, image, sends):
    picked = pick(chosen, image)
    for d, out in enumerate(sends):
        out[...] = picked[d * cap:(d + 1) * cap]


def arrived(recvs, image, unpack):
    blocks = [image] + [recv[...] for recv in recvs]
    rows = sum(b.shape[0] for b in blocks)
    if rows < unpack.shape[1]:
        blocks.append(jnp.zeros((unpack.shape[1] - rows, image.shape[1]), F32))
    return pick(unpack[...], jnp.concatenate(blocks, axis=0))


def settle(trial, floor, alive):
    return jnp.where(alive, jnp.maximum(trial, floor), 0.0)


def shared_residual(recvs, image, unpack, gap, size):
    own = image[...]
    jump = own - arrived(recvs, own, unpack)
    alive = live(size[0], 0, *own.shape)
    return jnp.where(alive, gap[...] - jump, 0.0), alive


def rest_first_kernel(given_parts, size, operator, *refs):
    if given_parts:
        low, mult_s, mult_n, mult_block, gap, modes, trial, coarse, halves = refs
        parts = operator[...], low[...]
    else:
        mult_s, mult_n, mult_block, gap, modes, trial, coarse, high, low, halves = refs
        parts = split(operator[...])
        high[...], low[...] = parts
    step = pl.program_id(0)
    rows, width = gap.shape
    fill_halves(step, mult_s, mult_n, halves)
    image = halved_product(parts, halves[...], width)
    alive = live(size[0], (step + 1) * rows, rows, width)
    residual = jnp.where(alive, gap[...] - image, 0.0)
    trial[...] = mult_block[...] + STEP * residual

    @pl.when(step == 0)
    def _():
        coarse[...] = jnp.zeros_like(coarse)

    coarse[...] += product(split(modes[...]), split(residual))


def fill_halves(step, mult_s, mult_n, halves):
    @pl.when(step == 0)
    def _():
        shared, width = mult_s.shape
        high, low = split(mult_s[...])
        halves[:shared, :width], halves[:shared, width:] = high, low
        high, low = split(mult_n[...])
        halves[shared:, :width], halves[shared:, width:] = high, low


def halved_product(parts, halves, width):
    both = mm(parts[0], halves)
    return both[:, :width] + (both[:, width:] + mm(parts[1], halves[:, :width]))


def rest_kernel(last, size, high, low, mult_s, mult_n, mult_block, gap, floor, *refs):
    halves = refs[-1]
    step = pl.program_id(0)
    rows, width = gap.shape
    fill_halves(step, mult_s, mult_n, halves)
    image = halved_product((high[...], low[...]), halves[...], width)
    alive = live(size[0], (step + 1) * rows, rows, width)
    residual = jnp.where(alive, gap[...] - image, 0.0)
    mult = settle(mult_block[...] + STEP * residual, floor[...], alive)
    if last:
        mult_out, residual_out, _ = refs
        mult_out[...] = mult
        residual_out[...] = residual
    else:
        across_high, across_low, mult_out, ahead, _ = refs
        mult_out[...] = mult

        @pl.when(step == 0)
        def _():
            ahead[...] = jnp.zeros_like(ahead)

        ahead[...] += product((across_high[...], across_low[...]), split(mult))


def coarse_kernel(n, size, *refs):
    recvs = refs[:n]
    image, unpack, gap, mult, modes, started, coarse, trial = refs[n:]
    residual, _ = shared_residual(recvs, image, unpack, gap, size)
    coarse[...] = started[...] + product(split(modes[...]), split(residual))
    trial[...] = mult[...] + STEP * residual


def tile_kernel(n, m, place, tile, *refs):
    blocks, outs, (gathered, parts) = refs[:n + 1], refs[n + 1:n + m + 2], refs[n + m + 2:]
    count = blocks[0].shape[0]
    for d, ref in enumerate(blocks):
        at = pl.multiple_of((place[0] ^ d) * count, count)
        gathered[pl.ds(at, count), :] = ref[...]
    parts[...] = product(split(tile[...]), split(gathered[...]))
    for d, out in enumerate(outs):
        at = pl.multiple_of((place[1] ^ d) * count, count)
        out[...] = parts[pl.ds(at, count), :]


def lift_kernel(n, m, cap, size, *refs):
    parts = refs[:m + 1]
    modes, trial_s, trial_n, floor, high, low, pack, mult_s, mult_n, image = refs[m + 1:m + 11]
    sends = refs[m + 11:]
    solved = parts[0][...]
    for part in parts[1:]:
        solved = solved + part[...]
    shared, width = trial_s.shape
    order = floor.shape[0]
    basis = modes[...].T
    lifted = product(split(basis), split(solved))
    alive = live(size[0], 0, order, width)
    first = settle(trial_s[...] + lifted[:shared], floor[:shared], alive[:shared])
    rest = settle(trial_n[...] + lifted[shared:], floor[shared:], alive[shared:])
    mult_s[...] = first
    mult_n[...] = rest
    value = product((high[...], low[...]), split(jnp.concatenate([first, rest], axis=0)))
    image[...] = value
    send(cap, pack[...], value, sends)


def sweep_kernel(n, cap, size, *refs):
    recvs = refs[:n]
    image, unpack, gap, mult, floor, high, low, ahead, pack, mult_out, image_out = refs[n:n + 11]
    sends = refs[n + 11:]
    residual, alive = shared_residual(recvs, image, unpack, gap, size)
    value = settle(mult[...] + STEP * residual, floor[...], alive)
    mult_out[...] = value
    value = ahead[...] + product((high[...], low[...]), split(value))
    image_out[...] = value
    send(cap, pack[...], value, sends)


def last_kernel(n, size, *refs):
    recvs = refs[:n]
    image, unpack, gap, mult, floor, _, _, mult_out, residual_out = refs[n:]
    residual, alive = shared_residual(recvs, image, unpack, gap, size)
    mult_out[...] = settle(mult[...] + STEP * residual, floor[...], alive)
    residual_out[...] = residual


def swap(block, axis, count, d):
    return lax.ppermute(block, axis, [(i, i ^ d) for i in range(count)])


def distances(count):
    return sorted(range(1, count), reverse=True)


def swap_all(blocks, axis, count):
    got = {d: swap(blocks[d - 1], axis, count, d) for d in distances(count)}
    return [got[d] for d in range(1, count)]


def local(
    wide,
    narrow,
    operators,
    coarse_inverse,
    modes,
    gap,
    start_mult,
    peer_list,
    partner_row,
    interface_size,
    contact_rows,
):
    operator = operators[0]
    modes = modes[0]
    gap = gap[0]
    mult = start_mult[0]
    order, loads = mult.shape
    shared = partner_row.shape[1]
    count = modes.shape[0]
    rest = order - shared
    steps = rest // shared
    n, m = wide - 1, narrow - 1
    cap = 2 * shared // wide
    listed = n * cap
    padded = -(-listed // 128) * 128
    place = jnp.stack([lax.axis_index("wide"), lax.axis_index("narrow")]).astype(jnp.int32)
    size = interface_size
    floor = jnp.broadcast_to(
        jnp.where(contact_rows[0] == 1, 0.0, -jnp.inf).astype(F32)[:, None], (order, loads)
    )
    top = whole((shared, loads))
    sent = [shape(cap, loads)] * n
    sent_specs = [whole((cap, loads))] * n
    full = 2 * order * loads

    unpack, asked = call(
        functools.partial(lists_kernel, cap),
        (place, peer_list[0].reshape(1, shared), partner_row),
        [SMEM, whole((1, shared)), whole((1, shared))],
        [shape(shared, shared + padded, BF16), shape(1, listed)],
        [whole((shared, shared + padded)), whole((1, listed))],
        moved=shared * padded * 2,
        name="lists",
    )
    given = swap_all([asked[:, d * cap:(d + 1) * cap] for d in range(n)], "wide", wide)
    given = jnp.pad(jnp.concatenate(given, axis=1), ((0, 0), (0, padded - listed)))
    top_high, top_low, image = call(
        first_kernel,
        (operator, mult),
        [whole((shared, order)), whole((order, loads))],
        [shape(shared, order, BF16)] * 2 + [shape(shared, loads)],
        [whole((shared, order))] * 2 + [top],
        flops=3 * full * shared,
        moved=8 * shared * order,
        name="first",
    )
    pack, *sends = call(
        functools.partial(pack_kernel, cap),
        (given, image),
        [whole((1, padded)), top],
        [shape(padded, shared, BF16)] + sent,
        [whole((padded, shared))] + sent_specs,
        flops=6 * padded * shared * loads,
        moved=4 * padded * shared,
        name="pack",
    )
    mult_s, mult_n = mult[:shared], mult[shared:]
    unpack_spec = whole(unpack.shape)
    pack_spec = whole(pack.shape)
    high = low = None
    for outer in range(OUTER):
        recvs = swap_all(sends, "wide", wide)
        rest_ins = (mult_s, mult_n, mult_n, gap, modes)
        rest_specs = [
            top,
            whole((rest, loads)),
            block((shared, loads)),
            block((shared, loads), 1),
            block((count, shared), 1, across=True),
        ]
        rest_outs = [shape(rest, loads), shape(count, loads)]
        rest_out_specs = [block((shared, loads)), whole((count, loads))]
        row_block = block((shared, order))
        if high is None:
            ins, specs = (size, operator), [SMEM, block((shared, order), 1)]
            rest_outs = rest_outs + [shape(rest, order, BF16)] * 2
            rest_out_specs = rest_out_specs + [row_block] * 2
        else:
            ins, specs = (size, high, low), [SMEM, row_block, row_block]
        trial_n, started, *parts = call(
            functools.partial(rest_first_kernel, high is not None),
            ins + rest_ins,
            specs + rest_specs,
            rest_outs,
            rest_out_specs,
            scratch=[pltpu.VMEM((order, 2 * loads), BF16)],
            grid=(steps,),
            flops=3 * full * rest,
            moved=4 * rest * order,
            name="rest_first",
        )
        if parts:
            high, low = parts
        coarse, trial_s = call(
            functools.partial(coarse_kernel, n),
            (size, *recvs, image, unpack, gap, mult_s, modes, started),
            [SMEM] + sent_specs
            + [top, unpack_spec, top, top, whole((count, shared)), whole((count, loads))],
            [shape(count, loads), shape(shared, loads)],
            [whole((count, loads)), top],
            flops=6 * shared * loads * unpack.shape[1],
            moved=2 * shared * unpack.shape[1],
            name="coarse",
        )
        blocks = [coarse] + swap_all([coarse] * n, "wide", wide)
        part_spec = whole((count, loads))
        own, *parts = call(
            functools.partial(tile_kernel, n, m),
            (place, coarse_inverse, *blocks),
            [SMEM, whole(coarse_inverse.shape)] + [part_spec] * wide,
            [shape(count, loads)] * narrow,
            [part_spec] * narrow,
            scratch=[
                pltpu.VMEM((wide * count, loads), F32),
                pltpu.VMEM((narrow * count, loads), F32),
            ],
            flops=6 * coarse_inverse.size * loads,
            moved=4 * coarse_inverse.size,
            name="tile",
        )
        parts = [own] + swap_all(parts, "narrow", narrow)
        mult_s, mult_n, image, *sends = call(
            functools.partial(lift_kernel, n, m, cap),
            (size, *parts, modes, trial_s, trial_n, floor, top_high, top_low, pack),
            [SMEM] + [part_spec] * narrow
            + [whole(modes.shape), top, whole((rest, loads)), whole((order, loads))]
            + [whole((shared, order))] * 2 + [pack_spec],
            [shape(shared, loads), shape(rest, loads), shape(shared, loads)] + sent,
            [top, whole((rest, loads)), top] + sent_specs,
            flops=3 * full * shared,
            moved=4 * order * shared,
            name="lift",
        )
        for inner in range(1, INNER):
            last = outer == OUTER - 1 and inner == INNER - 1
            recvs = swap_all(sends, "wide", wide)
            ins = (size, high, low, mult_s, mult_n, mult_n, gap, floor)
            specs = [
                SMEM,
                row_block,
                row_block,
                top,
                whole((rest, loads)),
                block((shared, loads)),
                block((shared, loads), 1),
                block((shared, loads), 1),
            ]
            if last:
                outs = [shape(order, loads)] * 2
                out_specs = [block((shared, loads), 1)] * 2
            else:
                ins = ins + (top_high, top_low)
                specs = specs + [block((shared, shared), 1, across=True)] * 2
                outs = [shape(rest, loads), shape(shared, loads)]
                out_specs = [block((shared, loads)), top]
            rest_got = call(
                functools.partial(rest_kernel, last),
                ins,
                specs,
                outs,
                out_specs,
                scratch=[pltpu.VMEM((order, 2 * loads), BF16)],
                grid=(steps,),
                flops=3 * full * order,
                moved=4 * order * order,
                name="rest",
            )
            ins = (size, *recvs, image, unpack, gap, mult_s, floor)
            specs = [SMEM] + sent_specs + [top, unpack_spec, top, top, top]
            if last:
                return tuple(
                    out[None]
                    for out in call(
                        functools.partial(last_kernel, n),
                        ins + tuple(rest_got),
                        specs + [pl.BlockSpec(memory_space=pl.ANY)] * 2,
                        [shape(order, loads)] * 2,
                        [top] * 2,
                        alias={len(ins): 0, len(ins) + 1: 1},
                        flops=6 * shared * loads * unpack.shape[1],
                        moved=2 * shared * unpack.shape[1],
                        name="last",
                    )
                )
            mult_n, ahead = rest_got
            square = whole((shared, shared))
            mult_s, image, *sends = call(
                functools.partial(sweep_kernel, n, cap),
                ins + (top_high, top_low, ahead, pack),
                specs + [square, square, top, pack_spec],
                [shape(shared, loads)] * 2 + sent,
                [top] * 2 + sent_specs,
                flops=12 * shared * loads * unpack.shape[1],
                moved=4 * shared * unpack.shape[1],
                name="sweep",
            )


def solution(mesh):
    wide = mesh.shape["wide"]
    narrow = mesh.shape["narrow"]

    def body(*args):
        return local(wide, narrow, *args)

    return jax.shard_map(
        body,
        mesh=mesh,
        in_specs=(
            P(("groups", "wide", "narrow"), None, None),
            P(("groups", "wide"), "narrow"),
            P(("groups", "wide", "narrow"), None, None),
            P(("groups", "wide", "narrow"), None, None),
            P(("groups", "wide", "narrow"), None, None),
            P(("groups", "wide", "narrow"), None, None),
            P(("groups", "wide", "narrow"), None),
            P(("groups", "wide", "narrow")),
            P(("groups", "wide", "narrow"), None),
        ),
        out_specs=(
            P(("groups", "wide", "narrow"), None, None),
            P(("groups", "wide", "narrow"), None, None),
        ),
        check_vma=False,
    )
```

```python
import functools

import jax
import jax.numpy as jnp
from jax import lax
from jax.experimental import pallas as pl
from jax.experimental.pallas import tpu as pltpu
from jax.sharding import PartitionSpec as P

OUTER = 2
INNER = 3
STEP = 0.3
LEADS = ((1, 3), (3, 1), (1, 2), (2, 1))
F32 = jnp.float32
BF16 = jnp.bfloat16
PARAMS = pltpu.CompilerParams(vmem_limit_bytes=24 * 1024 * 1024)


def split(value):
    high = value.astype(BF16)
    return high, (value - high.astype(F32)).astype(BF16)


def mm(left, right):
    return jnp.dot(left, right, preferred_element_type=F32)


def product(left, right):
    (left_high, left_low), (right_high, right_low) = left, right
    width = right_high.shape[1]
    both = mm(left_high, jnp.concatenate([right_high, right_low], axis=1))
    return both[:, :width] + (both[:, width:] + mm(left_low, right_high))


def pick(chosen, value):
    width = value.shape[1]
    both = mm(chosen, jnp.concatenate(split(value), axis=1))
    return both[:, :width] + both[:, width:]


def live(size, start, rows, width):
    return lax.broadcasted_iota(jnp.int32, (rows, width), 0) + start < size


def call(body, ins, in_specs, outs, out_specs, scratch=(), grid=(1,), flops=0, moved=0, alias=None, name=None):
    return pl.pallas_call(
        body,
        out_shape=outs,
        grid_spec=pl.GridSpec(grid=grid, in_specs=in_specs, out_specs=out_specs, scratch_shapes=list(scratch)),
        compiler_params=PARAMS,
        cost_estimate=pl.CostEstimate(flops=flops, bytes_accessed=moved, transcendentals=0),
        input_output_aliases=alias or {},
        name=name,
    )(*ins)


def whole(shape):
    return pl.BlockSpec(shape, lambda *i: (0,) * len(shape))


def block(shape, at=0, across=False):
    if across:
        return pl.BlockSpec(shape, lambda i: (0, i + at))
    return pl.BlockSpec(shape, lambda i: (i + at, 0))


SMEM = pl.BlockSpec(memory_space=pltpu.SMEM)
HBM = pl.BlockSpec(memory_space=pltpu.HBM)


def shape(rows, columns, dtype=F32):
    return jax.ShapeDtypeStruct((rows, columns), dtype)


def first_kernel(wide, cap, peers_at, rows_at, operator_at, mult_at, *refs):
    unpack_all, unpack, high, low, image = refs[:5]
    sends, (peers, rows, operator, mult, done) = refs[5:4 + wide], refs[4 + wide:]
    shared, width = image.shape
    copies = [
        pltpu.make_async_copy(source, target, done.at[i])
        for i, (source, target) in enumerate(
            ((peers_at, peers), (rows_at, rows), (mult_at, mult), (operator_at.at[pl.ds(0, shared)], operator))
        )
    ]
    for copy in copies:
        copy.start()
    copies[0].wait()
    copies[1].wait()
    across = jnp.broadcast_to(peers[...], (shared, shared))
    down = across.T
    first = lax.broadcasted_iota(jnp.int32, (shared, shared), 0)
    second = lax.broadcasted_iota(jnp.int32, (shared, shared), 1)
    slot = jnp.sum(
        jnp.where((across == down) & (second < first), 1.0, 0.0), axis=1, keepdims=True
    ).astype(jnp.int32)
    wanted = jnp.broadcast_to(rows[...], (shared, shared)).T[:, :1]
    far = down[:, :1] ^ lax.axis_index("wide")

    def marks(key, columns):
        hit = key == lax.broadcasted_iota(jnp.int32, (shared, columns), 1)
        return jnp.where(hit, 1.0, 0.0).astype(BF16)

    unpack_all[...] = marks(far * shared + wanted, unpack_all.shape[1])
    unpack[...] = marks(
        jnp.where(far == 0, wanted, shared + (far - 1) * cap + slot), unpack.shape[1]
    )
    lane = lax.broadcasted_iota(jnp.int32, (shared, width), 1)
    for d, out in enumerate(sends, 1):
        out[shared:, :] = jnp.zeros((out.shape[0] - shared, width), F32)
        for c in range(-(-cap // width)):
            hit = (far == d) & (slot == lane + c * width)
            out[shared + c:shared + c + 1, :] = jnp.sum(
                jnp.where(hit, wanted.astype(F32), 0.0), axis=0, keepdims=True
            )
    copies[2].wait()
    copies[3].wait()
    parts = split(operator[...])
    high[...], low[...] = parts
    value = product(parts, split(mult[...]))
    image[...] = value
    for out in sends:
        out[:shared, :] = value


def pack_kernel(n, cap, *refs):
    recvs, pack = refs[:n], refs[n]
    shared = pack.shape[1]
    width = recvs[0].shape[1]
    column = lax.broadcasted_iota(jnp.int32, (width, shared), 1).astype(F32)
    if n * cap < pack.shape[0]:
        pack[n * cap:, :] = jnp.zeros((pack.shape[0] - n * cap, shared), BF16)
    for d, recv in enumerate(recvs):
        for c in range(-(-cap // width)):
            wanted = jnp.broadcast_to(recv[shared + c:shared + c + 1, :], (shared, width)).T
            chosen = jnp.where(wanted == column, 1.0, 0.0).astype(BF16)
            size = min(width, cap - c * width)
            pack[d * cap + c * width:d * cap + c * width + size, :] = chosen[:size]


def prepare_kernel(contact, modes, tile, floor, basis_high, basis_low, tile_high, tile_low):
    order, width = floor.shape
    for at in range(0, order, width):
        flag = jnp.broadcast_to(contact[:, at:at + width], (width, width)).T
        floor[at:at + width, :] = jnp.where(flag == 1, 0.0, -jnp.inf)
    basis_high[...], basis_low[...] = split(modes[...].T)
    tile_high[...], tile_low[...] = split(tile[...])


def send(cap, chosen, image, sends):
    picked = pick(chosen, image)
    for d, out in enumerate(sends):
        out[...] = picked[d * cap:(d + 1) * cap]


def arrived(recvs, image, unpack):
    shared = image.shape[0]
    blocks = [image] + [recv[...][:shared] for recv in recvs]
    rows = sum(b.shape[0] for b in blocks)
    if rows < unpack.shape[1]:
        blocks.append(jnp.zeros((unpack.shape[1] - rows, image.shape[1]), F32))
    return pick(unpack[...], jnp.concatenate(blocks, axis=0))


def settle(trial, floor, alive):
    return jnp.where(alive, jnp.maximum(trial, floor), 0.0)


def shared_residual(recvs, image, unpack, gap, size):
    own = image[...]
    jump = own - arrived(recvs, own, unpack)
    alive = live(size[0], 0, *own.shape)
    return jnp.where(alive, gap[...] - jump, 0.0), alive


def rest_first_kernel(pieces, given_parts, size, operator, *refs):
    if given_parts:
        low, refs = refs[0], refs[1:]
    mults, (mult_block, gap, modes, trial, coarse), outs = refs[:pieces], refs[pieces:pieces + 5], refs[pieces + 5:]
    halves = outs[-1]
    if given_parts:
        parts = operator[...], low[...]
    else:
        parts = split(operator[...])
        outs[0][...], outs[1][...] = parts
    step = pl.program_id(0)
    rows, width = gap.shape
    fill_halves(step, mults, halves)
    image = halved_product(parts, halves[...], width)
    alive = live(size[0], (step + 1) * rows, rows, width)
    residual = jnp.where(alive, gap[...] - image, 0.0)
    trial[...] = mult_block[...] + STEP * residual

    @pl.when(step == 0)
    def _():
        coarse[...] = jnp.zeros_like(coarse)

    coarse[...] += product(split(modes[...]), split(residual))


def fill_halves(step, mults, halves):
    @pl.when(step == 0)
    def _():
        at = 0
        for mult in mults:
            rows, width = mult.shape
            halves[at:at + rows, :width], halves[at:at + rows, width:] = split(mult[...])
            at += rows


def halved_product(parts, halves, width):
    both = mm(parts[0], halves)
    return both[:, :width] + (both[:, width:] + mm(parts[1], halves[:, :width]))


def rest_kernel(last, size, high, low, mult_s, mult_n, mult_block, gap, floor, *refs):
    halves = refs[-1]
    step = pl.program_id(0)
    rows, width = gap.shape
    fill_halves(step, (mult_s, mult_n), halves)
    image = halved_product((high[...], low[...]), halves[...], width)
    alive = live(size[0], (step + 1) * rows, rows, width)
    residual = jnp.where(alive, gap[...] - image, 0.0)
    mult = settle(mult_block[...] + STEP * residual, floor[...], alive)
    if last:
        mult_out, residual_out, _ = refs
        mult_out[...] = mult
        residual_out[...] = residual
    else:
        across_high, across_low, mult_out, ahead, _ = refs
        mult_out[...] = mult

        @pl.when(step == 0)
        def _():
            ahead[...] = jnp.zeros_like(ahead)

        ahead[...] += product((across_high[...], across_low[...]), split(mult))


def coarse_kernel(n, size, *refs):
    recvs = refs[:n]
    image, unpack, gap, mult, modes, started, trial = refs[n:n + 7]
    residual, _ = shared_residual(recvs, image, unpack, gap, size)
    coarse = started[...] + product(split(modes[...]), split(residual))
    for out in refs[n + 7:]:
        out[...] = coarse
    trial[...] = mult[...] + STEP * residual


def tile_kernel(n, m, high, low, *refs):
    blocks, outs, (gathered, parts) = refs[:n + 1], refs[n + 1:n + m + 2], refs[n + m + 2:]
    count = blocks[0].shape[0]
    for d, ref in enumerate(blocks):
        at = pl.multiple_of((lax.axis_index("wide") ^ d) * count, count)
        gathered[pl.ds(at, count), :] = ref[...]
    parts[...] = product((high[...], low[...]), split(gathered[...]))
    for d, out in enumerate(outs):
        at = pl.multiple_of((lax.axis_index("narrow") ^ d) * count, count)
        out[...] = parts[pl.ds(at, count), :]


def lift_kernel(n, m, cap, size, *refs):
    parts = refs[:m + 1]
    ins, (mult_s, mult_n, image), sends = refs[m + 1:m + 9], refs[m + 9:m + 12], refs[m + 12:]
    basis_high, basis_low, trial_s, trial_n, floor, high, low, pack = ins
    solved = parts[0][...]
    for part in parts[1:]:
        solved = solved + part[...]
    shared, width = trial_s.shape
    order = floor.shape[0]
    lifted = product((basis_high[...], basis_low[...]), split(solved))
    alive = live(size[0], 0, order, width)
    first = settle(trial_s[...] + lifted[:shared], floor[:shared], alive[:shared])
    rest = settle(trial_n[...] + lifted[shared:], floor[shared:], alive[shared:])
    mult_s[...] = first
    mult_n[...] = rest
    value = product((high[...], low[...]), split(jnp.concatenate([first, rest], axis=0)))
    image[...] = value
    send(cap, pack[...], value, sends)


def sweep_kernel(n, cap, size, *refs):
    recvs = refs[:n]
    image, unpack, gap, mult, floor, high, low, ahead, pack, mult_out, image_out = refs[n:n + 11]
    sends = refs[n + 11:]
    residual, alive = shared_residual(recvs, image, unpack, gap, size)
    value = settle(mult[...] + STEP * residual, floor[...], alive)
    mult_out[...] = value
    value = ahead[...] + product((high[...], low[...]), split(value))
    image_out[...] = value
    send(cap, pack[...], value, sends)


def last_kernel(n, size, *refs):
    recvs = refs[:n]
    image, unpack, gap, mult, floor, _, _, mult_out, residual_out = refs[n:]
    residual, alive = shared_residual(recvs, image, unpack, gap, size)
    mult_out[...] = settle(mult[...] + STEP * residual, floor[...], alive)
    residual_out[...] = residual


def swap(block, axis, count, d):
    return lax.ppermute(block, axis, [(i, i ^ d) for i in range(count)])


def swap_all(blocks, axis, count, lead=()):
    lead = [d for d in lead if d < count]
    order = lead + [d for d in range(count - 1, 0, -1) if d not in lead]
    got = {d: swap(blocks[d - 1], axis, count, d) for d in order}
    return [got[d] for d in range(1, count)]


def local(
    wide,
    narrow,
    operators,
    coarse_inverse,
    modes,
    gap,
    start_mult,
    peer_list,
    partner_row,
    interface_size,
    contact_rows,
):
    operator = operators[0]
    modes = modes[0]
    gap = gap[0]
    mult = start_mult[0]
    order, loads = mult.shape
    shared = partner_row.shape[1]
    count = modes.shape[0]
    rest = order - shared
    steps = rest // shared
    n, m = wide - 1, narrow - 1
    cap = 2 * shared // wide
    listed = n * cap
    padded = -(-listed // 128) * 128
    size = interface_size
    top = whole((shared, loads))
    sent = [shape(cap, loads)] * n
    sent_specs = [whole((cap, loads))] * n
    full = 2 * order * loads

    list_rows = -(-(-(-cap // loads)) // 8) * 8
    unpack_all, unpack, top_high, top_low, image, *sends = call(
        functools.partial(first_kernel, wide, cap),
        (peer_list[0].reshape(1, shared), partner_row, operator, mult),
        [HBM] * 4,
        [shape(shared, wide * shared, BF16), shape(shared, shared + padded, BF16)]
        + [shape(shared, order, BF16)] * 2
        + [shape(shared, loads)]
        + [shape(shared + list_rows, loads)] * n,
        [whole((shared, wide * shared)), whole((shared, shared + padded))]
        + [whole((shared, order))] * 2
        + [top]
        + [whole((shared + list_rows, loads))] * n,
        scratch=[
            pltpu.VMEM((1, shared), jnp.int32),
            pltpu.VMEM((1, shared), jnp.int32),
            pltpu.VMEM((shared, order), F32),
            pltpu.VMEM((order, loads), F32),
            pltpu.SemaphoreType.DMA((4,)),
        ],
        flops=3 * full * shared,
        moved=8 * shared * order,
        name="first",
    )
    floor, basis_high, basis_low, tile_high, tile_low = call(
        prepare_kernel,
        (contact_rows, modes, coarse_inverse),
        [whole((1, order)), whole(modes.shape), whole(coarse_inverse.shape)],
        [shape(order, loads)] + [shape(order, count, BF16)] * 2 + [shape(*coarse_inverse.shape, BF16)] * 2,
        [whole((order, loads))] + [whole((order, count))] * 2 + [whole(coarse_inverse.shape)] * 2,
        flops=full * count,
        moved=8 * coarse_inverse.size + 4 * full,
        name="prepare",
    )
    mults, mult_s = (mult,), mult
    unpack_spec = whole(unpack.shape)
    for outer in range(OUTER):
        start = outer == 0
        recvs = swap_all(sends, "wide", wide, (1,))
        recv_spec = whole(sends[0].shape)
        rest_ins = (*mults, mults[-1], gap, modes)
        rest_specs = [whole(piece.shape) for piece in mults] + [
            block((shared, loads), 1 if start else 0),
            block((shared, loads), 1),
            block((count, shared), 1, across=True),
        ]
        rest_outs = [shape(rest, loads), shape(count, loads)]
        rest_out_specs = [block((shared, loads)), whole((count, loads))]
        row_block = block((shared, order))
        if start:
            ins, specs = (size, operator), [SMEM, block((shared, order), 1)]
            rest_outs = rest_outs + [shape(rest, order, BF16)] * 2
            rest_out_specs = rest_out_specs + [row_block] * 2
        else:
            ins, specs = (size, high, low), [SMEM, row_block, row_block]
        trial_n, started, *parts = call(
            functools.partial(rest_first_kernel, len(mults), not start),
            ins + rest_ins,
            specs + rest_specs,
            rest_outs,
            rest_out_specs,
            scratch=[pltpu.VMEM((order, 2 * loads), BF16)],
            grid=(steps,),
            flops=3 * full * rest,
            moved=4 * rest * order,
            name="rest_first",
        )
        marks = unpack
        if start:
            high, low = parts
            marks = unpack_all
            pack = call(
                functools.partial(pack_kernel, n, cap),
                tuple(recvs),
                [recv_spec] * n,
                [shape(padded, shared, BF16)],
                [whole((padded, shared))],
                flops=full,
                moved=4 * padded * shared,
                name="pack",
            )[0]
            pack_spec = whole(pack.shape)
        trial_s, own, *coarse = call(
            functools.partial(coarse_kernel, n),
            (size, *recvs, image, marks, gap, mult_s, modes, started),
            [SMEM] + [recv_spec] * n
            + [top, whole(marks.shape), top, top, whole((count, shared)), whole((count, loads))],
            [shape(shared, loads)] + [shape(count, loads)] * wide,
            [top] + [whole((count, loads))] * wide,
            flops=6 * shared * loads * unpack.shape[1],
            moved=2 * shared * unpack.shape[1],
            name="coarse",
        )
        blocks = [own] + swap_all(coarse, "wide", wide, (3, 2) if start else (2, 3))
        part_spec = whole((count, loads))
        own, *parts = call(
            functools.partial(tile_kernel, n, m),
            (tile_high, tile_low, *blocks),
            [whole(coarse_inverse.shape)] * 2 + [part_spec] * wide,
            [shape(count, loads)] * narrow,
            [part_spec] * narrow,
            scratch=[
                pltpu.VMEM((wide * count, loads), F32),
                pltpu.VMEM((narrow * count, loads), F32),
            ],
            flops=6 * coarse_inverse.size * loads,
            moved=4 * coarse_inverse.size,
            name="tile",
        )
        parts = [own] + swap_all(parts, "narrow", narrow, (1, 2) if start else (1, 3))
        mult_s, mult_n, image, *sends = call(
            functools.partial(lift_kernel, n, m, cap),
            (size, *parts, basis_high, basis_low, trial_s, trial_n, floor, top_high, top_low, pack),
            [SMEM] + [part_spec] * narrow
            + [whole((order, count))] * 2 + [top, whole((rest, loads)), whole((order, loads))]
            + [whole((shared, order))] * 2 + [pack_spec],
            [shape(shared, loads), shape(rest, loads), shape(shared, loads)] + sent,
            [top, whole((rest, loads)), top] + sent_specs,
            flops=3 * full * shared,
            moved=4 * order * shared,
            name="lift",
        )
        for inner in range(1, INNER):
            last = outer == OUTER - 1 and inner == INNER - 1
            recvs = swap_all(sends, "wide", wide, LEADS[2 * outer + inner - 1])
            ins = (size, high, low, mult_s, mult_n, mult_n, gap, floor)
            specs = [
                SMEM,
                row_block,
                row_block,
                top,
                whole((rest, loads)),
                block((shared, loads)),
                block((shared, loads), 1),
                block((shared, loads), 1),
            ]
            if last:
                outs = [shape(order, loads)] * 2
                out_specs = [block((shared, loads), 1)] * 2
            else:
                ins = ins + (top_high, top_low)
                specs = specs + [block((shared, shared), 1, across=True)] * 2
                outs = [shape(rest, loads), shape(shared, loads)]
                out_specs = [block((shared, loads)), top]
            rest_got = call(
                functools.partial(rest_kernel, last),
                ins,
                specs,
                outs,
                out_specs,
                scratch=[pltpu.VMEM((order, 2 * loads), BF16)],
                grid=(steps,),
                flops=3 * full * order,
                moved=4 * order * order,
                name="rest",
            )
            ins = (size, *recvs, image, unpack, gap, mult_s, floor)
            specs = [SMEM] + sent_specs + [top, unpack_spec, top, top, top]
            if last:
                return tuple(
                    out[None]
                    for out in call(
                        functools.partial(last_kernel, n),
                        ins + tuple(rest_got),
                        specs + [pl.BlockSpec(memory_space=pl.ANY)] * 2,
                        [shape(order, loads)] * 2,
                        [top] * 2,
                        alias={len(ins): 0, len(ins) + 1: 1},
                        flops=6 * shared * loads * unpack.shape[1],
                        moved=2 * shared * unpack.shape[1],
                        name="last",
                    )
                )
            mult_n, ahead = rest_got
            square = whole((shared, shared))
            mult_s, image, *sends = call(
                functools.partial(sweep_kernel, n, cap),
                ins + (top_high, top_low, ahead, pack),
                specs + [square, square, top, pack_spec],
                [shape(shared, loads)] * 2 + sent,
                [top] * 2 + sent_specs,
                flops=12 * shared * loads * unpack.shape[1],
                moved=4 * shared * unpack.shape[1],
                name="sweep",
            )
            mults = mult_s, mult_n


def solution(mesh):
    wide = mesh.shape["wide"]
    narrow = mesh.shape["narrow"]

    def body(*args):
        return local(wide, narrow, *args)

    return jax.shard_map(
        body,
        mesh=mesh,
        in_specs=(
            P(("groups", "wide", "narrow"), None, None),
            P(("groups", "wide"), "narrow"),
            P(("groups", "wide", "narrow"), None, None),
            P(("groups", "wide", "narrow"), None, None),
            P(("groups", "wide", "narrow"), None, None),
            P(("groups", "wide", "narrow"), None, None),
            P(("groups", "wide", "narrow"), None),
            P(("groups", "wide", "narrow")),
            P(("groups", "wide", "narrow"), None),
        ),
        out_specs=(
            P(("groups", "wide", "narrow"), None, None),
            P(("groups", "wide", "narrow"), None, None),
        ),
        check_vma=False,
    )
```

```python
import functools

import jax
import jax.numpy as jnp
from jax import lax
from jax.experimental import pallas as pl
from jax.experimental.pallas import tpu as pltpu
from jax.sharding import PartitionSpec as P

OUTER = 2
INNER = 3
STEP = 0.3
F32 = jnp.float32
BF16 = jnp.bfloat16
PARAMS = pltpu.CompilerParams(vmem_limit_bytes=24 * 1024 * 1024)


def split(value):
    high = value.astype(BF16)
    return high, (value - high.astype(F32)).astype(BF16)


def mm(left, right):
    return jnp.dot(left, right, preferred_element_type=F32)


def product(left, right):
    (left_high, left_low), (right_high, right_low) = left, right
    width = right_high.shape[1]
    both = mm(left_high, jnp.concatenate([right_high, right_low], axis=1))
    return both[:, :width] + (both[:, width:] + mm(left_low, right_high))


def pick(chosen, value):
    width = value.shape[1]
    both = mm(chosen, jnp.concatenate(split(value), axis=1))
    return both[:, :width] + both[:, width:]


def live(size, start, rows, width):
    return lax.broadcasted_iota(jnp.int32, (rows, width), 0) + start < size


def call(body, ins, outs, in_specs=None, out_specs=None, scratch=(), grid=(), flops=0, moved=0, alias=None, name=None):
    if in_specs is None:
        in_specs = [SMEM if value.ndim == 1 else VMEM for value in ins]
    if out_specs is None:
        out_specs = [VMEM] * len(outs)
    return pl.pallas_call(
        body,
        out_shape=outs,
        grid=grid,
        in_specs=in_specs,
        out_specs=out_specs,
        scratch_shapes=list(scratch),
        compiler_params=PARAMS,
        cost_estimate=pl.CostEstimate(flops=flops, bytes_accessed=moved, transcendentals=0),
        input_output_aliases=alias or {},
        name=name,
    )(*ins)


def whole(shape):
    return pl.BlockSpec(shape, lambda *i: (0,) * len(shape))


def block(shape, at=0, across=False):
    if across:
        return pl.BlockSpec(shape, lambda i: (0, i + at))
    return pl.BlockSpec(shape, lambda i: (i + at, 0))


SMEM = pl.BlockSpec(memory_space=pltpu.SMEM)
HBM = pl.BlockSpec(memory_space=pltpu.HBM)
VMEM = pl.BlockSpec(memory_space=pltpu.VMEM)


def shape(rows, columns, dtype=F32):
    return jax.ShapeDtypeStruct((rows, columns), dtype)


def first_kernel(order, cap, peers_at, rows_at, operator_at, mult_at, *refs):
    unpack_all, unpack, high, low, image = refs[:5]
    n = len(order)
    sends, (peers, rows, operator, mult, done) = refs[5:5 + n], refs[5 + n:]
    shared, width = image.shape
    copies = [
        pltpu.make_async_copy(source, target, done.at[i])
        for i, (source, target) in enumerate(
            ((peers_at, peers), (rows_at, rows), (mult_at, mult), (operator_at.at[pl.ds(0, shared)], operator))
        )
    ]
    for copy in copies:
        copy.start()
    copies[0].wait()
    copies[1].wait()
    across = jnp.broadcast_to(peers[...], (shared, shared))
    down = across.T
    first = lax.broadcasted_iota(jnp.int32, (shared, shared), 0)
    second = lax.broadcasted_iota(jnp.int32, (shared, shared), 1)
    slot = jnp.sum(
        jnp.where((across == down) & (second < first), 1.0, 0.0), axis=1, keepdims=True
    ).astype(jnp.int32)
    wanted = jnp.broadcast_to(rows[...], (shared, shared)).T[:, :1]
    far = down[:, :1] ^ lax.axis_index("wide")
    at = jnp.zeros_like(far)
    for k, d in enumerate(order, 1):
        at = jnp.where(far == d, k, at)

    def marks(key, columns):
        hit = key == lax.broadcasted_iota(jnp.int32, (shared, columns), 1)
        return jnp.where(hit, 1.0, 0.0).astype(BF16)

    unpack_all[...] = marks(at * shared + wanted, unpack_all.shape[1])
    unpack[...] = marks(
        jnp.where(at == 0, wanted, shared + (at - 1) * cap + slot), unpack.shape[1]
    )
    lane = lax.broadcasted_iota(jnp.int32, (shared, width), 1)
    for k, out in enumerate(sends, 1):
        out[shared:, :] = jnp.zeros((out.shape[0] - shared, width), F32)
        for c in range(-(-cap // width)):
            hit = (at == k) & (slot == lane + c * width)
            out[shared + c:shared + c + 1, :] = jnp.sum(
                jnp.where(hit, wanted.astype(F32), 0.0), axis=0, keepdims=True
            )
    copies[2].wait()
    copies[3].wait()
    parts = split(operator[...])
    high[...], low[...] = parts
    value = product(parts, split(mult[...]))
    image[...] = value
    for out in sends:
        out[:shared, :] = value


def pack_kernel(n, cap, *refs):
    recvs, pack = refs[:n], refs[n]
    shared = pack.shape[1]
    width = recvs[0].shape[1]
    column = lax.broadcasted_iota(jnp.int32, (width, shared), 1).astype(F32)
    if n * cap < pack.shape[0]:
        pack[n * cap:, :] = jnp.zeros((pack.shape[0] - n * cap, shared), BF16)
    for d, recv in enumerate(recvs):
        for c in range(-(-cap // width)):
            wanted = jnp.broadcast_to(recv[shared + c:shared + c + 1, :], (shared, width)).T
            chosen = jnp.where(wanted == column, 1.0, 0.0).astype(BF16)
            size = min(width, cap - c * width)
            pack[d * cap + c * width:d * cap + c * width + size, :] = chosen[:size]


def prepare_kernel(contact, modes, tile, floor, basis_high, basis_low, tile_high, tile_low):
    order, width = floor.shape
    for at in range(0, order, width):
        flag = jnp.broadcast_to(contact[:, at:at + width], (width, width)).T
        floor[at:at + width, :] = jnp.where(flag == 1, 0.0, -jnp.inf)
    basis_high[...], basis_low[...] = split(modes[...].T)
    tile_high[...], tile_low[...] = split(tile[...])


def send(cap, chosen, image, sends):
    picked = pick(chosen, image)
    for d, out in enumerate(sends):
        out[...] = picked[d * cap:(d + 1) * cap]


def arrived(recvs, image, unpack):
    shared = image.shape[0]
    blocks = [image] + [recv[...][:shared] for recv in recvs]
    rows = sum(b.shape[0] for b in blocks)
    if rows < unpack.shape[1]:
        blocks.append(jnp.zeros((unpack.shape[1] - rows, image.shape[1]), F32))
    return pick(unpack[...], jnp.concatenate(blocks, axis=0))


def settle(trial, floor, alive):
    return jnp.where(alive, jnp.maximum(trial, floor), 0.0)


def shared_residual(recvs, image, unpack, gap, size):
    own = image[...]
    jump = own - arrived(recvs, own, unpack)
    alive = live(size[0], 0, *own.shape)
    return jnp.where(alive, gap[:own.shape[0], :] - jump, 0.0), alive


def rest_first_kernel(pieces, given_parts, size, operator, *refs):
    if given_parts:
        low, refs = refs[0], refs[1:]
    mults, (mult_block, gap, modes, trial, coarse), outs = refs[:pieces], refs[pieces:pieces + 5], refs[pieces + 5:]
    halves = outs[-1]
    if given_parts:
        parts = operator[...], low[...]
    else:
        parts = split(operator[...])
        outs[0][...], outs[1][...] = parts
    step = pl.program_id(0)
    rows, width = gap.shape
    fill_halves(step, mults, halves)
    image = halved_product(parts, halves[...], width)
    alive = live(size[0], (step + 1) * rows, rows, width)
    residual = jnp.where(alive, gap[...] - image, 0.0)
    trial[...] = mult_block[...] + STEP * residual

    @pl.when(step == 0)
    def _():
        coarse[...] = jnp.zeros_like(coarse)

    coarse[...] += product(split(modes[...]), split(residual))


def fill_halves(step, mults, halves):
    @pl.when(step == 0)
    def _():
        at = 0
        for mult in mults:
            rows, width = mult.shape
            halves[at:at + rows, :width], halves[at:at + rows, width:] = split(mult[...])
            at += rows


def halved_product(parts, halves, width):
    both = mm(parts[0], halves)
    return both[:, :width] + (both[:, width:] + mm(parts[1], halves[:, :width]))


def rest_kernel(last, size, high, low, mult_s, mult_n, mult_block, gap, floor, *refs):
    halves = refs[-1]
    step = pl.program_id(0)
    rows, width = gap.shape
    fill_halves(step, (mult_s, mult_n), halves)
    image = halved_product((high[...], low[...]), halves[...], width)
    alive = live(size[0], (step + 1) * rows, rows, width)
    residual = jnp.where(alive, gap[...] - image, 0.0)
    mult = settle(mult_block[...] + STEP * residual, floor[...], alive)
    if last:
        mult_out, residual_out, _ = refs
        mult_out[...] = mult
        residual_out[...] = residual
    else:
        across_high, across_low, mult_out, ahead, _ = refs
        mult_out[...] = mult

        @pl.when(step == 0)
        def _():
            ahead[...] = jnp.zeros_like(ahead)

        ahead[...] += product((across_high[...], across_low[...]), split(mult))


def coarse_kernel(n, size, *refs):
    recvs = refs[:n]
    image, unpack, gap, mult, modes, started, trial = refs[n:n + 7]
    residual, _ = shared_residual(recvs, image, unpack, gap, size)
    coarse = started[...] + product(split(modes[:, :image.shape[0]]), split(residual))
    for out in refs[n + 7:]:
        out[...] = coarse
    trial[...] = mult[:image.shape[0], :] + STEP * residual


def tile_kernel(wide_order, narrow_order, high, low, *refs):
    n, m = len(wide_order), len(narrow_order)
    blocks, outs, (gathered, parts) = refs[:n + 1], refs[n + 1:n + m + 2], refs[n + m + 2:]
    count = blocks[0].shape[0]
    for d, ref in zip((0, *wide_order), blocks):
        at = pl.multiple_of((lax.axis_index("wide") ^ d) * count, count)
        gathered[pl.ds(at, count), :] = ref[...]
    parts[...] = product((high[...], low[...]), split(gathered[...]))
    for d, out in zip((0, *narrow_order), outs):
        at = pl.multiple_of((lax.axis_index("narrow") ^ d) * count, count)
        out[...] = parts[pl.ds(at, count), :]


def lift_kernel(n, m, cap, size, *refs):
    parts = refs[:m + 1]
    ins, (mult_s, mult_n, image), sends = refs[m + 1:m + 9], refs[m + 9:m + 12], refs[m + 12:]
    basis_high, basis_low, trial_s, trial_n, floor, high, low, pack = ins
    solved = parts[0][...]
    for part in parts[1:]:
        solved = solved + part[...]
    shared, width = trial_s.shape
    order = floor.shape[0]
    lifted = product((basis_high[...], basis_low[...]), split(solved))
    alive = live(size[0], 0, order, width)
    first = settle(trial_s[...] + lifted[:shared], floor[:shared], alive[:shared])
    rest = settle(trial_n[...] + lifted[shared:], floor[shared:], alive[shared:])
    mult_s[...] = first
    mult_n[...] = rest
    value = product((high[...], low[...]), split(jnp.concatenate([first, rest], axis=0)))
    image[...] = value
    send(cap, pack[...], value, sends)


def sweep_kernel(n, cap, size, *refs):
    recvs = refs[:n]
    image, unpack, gap, mult, floor, high, low, ahead, pack, mult_out, image_out = refs[n:n + 11]
    sends = refs[n + 11:]
    residual, alive = shared_residual(recvs, image, unpack, gap, size)
    shared = image.shape[0]
    value = settle(mult[...] + STEP * residual, floor[:shared, :], alive)
    mult_out[...] = value
    value = ahead[...] + product((high[:, :shared], low[:, :shared]), split(value))
    image_out[...] = value
    send(cap, pack[...], value, sends)


def last_kernel(n, size, *refs):
    recvs = refs[:n]
    image, unpack, gap, mult, floor, _, _, mult_out, residual_out, settled, left, done = refs[n:]
    shared = image.shape[0]
    residual, alive = shared_residual(recvs, image, unpack, gap, size)
    left[...] = residual
    first = pltpu.make_async_copy(left, residual_out.at[pl.ds(0, shared)], done.at[0])
    first.start()
    settled[...] = settle(mult[...] + STEP * residual, floor[:shared, :], alive)
    second = pltpu.make_async_copy(settled, mult_out.at[pl.ds(0, shared)], done.at[1])
    second.start()
    first.wait()
    second.wait()


def swap(block, axis, count, d):
    return lax.ppermute(block, axis, [(i, i ^ d) for i in range(count)])


def swap_all(blocks, axis, count, order):
    return [swap(block, axis, count, d) for block, d in zip(blocks, order)]


def middle_first(count):
    return (count - 1, *range(1, count - 1))


def far_first(count):
    return tuple(range(count - 1, 0, -1))


def local(
    wide,
    narrow,
    operators,
    coarse_inverse,
    modes,
    gap,
    start_mult,
    peer_list,
    partner_row,
    interface_size,
    contact_rows,
):
    operator = operators[0]
    modes = modes[0]
    gap = gap[0]
    mult = start_mult[0]
    order, loads = mult.shape
    shared = partner_row.shape[1]
    count = modes.shape[0]
    rest = order - shared
    steps = rest // shared
    n, m = wide - 1, narrow - 1
    cap = 2 * shared // wide
    listed = n * cap
    padded = -(-listed // 128) * 128
    size = interface_size
    rows_order, coarse_order, part_order = middle_first(wide), far_first(wide), far_first(narrow)
    top = whole((shared, loads))
    sent = [shape(cap, loads)] * n
    full = 2 * order * loads

    list_rows = -(-(-(-cap // loads)) // 8) * 8
    unpack_all, unpack, top_high, top_low, image, *sends = call(
        functools.partial(first_kernel, rows_order, cap),
        tuple(
            pltpu.with_memory_space_constraint(value, pltpu.HBM)
            for value in (peer_list[0].reshape(1, shared), partner_row, operator, mult)
        ),
        [shape(shared, wide * shared, BF16), shape(shared, shared + padded, BF16)]
        + [shape(shared, order, BF16)] * 2
        + [shape(shared, loads)]
        + [shape(shared + list_rows, loads)] * n,
        in_specs=[HBM] * 4,
        scratch=[
            pltpu.VMEM((1, shared), jnp.int32),
            pltpu.VMEM((1, shared), jnp.int32),
            pltpu.VMEM((shared, order), F32),
            pltpu.VMEM((order, loads), F32),
            pltpu.SemaphoreType.DMA((4,)),
        ],
        flops=3 * full * shared,
        moved=8 * shared * order,
        name="first",
    )
    floor, basis_high, basis_low, tile_high, tile_low = call(
        prepare_kernel,
        (contact_rows, modes, coarse_inverse),
        [shape(order, loads)] + [shape(order, count, BF16)] * 2 + [shape(*coarse_inverse.shape, BF16)] * 2,
        flops=full * count,
        moved=8 * coarse_inverse.size + 4 * full,
        name="prepare",
    )
    mults, mult_s = (mult,), mult
    for outer in range(OUTER):
        start = outer == 0
        recvs = swap_all(sends, "wide", wide, rows_order)
        rest_ins = (*mults, mults[-1], gap, modes)
        rest_specs = [whole(piece.shape) for piece in mults] + [
            block((shared, loads), 1 if start else 0),
            block((shared, loads), 1),
            block((count, shared), 1, across=True),
        ]
        rest_outs = [shape(rest, loads), shape(count, loads)]
        rest_out_specs = [block((shared, loads)), whole((count, loads))]
        row_block = block((shared, order))
        if start:
            ins, specs = (size, operator), [SMEM, block((shared, order), 1)]
            rest_outs = rest_outs + [shape(rest, order, BF16)] * 2
            rest_out_specs = rest_out_specs + [row_block] * 2
        else:
            ins, specs = (size, high, low), [SMEM, row_block, row_block]
        trial_n, started, *parts = call(
            functools.partial(rest_first_kernel, len(mults), not start),
            ins + rest_ins,
            rest_outs,
            specs + rest_specs,
            rest_out_specs,
            scratch=[pltpu.VMEM((order, 2 * loads), BF16)],
            grid=(steps,),
            flops=3 * full * rest,
            moved=4 * rest * order,
            name="rest_first",
        )
        marks = unpack
        if start:
            high, low = parts
            marks = unpack_all
            pack = call(
                functools.partial(pack_kernel, n, cap),
                tuple(recvs),
                [shape(padded, shared, BF16)],
                flops=full,
                moved=4 * padded * shared,
                name="pack",
            )[0]
        trial_s, own, *coarse = call(
            functools.partial(coarse_kernel, n),
            (size, *recvs, image, marks, gap, mult_s, modes, started),
            [shape(shared, loads)] + [shape(count, loads)] * wide,
            flops=6 * shared * loads * unpack.shape[1],
            moved=2 * shared * unpack.shape[1],
            name="coarse",
        )
        blocks = [own] + swap_all(coarse, "wide", wide, coarse_order)
        own, *parts = call(
            functools.partial(tile_kernel, coarse_order, part_order),
            (tile_high, tile_low, *blocks),
            [shape(count, loads)] * narrow,
            scratch=[
                pltpu.VMEM((wide * count, loads), F32),
                pltpu.VMEM((narrow * count, loads), F32),
            ],
            flops=6 * coarse_inverse.size * loads,
            moved=4 * coarse_inverse.size,
            name="tile",
        )
        parts = [own] + swap_all(parts, "narrow", narrow, part_order)
        mult_s, mult_n, image, *sends = call(
            functools.partial(lift_kernel, n, m, cap),
            (size, *parts, basis_high, basis_low, trial_s, trial_n, floor, top_high, top_low, pack),
            [shape(shared, loads), shape(rest, loads), shape(shared, loads)] + sent,
            flops=3 * full * shared,
            moved=4 * order * shared,
            name="lift",
        )
        for inner in range(1, INNER):
            last = outer == OUTER - 1 and inner == INNER - 1
            recvs = swap_all(sends, "wide", wide, rows_order)
            ins = (size, high, low, mult_s, mult_n, mult_n, gap, floor)
            specs = [
                SMEM,
                row_block,
                row_block,
                top,
                whole((rest, loads)),
                block((shared, loads)),
                block((shared, loads), 1),
                block((shared, loads), 1),
            ]
            if last:
                outs = [shape(order, loads)] * 2
                out_specs = [block((shared, loads), 1)] * 2
            else:
                ins = ins + (top_high, top_low)
                specs = specs + [block((shared, shared), 1, across=True)] * 2
                outs = [shape(rest, loads), shape(shared, loads)]
                out_specs = [block((shared, loads)), top]
            rest_got = call(
                functools.partial(rest_kernel, last),
                ins,
                outs,
                specs,
                out_specs,
                scratch=[pltpu.VMEM((order, 2 * loads), BF16)],
                grid=(steps,),
                flops=3 * full * order,
                moved=4 * order * order,
                name="rest",
            )
            ins = (size, *recvs, image, unpack, gap, mult_s, floor)
            if last:
                return tuple(
                    out[None]
                    for out in call(
                        functools.partial(last_kernel, n),
                        ins + tuple(rest_got),
                        [shape(order, loads)] * 2,
                        in_specs=[SMEM] + [VMEM] * (len(ins) - 1) + [HBM] * 2,
                        out_specs=[HBM] * 2,
                        scratch=[
                            pltpu.VMEM((shared, loads), F32),
                            pltpu.VMEM((shared, loads), F32),
                            pltpu.SemaphoreType.DMA((2,)),
                        ],
                        alias={len(ins): 0, len(ins) + 1: 1},
                        flops=6 * shared * loads * unpack.shape[1],
                        moved=2 * shared * unpack.shape[1],
                        name="last",
                    )
                )
            mult_n, ahead = rest_got
            mult_s, image, *sends = call(
                functools.partial(sweep_kernel, n, cap),
                ins + (top_high, top_low, ahead, pack),
                [shape(shared, loads)] * 2 + sent,
                flops=12 * shared * loads * unpack.shape[1],
                moved=4 * shared * unpack.shape[1],
                name="sweep",
            )
            mults = mult_s, mult_n


def solution(mesh):
    wide = mesh.shape["wide"]
    narrow = mesh.shape["narrow"]

    def body(*args):
        return local(wide, narrow, *args)

    return jax.shard_map(
        body,
        mesh=mesh,
        in_specs=(
            P(("groups", "wide", "narrow"), None, None),
            P(("groups", "wide"), "narrow"),
            P(("groups", "wide", "narrow"), None, None),
            P(("groups", "wide", "narrow"), None, None),
            P(("groups", "wide", "narrow"), None, None),
            P(("groups", "wide", "narrow"), None, None),
            P(("groups", "wide", "narrow"), None),
            P(("groups", "wide", "narrow")),
            P(("groups", "wide", "narrow"), None),
        ),
        out_specs=(
            P(("groups", "wide", "narrow"), None, None),
            P(("groups", "wide", "narrow"), None, None),
        ),
        check_vma=False,
    )
```

```python
import functools

import jax
import jax.numpy as jnp
from jax import lax
from jax.experimental import pallas as pl
from jax.experimental.pallas import tpu as pltpu
from jax.sharding import PartitionSpec as P

OUTER = 2
INNER = 3
STEP = 0.3
F32 = jnp.float32
BF16 = jnp.bfloat16
PARAMS = pltpu.CompilerParams(vmem_limit_bytes=24 * 1024 * 1024)


def split(value):
    high = value.astype(BF16)
    return high, (value - high.astype(F32)).astype(BF16)


def mm(left, right):
    return jnp.dot(left, right, preferred_element_type=F32)


def product(left, right):
    (left_high, left_low), (right_high, right_low) = left, right
    width = right_high.shape[1]
    both = mm(left_high, jnp.concatenate([right_high, right_low], axis=1))
    return both[:, :width] + (both[:, width:] + mm(left_low, right_high))


def pick(chosen, value):
    width = value.shape[1]
    both = mm(chosen, jnp.concatenate(split(value), axis=1))
    return both[:, :width] + both[:, width:]


def live(size, start, rows, width):
    return lax.broadcasted_iota(jnp.int32, (rows, width), 0) + start < size


def call(body, ins, outs, in_specs=None, out_specs=None, scratch=(), grid=(), flops=0, moved=0, alias=None, name=None):
    if in_specs is None:
        in_specs = [SMEM if value.ndim == 1 else VMEM for value in ins]
    if out_specs is None:
        out_specs = [VMEM] * len(outs)
    return pl.pallas_call(
        body,
        out_shape=outs,
        grid=grid,
        in_specs=in_specs,
        out_specs=out_specs,
        scratch_shapes=list(scratch),
        compiler_params=PARAMS,
        cost_estimate=pl.CostEstimate(flops=flops, bytes_accessed=moved, transcendentals=0),
        input_output_aliases=alias or {},
        name=name,
    )(*ins)


def whole(shape):
    return pl.BlockSpec(shape, lambda *i: (0,) * len(shape))


def block(shape, at=0, across=False):
    if across:
        return pl.BlockSpec(shape, lambda i: (0, i + at))
    return pl.BlockSpec(shape, lambda i: (i + at, 0))


SMEM = pl.BlockSpec(memory_space=pltpu.SMEM)
HBM = pl.BlockSpec(memory_space=pltpu.HBM)
VMEM = pl.BlockSpec(memory_space=pltpu.VMEM)


def shape(rows, columns, dtype=F32):
    return jax.ShapeDtypeStruct((rows, columns), dtype)


def first_kernel(orders, cap, peers_at, rows_at, operator_at, mult_at, *refs):
    unpack_all, unpack, high, low, image = refs[:5]
    n = len(orders[0])
    sends, (peers, rows, operator, mult, done) = refs[5:5 + n], refs[5 + n:]
    shared, width = image.shape
    copies = [
        pltpu.make_async_copy(source, target, done.at[i])
        for i, (source, target) in enumerate(
            ((peers_at, peers), (rows_at, rows), (mult_at, mult), (operator_at.at[pl.ds(0, shared)], operator))
        )
    ]
    for copy in copies:
        copy.start()
    copies[0].wait()
    copies[1].wait()
    across = jnp.broadcast_to(peers[...], (shared, shared))
    down = across.T
    first = lax.broadcasted_iota(jnp.int32, (shared, shared), 0)
    second = lax.broadcasted_iota(jnp.int32, (shared, shared), 1)
    slot = jnp.sum(
        jnp.where((across == down) & (second < first), 1.0, 0.0), axis=1, keepdims=True
    ).astype(jnp.int32)
    wanted = jnp.broadcast_to(rows[...], (shared, shared)).T[:, :1]
    far = down[:, :1] ^ lax.axis_index("wide")
    at = jnp.zeros_like(far)
    odd = lax.axis_index("narrow") % 2 == 1
    for k, (even_d, odd_d) in enumerate(zip(*orders), 1):
        at = jnp.where(far == jnp.where(odd, odd_d, even_d), k, at)

    def marks(key, columns):
        hit = key == lax.broadcasted_iota(jnp.int32, (shared, columns), 1)
        return jnp.where(hit, 1.0, 0.0).astype(BF16)

    unpack_all[...] = marks(at * shared + wanted, unpack_all.shape[1])
    unpack[...] = marks(
        jnp.where(at == 0, wanted, shared + (at - 1) * cap + slot), unpack.shape[1]
    )
    lane = lax.broadcasted_iota(jnp.int32, (shared, width), 1)
    for k, out in enumerate(sends, 1):
        out[shared:, :] = jnp.zeros((out.shape[0] - shared, width), F32)
        for c in range(-(-cap // width)):
            hit = (at == k) & (slot == lane + c * width)
            out[shared + c:shared + c + 1, :] = jnp.sum(
                jnp.where(hit, wanted.astype(F32), 0.0), axis=0, keepdims=True
            )
    copies[2].wait()
    copies[3].wait()
    parts = split(operator[...])
    high[...], low[...] = parts
    value = product(parts, split(mult[...]))
    image[...] = value
    for out in sends:
        out[:shared, :] = value


def pack_kernel(n, cap, *refs):
    recvs, pack = refs[:n], refs[n]
    shared = pack.shape[1]
    width = recvs[0].shape[1]
    column = lax.broadcasted_iota(jnp.int32, (width, shared), 1).astype(F32)
    if n * cap < pack.shape[0]:
        pack[n * cap:, :] = jnp.zeros((pack.shape[0] - n * cap, shared), BF16)
    for d, recv in enumerate(recvs):
        for c in range(-(-cap // width)):
            wanted = jnp.broadcast_to(recv[shared + c:shared + c + 1, :], (shared, width)).T
            chosen = jnp.where(wanted == column, 1.0, 0.0).astype(BF16)
            size = min(width, cap - c * width)
            pack[d * cap + c * width:d * cap + c * width + size, :] = chosen[:size]


def prepare_kernel(contact, modes, tile, floor, basis_high, basis_low, tile_high, tile_low):
    order, width = floor.shape
    for at in range(0, order, width):
        flag = jnp.broadcast_to(contact[:, at:at + width], (width, width)).T
        floor[at:at + width, :] = jnp.where(flag == 1, 0.0, -jnp.inf)
    basis_high[...], basis_low[...] = split(modes[...].T)
    tile_high[...], tile_low[...] = split(tile[...])


def send(cap, chosen, image, sends):
    picked = pick(chosen, image)
    for d, out in enumerate(sends):
        out[...] = picked[d * cap:(d + 1) * cap]


def arrived(recvs, image, unpack):
    shared = image.shape[0]
    blocks = [image] + [recv[...][:shared] for recv in recvs]
    rows = sum(b.shape[0] for b in blocks)
    if rows < unpack.shape[1]:
        blocks.append(jnp.zeros((unpack.shape[1] - rows, image.shape[1]), F32))
    return pick(unpack[...], jnp.concatenate(blocks, axis=0))


def settle(trial, floor, alive):
    return jnp.where(alive, jnp.maximum(trial, floor), 0.0)


def shared_residual(recvs, image, unpack, gap, size):
    own = image[...]
    jump = own - arrived(recvs, own, unpack)
    alive = live(size[0], 0, *own.shape)
    return jnp.where(alive, gap[:own.shape[0], :] - jump, 0.0), alive


def rest_first_kernel(pieces, given_parts, size, operator, *refs):
    if given_parts:
        low, refs = refs[0], refs[1:]
    mults, (mult_block, gap, modes, trial, coarse), outs = refs[:pieces], refs[pieces:pieces + 5], refs[pieces + 5:]
    halves = outs[-1]
    if given_parts:
        parts = operator[...], low[...]
    else:
        parts = split(operator[...])
        outs[0][...], outs[1][...] = parts
    step = pl.program_id(0)
    rows, width = gap.shape
    fill_halves(step, mults, halves)
    image = halved_product(parts, halves[...], width)
    alive = live(size[0], (step + 1) * rows, rows, width)
    residual = jnp.where(alive, gap[...] - image, 0.0)
    trial[...] = mult_block[...] + STEP * residual

    @pl.when(step == 0)
    def _():
        coarse[...] = jnp.zeros_like(coarse)

    coarse[...] += product(split(modes[...]), split(residual))


def fill_halves(step, mults, halves):
    @pl.when(step == 0)
    def _():
        at = 0
        for mult in mults:
            rows, width = mult.shape
            halves[at:at + rows, :width], halves[at:at + rows, width:] = split(mult[...])
            at += rows


def halved_product(parts, halves, width):
    both = mm(parts[0], halves)
    return both[:, :width] + (both[:, width:] + mm(parts[1], halves[:, :width]))


def rest_kernel(last, size, high, low, mult_s, mult_n, mult_block, gap, floor, *refs):
    halves = refs[-1]
    step = pl.program_id(0)
    rows, width = gap.shape
    fill_halves(step, (mult_s, mult_n), halves)
    image = halved_product((high[...], low[...]), halves[...], width)
    alive = live(size[0], (step + 1) * rows, rows, width)
    residual = jnp.where(alive, gap[...] - image, 0.0)
    mult = settle(mult_block[...] + STEP * residual, floor[...], alive)
    if last:
        mult_out, residual_out, _ = refs
        mult_out[...] = mult
        residual_out[...] = residual
    else:
        across_high, across_low, mult_out, ahead, _ = refs
        mult_out[...] = mult

        @pl.when(step == 0)
        def _():
            ahead[...] = jnp.zeros_like(ahead)

        ahead[...] += product((across_high[...], across_low[...]), split(mult))


def coarse_kernel(n, size, *refs):
    recvs = refs[:n]
    image, unpack, gap, mult, modes, started, trial = refs[n:n + 7]
    residual, _ = shared_residual(recvs, image, unpack, gap, size)
    coarse = started[...] + product(split(modes[:, :image.shape[0]]), split(residual))
    for out in refs[n + 7:]:
        out[...] = coarse
    trial[...] = mult[:image.shape[0], :] + STEP * residual


def tile_kernel(wide_order, narrow_order, high, low, *refs):
    n, m = len(wide_order), len(narrow_order)
    blocks, outs, (gathered, parts) = refs[:n + 1], refs[n + 1:n + m + 2], refs[n + m + 2:]
    count = blocks[0].shape[0]
    for d, ref in zip((0, *wide_order), blocks):
        at = pl.multiple_of((lax.axis_index("wide") ^ d) * count, count)
        gathered[pl.ds(at, count), :] = ref[...]
    parts[...] = product((high[...], low[...]), split(gathered[...]))
    for d, out in zip((0, *narrow_order), outs):
        at = pl.multiple_of((lax.axis_index("narrow") ^ d) * count, count)
        out[...] = parts[pl.ds(at, count), :]


def lift_kernel(n, m, cap, size, *refs):
    parts = refs[:m + 1]
    ins, (mult_s, mult_n, image), sends = refs[m + 1:m + 9], refs[m + 9:m + 12], refs[m + 12:]
    basis_high, basis_low, trial_s, trial_n, floor, high, low, pack = ins
    solved = parts[0][...]
    for part in parts[1:]:
        solved = solved + part[...]
    shared, width = trial_s.shape
    order = floor.shape[0]
    lifted = product((basis_high[...], basis_low[...]), split(solved))
    alive = live(size[0], 0, order, width)
    first = settle(trial_s[...] + lifted[:shared], floor[:shared], alive[:shared])
    rest = settle(trial_n[...] + lifted[shared:], floor[shared:], alive[shared:])
    mult_s[...] = first
    mult_n[...] = rest
    value = product((high[...], low[...]), split(jnp.concatenate([first, rest], axis=0)))
    image[...] = value
    send(cap, pack[...], value, sends)


def sweep_kernel(n, cap, size, *refs):
    recvs = refs[:n]
    image, unpack, gap, mult, floor, high, low, ahead, pack, mult_out, image_out = refs[n:n + 11]
    sends = refs[n + 11:]
    residual, alive = shared_residual(recvs, image, unpack, gap, size)
    shared = image.shape[0]
    value = settle(mult[...] + STEP * residual, floor[:shared, :], alive)
    mult_out[...] = value
    value = ahead[...] + product((high[:, :shared], low[:, :shared]), split(value))
    image_out[...] = value
    send(cap, pack[...], value, sends)


def last_kernel(n, size, *refs):
    recvs = refs[:n]
    image, unpack, gap, mult, floor, _, _, mult_out, residual_out, settled, left, done = refs[n:]
    shared = image.shape[0]
    residual, alive = shared_residual(recvs, image, unpack, gap, size)
    left[...] = residual
    first = pltpu.make_async_copy(left, residual_out.at[pl.ds(0, shared)], done.at[0])
    first.start()
    settled[...] = settle(mult[...] + STEP * residual, floor[:shared, :], alive)
    second = pltpu.make_async_copy(settled, mult_out.at[pl.ds(0, shared)], done.at[1])
    second.start()
    first.wait()
    second.wait()


def swap(block, axis, count, d):
    return lax.ppermute(block, axis, [(i, i ^ d) for i in range(count)])


def swap_all(blocks, axis, count, order):
    return [swap(block, axis, count, d) for block, d in zip(blocks, order)]


def swap_rows(blocks, wide, narrow, orders):
    return [
        lax.ppermute(
            block,
            ("wide", "narrow"),
            [(w * narrow + i, (w ^ ds[i % 2]) * narrow + i) for w in range(wide) for i in range(narrow)],
        )
        for block, ds in zip(blocks, zip(*orders))
    ]


def far_first(count):
    return tuple(range(count - 1, 0, -1))


def local(
    wide,
    narrow,
    operators,
    coarse_inverse,
    modes,
    gap,
    start_mult,
    peer_list,
    partner_row,
    interface_size,
    contact_rows,
):
    operator = operators[0]
    modes = modes[0]
    gap = gap[0]
    mult = start_mult[0]
    order, loads = mult.shape
    shared = partner_row.shape[1]
    count = modes.shape[0]
    rest = order - shared
    steps = rest // shared
    n, m = wide - 1, narrow - 1
    cap = 2 * shared // wide
    listed = n * cap
    padded = -(-listed // 128) * 128
    size = interface_size
    coarse_order, part_order = far_first(wide), far_first(narrow)
    rows_orders = far_first(wide), tuple(range(1, wide))
    top = whole((shared, loads))
    sent = [shape(cap, loads)] * n
    full = 2 * order * loads

    list_rows = -(-(-(-cap // loads)) // 8) * 8
    unpack_all, unpack, top_high, top_low, image, *sends = call(
        functools.partial(first_kernel, rows_orders, cap),
        tuple(
            pltpu.with_memory_space_constraint(value, pltpu.HBM)
            for value in (peer_list[0].reshape(1, shared), partner_row, operator, mult)
        ),
        [shape(shared, wide * shared, BF16), shape(shared, shared + padded, BF16)]
        + [shape(shared, order, BF16)] * 2
        + [shape(shared, loads)]
        + [shape(shared + list_rows, loads)] * n,
        in_specs=[HBM] * 4,
        scratch=[
            pltpu.VMEM((1, shared), jnp.int32),
            pltpu.VMEM((1, shared), jnp.int32),
            pltpu.VMEM((shared, order), F32),
            pltpu.VMEM((order, loads), F32),
            pltpu.SemaphoreType.DMA((4,)),
        ],
        flops=3 * full * shared,
        moved=8 * shared * order,
        name="first",
    )
    floor, basis_high, basis_low, tile_high, tile_low = call(
        prepare_kernel,
        (contact_rows, modes, coarse_inverse),
        [shape(order, loads)] + [shape(order, count, BF16)] * 2 + [shape(*coarse_inverse.shape, BF16)] * 2,
        flops=full * count,
        moved=8 * coarse_inverse.size + 4 * full,
        name="prepare",
    )
    mults, mult_s = (mult,), mult
    for outer in range(OUTER):
        start = outer == 0
        recvs = swap_rows(sends, wide, narrow, rows_orders)
        rest_ins = (*mults, mults[-1], gap, modes)
        rest_specs = [whole(piece.shape) for piece in mults] + [
            block((shared, loads), 1 if start else 0),
            block((shared, loads), 1),
            block((count, shared), 1, across=True),
        ]
        rest_outs = [shape(rest, loads), shape(count, loads)]
        rest_out_specs = [block((shared, loads)), whole((count, loads))]
        row_block = block((shared, order))
        if start:
            ins, specs = (size, operator), [SMEM, block((shared, order), 1)]
            rest_outs = rest_outs + [shape(rest, order, BF16)] * 2
            rest_out_specs = rest_out_specs + [row_block] * 2
        else:
            ins, specs = (size, high, low), [SMEM, row_block, row_block]
        trial_n, started, *parts = call(
            functools.partial(rest_first_kernel, len(mults), not start),
            ins + rest_ins,
            rest_outs,
            specs + rest_specs,
            rest_out_specs,
            scratch=[pltpu.VMEM((order, 2 * loads), BF16)],
            grid=(steps,),
            flops=3 * full * rest,
            moved=4 * rest * order,
            name="rest_first",
        )
        marks = unpack
        if start:
            high, low = parts
            marks = unpack_all
            pack = call(
                functools.partial(pack_kernel, n, cap),
                tuple(recvs),
                [shape(padded, shared, BF16)],
                flops=full,
                moved=4 * padded * shared,
                name="pack",
            )[0]
        trial_s, own, *coarse = call(
            functools.partial(coarse_kernel, n),
            (size, *recvs, image, marks, gap, mult_s, modes, started),
            [shape(shared, loads)] + [shape(count, loads)] * wide,
            flops=6 * shared * loads * unpack.shape[1],
            moved=2 * shared * unpack.shape[1],
            name="coarse",
        )
        blocks = [own] + swap_all(coarse, "wide", wide, coarse_order)
        own, *parts = call(
            functools.partial(tile_kernel, coarse_order, part_order),
            (tile_high, tile_low, *blocks),
            [shape(count, loads)] * narrow,
            scratch=[
                pltpu.VMEM((wide * count, loads), F32),
                pltpu.VMEM((narrow * count, loads), F32),
            ],
            flops=6 * coarse_inverse.size * loads,
            moved=4 * coarse_inverse.size,
            name="tile",
        )
        parts = [own] + swap_all(parts, "narrow", narrow, part_order)
        mult_s, mult_n, image, *sends = call(
            functools.partial(lift_kernel, n, m, cap),
            (size, *parts, basis_high, basis_low, trial_s, trial_n, floor, top_high, top_low, pack),
            [shape(shared, loads), shape(rest, loads), shape(shared, loads)] + sent,
            flops=3 * full * shared,
            moved=4 * order * shared,
            name="lift",
        )
        for inner in range(1, INNER):
            last = outer == OUTER - 1 and inner == INNER - 1
            recvs = swap_rows(sends, wide, narrow, rows_orders)
            ins = (size, high, low, mult_s, mult_n, mult_n, gap, floor)
            specs = [
                SMEM,
                row_block,
                row_block,
                top,
                whole((rest, loads)),
                block((shared, loads)),
                block((shared, loads), 1),
                block((shared, loads), 1),
            ]
            if last:
                outs = [shape(order, loads)] * 2
                out_specs = [block((shared, loads), 1)] * 2
            else:
                ins = ins + (top_high, top_low)
                specs = specs + [block((shared, shared), 1, across=True)] * 2
                outs = [shape(rest, loads), shape(shared, loads)]
                out_specs = [block((shared, loads)), top]
            rest_got = call(
                functools.partial(rest_kernel, last),
                ins,
                outs,
                specs,
                out_specs,
                scratch=[pltpu.VMEM((order, 2 * loads), BF16)],
                grid=(steps,),
                flops=3 * full * order,
                moved=4 * order * order,
                name="rest",
            )
            ins = (size, *recvs, image, unpack, gap, mult_s, floor)
            if last:
                return tuple(
                    out[None]
                    for out in call(
                        functools.partial(last_kernel, n),
                        ins + tuple(rest_got),
                        [shape(order, loads)] * 2,
                        in_specs=[SMEM] + [VMEM] * (len(ins) - 1) + [HBM] * 2,
                        out_specs=[HBM] * 2,
                        scratch=[
                            pltpu.VMEM((shared, loads), F32),
                            pltpu.VMEM((shared, loads), F32),
                            pltpu.SemaphoreType.DMA((2,)),
                        ],
                        alias={len(ins): 0, len(ins) + 1: 1},
                        flops=6 * shared * loads * unpack.shape[1],
                        moved=2 * shared * unpack.shape[1],
                        name="last",
                    )
                )
            mult_n, ahead = rest_got
            mult_s, image, *sends = call(
                functools.partial(sweep_kernel, n, cap),
                ins + (top_high, top_low, ahead, pack),
                [shape(shared, loads)] * 2 + sent,
                flops=12 * shared * loads * unpack.shape[1],
                moved=4 * shared * unpack.shape[1],
                name="sweep",
            )
            mults = mult_s, mult_n


def solution(mesh):
    wide = mesh.shape["wide"]
    narrow = mesh.shape["narrow"]

    def body(*args):
        return local(wide, narrow, *args)

    return jax.shard_map(
        body,
        mesh=mesh,
        in_specs=(
            P(("groups", "wide", "narrow"), None, None),
            P(("groups", "wide"), "narrow"),
            P(("groups", "wide", "narrow"), None, None),
            P(("groups", "wide", "narrow"), None, None),
            P(("groups", "wide", "narrow"), None, None),
            P(("groups", "wide", "narrow"), None, None),
            P(("groups", "wide", "narrow"), None),
            P(("groups", "wide", "narrow")),
            P(("groups", "wide", "narrow"), None),
        ),
        out_specs=(
            P(("groups", "wide", "narrow"), None, None),
            P(("groups", "wide", "narrow"), None, None),
        ),
        check_vma=False,
    )
```

```python
import functools

import jax
import jax.numpy as jnp
from jax import lax
from jax.experimental import pallas as pl
from jax.experimental.pallas import tpu as pltpu
from jax.sharding import PartitionSpec as P

OUTER = 2
INNER = 3
STEP = 0.3
F32 = jnp.float32
BF16 = jnp.bfloat16
PARAMS = pltpu.CompilerParams(vmem_limit_bytes=24 * 1024 * 1024)


def split(value):
    high = value.astype(BF16)
    return high, (value - high.astype(F32)).astype(BF16)


def mm(left, right):
    return jnp.dot(left, right, preferred_element_type=F32)


def product(left, right):
    (left_high, left_low), (right_high, right_low) = left, right
    width = right_high.shape[1]
    both = mm(left_high, jnp.concatenate([right_high, right_low], axis=1))
    return both[:, :width] + (both[:, width:] + mm(left_low, right_high))


def pick(chosen, value):
    width = value.shape[1]
    both = mm(chosen, jnp.concatenate(split(value), axis=1))
    return both[:, :width] + both[:, width:]


def live(size, start, rows, width):
    return lax.broadcasted_iota(jnp.int32, (rows, width), 0) + start < size


def call(body, ins, outs, in_specs=None, out_specs=None, scratch=(), grid=(), flops=0, moved=0, alias=None, name=None):
    if in_specs is None:
        in_specs = [SMEM if value.ndim == 1 else VMEM for value in ins]
    if out_specs is None:
        out_specs = [VMEM] * len(outs)
    return pl.pallas_call(
        body,
        out_shape=outs,
        grid=grid,
        in_specs=in_specs,
        out_specs=out_specs,
        scratch_shapes=list(scratch),
        compiler_params=PARAMS,
        cost_estimate=pl.CostEstimate(flops=flops, bytes_accessed=moved, transcendentals=0),
        input_output_aliases=alias or {},
        name=name,
    )(*ins)


def whole(shape):
    return pl.BlockSpec(shape, lambda *i: (0,) * len(shape))


def block(shape, at=0, across=False):
    if across:
        return pl.BlockSpec(shape, lambda i: (0, i + at))
    return pl.BlockSpec(shape, lambda i: (i + at, 0))


SMEM = pl.BlockSpec(memory_space=pltpu.SMEM)
HBM = pl.BlockSpec(memory_space=pltpu.HBM)
VMEM = pl.BlockSpec(memory_space=pltpu.VMEM)


def shape(rows, columns, dtype=F32):
    return jax.ShapeDtypeStruct((rows, columns), dtype)


def first_kernel(n, cap, peers_at, rows_at, operator_at, mult_at, *refs):
    unpack_own, unpack_all, unpack, high, low, image = refs[:6]
    sends, (peers, rows, operator, mult, done) = refs[6:6 + n], refs[6 + n:]
    shared, width = image.shape
    copies = [
        pltpu.make_async_copy(source, target, done.at[i])
        for i, (source, target) in enumerate(
            ((peers_at, peers), (rows_at, rows), (mult_at, mult), (operator_at.at[pl.ds(0, shared)], operator))
        )
    ]
    for copy in copies:
        copy.start()
    copies[0].wait()
    copies[1].wait()
    across = jnp.broadcast_to(peers[...], (shared, shared))
    down = across.T
    first = lax.broadcasted_iota(jnp.int32, (shared, shared), 0)
    second = lax.broadcasted_iota(jnp.int32, (shared, shared), 1)
    slot = jnp.sum(
        jnp.where((across == down) & (second < first), 1.0, 0.0), axis=1, keepdims=True
    ).astype(jnp.int32)
    wanted = jnp.broadcast_to(rows[...], (shared, shared)).T[:, :1]
    far = down[:, :1] ^ lax.axis_index("wide")

    def marks(key, columns):
        hit = key == lax.broadcasted_iota(jnp.int32, (shared, columns), 1)
        return jnp.where(hit, 1.0, 0.0).astype(BF16)

    unpack_own[...] = marks(jnp.where(far == 0, wanted, -1), shared)
    unpack_all[...] = marks(jnp.where(far == 0, -1, (far - 1) * shared + wanted), unpack_all.shape[1])
    unpack[...] = marks(jnp.where(far == 0, -1, (far - 1) * cap + slot), unpack.shape[1])
    lane = lax.broadcasted_iota(jnp.int32, (shared, width), 1)
    for d, out in enumerate(sends, 1):
        out[shared:, :] = jnp.zeros((out.shape[0] - shared, width), F32)
        for c in range(-(-cap // width)):
            hit = (far == d) & (slot == lane + c * width)
            out[shared + c:shared + c + 1, :] = jnp.sum(
                jnp.where(hit, wanted.astype(F32), 0.0), axis=0, keepdims=True
            )
    copies[2].wait()
    copies[3].wait()
    parts = split(operator[...])
    high[...], low[...] = parts
    value = product(parts, split(mult[...]))
    image[...] = value
    for out in sends:
        out[:shared, :] = value


def pack_kernel(times, cap, *refs):
    n = len(times)
    recvs, (high, low, pack, stack_high, stack_low) = refs[:n], refs[n:]
    shared = pack.shape[1]
    width = recvs[0].shape[1]
    column = lax.broadcasted_iota(jnp.int32, (width, shared), 1).astype(F32)
    if n * cap < pack.shape[0]:
        pack[n * cap:, :] = jnp.zeros((pack.shape[0] - n * cap, shared), BF16)
    for d, recv in zip(times, recvs):
        for c in range(-(-cap // width)):
            wanted = jnp.broadcast_to(recv[shared + c:shared + c + 1, :], (shared, width)).T
            chosen = jnp.where(wanted == column, 1.0, 0.0).astype(BF16)
            size = min(width, cap - c * width)
            at = (d - 1) * cap + c * width
            pack[at:at + size, :] = chosen[:size]
    for source, stack in ((high, stack_high), (low, stack_low)):
        square = source[:, :shared]
        stack[:shared, :] = square
        stack[shared:, :] = mm(pack[...], square).astype(BF16)


def prepare_kernel(contact, modes, tile, floor, basis, tile_high, tile_low):
    order, width = floor.shape
    for at in range(0, order, width):
        flag = jnp.broadcast_to(contact[:, at:at + width], (width, width)).T
        floor[at:at + width, :] = jnp.where(flag == 1, 0.0, -jnp.inf)
    high, low = [part.astype(F32) for part in split(modes[...])]
    basis[...] = jnp.concatenate([high, high, low], axis=0).T.astype(BF16)
    tile_high[...], tile_low[...] = split(tile[...])


def send(cap, chosen, image, sends):
    picked = pick(chosen, image)
    for d, out in enumerate(sends):
        out[...] = picked[d * cap:(d + 1) * cap]


def arrived(times, recvs, shared, unpack):
    blocks = [recvs[times.index(d)][...][:shared] for d in sorted(times)]
    rows = sum(b.shape[0] for b in blocks)
    if rows < unpack.shape[1]:
        blocks.append(jnp.zeros((unpack.shape[1] - rows, blocks[0].shape[1]), F32))
    return pick(unpack[...], jnp.concatenate(blocks, axis=0))


def base_kernel(image, unpack_own, gap, base):
    own = image[...]
    base[...] = gap[:own.shape[0], :] - own + pick(unpack_own[...], own)


def settle(trial, floor, alive):
    return jnp.where(alive, jnp.maximum(trial, floor), 0.0)


def shared_residual(times, recvs, base, unpack, size):
    known = base[...]
    alive = live(size[0], 0, *known.shape)
    return jnp.where(alive, known + arrived(times, recvs, known.shape[0], unpack), 0.0), alive


def rest_start_kernel(size, operator, mult, mult_block, gap, modes, trial, coarse, high, low, halves):
    step = pl.program_id(0)
    rows, width = gap.shape

    @pl.when(step == 0)
    def _():
        halves[:, :width], halves[:, width:] = split(mult[...])
        coarse[...] = jnp.zeros_like(coarse)

    parts = split(operator[...])
    high[...], low[...] = parts
    both = mm(parts[0], halves[...])
    image = both[:, :width] + (both[:, width:] + mm(parts[1], halves[:, :width]))
    alive = live(size[0], (step + 1) * rows, rows, width)
    residual = jnp.where(alive, gap[...] - image, 0.0)
    trial[...] = mult_block[...] + STEP * residual
    coarse[...] += product(split(modes[...]), split(residual))


def rest_residual(size, high, low, mult_s, mult_n, gap):
    shared, (rows, width) = mult_s.shape[0], mult_n.shape
    mult = jnp.concatenate([mult_s[...], mult_n[...]], axis=0)
    image = product((high[...], low[...]), split(mult))
    alive = live(size[0], shared, rows, width)
    return jnp.where(alive, gap[shared:, :] - image, 0.0), alive


def rest_first_kernel(size, high, low, mult_s, mult_n, gap, modes, trial, coarse):
    residual, _ = rest_residual(size, high, low, mult_s, mult_n, gap)
    trial[...] = mult_n[...] + STEP * residual
    coarse[...] = product(split(modes[:, mult_s.shape[0]:]), split(residual))


def rest_kernel(size, high, low, mult_s, mult_n, gap, floor, top_high, top_low, pack, mult_out, ahead):
    shared = mult_s.shape[0]
    residual, alive = rest_residual(size, high, low, mult_s, mult_n, gap)
    mult = settle(mult_n[...] + STEP * residual, floor[shared:, :], alive)
    mult_out[...] = mult
    value = product((top_high[:, shared:], top_low[:, shared:]), split(mult))
    ahead[:shared, :] = value
    ahead[shared:, :] = pick(pack[...], value)


def rest_last_kernel(size, high, low, mult_s, mult_n, gap, floor, mult_out, residual_out, settled, left, done):
    shared, rows = mult_s.shape[0], mult_n.shape[0]
    residual, alive = rest_residual(size, high, low, mult_s, mult_n, gap)
    left[...] = residual
    settled[...] = settle(mult_n[...] + STEP * residual, floor[shared:, :], alive)
    copies = [
        pltpu.make_async_copy(source, target.at[pl.ds(shared, rows)], done.at[i])
        for i, (source, target) in enumerate(((left, residual_out), (settled, mult_out)))
    ]
    for copy in copies:
        copy.start()
    for copy in copies:
        copy.wait()


def coarse_kernel(times, size, *refs):
    n = len(times)
    recvs = refs[:n]
    base, unpack, mult, modes, started, trial = refs[n:n + 6]
    shared = base.shape[0]
    residual, _ = shared_residual(times, recvs, base, unpack, size)
    coarse = started[...] + product(split(modes[:, :shared]), split(residual))
    for out in refs[n + 6:]:
        out[...] = coarse
    trial[...] = mult[:shared, :] + STEP * residual


def tile_kernel(wide_order, narrow_order, high, low, *refs):
    n, m = len(wide_order), len(narrow_order)
    blocks, outs, (gathered, parts) = refs[:n + 1], refs[n + 1:n + m + 2], refs[n + m + 2:]
    count = blocks[0].shape[0]
    for d, ref in zip((0, *wide_order), blocks):
        at = pl.multiple_of((lax.axis_index("wide") ^ d) * count, count)
        gathered[pl.ds(at, count), :] = ref[...]
    parts[...] = product((high[...], low[...]), split(gathered[...]))
    for d, out in zip((0, *narrow_order), outs):
        at = pl.multiple_of((lax.axis_index("narrow") ^ d) * count, count)
        out[...] = parts[pl.ds(at, count), :]


def lift_kernel(n, m, cap, size, *refs):
    parts = refs[:m + 1]
    ins, (mult_s, mult_n, image), sends = refs[m + 1:m + 8], refs[m + 8:m + 11], refs[m + 11:]
    basis, trial_s, trial_n, floor, high, low, pack = ins
    solved = parts[0][...]
    for part in parts[1:]:
        solved = solved + part[...]
    shared, width = trial_s.shape
    order = floor.shape[0]
    high_part, low_part = split(solved)
    lifted = mm(basis[...], jnp.concatenate([high_part, low_part, high_part], axis=0))
    alive = live(size[0], 0, order, width)
    first = settle(trial_s[...] + lifted[:shared], floor[:shared], alive[:shared])
    rest = settle(trial_n[...] + lifted[shared:], floor[shared:], alive[shared:])
    mult_s[...] = first
    mult_n[...] = rest
    value = product((high[...], low[...]), split(jnp.concatenate([first, rest], axis=0)))
    image[...] = value
    send(cap, pack[...], value, sends)


def sweep_kernel(times, cap, size, *refs):
    n = len(times)
    recvs = refs[:n]
    base, unpack, mult, floor, high, low, ahead, mult_out, image_out = refs[n:n + 9]
    shared = base.shape[0]
    residual, alive = shared_residual(times, recvs, base, unpack, size)
    value = settle(mult[...] + STEP * residual, floor[:shared, :], alive)
    mult_out[...] = value
    both = ahead[...] + product((high[...], low[...]), split(value))
    image_out[...] = both[:shared]
    for d, out in enumerate(refs[n + 9:]):
        out[...] = both[shared + d * cap:shared + (d + 1) * cap]


def last_kernel(times, size, *refs):
    n = len(times)
    recvs = refs[:n]
    base, unpack, mult, floor, _, _, mult_out, residual_out, settled, left, done = refs[n:]
    shared = base.shape[0]
    residual, alive = shared_residual(times, recvs, base, unpack, size)
    left[...] = residual
    first = pltpu.make_async_copy(left, residual_out.at[pl.ds(0, shared)], done.at[0])
    first.start()
    settled[...] = settle(mult[...] + STEP * residual, floor[:shared, :], alive)
    second = pltpu.make_async_copy(settled, mult_out.at[pl.ds(0, shared)], done.at[1])
    second.start()
    first.wait()
    second.wait()


def swap(block, axis, count, d):
    return lax.ppermute(block, axis, [(i, i ^ d) for i in range(count)])


def swap_all(blocks, axis, count, order):
    return [swap(block, axis, count, d) for block, d in zip(blocks, order)]


def swap_rows(blocks, axis, count, times):
    return [swap(blocks[d - 1], axis, count, d) for d in times]


def half_first(count, back):
    half = count // 2
    others = [d for d in range(1, count) if d != half]
    return (half, *(others[::-1] if back else others))


def middle_first(count):
    return (count - 1, *range(1, count - 1))


def far_first(count):
    return tuple(range(count - 1, 0, -1))


def local(
    wide,
    narrow,
    operators,
    coarse_inverse,
    modes,
    gap,
    start_mult,
    peer_list,
    partner_row,
    interface_size,
    contact_rows,
):
    operator = operators[0]
    modes = modes[0]
    gap = gap[0]
    mult = start_mult[0]
    order, loads = mult.shape
    shared = partner_row.shape[1]
    count = modes.shape[0]
    rest = order - shared
    steps = rest // shared
    n, m = wide - 1, narrow - 1
    cap = 2 * shared // wide
    listed = n * cap
    padded = -(-listed // 128) * 128
    size = interface_size
    coarse_order, part_order = far_first(wide), far_first(narrow)
    half, half_back, middle = half_first(wide, False), half_first(wide, True), middle_first(wide)
    orders = ((half_back, half, middle), (half_back, half, half_back))
    sent = [shape(cap, loads)] * n
    full = 2 * order * loads

    list_rows = -(-(-(-cap // loads)) // 8) * 8
    unpack_own, unpack_all, unpack, top_high, top_low, image, *sends = call(
        functools.partial(first_kernel, n, cap),
        tuple(
            pltpu.with_memory_space_constraint(value, pltpu.HBM)
            for value in (peer_list[0].reshape(1, shared), partner_row, operator, mult)
        ),
        [shape(shared, shared, BF16), shape(shared, n * shared, BF16), shape(shared, padded, BF16)]
        + [shape(shared, order, BF16)] * 2
        + [shape(shared, loads)]
        + [shape(shared + list_rows, loads)] * n,
        in_specs=[HBM] * 4,
        scratch=[
            pltpu.VMEM((1, shared), jnp.int32),
            pltpu.VMEM((1, shared), jnp.int32),
            pltpu.VMEM((shared, order), F32),
            pltpu.VMEM((order, loads), F32),
            pltpu.SemaphoreType.DMA((4,)),
        ],
        flops=3 * full * shared,
        moved=8 * shared * order,
        name="first",
    )
    floor, basis, tile_high, tile_low = call(
        prepare_kernel,
        (contact_rows, modes, coarse_inverse),
        [shape(order, loads)] + [shape(order, 3 * count, BF16)] + [shape(*coarse_inverse.shape, BF16)] * 2,
        flops=full * count,
        moved=8 * coarse_inverse.size + 4 * full,
        name="prepare",
    )
    mult_s = mult
    scratch = [pltpu.VMEM((order, 2 * loads), BF16)]
    for outer in range(OUTER):
        times = orders[outer][0]
        recvs = swap_rows(sends, "wide", wide, times)
        base = call(
            base_kernel,
            (image, unpack_own, gap),
            [shape(shared, loads)],
            flops=4 * shared * shared * loads,
            moved=8 * shared * loads,
            name="base",
        )[0]
        if outer == 0:
            row_block, load_block = block((shared, order)), block((shared, loads))
            next_loads = block((shared, loads), 1)
            trial_n, started, high, low = call(
                rest_start_kernel,
                (size, operator, mult, mult, gap, modes),
                [shape(rest, loads), shape(count, loads)] + [shape(rest, order, BF16)] * 2,
                [
                    SMEM,
                    block((shared, order), 1),
                    whole((order, loads)),
                    next_loads,
                    next_loads,
                    block((count, shared), 1, across=True),
                ],
                [load_block, whole((count, loads)), row_block, row_block],
                scratch=scratch,
                grid=(steps,),
                flops=3 * full * rest,
                moved=8 * rest * order,
                name="rest_start",
            )
            marks = unpack_all
            pack, stack_high, stack_low = call(
                functools.partial(pack_kernel, times, cap),
                (*recvs, top_high, top_low),
                [shape(padded, shared, BF16)] + [shape(shared + padded, shared, BF16)] * 2,
                flops=8 * padded * shared * shared,
                moved=8 * padded * shared,
                name="pack",
            )
        else:
            trial_n, started = call(
                rest_first_kernel,
                (size, high, low, mult_s, mult_n, gap, modes),
                [shape(rest, loads), shape(count, loads)],
                flops=3 * full * rest,
                moved=4 * rest * order,
                name="rest_first",
            )
            marks = unpack
        trial_s, own, *coarse = call(
            functools.partial(coarse_kernel, times),
            (size, *recvs, base, marks, mult_s, modes, started),
            [shape(shared, loads)] + [shape(count, loads)] * wide,
            flops=6 * shared * loads * unpack.shape[1],
            moved=2 * shared * unpack.shape[1],
            name="coarse",
        )
        blocks = [own] + swap_all(coarse, "wide", wide, coarse_order)
        own, *parts = call(
            functools.partial(tile_kernel, coarse_order, part_order),
            (tile_high, tile_low, *blocks),
            [shape(count, loads)] * narrow,
            scratch=[
                pltpu.VMEM((wide * count, loads), F32),
                pltpu.VMEM((narrow * count, loads), F32),
            ],
            flops=6 * coarse_inverse.size * loads,
            moved=4 * coarse_inverse.size,
            name="tile",
        )
        parts = [own] + swap_all(parts, "narrow", narrow, part_order)
        mult_s, mult_n, image, *sends = call(
            functools.partial(lift_kernel, n, m, cap),
            (size, *parts, basis, trial_s, trial_n, floor, top_high, top_low, pack),
            [shape(shared, loads), shape(rest, loads), shape(shared, loads)] + sent,
            flops=3 * full * shared,
            moved=4 * order * shared,
            name="lift",
        )
        for inner in range(1, INNER):
            last = outer == OUTER - 1 and inner == INNER - 1
            times = orders[outer][inner]
            recvs = swap_rows(sends, "wide", wide, times)
            base = call(
                base_kernel,
                (image, unpack_own, gap),
                [shape(shared, loads)],
                flops=4 * shared * shared * loads,
                moved=8 * shared * loads,
                name="base",
            )[0]
            ins = (size, high, low, mult_s, mult_n, gap, floor)
            shadow = (size, *recvs, base, unpack, mult_s, floor)
            cost = dict(flops=6 * shared * loads * unpack.shape[1], moved=2 * shared * unpack.shape[1])
            if last:
                outs = call(
                    rest_last_kernel,
                    ins,
                    [shape(order, loads)] * 2,
                    out_specs=[HBM] * 2,
                    scratch=[pltpu.VMEM((rest, loads), F32)] * 2 + [pltpu.SemaphoreType.DMA((2,))],
                    flops=3 * full * rest,
                    moved=4 * rest * order,
                    name="rest_last",
                )
                outs = call(
                    functools.partial(last_kernel, times),
                    (*shadow, *outs),
                    [shape(order, loads)] * 2,
                    in_specs=[SMEM] + [VMEM] * (len(shadow) - 1) + [HBM] * 2,
                    out_specs=[HBM] * 2,
                    scratch=[pltpu.VMEM((shared, loads), F32)] * 2 + [pltpu.SemaphoreType.DMA((2,))],
                    alias={len(shadow): 0, len(shadow) + 1: 1},
                    name="last",
                    **cost,
                )
                return tuple(out[None] for out in outs)
            mult_n, ahead = call(
                rest_kernel,
                (*ins, top_high, top_low, pack),
                [shape(rest, loads), shape(shared + padded, loads)],
                flops=3 * full * order,
                moved=4 * order * order,
                name="rest",
            )
            mult_s, image, *sends = call(
                functools.partial(sweep_kernel, times, cap),
                (*shadow, stack_high, stack_low, ahead),
                [shape(shared, loads)] * 2 + sent,
                name="sweep",
                **cost,
            )


def solution(mesh):
    wide = mesh.shape["wide"]
    narrow = mesh.shape["narrow"]

    def body(*args):
        return local(wide, narrow, *args)

    return jax.shard_map(
        body,
        mesh=mesh,
        in_specs=(
            P(("groups", "wide", "narrow"), None, None),
            P(("groups", "wide"), "narrow"),
            P(("groups", "wide", "narrow"), None, None),
            P(("groups", "wide", "narrow"), None, None),
            P(("groups", "wide", "narrow"), None, None),
            P(("groups", "wide", "narrow"), None, None),
            P(("groups", "wide", "narrow"), None),
            P(("groups", "wide", "narrow")),
            P(("groups", "wide", "narrow"), None),
        ),
        out_specs=(
            P(("groups", "wide", "narrow"), None, None),
            P(("groups", "wide", "narrow"), None, None),
        ),
        check_vma=False,
    )
```

```python
import functools

import jax
import jax.numpy as jnp
from jax import lax
from jax.experimental import pallas as pl
from jax.experimental.pallas import tpu as pltpu
from jax.sharding import PartitionSpec as P

OUTER = 2
INNER = 3
STEP = 0.3
F32 = jnp.float32
BF16 = jnp.bfloat16
PARAMS = pltpu.CompilerParams(vmem_limit_bytes=24 * 1024 * 1024)


def split(value):
    high = value.astype(BF16)
    return high, (value - high.astype(F32)).astype(BF16)


def mm(left, right):
    return jnp.dot(left, right, preferred_element_type=F32)


def product(left, right):
    (left_high, left_low), (right_high, right_low) = left, right
    width = right_high.shape[1]
    both = mm(left_high, jnp.concatenate([right_high, right_low], axis=1))
    return both[:, :width] + (both[:, width:] + mm(left_low, right_high))


def pick(chosen, value):
    width = value.shape[1]
    both = mm(chosen, jnp.concatenate(split(value), axis=1))
    return both[:, :width] + both[:, width:]


def live(size, start, rows, width):
    return lax.broadcasted_iota(jnp.int32, (rows, width), 0) + start < size


def call(body, ins, outs, in_specs=None, out_specs=None, scratch=(), grid=(), flops=0, moved=0, alias=None, name=None):
    if in_specs is None:
        in_specs = [SMEM if value.ndim == 1 else VMEM for value in ins]
    if out_specs is None:
        out_specs = [VMEM] * len(outs)
    return pl.pallas_call(
        body,
        out_shape=outs,
        grid=grid,
        in_specs=in_specs,
        out_specs=out_specs,
        scratch_shapes=list(scratch),
        compiler_params=PARAMS,
        cost_estimate=pl.CostEstimate(flops=flops, bytes_accessed=moved, transcendentals=0),
        input_output_aliases=alias or {},
        name=name,
    )(*ins)


def whole(shape):
    return pl.BlockSpec(shape, lambda *i: (0,) * len(shape))


def block(shape, at=0, across=False):
    if across:
        return pl.BlockSpec(shape, lambda i: (0, i + at))
    return pl.BlockSpec(shape, lambda i: (i + at, 0))


SMEM = pl.BlockSpec(memory_space=pltpu.SMEM)
HBM = pl.BlockSpec(memory_space=pltpu.HBM)
VMEM = pl.BlockSpec(memory_space=pltpu.VMEM)


def shape(rows, columns, dtype=F32):
    return jax.ShapeDtypeStruct((rows, columns), dtype)


def places(peers, rows):
    shared = peers.shape[1]
    across = jnp.broadcast_to(peers[...], (shared, shared))
    down = across.T
    first = lax.broadcasted_iota(jnp.int32, (shared, shared), 0)
    second = lax.broadcasted_iota(jnp.int32, (shared, shared), 1)
    slot = jnp.sum(
        jnp.where((across == down) & (second < first), 1.0, 0.0), axis=1, keepdims=True
    ).astype(jnp.int32)
    wanted = jnp.broadcast_to(rows[...], (shared, shared)).T[:, :1]
    return down[:, :1] ^ lax.axis_index("wide"), slot, wanted


def first_kernel(n, cap, peers_at, rows_at, operator_at, mult_at, *refs):
    high, low, image = refs[:3]
    sends, (peers, rows, operator, mult, done) = refs[3:3 + n], refs[3 + n:]
    shared, width = image.shape
    copies = [
        pltpu.make_async_copy(source, target, done.at[i])
        for i, (source, target) in enumerate(
            ((peers_at, peers), (rows_at, rows), (mult_at, mult), (operator_at.at[pl.ds(0, shared)], operator))
        )
    ]
    for copy in copies:
        copy.start()
    copies[0].wait()
    copies[1].wait()
    far, slot, wanted = places(peers, rows)
    wanted = wanted.astype(F32)
    lane = lax.broadcasted_iota(jnp.int32, (shared, width), 1)
    for d, out in enumerate(sends, 1):
        out[shared:, :] = jnp.zeros((out.shape[0] - shared, width), F32)
        for c in range(-(-cap // width)):
            hit = (far == d) & (slot == lane + c * width)
            out[shared + c:shared + c + 1, :] = jnp.sum(
                jnp.where(hit, wanted, 0.0), axis=0, keepdims=True
            )
    copies[2].wait()
    copies[3].wait()
    parts = split(operator[...])
    high[...], low[...] = parts
    value = product(parts, split(mult[...]))
    image[...] = value
    for out in sends:
        out[:shared, :] = value


def marks_kernel(cap, peers, rows, unpack_own, unpack_all, unpack):
    far, slot, wanted = places(peers, rows)
    shared = peers.shape[1]
    for key, out in (
        (jnp.where(far == 0, wanted, -1), unpack_own),
        (jnp.where(far == 0, -1, (far - 1) * shared + wanted), unpack_all),
        (jnp.where(far == 0, -1, (far - 1) * cap + slot), unpack),
    ):
        hit = key == lax.broadcasted_iota(jnp.int32, out.shape, 1)
        out[...] = jnp.where(hit, 1.0, 0.0).astype(BF16)


def pack_kernel(times, cap, *refs):
    n = len(times)
    recvs, (high, low, pack, stack_high, stack_low) = refs[:n], refs[n:]
    shared = pack.shape[1]
    width = recvs[0].shape[1]
    column = lax.broadcasted_iota(jnp.int32, (width, shared), 1).astype(F32)
    if n * cap < pack.shape[0]:
        pack[n * cap:, :] = jnp.zeros((pack.shape[0] - n * cap, shared), BF16)
    for d, recv in zip(times, recvs):
        for c in range(-(-cap // width)):
            wanted = jnp.broadcast_to(recv[shared + c:shared + c + 1, :], (shared, width)).T
            chosen = jnp.where(wanted == column, 1.0, 0.0).astype(BF16)
            size = min(width, cap - c * width)
            at = (d - 1) * cap + c * width
            pack[at:at + size, :] = chosen[:size]
    for source, stack in ((high, stack_high), (low, stack_low)):
        square = source[:, :shared]
        stack[:shared, :] = square
        stack[shared:, :] = mm(pack[...], square).astype(BF16)


def prepare_kernel(contact, modes, tile, floor, basis, tile_high, tile_low):
    order, width = floor.shape
    for at in range(0, order, width):
        flag = jnp.broadcast_to(contact[:, at:at + width], (width, width)).T
        floor[at:at + width, :] = jnp.where(flag == 1, 0.0, -jnp.inf)
    high, low = [part.astype(F32) for part in split(modes[...])]
    basis[...] = jnp.concatenate([high, high, low], axis=0).T.astype(BF16)
    tile_high[...], tile_low[...] = split(tile[...])


def send(cap, chosen, image, sends):
    picked = pick(chosen, image)
    for d, out in enumerate(sends):
        out[...] = picked[d * cap:(d + 1) * cap]


def arrived(times, recvs, shared, unpack):
    blocks = [recvs[times.index(d)][...][:shared] for d in sorted(times)]
    rows = sum(b.shape[0] for b in blocks)
    if rows < unpack.shape[1]:
        blocks.append(jnp.zeros((unpack.shape[1] - rows, blocks[0].shape[1]), F32))
    return pick(unpack[...], jnp.concatenate(blocks, axis=0))


def base_kernel(image, unpack_own, gap, base):
    own = image[...]
    base[...] = gap[:own.shape[0], :] - own + pick(unpack_own[...], own)


def settle(trial, floor, alive):
    return jnp.where(alive, jnp.maximum(trial, floor), 0.0)


def shared_residual(times, recvs, base, unpack, size):
    known = base[...]
    alive = live(size[0], 0, *known.shape)
    return jnp.where(alive, known + arrived(times, recvs, known.shape[0], unpack), 0.0), alive


def rest_start_kernel(size, operator, mult, mult_block, gap, modes, trial, coarse, high, low, halves):
    step = pl.program_id(0)
    rows, width = gap.shape

    @pl.when(step == 0)
    def _():
        halves[:, :width], halves[:, width:] = split(mult[...])
        coarse[...] = jnp.zeros_like(coarse)

    parts = split(operator[...])
    high[...], low[...] = parts
    both = mm(parts[0], halves[...])
    image = both[:, :width] + (both[:, width:] + mm(parts[1], halves[:, :width]))
    alive = live(size[0], (step + 1) * rows, rows, width)
    residual = jnp.where(alive, gap[...] - image, 0.0)
    trial[...] = mult_block[...] + STEP * residual
    coarse[...] += product(split(modes[...]), split(residual))


def rest_residual(size, high, low, mult_s, mult_n, gap):
    shared, (rows, width) = mult_s.shape[0], mult_n.shape
    mult = jnp.concatenate([mult_s[...], mult_n[...]], axis=0)
    image = product((high[...], low[...]), split(mult))
    alive = live(size[0], shared, rows, width)
    return jnp.where(alive, gap[shared:, :] - image, 0.0), alive


def rest_first_kernel(size, high, low, mult_s, mult_n, gap, modes, trial, coarse):
    residual, _ = rest_residual(size, high, low, mult_s, mult_n, gap)
    trial[...] = mult_n[...] + STEP * residual
    coarse[...] = product(split(modes[:, mult_s.shape[0]:]), split(residual))


def rest_kernel(size, high, low, mult_s, mult_n, gap, floor, top_high, top_low, pack, mult_out, ahead):
    shared = mult_s.shape[0]
    residual, alive = rest_residual(size, high, low, mult_s, mult_n, gap)
    mult = settle(mult_n[...] + STEP * residual, floor[shared:, :], alive)
    mult_out[...] = mult
    value = product((top_high[:, shared:], top_low[:, shared:]), split(mult))
    ahead[:shared, :] = value
    ahead[shared:, :] = pick(pack[...], value)


def rest_last_kernel(size, high, low, mult_s, mult_n, gap, floor, mult_out, residual_out, settled, left, done):
    shared, rows = mult_s.shape[0], mult_n.shape[0]
    residual, alive = rest_residual(size, high, low, mult_s, mult_n, gap)
    left[...] = residual
    settled[...] = settle(mult_n[...] + STEP * residual, floor[shared:, :], alive)
    copies = [
        pltpu.make_async_copy(source, target.at[pl.ds(shared, rows)], done.at[i])
        for i, (source, target) in enumerate(((left, residual_out), (settled, mult_out)))
    ]
    for copy in copies:
        copy.start()
    for copy in copies:
        copy.wait()


def coarse_kernel(times, size, *refs):
    n = len(times)
    recvs = refs[:n]
    base, unpack, mult, modes, started, trial = refs[n:n + 6]
    shared = base.shape[0]
    residual, _ = shared_residual(times, recvs, base, unpack, size)
    coarse = started[...] + product(split(modes[:, :shared]), split(residual))
    for out in refs[n + 6:]:
        out[...] = coarse
    trial[...] = mult[:shared, :] + STEP * residual


def tile_kernel(wide_order, narrow_order, high, low, *refs):
    n, m = len(wide_order), len(narrow_order)
    blocks, outs, (gathered, parts) = refs[:n + 1], refs[n + 1:n + m + 2], refs[n + m + 2:]
    count = blocks[0].shape[0]
    for d, ref in zip((0, *wide_order), blocks):
        at = pl.multiple_of((lax.axis_index("wide") ^ d) * count, count)
        gathered[pl.ds(at, count), :] = ref[...]
    parts[...] = product((high[...], low[...]), split(gathered[...]))
    for d, out in zip((0, *narrow_order), outs):
        at = pl.multiple_of((lax.axis_index("narrow") ^ d) * count, count)
        out[...] = parts[pl.ds(at, count), :]


def lift_kernel(n, m, cap, size, *refs):
    parts = refs[:m + 1]
    ins, (mult_s, mult_n, image), sends = refs[m + 1:m + 8], refs[m + 8:m + 11], refs[m + 11:]
    basis, trial_s, trial_n, floor, high, low, pack = ins
    solved = parts[0][...]
    for part in parts[1:]:
        solved = solved + part[...]
    shared, width = trial_s.shape
    order = floor.shape[0]
    high_part, low_part = split(solved)
    solved = jnp.concatenate([high_part, low_part, high_part], axis=0)
    shared, width = trial_s.shape
    value = jnp.zeros((shared, width), F32)
    for at in range(0, floor.shape[0], shared):
        here = slice(at, at + shared)
        trial = trial_s[...] if at == 0 else trial_n[at - shared:at, :]
        alive = live(size[0], at, shared, width)
        mult = settle(trial + mm(basis[here, :], solved), floor[here, :], alive)
        if at == 0:
            mult_s[...] = mult
        else:
            mult_n[at - shared:at, :] = mult
        value = value + product((high[:, here], low[:, here]), split(mult))
    image[...] = value
    send(cap, pack[...], value, sends)


def sweep_kernel(times, cap, size, *refs):
    n = len(times)
    recvs = refs[:n]
    base, unpack, mult, floor, high, low, ahead, mult_out, image_out = refs[n:n + 9]
    shared = base.shape[0]
    residual, alive = shared_residual(times, recvs, base, unpack, size)
    value = settle(mult[...] + STEP * residual, floor[:shared, :], alive)
    mult_out[...] = value
    both = ahead[...] + product((high[...], low[...]), split(value))
    image_out[...] = both[:shared]
    for d, out in enumerate(refs[n + 9:]):
        out[...] = both[shared + d * cap:shared + (d + 1) * cap]


def last_kernel(times, size, *refs):
    n = len(times)
    recvs = refs[:n]
    base, unpack, mult, floor, _, _, mult_out, residual_out, settled, left, done = refs[n:]
    shared = base.shape[0]
    residual, alive = shared_residual(times, recvs, base, unpack, size)
    left[...] = residual
    first = pltpu.make_async_copy(left, residual_out.at[pl.ds(0, shared)], done.at[0])
    first.start()
    settled[...] = settle(mult[...] + STEP * residual, floor[:shared, :], alive)
    second = pltpu.make_async_copy(settled, mult_out.at[pl.ds(0, shared)], done.at[1])
    second.start()
    first.wait()
    second.wait()


def swap(block, axis, count, d):
    return lax.ppermute(block, axis, [(i, i ^ d) for i in range(count)])


def swap_all(blocks, axis, count, order):
    return [swap(block, axis, count, d) for block, d in zip(blocks, order)]


def swap_rows(blocks, axis, count, times):
    return [swap(blocks[d - 1], axis, count, d) for d in times]


def half_first(count):
    half = count // 2
    return (half, *(d for d in range(count - 1, 0, -1) if d != half))


def middle_first(count):
    return (count - 1, *range(1, count - 1))


def far_first(count):
    return tuple(range(count - 1, 0, -1))


def local(
    wide,
    narrow,
    operators,
    coarse_inverse,
    modes,
    gap,
    start_mult,
    peer_list,
    partner_row,
    interface_size,
    contact_rows,
):
    operator = operators[0]
    modes = modes[0]
    gap = gap[0]
    mult = start_mult[0]
    order, loads = mult.shape
    shared = partner_row.shape[1]
    count = modes.shape[0]
    rest = order - shared
    steps = rest // shared
    n, m = wide - 1, narrow - 1
    cap = 2 * shared // wide
    listed = n * cap
    padded = -(-listed // 128) * 128
    size = interface_size
    part_order = far_first(narrow)
    half_back, middle = half_first(wide), middle_first(wide)
    orders = ((middle, half_back, half_back), (half_back, far_first(wide), half_back))
    sent = [shape(cap, loads)] * n
    full = 2 * order * loads

    list_rows = -(-(-(-cap // loads)) // 8) * 8
    pairs = peer_list[0].reshape(1, shared), partner_row
    top_high, top_low, image, *sends = call(
        functools.partial(first_kernel, n, cap),
        tuple(pltpu.with_memory_space_constraint(value, pltpu.HBM) for value in (*pairs, operator, mult)),
        [shape(shared, order, BF16)] * 2
        + [shape(shared, loads)]
        + [shape(shared + list_rows, loads)] * n,
        in_specs=[HBM] * 4,
        scratch=[
            pltpu.VMEM((1, shared), jnp.int32),
            pltpu.VMEM((1, shared), jnp.int32),
            pltpu.VMEM((shared, order), F32),
            pltpu.VMEM((order, loads), F32),
            pltpu.SemaphoreType.DMA((4,)),
        ],
        flops=3 * full * shared,
        moved=8 * shared * order,
        name="first",
    )
    unpack_own, unpack_all, unpack = call(
        functools.partial(marks_kernel, cap),
        pairs,
        [shape(shared, shared, BF16), shape(shared, n * shared, BF16), shape(shared, padded, BF16)],
        flops=8 * shared * shared * wide,
        moved=2 * shared * shared * wide,
        name="marks",
    )
    floor, basis, tile_high, tile_low = call(
        prepare_kernel,
        (contact_rows, modes, coarse_inverse),
        [shape(order, loads)] + [shape(order, 3 * count, BF16)] + [shape(*coarse_inverse.shape, BF16)] * 2,
        flops=full * count,
        moved=8 * coarse_inverse.size + 4 * full,
        name="prepare",
    )
    mult_s = mult
    scratch = [pltpu.VMEM((order, 2 * loads), BF16)]
    for outer in range(OUTER):
        times = orders[outer][0]
        recvs = swap_rows(sends, "wide", wide, times)
        base = call(
            base_kernel,
            (image, unpack_own, gap),
            [shape(shared, loads)],
            flops=4 * shared * shared * loads,
            moved=8 * shared * loads,
            name="base",
        )[0]
        if outer == 0:
            row_block, load_block = block((shared, order)), block((shared, loads))
            next_loads = block((shared, loads), 1)
            trial_n, started, high, low = call(
                rest_start_kernel,
                (size, operator, mult, mult, gap, modes),
                [shape(rest, loads), shape(count, loads)] + [shape(rest, order, BF16)] * 2,
                [
                    SMEM,
                    block((shared, order), 1),
                    whole((order, loads)),
                    next_loads,
                    next_loads,
                    block((count, shared), 1, across=True),
                ],
                [load_block, whole((count, loads)), row_block, row_block],
                scratch=scratch,
                grid=(steps,),
                flops=3 * full * rest,
                moved=8 * rest * order,
                name="rest_start",
            )
            marks = unpack_all
            pack, stack_high, stack_low = call(
                functools.partial(pack_kernel, times, cap),
                (*recvs, top_high, top_low),
                [shape(padded, shared, BF16)] + [shape(shared + padded, shared, BF16)] * 2,
                flops=8 * padded * shared * shared,
                moved=8 * padded * shared,
                name="pack",
            )
        else:
            trial_n, started = call(
                rest_first_kernel,
                (size, high, low, mult_s, mult_n, gap, modes),
                [shape(rest, loads), shape(count, loads)],
                flops=3 * full * rest,
                moved=4 * rest * order,
                name="rest_first",
            )
            marks = unpack
        trial_s, own, *coarse = call(
            functools.partial(coarse_kernel, times),
            (size, *recvs, base, marks, mult_s, modes, started),
            [shape(shared, loads)] + [shape(count, loads)] * wide,
            flops=6 * shared * loads * unpack.shape[1],
            moved=2 * shared * unpack.shape[1],
            name="coarse",
        )
        coarse_order = half_back if outer == 0 else far_first(wide)
        blocks = [own] + swap_all(coarse, "wide", wide, coarse_order)
        own, *parts = call(
            functools.partial(tile_kernel, coarse_order, part_order),
            (tile_high, tile_low, *blocks),
            [shape(count, loads)] * narrow,
            scratch=[
                pltpu.VMEM((wide * count, loads), F32),
                pltpu.VMEM((narrow * count, loads), F32),
            ],
            flops=6 * coarse_inverse.size * loads,
            moved=4 * coarse_inverse.size,
            name="tile",
        )
        parts = [own] + swap_all(parts, "narrow", narrow, part_order)
        mult_s, mult_n, image, *sends = call(
            functools.partial(lift_kernel, n, m, cap),
            (size, *parts, basis, trial_s, trial_n, floor, top_high, top_low, pack),
            [shape(shared, loads), shape(rest, loads), shape(shared, loads)] + sent,
            flops=3 * full * shared,
            moved=4 * order * shared,
            name="lift",
        )
        for inner in range(1, INNER):
            last = outer == OUTER - 1 and inner == INNER - 1
            times = orders[outer][inner]
            recvs = swap_rows(sends, "wide", wide, times)
            base = call(
                base_kernel,
                (image, unpack_own, gap),
                [shape(shared, loads)],
                flops=4 * shared * shared * loads,
                moved=8 * shared * loads,
                name="base",
            )[0]
            ins = (size, high, low, mult_s, mult_n, gap, floor)
            shadow = (size, *recvs, base, unpack, mult_s, floor)
            cost = dict(flops=6 * shared * loads * unpack.shape[1], moved=2 * shared * unpack.shape[1])
            if last:
                outs = call(
                    rest_last_kernel,
                    ins,
                    [shape(order, loads)] * 2,
                    out_specs=[HBM] * 2,
                    scratch=[pltpu.VMEM((rest, loads), F32)] * 2 + [pltpu.SemaphoreType.DMA((2,))],
                    flops=3 * full * rest,
                    moved=4 * rest * order,
                    name="rest_last",
                )
                outs = call(
                    functools.partial(last_kernel, times),
                    (*shadow, *outs),
                    [shape(order, loads)] * 2,
                    in_specs=[SMEM] + [VMEM] * (len(shadow) - 1) + [HBM] * 2,
                    out_specs=[HBM] * 2,
                    scratch=[pltpu.VMEM((shared, loads), F32)] * 2 + [pltpu.SemaphoreType.DMA((2,))],
                    alias={len(shadow): 0, len(shadow) + 1: 1},
                    name="last",
                    **cost,
                )
                return tuple(out[None] for out in outs)
            mult_n, ahead = call(
                rest_kernel,
                (*ins, top_high, top_low, pack),
                [shape(rest, loads), shape(shared + padded, loads)],
                flops=3 * full * order,
                moved=4 * order * order,
                name="rest",
            )
            mult_s, image, *sends = call(
                functools.partial(sweep_kernel, times, cap),
                (*shadow, stack_high, stack_low, ahead),
                [shape(shared, loads)] * 2 + sent,
                name="sweep",
                **cost,
            )


def solution(mesh):
    wide = mesh.shape["wide"]
    narrow = mesh.shape["narrow"]

    def body(*args):
        return local(wide, narrow, *args)

    return jax.shard_map(
        body,
        mesh=mesh,
        in_specs=(
            P(("groups", "wide", "narrow"), None, None),
            P(("groups", "wide"), "narrow"),
            P(("groups", "wide", "narrow"), None, None),
            P(("groups", "wide", "narrow"), None, None),
            P(("groups", "wide", "narrow"), None, None),
            P(("groups", "wide", "narrow"), None, None),
            P(("groups", "wide", "narrow"), None),
            P(("groups", "wide", "narrow")),
            P(("groups", "wide", "narrow"), None),
        ),
        out_specs=(
            P(("groups", "wide", "narrow"), None, None),
            P(("groups", "wide", "narrow"), None, None),
        ),
        check_vma=False,
    )
```

```python
import functools

import jax
import jax.numpy as jnp
from jax import lax
from jax.experimental import pallas as pl
from jax.experimental.pallas import tpu as pltpu
from jax.sharding import PartitionSpec as P

OUTER = 2
INNER = 3
STEP = 0.3
F32 = jnp.float32
BF16 = jnp.bfloat16
PARAMS = pltpu.CompilerParams(vmem_limit_bytes=24 * 1024 * 1024)


def split(value):
    high = value.astype(BF16)
    return high, (value - high.astype(F32)).astype(BF16)


def mm(left, right):
    return jnp.dot(left, right, preferred_element_type=F32)


def stack(value):
    return jnp.concatenate(split(value), axis=0)


def product(left, right):
    rows, width = left.shape[0] // 2, right.shape[1]
    both = mm(left, jnp.concatenate(split(right), axis=1))
    return both[:rows, :width] + (both[:rows, width:] + both[rows:, :width] + both[rows:, width:])


def pick(chosen, value):
    width = value.shape[1]
    both = mm(chosen, jnp.concatenate(split(value), axis=1))
    return both[:, :width] + both[:, width:]


def live(size, start, rows, width):
    return lax.broadcasted_iota(jnp.int32, (rows, width), 0) + start < size


def call(body, ins, outs, in_specs=None, out_specs=None, scratch=(), grid=(), flops=0, moved=0, alias=None, name=None):
    if in_specs is None:
        in_specs = [SMEM if value.ndim == 1 else VMEM for value in ins]
    if out_specs is None:
        out_specs = [VMEM] * len(outs)
    return pl.pallas_call(
        body,
        out_shape=outs,
        grid=grid,
        in_specs=in_specs,
        out_specs=out_specs,
        scratch_shapes=list(scratch),
        compiler_params=PARAMS,
        cost_estimate=pl.CostEstimate(flops=flops, bytes_accessed=moved, transcendentals=0),
        input_output_aliases=alias or {},
        name=name,
    )(*ins)


def whole(shape):
    return pl.BlockSpec(shape, lambda *i: (0,) * len(shape))


def block(shape, at=0, across=False):
    if across:
        return pl.BlockSpec(shape, lambda i: (0, i + at))
    return pl.BlockSpec(shape, lambda i: (i + at, 0))


SMEM = pl.BlockSpec(memory_space=pltpu.SMEM)
HBM = pl.BlockSpec(memory_space=pltpu.HBM)
VMEM = pl.BlockSpec(memory_space=pltpu.VMEM)


def shape(rows, columns, dtype=F32):
    return jax.ShapeDtypeStruct((rows, columns), dtype)


def places(peers, rows):
    shared = peers.shape[1]
    across = jnp.broadcast_to(peers[...], (shared, shared))
    down = across.T
    first = lax.broadcasted_iota(jnp.int32, (shared, shared), 0)
    second = lax.broadcasted_iota(jnp.int32, (shared, shared), 1)
    slot = jnp.sum(
        jnp.where((across == down) & (second < first), 1.0, 0.0), axis=1, keepdims=True
    ).astype(jnp.int32)
    wanted = jnp.broadcast_to(rows[...], (shared, shared)).T[:, :1]
    return down[:, :1] ^ lax.axis_index("wide"), slot, wanted


def first_kernel(n, cap, peers_at, rows_at, operator_at, mult_at, *refs):
    top, image = refs[:2]
    sends, (peers, rows, operator, mult, done) = refs[2:2 + n], refs[2 + n:]
    shared, width = image.shape
    order = mult.shape[0]
    halves = [pl.ds(at, order // 2) for at in (0, order // 2)]
    copies = [
        pltpu.make_async_copy(source, target, done.at[i])
        for i, (source, target) in enumerate(
            [(peers_at, peers), (rows_at, rows), (mult_at, mult)]
            + [(operator_at.at[pl.ds(0, shared), half], operator.at[:, half]) for half in halves]
        )
    ]
    for copy in copies:
        copy.start()
    copies[0].wait()
    copies[1].wait()
    far, slot, wanted = places(peers, rows)
    wanted = wanted.astype(F32)
    lane = lax.broadcasted_iota(jnp.int32, (shared, width), 1)
    for d, out in enumerate(sends, 1):
        out[shared:, :] = jnp.zeros((out.shape[0] - shared, width), F32)
        for c in range(-(-cap // width)):
            hit = (far == d) & (slot == lane + c * width)
            out[shared + c:shared + c + 1, :] = jnp.sum(
                jnp.where(hit, wanted, 0.0), axis=0, keepdims=True
            )
    copies[2].wait()
    value = jnp.zeros((shared, width), F32)
    for copy, half in zip(copies[3:], halves):
        copy.wait()
        parts = stack(operator[:, half])
        top[:, half] = parts
        value = value + product(parts, mult[half, :])
    image[...] = value
    for out in sends:
        out[:shared, :] = value


def marks_kernel(cap, peers, rows, unpack_own, unpack_all, unpack):
    far, slot, wanted = places(peers, rows)
    shared = peers.shape[1]
    for key, out in (
        (jnp.where(far == 0, wanted, -1), unpack_own),
        (jnp.where(far == 0, -1, (far - 1) * shared + wanted), unpack_all),
        (jnp.where(far == 0, -1, (far - 1) * cap + slot), unpack),
    ):
        hit = key == lax.broadcasted_iota(jnp.int32, out.shape, 1)
        out[...] = jnp.where(hit, 1.0, 0.0).astype(BF16)


def pack_kernel(times, cap, *refs):
    n = len(times)
    recvs, (top, pack, square) = refs[:n], refs[n:]
    shared = pack.shape[1]
    width = recvs[0].shape[1]
    column = lax.broadcasted_iota(jnp.int32, (width, shared), 1).astype(F32)
    if n * cap < pack.shape[0]:
        pack[n * cap:, :] = jnp.zeros((pack.shape[0] - n * cap, shared), BF16)
    for d, recv in zip(times, recvs):
        for c in range(-(-cap // width)):
            wanted = jnp.broadcast_to(recv[shared + c:shared + c + 1, :], (shared, width)).T
            chosen = jnp.where(wanted == column, 1.0, 0.0).astype(BF16)
            size = min(width, cap - c * width)
            at = (d - 1) * cap + c * width
            pack[at:at + size, :] = chosen[:size]
    half = square.shape[0] // 2
    for i in range(2):
        part = top[i * shared:(i + 1) * shared, :shared]
        square[i * half:i * half + shared, :] = part
        square[i * half + shared:(i + 1) * half, :] = mm(pack[...], part).astype(BF16)


def prepare_kernel(contact, modes, tile, floor, basis, tile_parts):
    order, width = floor.shape
    for at in range(0, order, width):
        flag = jnp.broadcast_to(contact[:, at:at + width], (width, width)).T
        floor[at:at + width, :] = jnp.where(flag == 1, 0.0, -jnp.inf)
    high, low = [part.astype(F32) for part in split(modes[...])]
    basis[...] = jnp.concatenate([high, high, low], axis=0).T.astype(BF16)
    tile_parts[...] = stack(tile[...])


def send(cap, chosen, image, sends):
    picked = pick(chosen, image)
    for d, out in enumerate(sends):
        out[...] = picked[d * cap:(d + 1) * cap]


def arrived(times, recvs, shared, unpack):
    blocks = [recvs[times.index(d)][...][:shared] for d in sorted(times)]
    rows = sum(b.shape[0] for b in blocks)
    if rows < unpack.shape[1]:
        blocks.append(jnp.zeros((unpack.shape[1] - rows, blocks[0].shape[1]), F32))
    return pick(unpack[...], jnp.concatenate(blocks, axis=0))


def base_kernel(image, unpack_own, gap, base):
    own = image[...]
    base[...] = gap[:own.shape[0], :] - own + pick(unpack_own[...], own)


def settle(trial, floor, alive):
    return jnp.where(alive, jnp.maximum(trial, floor), 0.0)


def shared_residual(times, recvs, base, unpack, size):
    known = base[...]
    alive = live(size[0], 0, *known.shape)
    return jnp.where(alive, known + arrived(times, recvs, known.shape[0], unpack), 0.0), alive


def rest_start_kernel(size, operator, mult, mult_block, gap, modes, trial, coarse, parts, halves):
    step = pl.program_id(0)
    rows, width = gap.shape

    @pl.when(step == 0)
    def _():
        halves[:, :width], halves[:, width:] = split(mult[...])
        coarse[...] = jnp.zeros_like(coarse)

    high, low = split(operator[...])
    parts[0], parts[1] = high, low
    both = mm(jnp.concatenate([high, low], axis=0), halves[...])
    image = both[:rows, :width] + (both[:rows, width:] + both[rows:, :width] + both[rows:, width:])
    alive = live(size[0], (step + 1) * rows, rows, width)
    residual = jnp.where(alive, gap[...] - image, 0.0)
    trial[...] = mult_block[...] + STEP * residual
    coarse[...] += product(stack(modes[...]), residual)


def rest_residual(size, parts, mult_s, mult_n, gap):
    shared, (rows, width) = mult_s.shape[0], mult_n.shape
    mult = jnp.concatenate([mult_s[...], mult_n[...]], axis=0)
    image = product(parts[...].reshape(2 * rows, parts.shape[2]), mult)
    alive = live(size[0], shared, rows, width)
    return jnp.where(alive, gap[shared:, :] - image, 0.0), alive


def rest_first_kernel(size, parts, mult_s, mult_n, gap, modes, trial, coarse):
    residual, _ = rest_residual(size, parts, mult_s, mult_n, gap)
    trial[...] = mult_n[...] + STEP * residual
    coarse[...] = product(stack(modes[:, mult_s.shape[0]:]), residual)


def rest_kernel(size, parts, mult_s, mult_n, gap, floor, top, pack, mult_out, ahead):
    shared = mult_s.shape[0]
    residual, alive = rest_residual(size, parts, mult_s, mult_n, gap)
    mult = settle(mult_n[...] + STEP * residual, floor[shared:, :], alive)
    mult_out[...] = mult
    value = product(top[:, shared:], mult)
    ahead[:shared, :] = value
    ahead[shared:, :] = pick(pack[...], value)


def rest_last_kernel(size, parts, mult_s, mult_n, gap, floor, mult_out, residual_out, settled, left, done):
    shared, rows = mult_s.shape[0], mult_n.shape[0]
    residual, alive = rest_residual(size, parts, mult_s, mult_n, gap)
    left[...] = residual
    settled[...] = settle(mult_n[...] + STEP * residual, floor[shared:, :], alive)
    copies = [
        pltpu.make_async_copy(source, target.at[pl.ds(shared, rows)], done.at[i])
        for i, (source, target) in enumerate(((left, residual_out), (settled, mult_out)))
    ]
    for copy in copies:
        copy.start()
    for copy in copies:
        copy.wait()


def coarse_kernel(times, size, *refs):
    n = len(times)
    recvs = refs[:n]
    base, unpack, mult, modes, started, trial = refs[n:n + 6]
    shared = base.shape[0]
    residual, _ = shared_residual(times, recvs, base, unpack, size)
    coarse = started[...] + product(stack(modes[:, :shared]), residual)
    for out in refs[n + 6:]:
        out[...] = coarse
    trial[...] = mult[:shared, :] + STEP * residual


def tile_kernel(wide_order, narrow_order, tile, *refs):
    n, m = len(wide_order), len(narrow_order)
    blocks, outs, (gathered, parts) = refs[:n + 1], refs[n + 1:n + m + 2], refs[n + m + 2:]
    count = blocks[0].shape[0]
    for d, ref in zip((0, *wide_order), blocks):
        at = pl.multiple_of((lax.axis_index("wide") ^ d) * count, count)
        gathered[pl.ds(at, count), :] = ref[...]
    parts[...] = product(tile[...], gathered[...])
    for d, out in zip((0, *narrow_order), outs):
        at = pl.multiple_of((lax.axis_index("narrow") ^ d) * count, count)
        out[...] = parts[pl.ds(at, count), :]


def lift_kernel(n, m, cap, size, *refs):
    parts = refs[:m + 1]
    ins, (mult_s, mult_n, image), sends = refs[m + 1:m + 7], refs[m + 7:m + 10], refs[m + 10:]
    basis, trial_s, trial_n, floor, top, pack = ins
    solved = parts[0][...]
    for part in parts[1:]:
        solved = solved + part[...]
    shared, width = trial_s.shape
    order = floor.shape[0]
    high, low = split(solved)
    lifted = mm(basis[...], jnp.concatenate([high, low, high], axis=0))
    shared, width = trial_s.shape
    alive = live(size[0], 0, floor.shape[0], width)
    first = settle(trial_s[...] + lifted[:shared], floor[:shared, :], alive[:shared])
    rest = settle(trial_n[...] + lifted[shared:], floor[shared:, :], alive[shared:])
    mult_s[...] = first
    mult_n[...] = rest
    value = product(top[...], jnp.concatenate([first, rest], axis=0))
    image[...] = value
    send(cap, pack[...], value, sends)


def sweep_kernel(times, cap, size, *refs):
    n = len(times)
    recvs = refs[:n]
    base, unpack, mult, floor, square, ahead, mult_out, image_out = refs[n:n + 8]
    shared = base.shape[0]
    residual, alive = shared_residual(times, recvs, base, unpack, size)
    value = settle(mult[...] + STEP * residual, floor[:shared, :], alive)
    mult_out[...] = value
    both = ahead[...] + product(square[...], value)
    image_out[...] = both[:shared]
    for d, out in enumerate(refs[n + 8:]):
        out[...] = both[shared + d * cap:shared + (d + 1) * cap]


def last_kernel(times, size, *refs):
    n = len(times)
    recvs = refs[:n]
    base, unpack, mult, floor, _, _, mult_out, residual_out, settled, left, done = refs[n:]
    shared = base.shape[0]
    residual, alive = shared_residual(times, recvs, base, unpack, size)
    left[...] = residual
    first = pltpu.make_async_copy(left, residual_out.at[pl.ds(0, shared)], done.at[0])
    first.start()
    settled[...] = settle(mult[...] + STEP * residual, floor[:shared, :], alive)
    second = pltpu.make_async_copy(settled, mult_out.at[pl.ds(0, shared)], done.at[1])
    second.start()
    first.wait()
    second.wait()


def swap(block, axis, count, d):
    return lax.ppermute(block, axis, [(i, i ^ d) for i in range(count)])


def swap_all(blocks, axis, count, order):
    return [swap(block, axis, count, d) for block, d in zip(blocks, order)]


def swap_rows(blocks, axis, count, times):
    return [swap(blocks[d - 1], axis, count, d) for d in times]


def half_first(count):
    half = count // 2
    return (half, *(d for d in range(count - 1, 0, -1) if d != half))


def middle_first(count):
    return (count - 1, *range(1, count - 1))


def far_first(count):
    return tuple(range(count - 1, 0, -1))


def local(
    wide,
    narrow,
    operators,
    coarse_inverse,
    modes,
    gap,
    start_mult,
    peer_list,
    partner_row,
    interface_size,
    contact_rows,
):
    operator = operators[0]
    modes = modes[0]
    gap = gap[0]
    mult = start_mult[0]
    order, loads = mult.shape
    shared = partner_row.shape[1]
    count = modes.shape[0]
    rest = order - shared
    steps = rest // shared
    n, m = wide - 1, narrow - 1
    cap = 2 * shared // wide
    listed = n * cap
    padded = -(-listed // 128) * 128
    size = interface_size
    part_order = far_first(narrow)
    half_back, middle = half_first(wide), middle_first(wide)
    orders = ((middle, half_back, middle), (half_back, half_back, half_back))
    sent = [shape(cap, loads)] * n
    full = 2 * order * loads

    list_rows = -(-(-(-cap // loads)) // 8) * 8
    pairs = peer_list[0].reshape(1, shared), partner_row
    top, image, *sends = call(
        functools.partial(first_kernel, n, cap),
        tuple(pltpu.with_memory_space_constraint(value, pltpu.HBM) for value in (*pairs, operator, mult)),
        [shape(2 * shared, order, BF16), shape(shared, loads)]
        + [shape(shared + list_rows, loads)] * n,
        in_specs=[HBM] * 4,
        scratch=[
            pltpu.VMEM((1, shared), jnp.int32),
            pltpu.VMEM((1, shared), jnp.int32),
            pltpu.VMEM((shared, order), F32),
            pltpu.VMEM((order, loads), F32),
            pltpu.SemaphoreType.DMA((5,)),
        ],
        flops=3 * full * shared,
        moved=8 * shared * order,
        name="first",
    )
    unpack_own, unpack_all, unpack = call(
        functools.partial(marks_kernel, cap),
        pairs,
        [shape(shared, shared, BF16), shape(shared, n * shared, BF16), shape(shared, padded, BF16)],
        flops=8 * shared * shared * wide,
        moved=2 * shared * shared * wide,
        name="marks",
    )
    floor, basis, tile_parts = call(
        prepare_kernel,
        (contact_rows, modes, coarse_inverse),
        [shape(order, loads)] + [shape(order, 3 * count, BF16)] + [shape(2 * narrow * count, wide * count, BF16)],
        flops=full * count,
        moved=8 * coarse_inverse.size + 4 * full,
        name="prepare",
    )
    mult_s = mult
    scratch = [pltpu.VMEM((order, 2 * loads), BF16)]
    for outer in range(OUTER):
        times = orders[outer][0]
        recvs = swap_rows(sends, "wide", wide, times)
        base = call(
            base_kernel,
            (image, unpack_own, gap),
            [shape(shared, loads)],
            flops=4 * shared * shared * loads,
            moved=8 * shared * loads,
            name="base",
        )[0]
        if outer == 0:
            next_loads = block((shared, loads), 1)
            trial_n, started, parts = call(
                rest_start_kernel,
                (size, operator, mult, mult, gap, modes),
                [shape(rest, loads), shape(count, loads), jax.ShapeDtypeStruct((2, rest, order), BF16)],
                [
                    SMEM,
                    block((shared, order), 1),
                    whole((order, loads)),
                    next_loads,
                    next_loads,
                    block((count, shared), 1, across=True),
                ],
                [
                    block((shared, loads)),
                    whole((count, loads)),
                    pl.BlockSpec((2, shared, order), lambda i: (0, i, 0)),
                ],
                scratch=scratch,
                grid=(steps,),
                flops=3 * full * rest,
                moved=8 * rest * order,
                name="rest_start",
            )
            marks = unpack_all
            pack, square = call(
                functools.partial(pack_kernel, times, cap),
                (*recvs, top),
                [shape(padded, shared, BF16), shape(2 * (shared + padded), shared, BF16)],
                flops=8 * padded * shared * shared,
                moved=8 * padded * shared,
                name="pack",
            )
        else:
            trial_n, started = call(
                rest_first_kernel,
                (size, parts, mult_s, mult_n, gap, modes),
                [shape(rest, loads), shape(count, loads)],
                flops=3 * full * rest,
                moved=4 * rest * order,
                name="rest_first",
            )
            marks = unpack
        trial_s, own, *coarse = call(
            functools.partial(coarse_kernel, times),
            (size, *recvs, base, marks, mult_s, modes, started),
            [shape(shared, loads)] + [shape(count, loads)] * wide,
            flops=6 * shared * loads * unpack.shape[1],
            moved=2 * shared * unpack.shape[1],
            name="coarse",
        )
        coarse_order = half_back if outer == 0 else far_first(wide)
        blocks = [own] + swap_all(coarse, "wide", wide, coarse_order)
        own, *shares = call(
            functools.partial(tile_kernel, coarse_order, part_order),
            (tile_parts, *blocks),
            [shape(count, loads)] * narrow,
            scratch=[
                pltpu.VMEM((wide * count, loads), F32),
                pltpu.VMEM((narrow * count, loads), F32),
            ],
            flops=6 * coarse_inverse.size * loads,
            moved=4 * coarse_inverse.size,
            name="tile",
        )
        shares = [own] + swap_all(shares, "narrow", narrow, part_order)
        mult_s, mult_n, image, *sends = call(
            functools.partial(lift_kernel, n, m, cap),
            (size, *shares, basis, trial_s, trial_n, floor, top, pack),
            [shape(shared, loads), shape(rest, loads), shape(shared, loads)] + sent,
            flops=3 * full * shared,
            moved=4 * order * shared,
            name="lift",
        )
        for inner in range(1, INNER):
            last = outer == OUTER - 1 and inner == INNER - 1
            times = orders[outer][inner]
            recvs = swap_rows(sends, "wide", wide, times)
            base = call(
                base_kernel,
                (image, unpack_own, gap),
                [shape(shared, loads)],
                flops=4 * shared * shared * loads,
                moved=8 * shared * loads,
                name="base",
            )[0]
            ins = (size, parts, mult_s, mult_n, gap, floor)
            shadow = (size, *recvs, base, unpack, mult_s, floor)
            cost = dict(flops=6 * shared * loads * unpack.shape[1], moved=2 * shared * unpack.shape[1])
            if last:
                outs = call(
                    rest_last_kernel,
                    ins,
                    [shape(order, loads)] * 2,
                    out_specs=[HBM] * 2,
                    scratch=[pltpu.VMEM((rest, loads), F32)] * 2 + [pltpu.SemaphoreType.DMA((2,))],
                    flops=3 * full * rest,
                    moved=4 * rest * order,
                    name="rest_last",
                )
                outs = call(
                    functools.partial(last_kernel, times),
                    (*shadow, *outs),
                    [shape(order, loads)] * 2,
                    in_specs=[SMEM] + [VMEM] * (len(shadow) - 1) + [HBM] * 2,
                    out_specs=[HBM] * 2,
                    scratch=[pltpu.VMEM((shared, loads), F32)] * 2 + [pltpu.SemaphoreType.DMA((2,))],
                    alias={len(shadow): 0, len(shadow) + 1: 1},
                    name="last",
                    **cost,
                )
                return tuple(out[None] for out in outs)
            mult_n, ahead = call(
                rest_kernel,
                (*ins, top, pack),
                [shape(rest, loads), shape(shared + padded, loads)],
                flops=3 * full * order,
                moved=4 * order * order,
                name="rest",
            )
            mult_s, image, *sends = call(
                functools.partial(sweep_kernel, times, cap),
                (*shadow, square, ahead),
                [shape(shared, loads)] * 2 + sent,
                name="sweep",
                **cost,
            )


def solution(mesh):
    wide = mesh.shape["wide"]
    narrow = mesh.shape["narrow"]

    def body(*args):
        return local(wide, narrow, *args)

    return jax.shard_map(
        body,
        mesh=mesh,
        in_specs=(
            P(("groups", "wide", "narrow"), None, None),
            P(("groups", "wide"), "narrow"),
            P(("groups", "wide", "narrow"), None, None),
            P(("groups", "wide", "narrow"), None, None),
            P(("groups", "wide", "narrow"), None, None),
            P(("groups", "wide", "narrow"), None, None),
            P(("groups", "wide", "narrow"), None),
            P(("groups", "wide", "narrow")),
            P(("groups", "wide", "narrow"), None),
        ),
        out_specs=(
            P(("groups", "wide", "narrow"), None, None),
            P(("groups", "wide", "narrow"), None, None),
        ),
        check_vma=False,
    )
```

```python
import functools

import jax
import jax.numpy as jnp
from jax import lax
from jax.experimental import pallas as pl
from jax.experimental.pallas import tpu as pltpu
from jax.sharding import PartitionSpec as P

OUTER = 2
INNER = 3
STEP = 0.3
F32 = jnp.float32
BF16 = jnp.bfloat16
PARAMS = pltpu.CompilerParams(vmem_limit_bytes=24 * 1024 * 1024)


def split(value):
    high = value.astype(BF16)
    return high, (value - high.astype(F32)).astype(BF16)


def mm(left, right):
    return jnp.dot(left, right, preferred_element_type=F32)


def product(left, right):
    (left_high, left_low), (right_high, right_low) = left, right
    width = right_high.shape[1]
    both = mm(left_high, jnp.concatenate([right_high, right_low], axis=1))
    return both[:, :width] + (both[:, width:] + mm(left_low, right_high))


def pick(chosen, value):
    width = value.shape[1]
    both = mm(chosen, jnp.concatenate(split(value), axis=1))
    return both[:, :width] + both[:, width:]


def live(size, start, rows, width):
    return lax.broadcasted_iota(jnp.int32, (rows, width), 0) + start < size


def call(body, ins, outs, in_specs=None, out_specs=None, scratch=(), grid=(), flops=0, moved=0, alias=None, name=None):
    if in_specs is None:
        in_specs = [SMEM if value.ndim == 1 else VMEM for value in ins]
    if out_specs is None:
        out_specs = [VMEM] * len(outs)
    return pl.pallas_call(
        body,
        out_shape=outs,
        grid=grid,
        in_specs=in_specs,
        out_specs=out_specs,
        scratch_shapes=list(scratch),
        compiler_params=PARAMS,
        cost_estimate=pl.CostEstimate(flops=flops, bytes_accessed=moved, transcendentals=0),
        input_output_aliases=alias or {},
        name=name,
    )(*ins)


def whole(shape):
    return pl.BlockSpec(shape, lambda *i: (0,) * len(shape))


def block(shape, at=0, across=False):
    if across:
        return pl.BlockSpec(shape, lambda i: (0, i + at))
    return pl.BlockSpec(shape, lambda i: (i + at, 0))


SMEM = pl.BlockSpec(memory_space=pltpu.SMEM)
HBM = pl.BlockSpec(memory_space=pltpu.HBM)
VMEM = pl.BlockSpec(memory_space=pltpu.VMEM)


def shape(rows, columns, dtype=F32):
    return jax.ShapeDtypeStruct((rows, columns), dtype)


def first_kernel(n, cap, peers_at, rows_at, operator_at, mult_at, *refs):
    unpack_own, unpack_all, unpack, high, low, image = refs[:6]
    sends, (peers, rows, operator, mult, done) = refs[6:6 + n], refs[6 + n:]
    shared, width = image.shape
    copies = [
        pltpu.make_async_copy(source, target, done.at[i])
        for i, (source, target) in enumerate(
            ((peers_at, peers), (rows_at, rows), (mult_at, mult), (operator_at.at[pl.ds(0, shared)], operator))
        )
    ]
    for copy in copies:
        copy.start()
    copies[0].wait()
    copies[1].wait()
    across = jnp.broadcast_to(peers[...], (shared, shared))
    down = across.T
    first = lax.broadcasted_iota(jnp.int32, (shared, shared), 0)
    second = lax.broadcasted_iota(jnp.int32, (shared, shared), 1)
    slot = jnp.sum(
        jnp.where((across == down) & (second < first), 1.0, 0.0), axis=1, keepdims=True
    ).astype(jnp.int32)
    wanted = jnp.broadcast_to(rows[...], (shared, shared)).T[:, :1]
    far = down[:, :1] ^ lax.axis_index("wide")

    def marks(key, columns):
        hit = key == lax.broadcasted_iota(jnp.int32, (shared, columns), 1)
        return jnp.where(hit, 1.0, 0.0).astype(BF16)

    unpack_own[...] = marks(jnp.where(far == 0, wanted, -1), shared)
    unpack_all[...] = marks(jnp.where(far == 0, -1, (far - 1) * shared + wanted), unpack_all.shape[1])
    unpack[...] = marks(jnp.where(far == 0, -1, (far - 1) * cap + slot), unpack.shape[1])
    lane = lax.broadcasted_iota(jnp.int32, (shared, width), 1)
    for d, out in enumerate(sends, 1):
        out[shared:, :] = jnp.zeros((out.shape[0] - shared, width), F32)
        for c in range(-(-cap // width)):
            hit = (far == d) & (slot == lane + c * width)
            out[shared + c:shared + c + 1, :] = jnp.sum(
                jnp.where(hit, wanted.astype(F32), 0.0), axis=0, keepdims=True
            )
    copies[2].wait()
    copies[3].wait()
    parts = split(operator[...])
    high[...], low[...] = parts
    value = product(parts, split(mult[...]))
    image[...] = value
    for out in sends:
        out[:shared, :] = value


def pack_kernel(times, cap, *refs):
    n = len(times)
    recvs, (high, low, pack, stack_high, stack_low) = refs[:n], refs[n:]
    shared = pack.shape[1]
    width = recvs[0].shape[1]
    column = lax.broadcasted_iota(jnp.int32, (width, shared), 1).astype(F32)
    if n * cap < pack.shape[0]:
        pack[n * cap:, :] = jnp.zeros((pack.shape[0] - n * cap, shared), BF16)
    for d, recv in zip(times, recvs):
        for c in range(-(-cap // width)):
            wanted = jnp.broadcast_to(recv[shared + c:shared + c + 1, :], (shared, width)).T
            chosen = jnp.where(wanted == column, 1.0, 0.0).astype(BF16)
            size = min(width, cap - c * width)
            at = (d - 1) * cap + c * width
            pack[at:at + size, :] = chosen[:size]
    for source, stack in ((high, stack_high), (low, stack_low)):
        square = source[:, :shared]
        stack[:shared, :] = square
        stack[shared:, :] = mm(pack[...], square).astype(BF16)


def prepare_kernel(contact, modes, tile, floor, basis, tile_high, tile_low):
    order, width = floor.shape
    for at in range(0, order, width):
        flag = jnp.broadcast_to(contact[:, at:at + width], (width, width)).T
        floor[at:at + width, :] = jnp.where(flag == 1, 0.0, -jnp.inf)
    high, low = [part.astype(F32) for part in split(modes[...])]
    basis[...] = jnp.concatenate([high, high, low], axis=0).T.astype(BF16)
    tile_high[...], tile_low[...] = split(tile[...])


def send(cap, chosen, image, sends):
    picked = pick(chosen, image)
    for d, out in enumerate(sends):
        out[...] = picked[d * cap:(d + 1) * cap]


def arrived(times, recvs, shared, unpack):
    blocks = [recvs[times.index(d)][...][:shared] for d in sorted(times)]
    rows = sum(b.shape[0] for b in blocks)
    if rows < unpack.shape[1]:
        blocks.append(jnp.zeros((unpack.shape[1] - rows, blocks[0].shape[1]), F32))
    return pick(unpack[...], jnp.concatenate(blocks, axis=0))


def base_kernel(image, unpack_own, gap, base):
    own = image[...]
    base[...] = gap[:own.shape[0], :] - own + pick(unpack_own[...], own)


def settle(trial, floor, alive):
    return jnp.where(alive, jnp.maximum(trial, floor), 0.0)


def shared_residual(times, recvs, base, unpack, size):
    known = base[...]
    alive = live(size[0], 0, *known.shape)
    return jnp.where(alive, known + arrived(times, recvs, known.shape[0], unpack), 0.0), alive


def rest_start_kernel(size, operator, mult, mult_block, gap, modes, trial, coarse, high, low, halves):
    step = pl.program_id(0)
    rows, width = gap.shape

    @pl.when(step == 0)
    def _():
        halves[:, :width], halves[:, width:] = split(mult[...])
        coarse[...] = jnp.zeros_like(coarse)

    parts = split(operator[...])
    high[...], low[...] = parts
    both = mm(parts[0], halves[...])
    image = both[:, :width] + (both[:, width:] + mm(parts[1], halves[:, :width]))
    alive = live(size[0], (step + 1) * rows, rows, width)
    residual = jnp.where(alive, gap[...] - image, 0.0)
    trial[...] = mult_block[...] + STEP * residual
    coarse[...] += product(split(modes[...]), split(residual))


def rest_residual(size, high, low, mult_s, mult_n, gap):
    shared, (rows, width) = mult_s.shape[0], mult_n.shape
    mult = jnp.concatenate([mult_s[...], mult_n[...]], axis=0)
    image = product((high[...], low[...]), split(mult))
    alive = live(size[0], shared, rows, width)
    return jnp.where(alive, gap[shared:, :] - image, 0.0), alive


def rest_first_kernel(size, high, low, mult_s, mult_n, gap, modes, trial, coarse):
    residual, _ = rest_residual(size, high, low, mult_s, mult_n, gap)
    trial[...] = mult_n[...] + STEP * residual
    coarse[...] = product(split(modes[:, mult_s.shape[0]:]), split(residual))


def early():
    return lax.axis_index("narrow") % 2 == 1


def rest_update(size, high, low, mult_s, mult_n, gap, floor, top_high, top_low, pack, mult_out, ahead):
    shared = mult_s.shape[0]
    residual, alive = rest_residual(size, high, low, mult_s, mult_n, gap)
    mult = settle(mult_n[...] + STEP * residual, floor[shared:, :], alive)
    mult_out[...] = mult
    value = product((top_high[:, shared:], top_low[:, shared:]), split(mult))
    ahead[:shared, :] = value
    ahead[shared:, :] = pick(pack[...], value)


def rest_late_kernel(*refs):
    ins, (mult_done, ahead_done, mult_out, ahead) = refs[:-4], refs[-4:]

    @pl.when(early())
    def _():
        mult_out[...] = mult_done[...]
        ahead[...] = ahead_done[...]

    @pl.when(jnp.logical_not(early()))
    def _():
        rest_update(*ins, mult_out, ahead)


def rest_last_kernel(size, high, low, mult_s, mult_n, gap, floor, mult_out, residual_out, settled, left, done):
    shared, rows = mult_s.shape[0], mult_n.shape[0]
    residual, alive = rest_residual(size, high, low, mult_s, mult_n, gap)
    left[...] = residual
    settled[...] = settle(mult_n[...] + STEP * residual, floor[shared:, :], alive)
    copies = [
        pltpu.make_async_copy(source, target.at[pl.ds(shared, rows)], done.at[i])
        for i, (source, target) in enumerate(((left, residual_out), (settled, mult_out)))
    ]
    for copy in copies:
        copy.start()
    for copy in copies:
        copy.wait()


def coarse_kernel(times, size, *refs):
    n = len(times)
    recvs = refs[:n]
    base, unpack, mult, modes, started, trial = refs[n:n + 6]
    shared = base.shape[0]
    residual, _ = shared_residual(times, recvs, base, unpack, size)
    coarse = started[...] + product(split(modes[:, :shared]), split(residual))
    for out in refs[n + 6:]:
        out[...] = coarse
    trial[...] = mult[:shared, :] + STEP * residual


def tile_kernel(wide_order, narrow_order, high, low, *refs):
    n, m = len(wide_order), len(narrow_order)
    blocks, outs, (gathered, parts) = refs[:n + 1], refs[n + 1:n + m + 2], refs[n + m + 2:]
    count = blocks[0].shape[0]
    for d, ref in zip((0, *wide_order), blocks):
        at = pl.multiple_of((lax.axis_index("wide") ^ d) * count, count)
        gathered[pl.ds(at, count), :] = ref[...]
    parts[...] = product((high[...], low[...]), split(gathered[...]))
    for d, out in zip((0, *narrow_order), outs):
        at = pl.multiple_of((lax.axis_index("narrow") ^ d) * count, count)
        out[...] = parts[pl.ds(at, count), :]


def lift_kernel(n, m, cap, size, *refs):
    parts = refs[:m + 1]
    ins, outs, sends = refs[m + 1:m + 11], refs[m + 11:m + 16], refs[m + 16:]
    basis, trial_s, trial_n, floor, high, low, pack, rest_high, rest_low, gap = ins
    mult_s, mult_n, image, mult_done, ahead_done = outs
    solved = parts[0][...]
    for part in parts[1:]:
        solved = solved + part[...]
    shared, width = trial_s.shape
    order = floor.shape[0]
    high_part, low_part = split(solved)
    lifted = mm(basis[...], jnp.concatenate([high_part, low_part, high_part], axis=0))
    alive = live(size[0], 0, order, width)
    first = settle(trial_s[...] + lifted[:shared], floor[:shared], alive[:shared])
    rest = settle(trial_n[...] + lifted[shared:], floor[shared:], alive[shared:])
    mult_s[...] = first
    mult_n[...] = rest
    value = product((high[...], low[...]), split(jnp.concatenate([first, rest], axis=0)))
    image[...] = value
    send(cap, pack[...], value, sends)

    @pl.when(early())
    def _():
        rest_update(
            size, rest_high, rest_low, mult_s, mult_n, gap, floor, high, low, pack, mult_done, ahead_done
        )


def sweep_kernel(times, cap, size, *refs):
    n = len(times)
    recvs = refs[:n]
    base, unpack, mult, floor, high, low, ahead, mult_out, image_out = refs[n:n + 9]
    shared = base.shape[0]
    residual, alive = shared_residual(times, recvs, base, unpack, size)
    value = settle(mult[...] + STEP * residual, floor[:shared, :], alive)
    mult_out[...] = value
    both = ahead[...] + product((high[...], low[...]), split(value))
    image_out[...] = both[:shared]
    for d, out in enumerate(refs[n + 9:]):
        out[...] = both[shared + d * cap:shared + (d + 1) * cap]


def last_kernel(times, size, *refs):
    n = len(times)
    recvs = refs[:n]
    base, unpack, mult, floor, _, _, mult_out, residual_out, settled, left, done = refs[n:]
    shared = base.shape[0]
    residual, alive = shared_residual(times, recvs, base, unpack, size)
    left[...] = residual
    first = pltpu.make_async_copy(left, residual_out.at[pl.ds(0, shared)], done.at[0])
    first.start()
    settled[...] = settle(mult[...] + STEP * residual, floor[:shared, :], alive)
    second = pltpu.make_async_copy(settled, mult_out.at[pl.ds(0, shared)], done.at[1])
    second.start()
    first.wait()
    second.wait()


def swap(block, axis, count, d):
    return lax.ppermute(block, axis, [(i, i ^ d) for i in range(count)])


def swap_all(blocks, axis, count, order):
    return [swap(block, axis, count, d) for block, d in zip(blocks, order)]


def swap_rows(blocks, axis, count, times):
    return [swap(blocks[d - 1], axis, count, d) for d in times]


def half_first(count, back):
    half = count // 2
    others = [d for d in range(1, count) if d != half]
    return (half, *(others[::-1] if back else others))


def middle_first(count):
    return (count - 1, *range(1, count - 1))


def far_first(count):
    return tuple(range(count - 1, 0, -1))


def local(
    wide,
    narrow,
    operators,
    coarse_inverse,
    modes,
    gap,
    start_mult,
    peer_list,
    partner_row,
    interface_size,
    contact_rows,
):
    operator = operators[0]
    modes = modes[0]
    gap = gap[0]
    mult = start_mult[0]
    order, loads = mult.shape
    shared = partner_row.shape[1]
    count = modes.shape[0]
    rest = order - shared
    steps = rest // shared
    n, m = wide - 1, narrow - 1
    cap = 2 * shared // wide
    listed = n * cap
    padded = -(-listed // 128) * 128
    size = interface_size
    coarse_order, part_order = far_first(wide), far_first(narrow)
    half, half_back, middle = half_first(wide, False), half_first(wide, True), middle_first(wide)
    orders = ((middle, half, middle), (half_back, half, half_back))
    sent = [shape(cap, loads)] * n
    full = 2 * order * loads

    list_rows = -(-(-(-cap // loads)) // 8) * 8
    unpack_own, unpack_all, unpack, top_high, top_low, image, *sends = call(
        functools.partial(first_kernel, n, cap),
        tuple(
            pltpu.with_memory_space_constraint(value, pltpu.HBM)
            for value in (peer_list[0].reshape(1, shared), partner_row, operator, mult)
        ),
        [shape(shared, shared, BF16), shape(shared, n * shared, BF16), shape(shared, padded, BF16)]
        + [shape(shared, order, BF16)] * 2
        + [shape(shared, loads)]
        + [shape(shared + list_rows, loads)] * n,
        in_specs=[HBM] * 4,
        scratch=[
            pltpu.VMEM((1, shared), jnp.int32),
            pltpu.VMEM((1, shared), jnp.int32),
            pltpu.VMEM((shared, order), F32),
            pltpu.VMEM((order, loads), F32),
            pltpu.SemaphoreType.DMA((4,)),
        ],
        flops=3 * full * shared,
        moved=8 * shared * order,
        name="first",
    )
    floor, basis, tile_high, tile_low = call(
        prepare_kernel,
        (contact_rows, modes, coarse_inverse),
        [shape(order, loads)] + [shape(order, 3 * count, BF16)] + [shape(*coarse_inverse.shape, BF16)] * 2,
        flops=full * count,
        moved=8 * coarse_inverse.size + 4 * full,
        name="prepare",
    )
    mult_s = mult
    scratch = [pltpu.VMEM((order, 2 * loads), BF16)]
    for outer in range(OUTER):
        times = orders[outer][0]
        recvs = swap_rows(sends, "wide", wide, times)
        base = call(
            base_kernel,
            (image, unpack_own, gap),
            [shape(shared, loads)],
            flops=4 * shared * shared * loads,
            moved=8 * shared * loads,
            name="base",
        )[0]
        if outer == 0:
            row_block, load_block = block((shared, order)), block((shared, loads))
            next_loads = block((shared, loads), 1)
            trial_n, started, high, low = call(
                rest_start_kernel,
                (size, operator, mult, mult, gap, modes),
                [shape(rest, loads), shape(count, loads)] + [shape(rest, order, BF16)] * 2,
                [
                    SMEM,
                    block((shared, order), 1),
                    whole((order, loads)),
                    next_loads,
                    next_loads,
                    block((count, shared), 1, across=True),
                ],
                [load_block, whole((count, loads)), row_block, row_block],
                scratch=scratch,
                grid=(steps,),
                flops=3 * full * rest,
                moved=8 * rest * order,
                name="rest_start",
            )
            marks = unpack_all
            pack, stack_high, stack_low = call(
                functools.partial(pack_kernel, times, cap),
                (*recvs, top_high, top_low),
                [shape(padded, shared, BF16)] + [shape(shared + padded, shared, BF16)] * 2,
                flops=8 * padded * shared * shared,
                moved=8 * padded * shared,
                name="pack",
            )
        else:
            trial_n, started = call(
                rest_first_kernel,
                (size, high, low, mult_s, mult_n, gap, modes),
                [shape(rest, loads), shape(count, loads)],
                flops=3 * full * rest,
                moved=4 * rest * order,
                name="rest_first",
            )
            marks = unpack
        trial_s, own, *coarse = call(
            functools.partial(coarse_kernel, times),
            (size, *recvs, base, marks, mult_s, modes, started),
            [shape(shared, loads)] + [shape(count, loads)] * wide,
            flops=6 * shared * loads * unpack.shape[1],
            moved=2 * shared * unpack.shape[1],
            name="coarse",
        )
        blocks = [own] + swap_all(coarse, "wide", wide, coarse_order)
        own, *parts = call(
            functools.partial(tile_kernel, coarse_order, part_order),
            (tile_high, tile_low, *blocks),
            [shape(count, loads)] * narrow,
            scratch=[
                pltpu.VMEM((wide * count, loads), F32),
                pltpu.VMEM((narrow * count, loads), F32),
            ],
            flops=6 * coarse_inverse.size * loads,
            moved=4 * coarse_inverse.size,
            name="tile",
        )
        parts = [own] + swap_all(parts, "narrow", narrow, part_order)
        mult_s, mult_n, image, mult_done, ahead_done, *sends = call(
            functools.partial(lift_kernel, n, m, cap),
            (size, *parts, basis, trial_s, trial_n, floor, top_high, top_low, pack, high, low, gap),
            [shape(shared, loads), shape(rest, loads), shape(shared, loads)]
            + [shape(rest, loads), shape(shared + padded, loads)]
            + sent,
            flops=3 * full * shared,
            moved=4 * order * shared,
            name="lift",
        )
        for inner in range(1, INNER):
            last = outer == OUTER - 1 and inner == INNER - 1
            times = orders[outer][inner]
            recvs = swap_rows(sends, "wide", wide, times)
            base = call(
                base_kernel,
                (image, unpack_own, gap),
                [shape(shared, loads)],
                flops=4 * shared * shared * loads,
                moved=8 * shared * loads,
                name="base",
            )[0]
            ins = (size, high, low, mult_s, mult_n, gap, floor)
            shadow = (size, *recvs, base, unpack, mult_s, floor)
            cost = dict(flops=6 * shared * loads * unpack.shape[1], moved=2 * shared * unpack.shape[1])
            if last:
                outs = call(
                    rest_last_kernel,
                    ins,
                    [shape(order, loads)] * 2,
                    out_specs=[HBM] * 2,
                    scratch=[pltpu.VMEM((rest, loads), F32)] * 2 + [pltpu.SemaphoreType.DMA((2,))],
                    flops=3 * full * rest,
                    moved=4 * rest * order,
                    name="rest_last",
                )
                outs = call(
                    functools.partial(last_kernel, times),
                    (*shadow, *outs),
                    [shape(order, loads)] * 2,
                    in_specs=[SMEM] + [VMEM] * (len(shadow) - 1) + [HBM] * 2,
                    out_specs=[HBM] * 2,
                    scratch=[pltpu.VMEM((shared, loads), F32)] * 2 + [pltpu.SemaphoreType.DMA((2,))],
                    alias={len(shadow): 0, len(shadow) + 1: 1},
                    name="last",
                    **cost,
                )
                return tuple(out[None] for out in outs)
            mult_n, ahead = call(
                rest_late_kernel if inner == 1 else rest_update,
                (*ins, top_high, top_low, pack) + ((mult_done, ahead_done) if inner == 1 else ()),
                [shape(rest, loads), shape(shared + padded, loads)],
                flops=3 * full * order,
                moved=4 * order * order,
                name="rest",
            )
            mult_s, image, *sends = call(
                functools.partial(sweep_kernel, times, cap),
                (*shadow, stack_high, stack_low, ahead),
                [shape(shared, loads)] * 2 + sent,
                name="sweep",
                **cost,
            )


def solution(mesh):
    wide = mesh.shape["wide"]
    narrow = mesh.shape["narrow"]

    def body(*args):
        return local(wide, narrow, *args)

    return jax.shard_map(
        body,
        mesh=mesh,
        in_specs=(
            P(("groups", "wide", "narrow"), None, None),
            P(("groups", "wide"), "narrow"),
            P(("groups", "wide", "narrow"), None, None),
            P(("groups", "wide", "narrow"), None, None),
            P(("groups", "wide", "narrow"), None, None),
            P(("groups", "wide", "narrow"), None, None),
            P(("groups", "wide", "narrow"), None),
            P(("groups", "wide", "narrow")),
            P(("groups", "wide", "narrow"), None),
        ),
        out_specs=(
            P(("groups", "wide", "narrow"), None, None),
            P(("groups", "wide", "narrow"), None, None),
        ),
        check_vma=False,
    )
```

```python
import functools

import jax
import jax.numpy as jnp
from jax import lax
from jax.experimental import pallas as pl
from jax.experimental.pallas import tpu as pltpu
from jax.sharding import PartitionSpec as P

OUTER = 2
INNER = 3
STEP = 0.3
F32 = jnp.float32
BF16 = jnp.bfloat16
PARAMS = pltpu.CompilerParams(vmem_limit_bytes=24 * 1024 * 1024)


def split(value):
    high = value.astype(BF16)
    return high, (value - high.astype(F32)).astype(BF16)


def mm(left, right):
    return jnp.dot(left, right, preferred_element_type=F32)


def product(left, right):
    (left_high, left_low), (right_high, right_low) = left, right
    width = right_high.shape[1]
    both = mm(left_high, jnp.concatenate([right_high, right_low], axis=1))
    return both[:, :width] + (both[:, width:] + mm(left_low, right_high))


def pick(chosen, value):
    width = value.shape[1]
    both = mm(chosen, jnp.concatenate(split(value), axis=1))
    return both[:, :width] + both[:, width:]


def live(size, start, rows, width):
    return lax.broadcasted_iota(jnp.int32, (rows, width), 0) + start < size


def call(body, ins, outs, in_specs=None, out_specs=None, scratch=(), grid=(), flops=0, moved=0, alias=None, name=None):
    if in_specs is None:
        in_specs = [SMEM if value.ndim == 1 else VMEM for value in ins]
    if out_specs is None:
        out_specs = [VMEM] * len(outs)
    return pl.pallas_call(
        body,
        out_shape=outs,
        grid=grid,
        in_specs=in_specs,
        out_specs=out_specs,
        scratch_shapes=list(scratch),
        compiler_params=PARAMS,
        cost_estimate=pl.CostEstimate(flops=flops, bytes_accessed=moved, transcendentals=0),
        input_output_aliases=alias or {},
        name=name,
    )(*ins)


def whole(shape):
    return pl.BlockSpec(shape, lambda *i: (0,) * len(shape))


def block(shape, at=0, across=False):
    if across:
        return pl.BlockSpec(shape, lambda i: (0, i + at))
    return pl.BlockSpec(shape, lambda i: (i + at, 0))


SMEM = pl.BlockSpec(memory_space=pltpu.SMEM)
HBM = pl.BlockSpec(memory_space=pltpu.HBM)
VMEM = pl.BlockSpec(memory_space=pltpu.VMEM)


def shape(rows, columns, dtype=F32):
    return jax.ShapeDtypeStruct((rows, columns), dtype)


def by_line(even, odd):
    return even if odd is even else jnp.where(lax.axis_index("narrow") % 2 == 1, odd, even)


def first_kernel(n, cap, peers_at, rows_at, operator_at, mult_at, *refs):
    unpack_own, unpack_all, unpack, high, low, image = refs[:6]
    sends, (peers, rows, operator, mult, done) = refs[6:6 + n], refs[6 + n:]
    shared, width = image.shape
    copies = [
        pltpu.make_async_copy(source, target, done.at[i])
        for i, (source, target) in enumerate(
            ((peers_at, peers), (rows_at, rows), (mult_at, mult), (operator_at.at[pl.ds(0, shared)], operator))
        )
    ]
    for copy in copies:
        copy.start()
    copies[0].wait()
    copies[1].wait()
    across = jnp.broadcast_to(peers[...], (shared, shared))
    down = across.T
    first = lax.broadcasted_iota(jnp.int32, (shared, shared), 0)
    second = lax.broadcasted_iota(jnp.int32, (shared, shared), 1)
    slot = jnp.sum(
        jnp.where((across == down) & (second < first), 1.0, 0.0), axis=1, keepdims=True
    ).astype(jnp.int32)
    wanted = jnp.broadcast_to(rows[...], (shared, shared)).T[:, :1]
    far = down[:, :1] ^ lax.axis_index("wide")

    def marks(key, columns):
        hit = key == lax.broadcasted_iota(jnp.int32, (shared, columns), 1)
        return jnp.where(hit, 1.0, 0.0).astype(BF16)

    unpack_own[...] = marks(jnp.where(far == 0, wanted, -1), shared)
    unpack_all[...] = marks(jnp.where(far == 0, -1, (far - 1) * shared + wanted), unpack_all.shape[1])
    unpack[...] = marks(jnp.where(far == 0, -1, (far - 1) * cap + slot), unpack.shape[1])
    lane = lax.broadcasted_iota(jnp.int32, (shared, width), 1)
    for d, out in enumerate(sends, 1):
        out[shared:, :] = jnp.zeros((out.shape[0] - shared, width), F32)
        for c in range(-(-cap // width)):
            hit = (far == d) & (slot == lane + c * width)
            out[shared + c:shared + c + 1, :] = jnp.sum(
                jnp.where(hit, wanted.astype(F32), 0.0), axis=0, keepdims=True
            )
    copies[2].wait()
    copies[3].wait()
    parts = split(operator[...])
    high[...], low[...] = parts
    value = product(parts, split(mult[...]))
    image[...] = value
    for out in sends:
        out[:shared, :] = value


def pack_kernel(times, cap, *refs):
    n = len(times[0])
    recvs, (high, low, pack, stack_high, stack_low) = refs[:n], refs[n:]
    shared = pack.shape[1]
    width = recvs[0].shape[1]
    column = lax.broadcasted_iota(jnp.int32, (width, shared), 1).astype(F32)
    if n * cap < pack.shape[0]:
        pack[n * cap:, :] = jnp.zeros((pack.shape[0] - n * cap, shared), BF16)
    for d, recv in zip(times[0], recvs):
        for c in range(-(-cap // width)):
            wanted = jnp.broadcast_to(recv[shared + c:shared + c + 1, :], (shared, width)).T
            chosen = jnp.where(wanted == column, 1.0, 0.0).astype(BF16)
            size = min(width, cap - c * width)
            at = (d - 1) * cap + c * width
            pack[at:at + size, :] = chosen[:size]
    for source, stack in ((high, stack_high), (low, stack_low)):
        square = source[:, :shared]
        stack[:shared, :] = square
        stack[shared:, :] = mm(pack[...], square).astype(BF16)


def prepare_kernel(contact, modes, tile, floor, basis, tile_high, tile_low):
    order, width = floor.shape
    for at in range(0, order, width):
        flag = jnp.broadcast_to(contact[:, at:at + width], (width, width)).T
        floor[at:at + width, :] = jnp.where(flag == 1, 0.0, -jnp.inf)
    high, low = [part.astype(F32) for part in split(modes[...])]
    basis[...] = jnp.concatenate([high, high, low], axis=0).T.astype(BF16)
    tile_high[...], tile_low[...] = split(tile[...])


def send(times, cap, chosen, image, sends):
    picked = pick(chosen, image)
    rows = [picked[at:at + cap] for at in range(0, len(sends) * cap, cap)]
    for out, (even, odd) in zip(sends, zip(*times)):
        out[...] = by_line(rows[even - 1], rows[odd - 1])


def arrived(times, recvs, shared, unpack):
    got = [recv[...][:shared] for recv in recvs]
    blocks = [by_line(*(got[line.index(d)] for line in times)) for d in sorted(times[0])]
    rows = sum(b.shape[0] for b in blocks)
    if rows < unpack.shape[1]:
        blocks.append(jnp.zeros((unpack.shape[1] - rows, blocks[0].shape[1]), F32))
    return pick(unpack[...], jnp.concatenate(blocks, axis=0))


def base_kernel(image, unpack_own, gap, base):
    own = image[...]
    base[...] = gap[:own.shape[0], :] - own + pick(unpack_own[...], own)


def settle(trial, floor, alive):
    return jnp.where(alive, jnp.maximum(trial, floor), 0.0)


def shared_residual(times, recvs, base, unpack, size):
    known = base[...]
    alive = live(size[0], 0, *known.shape)
    return jnp.where(alive, known + arrived(times, recvs, known.shape[0], unpack), 0.0), alive


def rest_start_kernel(size, operator, mult, mult_block, gap, modes, trial, coarse, high, low, halves):
    step = pl.program_id(0)
    rows, width = gap.shape

    @pl.when(step == 0)
    def _():
        halves[:, :width], halves[:, width:] = split(mult[...])
        coarse[...] = jnp.zeros_like(coarse)

    parts = split(operator[...])
    high[...], low[...] = parts
    both = mm(parts[0], halves[...])
    image = both[:, :width] + (both[:, width:] + mm(parts[1], halves[:, :width]))
    alive = live(size[0], (step + 1) * rows, rows, width)
    residual = jnp.where(alive, gap[...] - image, 0.0)
    trial[...] = mult_block[...] + STEP * residual
    coarse[...] += product(split(modes[...]), split(residual))


def rest_residual(size, high, low, mult_s, mult_n, gap):
    shared, (rows, width) = mult_s.shape[0], mult_n.shape
    mult = jnp.concatenate([mult_s[...], mult_n[...]], axis=0)
    image = product((high[...], low[...]), split(mult))
    alive = live(size[0], shared, rows, width)
    return jnp.where(alive, gap[shared:, :] - image, 0.0), alive


def rest_first_kernel(size, high, low, mult_s, mult_n, gap, modes, trial, coarse):
    residual, _ = rest_residual(size, high, low, mult_s, mult_n, gap)
    trial[...] = mult_n[...] + STEP * residual
    coarse[...] = product(split(modes[:, mult_s.shape[0]:]), split(residual))


def rest_kernel(size, high, low, mult_s, mult_n, gap, floor, top_high, top_low, pack, mult_out, ahead):
    shared = mult_s.shape[0]
    residual, alive = rest_residual(size, high, low, mult_s, mult_n, gap)
    mult = settle(mult_n[...] + STEP * residual, floor[shared:, :], alive)
    mult_out[...] = mult
    value = product((top_high[:, shared:], top_low[:, shared:]), split(mult))
    ahead[:shared, :] = value
    ahead[shared:, :] = pick(pack[...], value)


def rest_last_kernel(size, high, low, mult_s, mult_n, gap, floor, mult_out, residual_out, settled, left, done):
    shared, rows = mult_s.shape[0], mult_n.shape[0]
    residual, alive = rest_residual(size, high, low, mult_s, mult_n, gap)
    left[...] = residual
    settled[...] = settle(mult_n[...] + STEP * residual, floor[shared:, :], alive)
    copies = [
        pltpu.make_async_copy(source, target.at[pl.ds(shared, rows)], done.at[i])
        for i, (source, target) in enumerate(((left, residual_out), (settled, mult_out)))
    ]
    for copy in copies:
        copy.start()
    for copy in copies:
        copy.wait()


def coarse_kernel(times, size, *refs):
    n = len(times[0])
    recvs = refs[:n]
    base, unpack, mult, modes, started, trial = refs[n:n + 6]
    shared = base.shape[0]
    residual, _ = shared_residual(times, recvs, base, unpack, size)
    coarse = started[...] + product(split(modes[:, :shared]), split(residual))
    for out in refs[n + 6:]:
        out[...] = coarse
    trial[...] = mult[:shared, :] + STEP * residual


def tile_kernel(wide_order, narrow_order, high, low, *refs):
    n, m = len(wide_order), len(narrow_order)
    blocks, outs, (gathered, parts) = refs[:n + 1], refs[n + 1:n + m + 2], refs[n + m + 2:]
    count = blocks[0].shape[0]
    for d, ref in zip((0, *wide_order), blocks):
        at = pl.multiple_of((lax.axis_index("wide") ^ d) * count, count)
        gathered[pl.ds(at, count), :] = ref[...]
    parts[...] = product((high[...], low[...]), split(gathered[...]))
    for d, out in zip((0, *narrow_order), outs):
        at = pl.multiple_of((lax.axis_index("narrow") ^ d) * count, count)
        out[...] = parts[pl.ds(at, count), :]


def lift_kernel(times, m, cap, size, *refs):
    parts = refs[:m + 1]
    ins, (mult_s, mult_n, image), sends = refs[m + 1:m + 8], refs[m + 8:m + 11], refs[m + 11:]
    basis, trial_s, trial_n, floor, high, low, pack = ins
    solved = parts[0][...]
    for part in parts[1:]:
        solved = solved + part[...]
    shared, width = trial_s.shape
    order = floor.shape[0]
    high_part, low_part = split(solved)
    lifted = mm(basis[...], jnp.concatenate([high_part, low_part, high_part], axis=0))
    alive = live(size[0], 0, order, width)
    first = settle(trial_s[...] + lifted[:shared], floor[:shared], alive[:shared])
    rest = settle(trial_n[...] + lifted[shared:], floor[shared:], alive[shared:])
    mult_s[...] = first
    mult_n[...] = rest
    value = product((high[...], low[...]), split(jnp.concatenate([first, rest], axis=0)))
    image[...] = value
    send(times, cap, pack[...], value, sends)


def sweep_kernel(times, cap, size, *refs):
    n = len(times[0])
    recvs = refs[:n]
    base, unpack, mult, floor, high, low, ahead, mult_out, image_out = refs[n:n + 9]
    shared = base.shape[0]
    residual, alive = shared_residual(times, recvs, base, unpack, size)
    value = settle(mult[...] + STEP * residual, floor[:shared, :], alive)
    mult_out[...] = value
    both = ahead[...] + product((high[...], low[...]), split(value))
    image_out[...] = both[:shared]
    for d, out in enumerate(refs[n + 9:]):
        out[...] = both[shared + d * cap:shared + (d + 1) * cap]


def last_kernel(times, size, *refs):
    n = len(times[0])
    recvs = refs[:n]
    base, unpack, mult, floor, _, _, mult_out, residual_out, settled, left, done = refs[n:]
    shared = base.shape[0]
    residual, alive = shared_residual(times, recvs, base, unpack, size)
    left[...] = residual
    first = pltpu.make_async_copy(left, residual_out.at[pl.ds(0, shared)], done.at[0])
    first.start()
    settled[...] = settle(mult[...] + STEP * residual, floor[:shared, :], alive)
    second = pltpu.make_async_copy(settled, mult_out.at[pl.ds(0, shared)], done.at[1])
    second.start()
    first.wait()
    second.wait()


def swap(block, axis, count, d):
    return lax.ppermute(block, axis, [(i, i ^ d) for i in range(count)])


def swap_all(blocks, axis, count, order):
    return [swap(block, axis, count, d) for block, d in zip(blocks, order)]


def swap_rows(blocks, wide, narrow, times):
    return [
        lax.ppermute(
            block,
            ("wide", "narrow"),
            [(w * narrow + i, (w ^ ds[i % 2]) * narrow + i) for w in range(wide) for i in range(narrow)],
        )
        for block, ds in zip(blocks, zip(*times))
    ]


def half_first(count):
    half = count // 2
    return (half, *(d for d in range(count - 1, 0, -1) if d != half))


def sorted_by(blocks, times):
    return [blocks[d - 1] for d in times[0]]


def middle_first(count):
    return (count - 1, *range(1, count - 1))


def far_first(count):
    return tuple(range(count - 1, 0, -1))


def local(
    wide,
    narrow,
    operators,
    coarse_inverse,
    modes,
    gap,
    start_mult,
    peer_list,
    partner_row,
    interface_size,
    contact_rows,
):
    operator = operators[0]
    modes = modes[0]
    gap = gap[0]
    mult = start_mult[0]
    order, loads = mult.shape
    shared = partner_row.shape[1]
    count = modes.shape[0]
    rest = order - shared
    steps = rest // shared
    n, m = wide - 1, narrow - 1
    cap = 2 * shared // wide
    listed = n * cap
    padded = -(-listed // 128) * 128
    size = interface_size
    coarse_order, part_order = far_first(wide), far_first(narrow)
    middle, half = middle_first(wide), half_first(wide)
    both, apart = (half, half), (tuple(range(1, wide)), half)
    orders = (((middle, middle), apart, both), (both, apart, both))
    sent = [shape(cap, loads)] * n
    full = 2 * order * loads

    list_rows = -(-(-(-cap // loads)) // 8) * 8
    unpack_own, unpack_all, unpack, top_high, top_low, image, *sends = call(
        functools.partial(first_kernel, n, cap),
        tuple(
            pltpu.with_memory_space_constraint(value, pltpu.HBM)
            for value in (peer_list[0].reshape(1, shared), partner_row, operator, mult)
        ),
        [shape(shared, shared, BF16), shape(shared, n * shared, BF16), shape(shared, padded, BF16)]
        + [shape(shared, order, BF16)] * 2
        + [shape(shared, loads)]
        + [shape(shared + list_rows, loads)] * n,
        in_specs=[HBM] * 4,
        scratch=[
            pltpu.VMEM((1, shared), jnp.int32),
            pltpu.VMEM((1, shared), jnp.int32),
            pltpu.VMEM((shared, order), F32),
            pltpu.VMEM((order, loads), F32),
            pltpu.SemaphoreType.DMA((4,)),
        ],
        flops=3 * full * shared,
        moved=8 * shared * order,
        name="first",
    )
    floor, basis, tile_high, tile_low = call(
        prepare_kernel,
        (contact_rows, modes, coarse_inverse),
        [shape(order, loads)] + [shape(order, 3 * count, BF16)] + [shape(*coarse_inverse.shape, BF16)] * 2,
        flops=full * count,
        moved=8 * coarse_inverse.size + 4 * full,
        name="prepare",
    )
    mult_s = mult
    scratch = [pltpu.VMEM((order, 2 * loads), BF16)]
    for outer in range(OUTER):
        times = orders[outer][0]
        recvs = swap_rows(sorted_by(sends, times), wide, narrow, times)
        base = call(
            base_kernel,
            (image, unpack_own, gap),
            [shape(shared, loads)],
            flops=4 * shared * shared * loads,
            moved=8 * shared * loads,
            name="base",
        )[0]
        if outer == 0:
            row_block, load_block = block((shared, order)), block((shared, loads))
            next_loads = block((shared, loads), 1)
            trial_n, started, high, low = call(
                rest_start_kernel,
                (size, operator, mult, mult, gap, modes),
                [shape(rest, loads), shape(count, loads)] + [shape(rest, order, BF16)] * 2,
                [
                    SMEM,
                    block((shared, order), 1),
                    whole((order, loads)),
                    next_loads,
                    next_loads,
                    block((count, shared), 1, across=True),
                ],
                [load_block, whole((count, loads)), row_block, row_block],
                scratch=scratch,
                grid=(steps,),
                flops=3 * full * rest,
                moved=8 * rest * order,
                name="rest_start",
            )
            marks = unpack_all
            pack, stack_high, stack_low = call(
                functools.partial(pack_kernel, times, cap),
                (*recvs, top_high, top_low),
                [shape(padded, shared, BF16)] + [shape(shared + padded, shared, BF16)] * 2,
                flops=8 * padded * shared * shared,
                moved=8 * padded * shared,
                name="pack",
            )
        else:
            trial_n, started = call(
                rest_first_kernel,
                (size, high, low, mult_s, mult_n, gap, modes),
                [shape(rest, loads), shape(count, loads)],
                flops=3 * full * rest,
                moved=4 * rest * order,
                name="rest_first",
            )
            marks = unpack
        trial_s, own, *coarse = call(
            functools.partial(coarse_kernel, times),
            (size, *recvs, base, marks, mult_s, modes, started),
            [shape(shared, loads)] + [shape(count, loads)] * wide,
            flops=6 * shared * loads * unpack.shape[1],
            moved=2 * shared * unpack.shape[1],
            name="coarse",
        )
        blocks = [own] + swap_all(coarse, "wide", wide, coarse_order)
        own, *parts = call(
            functools.partial(tile_kernel, coarse_order, part_order),
            (tile_high, tile_low, *blocks),
            [shape(count, loads)] * narrow,
            scratch=[
                pltpu.VMEM((wide * count, loads), F32),
                pltpu.VMEM((narrow * count, loads), F32),
            ],
            flops=6 * coarse_inverse.size * loads,
            moved=4 * coarse_inverse.size,
            name="tile",
        )
        parts = [own] + swap_all(parts, "narrow", narrow, part_order)
        mult_s, mult_n, image, *sends = call(
            functools.partial(lift_kernel, orders[outer][1], m, cap),
            (size, *parts, basis, trial_s, trial_n, floor, top_high, top_low, pack),
            [shape(shared, loads), shape(rest, loads), shape(shared, loads)] + sent,
            flops=3 * full * shared,
            moved=4 * order * shared,
            name="lift",
        )
        for inner in range(1, INNER):
            last = outer == OUTER - 1 and inner == INNER - 1
            times = orders[outer][inner]
            if inner > 1:
                sends = sorted_by(sends, times)
            recvs = swap_rows(sends, wide, narrow, times)
            base = call(
                base_kernel,
                (image, unpack_own, gap),
                [shape(shared, loads)],
                flops=4 * shared * shared * loads,
                moved=8 * shared * loads,
                name="base",
            )[0]
            ins = (size, high, low, mult_s, mult_n, gap, floor)
            shadow = (size, *recvs, base, unpack, mult_s, floor)
            cost = dict(flops=6 * shared * loads * unpack.shape[1], moved=2 * shared * unpack.shape[1])
            if last:
                outs = call(
                    rest_last_kernel,
                    ins,
                    [shape(order, loads)] * 2,
                    out_specs=[HBM] * 2,
                    scratch=[pltpu.VMEM((rest, loads), F32)] * 2 + [pltpu.SemaphoreType.DMA((2,))],
                    flops=3 * full * rest,
                    moved=4 * rest * order,
                    name="rest_last",
                )
                outs = call(
                    functools.partial(last_kernel, times),
                    (*shadow, *outs),
                    [shape(order, loads)] * 2,
                    in_specs=[SMEM] + [VMEM] * (len(shadow) - 1) + [HBM] * 2,
                    out_specs=[HBM] * 2,
                    scratch=[pltpu.VMEM((shared, loads), F32)] * 2 + [pltpu.SemaphoreType.DMA((2,))],
                    alias={len(shadow): 0, len(shadow) + 1: 1},
                    name="last",
                    **cost,
                )
                return tuple(out[None] for out in outs)
            mult_n, ahead = call(
                rest_kernel,
                (*ins, top_high, top_low, pack),
                [shape(rest, loads), shape(shared + padded, loads)],
                flops=3 * full * order,
                moved=4 * order * order,
                name="rest",
            )
            mult_s, image, *sends = call(
                functools.partial(sweep_kernel, times, cap),
                (*shadow, stack_high, stack_low, ahead),
                [shape(shared, loads)] * 2 + sent,
                name="sweep",
                **cost,
            )


def solution(mesh):
    wide = mesh.shape["wide"]
    narrow = mesh.shape["narrow"]

    def body(*args):
        return local(wide, narrow, *args)

    return jax.shard_map(
        body,
        mesh=mesh,
        in_specs=(
            P(("groups", "wide", "narrow"), None, None),
            P(("groups", "wide"), "narrow"),
            P(("groups", "wide", "narrow"), None, None),
            P(("groups", "wide", "narrow"), None, None),
            P(("groups", "wide", "narrow"), None, None),
            P(("groups", "wide", "narrow"), None, None),
            P(("groups", "wide", "narrow"), None),
            P(("groups", "wide", "narrow")),
            P(("groups", "wide", "narrow"), None),
        ),
        out_specs=(
            P(("groups", "wide", "narrow"), None, None),
            P(("groups", "wide", "narrow"), None, None),
        ),
        check_vma=False,
    )
```

```python
import functools

import jax
import jax.numpy as jnp
from jax import lax
from jax.experimental import pallas as pl
from jax.experimental.pallas import tpu as pltpu
from jax.sharding import PartitionSpec as P

OUTER = 2
INNER = 3
STEP = 0.3
F32 = jnp.float32
BF16 = jnp.bfloat16
PARAMS = pltpu.CompilerParams(vmem_limit_bytes=24 * 1024 * 1024)


def split(value):
    high = value.astype(BF16)
    return high, (value - high.astype(F32)).astype(BF16)


def mm(left, right):
    return jnp.dot(left, right, preferred_element_type=F32)


def product(left, right):
    (left_high, left_low), (right_high, right_low) = left, right
    width = right_high.shape[1]
    both = mm(left_high, jnp.concatenate([right_high, right_low], axis=1))
    return both[:, :width] + (both[:, width:] + mm(left_low, right_high))


def pick(chosen, value):
    width = value.shape[1]
    both = mm(chosen, jnp.concatenate(split(value), axis=1))
    return both[:, :width] + both[:, width:]


def live(size, start, rows, width):
    return lax.broadcasted_iota(jnp.int32, (rows, width), 0) + start < size


def call(body, ins, outs, in_specs=None, out_specs=None, scratch=(), grid=(), flops=0, moved=0, alias=None, name=None):
    if in_specs is None:
        in_specs = [SMEM if value.ndim == 1 else VMEM for value in ins]
    if out_specs is None:
        out_specs = [VMEM] * len(outs)
    return pl.pallas_call(
        body,
        out_shape=outs,
        grid=grid,
        in_specs=in_specs,
        out_specs=out_specs,
        scratch_shapes=list(scratch),
        compiler_params=PARAMS,
        cost_estimate=pl.CostEstimate(flops=flops, bytes_accessed=moved, transcendentals=0),
        input_output_aliases=alias or {},
        name=name,
    )(*ins)


def whole(shape):
    return pl.BlockSpec(shape, lambda *i: (0,) * len(shape))


def block(shape, at=0, across=False):
    if across:
        return pl.BlockSpec(shape, lambda i: (0, i + at))
    return pl.BlockSpec(shape, lambda i: (i + at, 0))


SMEM = pl.BlockSpec(memory_space=pltpu.SMEM)
HBM = pl.BlockSpec(memory_space=pltpu.HBM)
VMEM = pl.BlockSpec(memory_space=pltpu.VMEM)


def shape(rows, columns, dtype=F32):
    return jax.ShapeDtypeStruct((rows, columns), dtype)


def places(peers, rows):
    shared = peers.shape[1]
    across = jnp.broadcast_to(peers[...], (shared, shared))
    down = across.T
    first = lax.broadcasted_iota(jnp.int32, (shared, shared), 0)
    second = lax.broadcasted_iota(jnp.int32, (shared, shared), 1)
    slot = jnp.sum(
        jnp.where((across == down) & (second < first), 1.0, 0.0), axis=1, keepdims=True
    ).astype(jnp.int32)
    wanted = jnp.broadcast_to(rows[...], (shared, shared)).T[:, :1]
    return down[:, :1] ^ lax.axis_index("wide"), slot, wanted


def lists_kernel(n, peers_at, rows_at, operator_at, mult_at, operator, mult, *refs):
    lists, (peers, rows, done) = refs[:n], refs[n:]
    shared = operator.shape[0]
    copies = [
        pltpu.make_async_copy(source, target, done.at[i])
        for i, (source, target) in enumerate(
            ((peers_at, peers), (rows_at, rows), (mult_at, mult), (operator_at.at[pl.ds(0, shared)], operator))
        )
    ]
    for copy in copies:
        copy.start()
    copies[0].wait()
    copies[1].wait()
    far, slot, wanted = places(peers, rows)
    wanted = wanted.astype(F32)
    lane = lax.broadcasted_iota(jnp.int32, (shared, mult.shape[1]), 1)
    for d, out in enumerate(lists, 1):
        for c in range(out.shape[0]):
            hit = (far == d) & (slot == lane + c * out.shape[1])
            out[c:c + 1, :] = jnp.sum(jnp.where(hit, wanted, 0.0), axis=0, keepdims=True)
    copies[2].wait()
    copies[3].wait()


def first_kernel(operator, mult, high, low, image):
    parts = split(operator[...])
    high[...], low[...] = parts
    image[...] = product(parts, split(mult[...]))


def marks_kernel(cap, peers, rows, unpack_own, unpack):
    far, slot, wanted = places(peers, rows)
    for key, out in (
        (jnp.where(far == 0, wanted, -1), unpack_own),
        (jnp.where(far == 0, -1, (far - 1) * cap + slot), unpack),
    ):
        hit = key == lax.broadcasted_iota(jnp.int32, out.shape, 1)
        out[...] = jnp.where(hit, 1.0, 0.0).astype(BF16)


def pack_kernel(times, cap, *refs):
    n = len(times)
    lists, (image, pack), sends = refs[:n], refs[n:n + 2], refs[n + 2:]
    shared, width = image.shape
    column = lax.broadcasted_iota(jnp.int32, (width, shared), 1).astype(F32)
    if n * cap < pack.shape[0]:
        pack[n * cap:, :] = jnp.zeros((pack.shape[0] - n * cap, shared), BF16)
    for d, asked in zip(times, lists):
        for c in range(-(-cap // width)):
            wanted = jnp.broadcast_to(asked[c:c + 1, :], (shared, width)).T
            chosen = jnp.where(wanted == column, 1.0, 0.0).astype(BF16)
            size = min(width, cap - c * width)
            at = (d - 1) * cap + c * width
            pack[at:at + size, :] = chosen[:size]
    send(cap, pack[...], image[...], sends)


def square_kernel(high, low, pack, stack_high, stack_low):
    shared = pack.shape[1]
    for source, stack in ((high, stack_high), (low, stack_low)):
        square = source[:, :shared]
        stack[:shared, :] = square
        stack[shared:, :] = mm(pack[...], square).astype(BF16)


def prepare_kernel(contact, modes, tile, floor, basis, tile_high, tile_low):
    order, width = floor.shape
    for at in range(0, order, width):
        flag = jnp.broadcast_to(contact[:, at:at + width], (width, width)).T
        floor[at:at + width, :] = jnp.where(flag == 1, 0.0, -jnp.inf)
    high, low = [part.astype(F32) for part in split(modes[...])]
    basis[...] = jnp.concatenate([high, high, low], axis=0).T.astype(BF16)
    tile_high[...], tile_low[...] = split(tile[...])


def send(cap, chosen, image, sends):
    picked = pick(chosen, image)
    for d, out in enumerate(sends):
        out[...] = picked[d * cap:(d + 1) * cap]


def arrived(times, recvs, unpack):
    blocks = [recvs[times.index(d)][...] for d in sorted(times)]
    rows = sum(b.shape[0] for b in blocks)
    if rows < unpack.shape[1]:
        blocks.append(jnp.zeros((unpack.shape[1] - rows, blocks[0].shape[1]), F32))
    return pick(unpack[...], jnp.concatenate(blocks, axis=0))


def base_kernel(image, unpack_own, gap, base):
    own = image[...]
    base[...] = gap[:own.shape[0], :] - own + pick(unpack_own[...], own)


def settle(trial, floor, alive):
    return jnp.where(alive, jnp.maximum(trial, floor), 0.0)


def shared_residual(times, recvs, base, unpack, size):
    known = base[...]
    alive = live(size[0], 0, *known.shape)
    return jnp.where(alive, known + arrived(times, recvs, unpack), 0.0), alive


def rest_start_kernel(size, operator, mult, mult_block, gap, modes, trial, coarse, high, low, halves):
    step = pl.program_id(0)
    rows, width = gap.shape

    @pl.when(step == 0)
    def _():
        halves[:, :width], halves[:, width:] = split(mult[...])
        coarse[...] = jnp.zeros_like(coarse)

    parts = split(operator[...])
    high[...], low[...] = parts
    both = mm(parts[0], halves[...])
    image = both[:, :width] + (both[:, width:] + mm(parts[1], halves[:, :width]))
    alive = live(size[0], (step + 1) * rows, rows, width)
    residual = jnp.where(alive, gap[...] - image, 0.0)
    trial[...] = mult_block[...] + STEP * residual
    coarse[...] += product(split(modes[...]), split(residual))


def rest_residual(size, high, low, mult_s, mult_n, gap):
    shared, (rows, width) = mult_s.shape[0], mult_n.shape
    mult = jnp.concatenate([mult_s[...], mult_n[...]], axis=0)
    image = product((high[...], low[...]), split(mult))
    alive = live(size[0], shared, rows, width)
    return jnp.where(alive, gap[shared:, :] - image, 0.0), alive


def rest_first_kernel(size, high, low, mult_s, mult_n, gap, modes, trial, coarse):
    residual, _ = rest_residual(size, high, low, mult_s, mult_n, gap)
    trial[...] = mult_n[...] + STEP * residual
    coarse[...] = product(split(modes[:, mult_s.shape[0]:]), split(residual))


def rest_kernel(size, high, low, mult_s, mult_n, gap, floor, top_high, top_low, pack, mult_out, ahead):
    shared = mult_s.shape[0]
    residual, alive = rest_residual(size, high, low, mult_s, mult_n, gap)
    mult = settle(mult_n[...] + STEP * residual, floor[shared:, :], alive)
    mult_out[...] = mult
    value = product((top_high[:, shared:], top_low[:, shared:]), split(mult))
    ahead[:shared, :] = value
    ahead[shared:, :] = pick(pack[...], value)


def rest_last_kernel(size, high, low, mult_s, mult_n, gap, floor, mult_out, residual_out, settled, left, done):
    shared, rows = mult_s.shape[0], mult_n.shape[0]
    residual, alive = rest_residual(size, high, low, mult_s, mult_n, gap)
    left[...] = residual
    settled[...] = settle(mult_n[...] + STEP * residual, floor[shared:, :], alive)
    copies = [
        pltpu.make_async_copy(source, target.at[pl.ds(shared, rows)], done.at[i])
        for i, (source, target) in enumerate(((left, residual_out), (settled, mult_out)))
    ]
    for copy in copies:
        copy.start()
    for copy in copies:
        copy.wait()


def coarse_kernel(times, size, *refs):
    n = len(times)
    recvs = refs[:n]
    base, unpack, mult, modes, started, trial = refs[n:n + 6]
    shared = base.shape[0]
    residual, _ = shared_residual(times, recvs, base, unpack, size)
    coarse = started[...] + product(split(modes[:, :shared]), split(residual))
    for out in refs[n + 6:]:
        out[...] = coarse
    trial[...] = mult[:shared, :] + STEP * residual


def tile_kernel(wide_order, narrow_order, high, low, *refs):
    n, m = len(wide_order), len(narrow_order)
    blocks, outs, (gathered, parts) = refs[:n + 1], refs[n + 1:n + m + 2], refs[n + m + 2:]
    count = blocks[0].shape[0]
    for d, ref in zip((0, *wide_order), blocks):
        at = pl.multiple_of((lax.axis_index("wide") ^ d) * count, count)
        gathered[pl.ds(at, count), :] = ref[...]
    parts[...] = product((high[...], low[...]), split(gathered[...]))
    for d, out in zip((0, *narrow_order), outs):
        at = pl.multiple_of((lax.axis_index("narrow") ^ d) * count, count)
        out[...] = parts[pl.ds(at, count), :]


def lift_kernel(n, m, cap, size, *refs):
    parts = refs[:m + 1]
    ins, (mult_s, mult_n, image), sends = refs[m + 1:m + 8], refs[m + 8:m + 11], refs[m + 11:]
    basis, trial_s, trial_n, floor, high, low, pack = ins
    solved = parts[0][...]
    for part in parts[1:]:
        solved = solved + part[...]
    shared, width = trial_s.shape
    order = floor.shape[0]
    high_part, low_part = split(solved)
    lifted = mm(basis[...], jnp.concatenate([high_part, low_part, high_part], axis=0))
    alive = live(size[0], 0, order, width)
    first = settle(trial_s[...] + lifted[:shared], floor[:shared], alive[:shared])
    rest = settle(trial_n[...] + lifted[shared:], floor[shared:], alive[shared:])
    mult_s[...] = first
    mult_n[...] = rest
    value = product((high[...], low[...]), split(jnp.concatenate([first, rest], axis=0)))
    image[...] = value
    send(cap, pack[...], value, sends)


def sweep_kernel(times, cap, size, *refs):
    n = len(times)
    recvs = refs[:n]
    base, unpack, mult, floor, high, low, ahead, mult_out, image_out = refs[n:n + 9]
    shared = base.shape[0]
    residual, alive = shared_residual(times, recvs, base, unpack, size)
    value = settle(mult[...] + STEP * residual, floor[:shared, :], alive)
    mult_out[...] = value
    both = ahead[...] + product((high[...], low[...]), split(value))
    image_out[...] = both[:shared]
    for d, out in enumerate(refs[n + 9:]):
        out[...] = both[shared + d * cap:shared + (d + 1) * cap]


def last_kernel(times, size, *refs):
    n = len(times)
    recvs = refs[:n]
    base, unpack, mult, floor, _, _, mult_out, residual_out, settled, left, done = refs[n:]
    shared = base.shape[0]
    residual, alive = shared_residual(times, recvs, base, unpack, size)
    left[...] = residual
    first = pltpu.make_async_copy(left, residual_out.at[pl.ds(0, shared)], done.at[0])
    first.start()
    settled[...] = settle(mult[...] + STEP * residual, floor[:shared, :], alive)
    second = pltpu.make_async_copy(settled, mult_out.at[pl.ds(0, shared)], done.at[1])
    second.start()
    first.wait()
    second.wait()


def swap(block, axis, count, d):
    return lax.ppermute(block, axis, [(i, i ^ d) for i in range(count)])


def swap_all(blocks, axis, count, order):
    return [swap(block, axis, count, d) for block, d in zip(blocks, order)]


def swap_rows(blocks, axis, count, times):
    return [swap(blocks[d - 1], axis, count, d) for d in times]


def half_first(count):
    half = count // 2
    return (half, *(d for d in range(count - 1, 0, -1) if d != half))


def far_first(count):
    return tuple(range(count - 1, 0, -1))


def local(
    wide,
    narrow,
    operators,
    coarse_inverse,
    modes,
    gap,
    start_mult,
    peer_list,
    partner_row,
    interface_size,
    contact_rows,
):
    operator = operators[0]
    modes = modes[0]
    gap = gap[0]
    mult = start_mult[0]
    order, loads = mult.shape
    shared = partner_row.shape[1]
    count = modes.shape[0]
    rest = order - shared
    steps = rest // shared
    n, m = wide - 1, narrow - 1
    cap = 2 * shared // wide
    listed = n * cap
    padded = -(-listed // 128) * 128
    size = interface_size
    coarse_order, part_order, times = far_first(wide), far_first(narrow), half_first(wide)
    sent = [shape(cap, loads)] * n
    full = 2 * order * loads

    list_rows = -(-(-(-cap // loads)) // 8) * 8
    pairs = peer_list[0].reshape(1, shared), partner_row
    operator_top, mult_near, *lists = call(
        functools.partial(lists_kernel, n),
        tuple(pltpu.with_memory_space_constraint(value, pltpu.HBM) for value in (*pairs, operator, mult)),
        [shape(shared, order), shape(order, loads)] + [shape(list_rows, loads)] * n,
        in_specs=[HBM] * 4,
        scratch=[
            pltpu.VMEM((1, shared), jnp.int32),
            pltpu.VMEM((1, shared), jnp.int32),
            pltpu.SemaphoreType.DMA((4,)),
        ],
        flops=8 * shared * shared,
        moved=8 * shared * order,
        name="lists",
    )
    lists = swap_rows(lists, "wide", wide, times)
    top_high, top_low, image = call(
        first_kernel,
        (operator_top, mult_near),
        [shape(shared, order, BF16)] * 2 + [shape(shared, loads)],
        flops=3 * full * shared,
        moved=8 * shared * order,
        name="first",
    )
    pack, *sends = call(
        functools.partial(pack_kernel, times, cap),
        (*lists, image),
        [shape(padded, shared, BF16)] + sent,
        flops=4 * padded * shared * loads,
        moved=4 * padded * shared,
        name="pack",
    )
    stack_high, stack_low = call(
        square_kernel,
        (top_high, top_low, pack),
        [shape(shared + padded, shared, BF16)] * 2,
        flops=4 * padded * shared * shared,
        moved=8 * padded * shared,
        name="square",
    )
    unpack_own, unpack = call(
        functools.partial(marks_kernel, cap),
        pairs,
        [shape(shared, shared, BF16), shape(shared, padded, BF16)],
        flops=8 * shared * shared * wide,
        moved=2 * shared * shared * wide,
        name="marks",
    )
    floor, basis, tile_high, tile_low = call(
        prepare_kernel,
        (contact_rows, modes, coarse_inverse),
        [shape(order, loads)] + [shape(order, 3 * count, BF16)] + [shape(*coarse_inverse.shape, BF16)] * 2,
        flops=full * count,
        moved=8 * coarse_inverse.size + 4 * full,
        name="prepare",
    )
    mult_s = mult
    scratch = [pltpu.VMEM((order, 2 * loads), BF16)]
    for outer in range(OUTER):
        recvs = swap_rows(sends, "wide", wide, times)
        base = call(
            base_kernel,
            (image, unpack_own, gap),
            [shape(shared, loads)],
            flops=4 * shared * shared * loads,
            moved=8 * shared * loads,
            name="base",
        )[0]
        if outer == 0:
            row_block, load_block = block((shared, order)), block((shared, loads))
            next_loads = block((shared, loads), 1)
            trial_n, started, high, low = call(
                rest_start_kernel,
                (size, pltpu.with_memory_space_constraint(operator, pltpu.HBM), mult, mult, gap, modes),
                [shape(rest, loads), shape(count, loads)] + [shape(rest, order, BF16)] * 2,
                [
                    SMEM,
                    block((shared, order), 1),
                    whole((order, loads)),
                    next_loads,
                    next_loads,
                    block((count, shared), 1, across=True),
                ],
                [load_block, whole((count, loads)), row_block, row_block],
                scratch=scratch,
                grid=(steps,),
                flops=3 * full * rest,
                moved=8 * rest * order,
                name="rest_start",
            )
        else:
            trial_n, started = call(
                rest_first_kernel,
                (size, high, low, mult_s, mult_n, gap, modes),
                [shape(rest, loads), shape(count, loads)],
                flops=3 * full * rest,
                moved=4 * rest * order,
                name="rest_first",
            )
        trial_s, own, *coarse = call(
            functools.partial(coarse_kernel, times),
            (size, *recvs, base, unpack, mult_s, modes, started),
            [shape(shared, loads)] + [shape(count, loads)] * wide,
            flops=6 * shared * loads * unpack.shape[1],
            moved=2 * shared * unpack.shape[1],
            name="coarse",
        )
        blocks = [own] + swap_all(coarse, "wide", wide, coarse_order)
        own, *parts = call(
            functools.partial(tile_kernel, coarse_order, part_order),
            (tile_high, tile_low, *blocks),
            [shape(count, loads)] * narrow,
            scratch=[
                pltpu.VMEM((wide * count, loads), F32),
                pltpu.VMEM((narrow * count, loads), F32),
            ],
            flops=6 * coarse_inverse.size * loads,
            moved=4 * coarse_inverse.size,
            name="tile",
        )
        parts = [own] + swap_all(parts, "narrow", narrow, part_order)
        mult_s, mult_n, image, *sends = call(
            functools.partial(lift_kernel, n, m, cap),
            (size, *parts, basis, trial_s, trial_n, floor, top_high, top_low, pack),
            [shape(shared, loads), shape(rest, loads), shape(shared, loads)] + sent,
            flops=3 * full * shared,
            moved=4 * order * shared,
            name="lift",
        )
        for inner in range(1, INNER):
            last = outer == OUTER - 1 and inner == INNER - 1
            recvs = swap_rows(sends, "wide", wide, times)
            base = call(
                base_kernel,
                (image, unpack_own, gap),
                [shape(shared, loads)],
                flops=4 * shared * shared * loads,
                moved=8 * shared * loads,
                name="base",
            )[0]
            ins = (size, high, low, mult_s, mult_n, gap, floor)
            shadow = (size, *recvs, base, unpack, mult_s, floor)
            cost = dict(flops=6 * shared * loads * unpack.shape[1], moved=2 * shared * unpack.shape[1])
            if last:
                outs = call(
                    rest_last_kernel,
                    ins,
                    [shape(order, loads)] * 2,
                    out_specs=[HBM] * 2,
                    scratch=[pltpu.VMEM((rest, loads), F32)] * 2 + [pltpu.SemaphoreType.DMA((2,))],
                    flops=3 * full * rest,
                    moved=4 * rest * order,
                    name="rest_last",
                )
                outs = call(
                    functools.partial(last_kernel, times),
                    (*shadow, *outs),
                    [shape(order, loads)] * 2,
                    in_specs=[SMEM] + [VMEM] * (len(shadow) - 1) + [HBM] * 2,
                    out_specs=[HBM] * 2,
                    scratch=[pltpu.VMEM((shared, loads), F32)] * 2 + [pltpu.SemaphoreType.DMA((2,))],
                    alias={len(shadow): 0, len(shadow) + 1: 1},
                    name="last",
                    **cost,
                )
                return tuple(out[None] for out in outs)
            mult_n, ahead = call(
                rest_kernel,
                (*ins, top_high, top_low, pack),
                [shape(rest, loads), shape(shared + padded, loads)],
                flops=3 * full * order,
                moved=4 * order * order,
                name="rest",
            )
            mult_s, image, *sends = call(
                functools.partial(sweep_kernel, times, cap),
                (*shadow, stack_high, stack_low, ahead),
                [shape(shared, loads)] * 2 + sent,
                name="sweep",
                **cost,
            )


def solution(mesh):
    wide = mesh.shape["wide"]
    narrow = mesh.shape["narrow"]

    def body(*args):
        return local(wide, narrow, *args)

    return jax.shard_map(
        body,
        mesh=mesh,
        in_specs=(
            P(("groups", "wide", "narrow"), None, None),
            P(("groups", "wide"), "narrow"),
            P(("groups", "wide", "narrow"), None, None),
            P(("groups", "wide", "narrow"), None, None),
            P(("groups", "wide", "narrow"), None, None),
            P(("groups", "wide", "narrow"), None, None),
            P(("groups", "wide", "narrow"), None),
            P(("groups", "wide", "narrow")),
            P(("groups", "wide", "narrow"), None),
        ),
        out_specs=(
            P(("groups", "wide", "narrow"), None, None),
            P(("groups", "wide", "narrow"), None, None),
        ),
        check_vma=False,
    )
```

```python
import functools

import jax
import jax.numpy as jnp
from jax import lax
from jax.experimental import pallas as pl
from jax.experimental.pallas import tpu as pltpu
from jax.sharding import PartitionSpec as P

OUTER = 2
INNER = 3
STEP = 0.3
F32 = jnp.float32
BF16 = jnp.bfloat16
PARAMS = pltpu.CompilerParams(vmem_limit_bytes=24 * 1024 * 1024)


def split(value):
    high = value.astype(BF16)
    return high, (value - high.astype(F32)).astype(BF16)


def mm(left, right):
    return jnp.dot(left, right, preferred_element_type=F32)


def product(left, right):
    (left_high, left_low), (right_high, right_low) = left, right
    width = right_high.shape[1]
    both = mm(left_high, jnp.concatenate([right_high, right_low], axis=1))
    return both[:, :width] + (both[:, width:] + mm(left_low, right_high))


def pick(chosen, value):
    width = value.shape[1]
    both = mm(chosen, jnp.concatenate(split(value), axis=1))
    return both[:, :width] + both[:, width:]


def live(size, start, rows, width):
    return lax.broadcasted_iota(jnp.int32, (rows, width), 0) + start < size


def call(body, ins, outs, in_specs=None, out_specs=None, scratch=(), grid=(), flops=0, moved=0, alias=None, name=None):
    if in_specs is None:
        in_specs = [SMEM if value.ndim == 1 else VMEM for value in ins]
    if out_specs is None:
        out_specs = [VMEM] * len(outs)
    return pl.pallas_call(
        body,
        out_shape=outs,
        grid=grid,
        in_specs=in_specs,
        out_specs=out_specs,
        scratch_shapes=list(scratch),
        compiler_params=PARAMS,
        cost_estimate=pl.CostEstimate(flops=flops, bytes_accessed=moved, transcendentals=0),
        input_output_aliases=alias or {},
        name=name,
    )(*ins)


def whole(shape):
    return pl.BlockSpec(shape, lambda *i: (0,) * len(shape))


def block(shape, at=0, across=False):
    if across:
        return pl.BlockSpec(shape, lambda i: (0, i + at))
    return pl.BlockSpec(shape, lambda i: (i + at, 0))


SMEM = pl.BlockSpec(memory_space=pltpu.SMEM)
HBM = pl.BlockSpec(memory_space=pltpu.HBM)
VMEM = pl.BlockSpec(memory_space=pltpu.VMEM)


def shape(rows, columns, dtype=F32):
    return jax.ShapeDtypeStruct((rows, columns), dtype)


def first_kernel(n, cap, peers_at, rows_at, operator_at, mult_at, *refs):
    unpack_own, unpack_all, unpack_near, unpack_far, high, low, image = refs[:7]
    sends, (peers, rows, operator, mult, done) = refs[7:7 + n], refs[7 + n:]
    shared, width = image.shape
    copies = [
        pltpu.make_async_copy(source, target, done.at[i])
        for i, (source, target) in enumerate(
            ((peers_at, peers), (rows_at, rows), (mult_at, mult), (operator_at.at[pl.ds(0, shared)], operator))
        )
    ]
    for copy in copies:
        copy.start()
    copies[0].wait()
    copies[1].wait()
    across = jnp.broadcast_to(peers[...], (shared, shared))
    down = across.T
    first = lax.broadcasted_iota(jnp.int32, (shared, shared), 0)
    second = lax.broadcasted_iota(jnp.int32, (shared, shared), 1)
    slot = jnp.sum(
        jnp.where((across == down) & (second < first), 1.0, 0.0), axis=1, keepdims=True
    ).astype(jnp.int32)
    wanted = jnp.broadcast_to(rows[...], (shared, shared)).T[:, :1]
    far = down[:, :1] ^ lax.axis_index("wide")

    def marks(key, columns):
        hit = key == lax.broadcasted_iota(jnp.int32, (shared, columns), 1)
        return jnp.where(hit, 1.0, 0.0).astype(BF16)

    unpack_own[...] = marks(jnp.where(far == 0, wanted, -1), shared)
    unpack_all[...] = marks(jnp.where(far == 0, -1, (far - 1) * shared + wanted), unpack_all.shape[1])
    unpack_near[...] = marks(jnp.where(far == 1, slot, -1), unpack_near.shape[1])
    unpack_far[...] = marks(jnp.where(far > 1, (far - 2) * cap + slot, -1), unpack_far.shape[1])
    lane = lax.broadcasted_iota(jnp.int32, (shared, width), 1)
    for d, out in enumerate(sends, 1):
        out[shared:, :] = jnp.zeros((out.shape[0] - shared, width), F32)
        for c in range(-(-cap // width)):
            hit = (far == d) & (slot == lane + c * width)
            out[shared + c:shared + c + 1, :] = jnp.sum(
                jnp.where(hit, wanted.astype(F32), 0.0), axis=0, keepdims=True
            )
    copies[2].wait()
    copies[3].wait()
    parts = split(operator[...])
    high[...], low[...] = parts
    value = product(parts, split(mult[...]))
    image[...] = value
    for out in sends:
        out[:shared, :] = value


def pack_kernel(times, cap, *refs):
    n = len(times)
    recvs, (high, low, pack, stack_high, stack_low) = refs[:n], refs[n:]
    shared = pack.shape[1]
    width = recvs[0].shape[1]
    column = lax.broadcasted_iota(jnp.int32, (width, shared), 1).astype(F32)
    if n * cap < pack.shape[0]:
        pack[n * cap:, :] = jnp.zeros((pack.shape[0] - n * cap, shared), BF16)
    for d, recv in zip(times, recvs):
        for c in range(-(-cap // width)):
            wanted = jnp.broadcast_to(recv[shared + c:shared + c + 1, :], (shared, width)).T
            chosen = jnp.where(wanted == column, 1.0, 0.0).astype(BF16)
            size = min(width, cap - c * width)
            at = (d - 1) * cap + c * width
            pack[at:at + size, :] = chosen[:size]
    for source, stack in ((high, stack_high), (low, stack_low)):
        square = source[:, :shared]
        stack[:shared, :] = square
        stack[shared:, :] = mm(pack[...], square).astype(BF16)


def prepare_kernel(contact, modes, tile, floor, basis, tile_high, tile_low):
    order, width = floor.shape
    for at in range(0, order, width):
        flag = jnp.broadcast_to(contact[:, at:at + width], (width, width)).T
        floor[at:at + width, :] = jnp.where(flag == 1, 0.0, -jnp.inf)
    high, low = [part.astype(F32) for part in split(modes[...])]
    basis[...] = jnp.concatenate([high, high, low], axis=0).T.astype(BF16)
    tile_high[...], tile_low[...] = split(tile[...])


def send(cap, chosen, image, sends):
    picked = pick(chosen, image)
    for d, out in enumerate(sends):
        out[...] = picked[d * cap:(d + 1) * cap]


def arrived(times, recvs, shared, unpack):
    blocks = [recvs[times.index(d)][...][:shared] for d in sorted(times)]
    rows = sum(b.shape[0] for b in blocks)
    if rows < unpack.shape[1]:
        blocks.append(jnp.zeros((unpack.shape[1] - rows, blocks[0].shape[1]), F32))
    return pick(unpack[...], jnp.concatenate(blocks, axis=0))


def base_kernel(image, unpack_own, gap, base):
    own = image[...]
    base[...] = gap[:own.shape[0], :] - own + pick(unpack_own[...], own)


def far_kernel(times, *refs):
    recvs, (known, unpack, base) = refs[:len(times)], refs[len(times):]
    base[...] = known[...] + arrived(times, recvs, known.shape[0], unpack)


def settle(trial, floor, alive):
    return jnp.where(alive, jnp.maximum(trial, floor), 0.0)


def shared_residual(times, recvs, base, unpack, size):
    known = base[...]
    alive = live(size[0], 0, *known.shape)
    return jnp.where(alive, known + arrived(times, recvs, known.shape[0], unpack), 0.0), alive


def rest_start_kernel(size, operator, mult, mult_block, gap, modes, trial, coarse, high, low, halves):
    step = pl.program_id(0)
    rows, width = gap.shape

    @pl.when(step == 0)
    def _():
        halves[:, :width], halves[:, width:] = split(mult[...])
        coarse[...] = jnp.zeros_like(coarse)

    parts = split(operator[...])
    high[...], low[...] = parts
    both = mm(parts[0], halves[...])
    image = both[:, :width] + (both[:, width:] + mm(parts[1], halves[:, :width]))
    alive = live(size[0], (step + 1) * rows, rows, width)
    residual = jnp.where(alive, gap[...] - image, 0.0)
    trial[...] = mult_block[...] + STEP * residual
    coarse[...] += product(split(modes[...]), split(residual))


def rest_residual(size, high, low, mult_s, mult_n, gap):
    shared, (rows, width) = mult_s.shape[0], mult_n.shape
    mult = jnp.concatenate([mult_s[...], mult_n[...]], axis=0)
    image = product((high[...], low[...]), split(mult))
    alive = live(size[0], shared, rows, width)
    return jnp.where(alive, gap[shared:, :] - image, 0.0), alive


def rest_first_kernel(size, high, low, mult_s, mult_n, gap, modes, trial, coarse):
    residual, _ = rest_residual(size, high, low, mult_s, mult_n, gap)
    trial[...] = mult_n[...] + STEP * residual
    coarse[...] = product(split(modes[:, mult_s.shape[0]:]), split(residual))


def rest_kernel(size, high, low, mult_s, mult_n, gap, floor, top_high, top_low, pack, mult_out, ahead):
    shared = mult_s.shape[0]
    residual, alive = rest_residual(size, high, low, mult_s, mult_n, gap)
    mult = settle(mult_n[...] + STEP * residual, floor[shared:, :], alive)
    mult_out[...] = mult
    value = product((top_high[:, shared:], top_low[:, shared:]), split(mult))
    ahead[:shared, :] = value
    ahead[shared:, :] = pick(pack[...], value)


def rest_last_kernel(size, high, low, mult_s, mult_n, gap, floor, mult_out, residual_out, settled, left, done):
    shared, rows = mult_s.shape[0], mult_n.shape[0]
    residual, alive = rest_residual(size, high, low, mult_s, mult_n, gap)
    left[...] = residual
    settled[...] = settle(mult_n[...] + STEP * residual, floor[shared:, :], alive)
    copies = [
        pltpu.make_async_copy(source, target.at[pl.ds(shared, rows)], done.at[i])
        for i, (source, target) in enumerate(((left, residual_out), (settled, mult_out)))
    ]
    for copy in copies:
        copy.start()
    for copy in copies:
        copy.wait()


def coarse_kernel(times, size, *refs):
    n = len(times)
    base, recvs = refs[0], refs[1:n + 1]
    unpack, mult, modes, started, trial = refs[n + 1:n + 6]
    shared = base.shape[0]
    residual, _ = shared_residual(times, recvs, base, unpack, size)
    coarse = started[...] + product(split(modes[:, :shared]), split(residual))
    for out in refs[n + 6:]:
        out[...] = coarse
    trial[...] = mult[:shared, :] + STEP * residual


def tile_kernel(wide_order, narrow_order, high, low, *refs):
    n, m = len(wide_order), len(narrow_order)
    blocks, outs, (gathered, parts) = refs[:n + 1], refs[n + 1:n + m + 2], refs[n + m + 2:]
    count = blocks[0].shape[0]
    for d, ref in zip((0, *wide_order), blocks):
        at = pl.multiple_of((lax.axis_index("wide") ^ d) * count, count)
        gathered[pl.ds(at, count), :] = ref[...]
    parts[...] = product((high[...], low[...]), split(gathered[...]))
    for d, out in zip((0, *narrow_order), outs):
        at = pl.multiple_of((lax.axis_index("narrow") ^ d) * count, count)
        out[...] = parts[pl.ds(at, count), :]


def lift_kernel(n, m, cap, size, *refs):
    parts = refs[:m + 1]
    ins, (mult_s, mult_n, image), sends = refs[m + 1:m + 8], refs[m + 8:m + 11], refs[m + 11:]
    basis, trial_s, trial_n, floor, high, low, pack = ins
    solved = parts[0][...]
    for part in parts[1:]:
        solved = solved + part[...]
    shared, width = trial_s.shape
    order = floor.shape[0]
    high_part, low_part = split(solved)
    lifted = mm(basis[...], jnp.concatenate([high_part, low_part, high_part], axis=0))
    alive = live(size[0], 0, order, width)
    first = settle(trial_s[...] + lifted[:shared], floor[:shared], alive[:shared])
    rest = settle(trial_n[...] + lifted[shared:], floor[shared:], alive[shared:])
    mult_s[...] = first
    mult_n[...] = rest
    value = product((high[...], low[...]), split(jnp.concatenate([first, rest], axis=0)))
    image[...] = value
    send(cap, pack[...], value, sends)


def sweep_kernel(times, cap, size, *refs):
    n = len(times)
    base, recvs = refs[0], refs[1:n + 1]
    unpack, mult, floor, high, low, ahead, mult_out, image_out = refs[n + 1:n + 9]
    shared = base.shape[0]
    residual, alive = shared_residual(times, recvs, base, unpack, size)
    value = settle(mult[...] + STEP * residual, floor[:shared, :], alive)
    mult_out[...] = value
    both = ahead[...] + product((high[...], low[...]), split(value))
    image_out[...] = both[:shared]
    for d, out in enumerate(refs[n + 9:]):
        out[...] = both[shared + d * cap:shared + (d + 1) * cap]


def last_kernel(times, size, *refs):
    n = len(times)
    base, recvs = refs[0], refs[1:n + 1]
    unpack, mult, floor, _, _, mult_out, residual_out, settled, left, done = refs[n + 1:]
    shared = base.shape[0]
    residual, alive = shared_residual(times, recvs, base, unpack, size)
    left[...] = residual
    first = pltpu.make_async_copy(left, residual_out.at[pl.ds(0, shared)], done.at[0])
    first.start()
    settled[...] = settle(mult[...] + STEP * residual, floor[:shared, :], alive)
    second = pltpu.make_async_copy(settled, mult_out.at[pl.ds(0, shared)], done.at[1])
    second.start()
    first.wait()
    second.wait()


def swap(block, axis, count, d):
    return lax.ppermute(block, axis, [(i, i ^ d) for i in range(count)])


def swap_all(blocks, axis, count, order):
    return [swap(block, axis, count, d) for block, d in zip(blocks, order)]


def swap_rows(blocks, axis, count, times):
    return [swap(blocks[d - 1], axis, count, d) for d in times]


def half_first(count):
    half = count // 2
    return (half, *(d for d in range(count - 1, 1, -1) if d != half), *((1,) if half > 1 else ()))


def middle_first(count):
    return (count - 1, *range(1, count - 1))


def far_first(count):
    return tuple(range(count - 1, 0, -1))


def local(
    wide,
    narrow,
    operators,
    coarse_inverse,
    modes,
    gap,
    start_mult,
    peer_list,
    partner_row,
    interface_size,
    contact_rows,
):
    operator = operators[0]
    modes = modes[0]
    gap = gap[0]
    mult = start_mult[0]
    order, loads = mult.shape
    shared = partner_row.shape[1]
    count = modes.shape[0]
    rest = order - shared
    steps = rest // shared
    n, m = wide - 1, narrow - 1
    cap = 2 * shared // wide
    listed = n * cap
    padded = -(-listed // 128) * 128
    size = interface_size
    coarse_order, part_order = far_first(wide), far_first(narrow)
    far_times, padded_near = half_first(wide), -(-cap // 128) * 128
    padded_far = max(128, -(-(n - 1) * cap // 128) * 128)
    sent = [shape(cap, loads)] * n
    full = 2 * order * loads

    list_rows = -(-(-(-cap // loads)) // 8) * 8
    unpack_own, unpack_all, unpack_near, unpack_far, top_high, top_low, image, *sends = call(
        functools.partial(first_kernel, n, cap),
        tuple(
            pltpu.with_memory_space_constraint(value, pltpu.HBM)
            for value in (peer_list[0].reshape(1, shared), partner_row, operator, mult)
        ),
        [shape(shared, width, BF16) for width in (shared, n * shared, padded_near, padded_far)]
        + [shape(shared, order, BF16)] * 2
        + [shape(shared, loads)]
        + [shape(shared + list_rows, loads)] * n,
        in_specs=[HBM] * 4,
        scratch=[
            pltpu.VMEM((1, shared), jnp.int32),
            pltpu.VMEM((1, shared), jnp.int32),
            pltpu.VMEM((shared, order), F32),
            pltpu.VMEM((order, loads), F32),
            pltpu.SemaphoreType.DMA((4,)),
        ],
        flops=3 * full * shared,
        moved=8 * shared * order,
        name="first",
    )
    floor, basis, tile_high, tile_low = call(
        prepare_kernel,
        (contact_rows, modes, coarse_inverse),
        [shape(order, loads)] + [shape(order, 3 * count, BF16)] + [shape(*coarse_inverse.shape, BF16)] * 2,
        flops=full * count,
        moved=8 * coarse_inverse.size + 4 * full,
        name="prepare",
    )
    def add_far(recvs, times, base):
        if n > 1:
            base = call(
                functools.partial(far_kernel, times[:-1]),
                (*recvs[:-1], base, unpack_far),
                [shape(shared, loads)],
                flops=4 * shared * loads * padded_far,
                moved=2 * shared * padded_far,
                name="far",
            )[0]
        return recvs[-1:], times[-1:], base, unpack_near

    mult_s = mult
    scratch = [pltpu.VMEM((order, 2 * loads), BF16)]
    for outer in range(OUTER):
        times = middle_first(wide) if outer == 0 else far_times
        recvs = swap_rows(sends, "wide", wide, times)
        base = call(
            base_kernel,
            (image, unpack_own, gap),
            [shape(shared, loads)],
            flops=4 * shared * shared * loads,
            moved=8 * shared * loads,
            name="base",
        )[0]
        if outer == 0:
            row_block, load_block = block((shared, order)), block((shared, loads))
            next_loads = block((shared, loads), 1)
            trial_n, started, high, low = call(
                rest_start_kernel,
                (size, pltpu.with_memory_space_constraint(operator, pltpu.HBM), mult, mult, gap, modes),
                [shape(rest, loads), shape(count, loads)] + [shape(rest, order, BF16)] * 2,
                [
                    SMEM,
                    block((shared, order), 1),
                    whole((order, loads)),
                    next_loads,
                    next_loads,
                    block((count, shared), 1, across=True),
                ],
                [load_block, whole((count, loads)), row_block, row_block],
                scratch=scratch,
                grid=(steps,),
                flops=3 * full * rest,
                moved=8 * rest * order,
                name="rest_start",
            )
            marks = unpack_all
            pack, stack_high, stack_low = call(
                functools.partial(pack_kernel, times, cap),
                (*recvs, top_high, top_low),
                [shape(padded, shared, BF16)] + [shape(shared + padded, shared, BF16)] * 2,
                flops=8 * padded * shared * shared,
                moved=8 * padded * shared,
                name="pack",
            )
        else:
            trial_n, started = call(
                rest_first_kernel,
                (size, high, low, mult_s, mult_n, gap, modes),
                [shape(rest, loads), shape(count, loads)],
                flops=3 * full * rest,
                moved=4 * rest * order,
                name="rest_first",
            )
            recvs, times, base, marks = add_far(recvs, times, base)
        trial_s, own, *coarse = call(
            functools.partial(coarse_kernel, times),
            (size, base, *recvs, marks, mult_s, modes, started),
            [shape(shared, loads)] + [shape(count, loads)] * wide,
            flops=6 * shared * loads * padded,
            moved=2 * shared * padded,
            name="coarse",
        )
        blocks = [own] + swap_all(coarse, "wide", wide, coarse_order)
        own, *parts = call(
            functools.partial(tile_kernel, coarse_order, part_order),
            (tile_high, tile_low, *blocks),
            [shape(count, loads)] * narrow,
            scratch=[
                pltpu.VMEM((wide * count, loads), F32),
                pltpu.VMEM((narrow * count, loads), F32),
            ],
            flops=6 * coarse_inverse.size * loads,
            moved=4 * coarse_inverse.size,
            name="tile",
        )
        parts = [own] + swap_all(parts, "narrow", narrow, part_order)
        mult_s, mult_n, image, *sends = call(
            functools.partial(lift_kernel, n, m, cap),
            (size, *parts, basis, trial_s, trial_n, floor, top_high, top_low, pack),
            [shape(shared, loads), shape(rest, loads), shape(shared, loads)] + sent,
            flops=3 * full * shared,
            moved=4 * order * shared,
            name="lift",
        )
        for inner in range(1, INNER):
            last = outer == OUTER - 1 and inner == INNER - 1
            times = far_times
            recvs = swap_rows(sends, "wide", wide, times)
            base = call(
                base_kernel,
                (image, unpack_own, gap),
                [shape(shared, loads)],
                flops=4 * shared * shared * loads,
                moved=8 * shared * loads,
                name="base",
            )[0]
            ins = (size, high, low, mult_s, mult_n, gap, floor)
            recvs, times, base, marks = add_far(recvs, times, base)
            shadow = (size, base, *recvs, marks, mult_s, floor)
            cost = dict(flops=6 * shared * loads * padded, moved=2 * shared * padded)
            if last:
                outs = call(
                    rest_last_kernel,
                    ins,
                    [shape(order, loads)] * 2,
                    out_specs=[HBM] * 2,
                    scratch=[pltpu.VMEM((rest, loads), F32)] * 2 + [pltpu.SemaphoreType.DMA((2,))],
                    flops=3 * full * rest,
                    moved=4 * rest * order,
                    name="rest_last",
                )
                outs = call(
                    functools.partial(last_kernel, times),
                    (*shadow, *outs),
                    [shape(order, loads)] * 2,
                    in_specs=[SMEM] + [VMEM] * (len(shadow) - 1) + [HBM] * 2,
                    out_specs=[HBM] * 2,
                    scratch=[pltpu.VMEM((shared, loads), F32)] * 2 + [pltpu.SemaphoreType.DMA((2,))],
                    alias={len(shadow): 0, len(shadow) + 1: 1},
                    name="last",
                    **cost,
                )
                return tuple(out[None] for out in outs)
            mult_n, ahead = call(
                rest_kernel,
                (*ins, top_high, top_low, pack),
                [shape(rest, loads), shape(shared + padded, loads)],
                flops=3 * full * order,
                moved=4 * order * order,
                name="rest",
            )
            mult_s, image, *sends = call(
                functools.partial(sweep_kernel, times, cap),
                (*shadow, stack_high, stack_low, ahead),
                [shape(shared, loads)] * 2 + sent,
                name="sweep",
                **cost,
            )


def solution(mesh):
    wide = mesh.shape["wide"]
    narrow = mesh.shape["narrow"]

    def body(*args):
        return local(wide, narrow, *args)

    return jax.shard_map(
        body,
        mesh=mesh,
        in_specs=(
            P(("groups", "wide", "narrow"), None, None),
            P(("groups", "wide"), "narrow"),
            P(("groups", "wide", "narrow"), None, None),
            P(("groups", "wide", "narrow"), None, None),
            P(("groups", "wide", "narrow"), None, None),
            P(("groups", "wide", "narrow"), None, None),
            P(("groups", "wide", "narrow"), None),
            P(("groups", "wide", "narrow")),
            P(("groups", "wide", "narrow"), None),
        ),
        out_specs=(
            P(("groups", "wide", "narrow"), None, None),
            P(("groups", "wide", "narrow"), None, None),
        ),
        check_vma=False,
    )
```

```python
import functools

import jax
import jax.numpy as jnp
from jax import lax
from jax.experimental import pallas as pl
from jax.experimental.pallas import tpu as pltpu
from jax.sharding import PartitionSpec as P

OUTER = 2
INNER = 3
STEP = 0.3
F32 = jnp.float32
BF16 = jnp.bfloat16
PARAMS = pltpu.CompilerParams(vmem_limit_bytes=24 * 1024 * 1024)


def split(value):
    high = value.astype(BF16)
    return high, (value - high.astype(F32)).astype(BF16)


def mm(left, right):
    return jnp.dot(left, right, preferred_element_type=F32)


def product(left, right):
    (left_high, left_low), (right_high, right_low) = left, right
    width = right_high.shape[1]
    both = mm(left_high, jnp.concatenate([right_high, right_low], axis=1))
    return both[:, :width] + (both[:, width:] + mm(left_low, right_high))


def pick(chosen, value):
    width = value.shape[1]
    both = mm(chosen, jnp.concatenate(split(value), axis=1))
    return both[:, :width] + both[:, width:]


def live(size, start, rows, width):
    return lax.broadcasted_iota(jnp.int32, (rows, width), 0) + start < size


def call(body, ins, outs, in_specs=None, out_specs=None, scratch=(), grid=(), flops=0, moved=0, alias=None, name=None):
    if in_specs is None:
        in_specs = [SMEM if value.ndim == 1 else VMEM for value in ins]
    if out_specs is None:
        out_specs = [VMEM] * len(outs)
    return pl.pallas_call(
        body,
        out_shape=outs,
        grid=grid,
        in_specs=in_specs,
        out_specs=out_specs,
        scratch_shapes=list(scratch),
        compiler_params=PARAMS,
        cost_estimate=pl.CostEstimate(flops=flops, bytes_accessed=moved, transcendentals=0),
        input_output_aliases=alias or {},
        name=name,
    )(*ins)


def whole(shape):
    return pl.BlockSpec(shape, lambda *i: (0,) * len(shape))


def block(shape, at=0, across=False):
    if across:
        return pl.BlockSpec(shape, lambda i: (0, i + at))
    return pl.BlockSpec(shape, lambda i: (i + at, 0))


SMEM = pl.BlockSpec(memory_space=pltpu.SMEM)
HBM = pl.BlockSpec(memory_space=pltpu.HBM)
VMEM = pl.BlockSpec(memory_space=pltpu.VMEM)


def shape(rows, columns, dtype=F32):
    return jax.ShapeDtypeStruct((rows, columns), dtype)


def first_kernel(n, cap, peers_at, rows_at, operator_at, mult_at, *refs):
    unpack_own, unpack_all, unpack, high, low, image = refs[:6]
    sends, (peers, rows, operator, mult, done) = refs[6:6 + n], refs[6 + n:]
    shared, width = image.shape
    copies = [
        pltpu.make_async_copy(source, target, done.at[i])
        for i, (source, target) in enumerate(
            ((peers_at, peers), (rows_at, rows), (mult_at, mult), (operator_at.at[pl.ds(0, shared)], operator))
        )
    ]
    for copy in copies:
        copy.start()
    copies[0].wait()
    copies[1].wait()
    across = jnp.broadcast_to(peers[...], (shared, shared))
    down = across.T
    first = lax.broadcasted_iota(jnp.int32, (shared, shared), 0)
    second = lax.broadcasted_iota(jnp.int32, (shared, shared), 1)
    slot = jnp.sum(
        jnp.where((across == down) & (second < first), 1.0, 0.0), axis=1, keepdims=True
    ).astype(jnp.int32)
    wanted = jnp.broadcast_to(rows[...], (shared, shared)).T[:, :1]
    far = down[:, :1] ^ lax.axis_index("wide")

    def marks(key, columns):
        hit = key == lax.broadcasted_iota(jnp.int32, (shared, columns), 1)
        return jnp.where(hit, 1.0, 0.0).astype(BF16)

    unpack_own[...] = marks(jnp.where(far == 0, wanted, -1), shared)
    unpack_all[...] = marks(jnp.where(far == 0, -1, (far - 1) * shared + wanted), unpack_all.shape[1])
    unpack[...] = marks(jnp.where(far == 0, -1, (far - 1) * cap + slot), unpack.shape[1])
    lane = lax.broadcasted_iota(jnp.int32, (shared, width), 1)
    for d, out in enumerate(sends, 1):
        out[shared:, :] = jnp.zeros((out.shape[0] - shared, width), F32)
        for c in range(-(-cap // width)):
            hit = (far == d) & (slot == lane + c * width)
            out[shared + c:shared + c + 1, :] = jnp.sum(
                jnp.where(hit, wanted.astype(F32), 0.0), axis=0, keepdims=True
            )
    copies[2].wait()
    copies[3].wait()
    parts = split(operator[...])
    high[...], low[...] = parts
    value = product(parts, split(mult[...]))
    image[...] = value
    for out in sends:
        out[:shared, :] = value


def pack_kernel(times, cap, *refs):
    n = len(times)
    recvs, (high, low, pack, pack_high, pack_low) = refs[:n], refs[n:]
    shared = pack.shape[1]
    width = recvs[0].shape[1]
    column = lax.broadcasted_iota(jnp.int32, (width, shared), 1).astype(F32)
    if n * cap < pack.shape[0]:
        pack[n * cap:, :] = jnp.zeros((pack.shape[0] - n * cap, shared), BF16)
    for d, recv in zip(times, recvs):
        for c in range(-(-cap // width)):
            wanted = jnp.broadcast_to(recv[shared + c:shared + c + 1, :], (shared, width)).T
            chosen = jnp.where(wanted == column, 1.0, 0.0).astype(BF16)
            size = min(width, cap - c * width)
            at = (d - 1) * cap + c * width
            pack[at:at + size, :] = chosen[:size]
    for source, picked in ((high, pack_high), (low, pack_low)):
        picked[...] = mm(pack[...], source[:, :shared]).astype(BF16)


def prepare_kernel(contact, modes, tile, floor, basis, tile_high, tile_low):
    order, width = floor.shape
    for at in range(0, order, width):
        flag = jnp.broadcast_to(contact[:, at:at + width], (width, width)).T
        floor[at:at + width, :] = jnp.where(flag == 1, 0.0, -jnp.inf)
    high, low = [part.astype(F32) for part in split(modes[...])]
    basis[...] = jnp.concatenate([high, high, low], axis=0).T.astype(BF16)
    tile_high[...], tile_low[...] = split(tile[...])


def send(cap, chosen, image, sends):
    picked = pick(chosen, image)
    for d, out in enumerate(sends):
        out[...] = picked[d * cap:(d + 1) * cap]


def arrived(times, recvs, shared, unpack):
    blocks = [recvs[times.index(d)][...][:shared] for d in sorted(times)]
    rows = sum(b.shape[0] for b in blocks)
    if rows < unpack.shape[1]:
        blocks.append(jnp.zeros((unpack.shape[1] - rows, blocks[0].shape[1]), F32))
    return pick(unpack[...], jnp.concatenate(blocks, axis=0))


def base_kernel(image, unpack_own, gap, base):
    own = image[...]
    base[...] = gap[:own.shape[0], :] - own + pick(unpack_own[...], own)


def image_base_kernel(ahead, high, low, mult, unpack_own, gap, base):
    shared = mult.shape[0]
    own = ahead[:shared, :] + product((high[:, :shared], low[:, :shared]), split(mult[...]))
    base[...] = gap[:shared, :] - own + pick(unpack_own[...], own)


def settle(trial, floor, alive):
    return jnp.where(alive, jnp.maximum(trial, floor), 0.0)


def shared_residual(times, recvs, base, unpack, size):
    known = base[...]
    alive = live(size[0], 0, *known.shape)
    return jnp.where(alive, known + arrived(times, recvs, known.shape[0], unpack), 0.0), alive


def rest_start_kernel(size, operator, mult, mult_block, gap, modes, trial, coarse, high, low, halves):
    step = pl.program_id(0)
    rows, width = gap.shape

    @pl.when(step == 0)
    def _():
        halves[:, :width], halves[:, width:] = split(mult[...])
        coarse[...] = jnp.zeros_like(coarse)

    parts = split(operator[...])
    high[...], low[...] = parts
    both = mm(parts[0], halves[...])
    image = both[:, :width] + (both[:, width:] + mm(parts[1], halves[:, :width]))
    alive = live(size[0], (step + 1) * rows, rows, width)
    residual = jnp.where(alive, gap[...] - image, 0.0)
    trial[...] = mult_block[...] + STEP * residual
    coarse[...] += product(split(modes[...]), split(residual))


def rest_residual(size, high, low, mult_s, mult_n, gap):
    shared, (rows, width) = mult_s.shape[0], mult_n.shape
    mult = jnp.concatenate([mult_s[...], mult_n[...]], axis=0)
    image = product((high[...], low[...]), split(mult))
    alive = live(size[0], shared, rows, width)
    return jnp.where(alive, gap[shared:, :] - image, 0.0), alive


def rest_first_kernel(size, high, low, mult_s, mult_n, gap, modes, trial, coarse):
    residual, _ = rest_residual(size, high, low, mult_s, mult_n, gap)
    trial[...] = mult_n[...] + STEP * residual
    coarse[...] = product(split(modes[:, mult_s.shape[0]:]), split(residual))


def rest_kernel(size, high, low, mult_s, mult_n, gap, floor, top_high, top_low, pack, mult_out, ahead):
    shared = mult_s.shape[0]
    residual, alive = rest_residual(size, high, low, mult_s, mult_n, gap)
    mult = settle(mult_n[...] + STEP * residual, floor[shared:, :], alive)
    mult_out[...] = mult
    value = product((top_high[:, shared:], top_low[:, shared:]), split(mult))
    ahead[:shared, :] = value
    ahead[shared:, :] = pick(pack[...], value)


def rest_last_kernel(size, high, low, mult_s, mult_n, gap, floor, mult_out, residual_out, settled, left, done):
    shared, rows = mult_s.shape[0], mult_n.shape[0]
    residual, alive = rest_residual(size, high, low, mult_s, mult_n, gap)
    left[...] = residual
    settled[...] = settle(mult_n[...] + STEP * residual, floor[shared:, :], alive)
    copies = [
        pltpu.make_async_copy(source, target.at[pl.ds(shared, rows)], done.at[i])
        for i, (source, target) in enumerate(((left, residual_out), (settled, mult_out)))
    ]
    for copy in copies:
        copy.start()
    for copy in copies:
        copy.wait()


def coarse_kernel(times, size, *refs):
    n = len(times)
    recvs = refs[:n]
    base, unpack, mult, modes, started, trial = refs[n:n + 6]
    shared = base.shape[0]
    residual, _ = shared_residual(times, recvs, base, unpack, size)
    coarse = started[...] + product(split(modes[:, :shared]), split(residual))
    for out in refs[n + 6:]:
        out[...] = coarse
    trial[...] = mult[:shared, :] + STEP * residual


def tile_kernel(wide_order, narrow_order, high, low, *refs):
    n, m = len(wide_order), len(narrow_order)
    blocks, outs, (gathered, parts) = refs[:n + 1], refs[n + 1:n + m + 2], refs[n + m + 2:]
    count = blocks[0].shape[0]
    for d, ref in zip((0, *wide_order), blocks):
        at = pl.multiple_of((lax.axis_index("wide") ^ d) * count, count)
        gathered[pl.ds(at, count), :] = ref[...]
    parts[...] = product((high[...], low[...]), split(gathered[...]))
    for d, out in zip((0, *narrow_order), outs):
        at = pl.multiple_of((lax.axis_index("narrow") ^ d) * count, count)
        out[...] = parts[pl.ds(at, count), :]


def lift_kernel(n, m, cap, size, *refs):
    parts = refs[:m + 1]
    ins, (mult_s, mult_n, image), sends = refs[m + 1:m + 8], refs[m + 8:m + 11], refs[m + 11:]
    basis, trial_s, trial_n, floor, high, low, pack = ins
    solved = parts[0][...]
    for part in parts[1:]:
        solved = solved + part[...]
    shared, width = trial_s.shape
    order = floor.shape[0]
    high_part, low_part = split(solved)
    lifted = mm(basis[...], jnp.concatenate([high_part, low_part, high_part], axis=0))
    alive = live(size[0], 0, order, width)
    first = settle(trial_s[...] + lifted[:shared], floor[:shared], alive[:shared])
    rest = settle(trial_n[...] + lifted[shared:], floor[shared:], alive[shared:])
    mult_s[...] = first
    mult_n[...] = rest
    value = product((high[...], low[...]), split(jnp.concatenate([first, rest], axis=0)))
    image[...] = value
    send(cap, pack[...], value, sends)


def sweep_kernel(times, cap, size, *refs):
    n = len(times)
    recvs = refs[:n]
    base, unpack, mult, floor, high, low, ahead, mult_out = refs[n:n + 8]
    shared = base.shape[0]
    residual, alive = shared_residual(times, recvs, base, unpack, size)
    value = settle(mult[...] + STEP * residual, floor[:shared, :], alive)
    mult_out[...] = value
    rows = ahead[shared:, :] + product((high[...], low[...]), split(value))
    for d, out in enumerate(refs[n + 8:]):
        out[...] = rows[d * cap:(d + 1) * cap]


def last_kernel(times, size, *refs):
    n = len(times)
    recvs = refs[:n]
    base, unpack, mult, floor, _, _, mult_out, residual_out, settled, left, done = refs[n:]
    shared = base.shape[0]
    residual, alive = shared_residual(times, recvs, base, unpack, size)
    left[...] = residual
    first = pltpu.make_async_copy(left, residual_out.at[pl.ds(0, shared)], done.at[0])
    first.start()
    settled[...] = settle(mult[...] + STEP * residual, floor[:shared, :], alive)
    second = pltpu.make_async_copy(settled, mult_out.at[pl.ds(0, shared)], done.at[1])
    second.start()
    first.wait()
    second.wait()


def swap(block, axis, count, d):
    return lax.ppermute(block, axis, [(i, i ^ d) for i in range(count)])


def swap_all(blocks, axis, count, order):
    return [swap(block, axis, count, d) for block, d in zip(blocks, order)]


def swap_rows(blocks, axis, count, times):
    return [swap(blocks[d - 1], axis, count, d) for d in times]


def half_first(count):
    half = count // 2
    return (half, *(d for d in range(count - 1, 0, -1) if d != half))


def middle_first(count):
    return (count - 1, *range(1, count - 1))


def far_first(count):
    return tuple(range(count - 1, 0, -1))


def local(
    wide,
    narrow,
    operators,
    coarse_inverse,
    modes,
    gap,
    start_mult,
    peer_list,
    partner_row,
    interface_size,
    contact_rows,
):
    operator = operators[0]
    modes = modes[0]
    gap = gap[0]
    mult = start_mult[0]
    order, loads = mult.shape
    shared = partner_row.shape[1]
    count = modes.shape[0]
    rest = order - shared
    steps = rest // shared
    n, m = wide - 1, narrow - 1
    cap = 2 * shared // wide
    listed = n * cap
    padded = -(-listed // 128) * 128
    size = interface_size
    coarse_order, part_order = far_first(wide), far_first(narrow)
    middle, half = middle_first(wide), half_first(wide)
    orders = ((middle, half, half), (half, half, half))
    sent = [shape(cap, loads)] * n
    full = 2 * order * loads

    list_rows = -(-(-(-cap // loads)) // 8) * 8
    unpack_own, unpack_all, unpack, top_high, top_low, image, *sends = call(
        functools.partial(first_kernel, n, cap),
        tuple(
            pltpu.with_memory_space_constraint(value, pltpu.HBM)
            for value in (peer_list[0].reshape(1, shared), partner_row, operator, mult)
        ),
        [shape(shared, shared, BF16), shape(shared, n * shared, BF16), shape(shared, padded, BF16)]
        + [shape(shared, order, BF16)] * 2
        + [shape(shared, loads)]
        + [shape(shared + list_rows, loads)] * n,
        in_specs=[HBM] * 4,
        scratch=[
            pltpu.VMEM((1, shared), jnp.int32),
            pltpu.VMEM((1, shared), jnp.int32),
            pltpu.VMEM((shared, order), F32),
            pltpu.VMEM((order, loads), F32),
            pltpu.SemaphoreType.DMA((4,)),
        ],
        flops=3 * full * shared,
        moved=8 * shared * order,
        name="first",
    )
    floor, basis, tile_high, tile_low = call(
        prepare_kernel,
        (contact_rows, modes, coarse_inverse),
        [shape(order, loads)] + [shape(order, 3 * count, BF16)] + [shape(*coarse_inverse.shape, BF16)] * 2,
        flops=full * count,
        moved=8 * coarse_inverse.size + 4 * full,
        name="prepare",
    )
    def base_of(known):
        ins = (image,) if known else (ahead, top_high, top_low, mult_s)
        return call(
            base_kernel if known else image_base_kernel,
            (*ins, unpack_own, gap),
            [shape(shared, loads)],
            flops=10 * shared * shared * loads,
            moved=8 * shared * loads,
            name="base",
        )[0]

    mult_s = mult
    scratch = [pltpu.VMEM((order, 2 * loads), BF16)]
    for outer in range(OUTER):
        times = orders[outer][0]
        recvs = swap_rows(sends, "wide", wide, times)
        base = base_of(outer == 0)
        if outer == 0:
            row_block, load_block = block((shared, order)), block((shared, loads))
            next_loads = block((shared, loads), 1)
            trial_n, started, high, low = call(
                rest_start_kernel,
                (size, operator, mult, mult, gap, modes),
                [shape(rest, loads), shape(count, loads)] + [shape(rest, order, BF16)] * 2,
                [
                    SMEM,
                    block((shared, order), 1),
                    whole((order, loads)),
                    next_loads,
                    next_loads,
                    block((count, shared), 1, across=True),
                ],
                [load_block, whole((count, loads)), row_block, row_block],
                scratch=scratch,
                grid=(steps,),
                flops=3 * full * rest,
                moved=8 * rest * order,
                name="rest_start",
            )
            marks = unpack_all
            pack, pack_high, pack_low = call(
                functools.partial(pack_kernel, times, cap),
                (*recvs, top_high, top_low),
                [shape(padded, shared, BF16)] * 3,
                flops=8 * padded * shared * shared,
                moved=8 * padded * shared,
                name="pack",
            )
        else:
            trial_n, started = call(
                rest_first_kernel,
                (size, high, low, mult_s, mult_n, gap, modes),
                [shape(rest, loads), shape(count, loads)],
                flops=3 * full * rest,
                moved=4 * rest * order,
                name="rest_first",
            )
            marks = unpack
        trial_s, own, *coarse = call(
            functools.partial(coarse_kernel, times),
            (size, *recvs, base, marks, mult_s, modes, started),
            [shape(shared, loads)] + [shape(count, loads)] * wide,
            flops=6 * shared * loads * unpack.shape[1],
            moved=2 * shared * unpack.shape[1],
            name="coarse",
        )
        blocks = [own] + swap_all(coarse, "wide", wide, coarse_order)
        own, *parts = call(
            functools.partial(tile_kernel, coarse_order, part_order),
            (tile_high, tile_low, *blocks),
            [shape(count, loads)] * narrow,
            scratch=[
                pltpu.VMEM((wide * count, loads), F32),
                pltpu.VMEM((narrow * count, loads), F32),
            ],
            flops=6 * coarse_inverse.size * loads,
            moved=4 * coarse_inverse.size,
            name="tile",
        )
        parts = [own] + swap_all(parts, "narrow", narrow, part_order)
        mult_s, mult_n, image, *sends = call(
            functools.partial(lift_kernel, n, m, cap),
            (size, *parts, basis, trial_s, trial_n, floor, top_high, top_low, pack),
            [shape(shared, loads), shape(rest, loads), shape(shared, loads)] + sent,
            flops=3 * full * shared,
            moved=4 * order * shared,
            name="lift",
        )
        for inner in range(1, INNER):
            last = outer == OUTER - 1 and inner == INNER - 1
            times = orders[outer][inner]
            recvs = swap_rows(sends, "wide", wide, times)
            base = base_of(inner == 1)
            ins = (size, high, low, mult_s, mult_n, gap, floor)
            shadow = (size, *recvs, base, unpack, mult_s, floor)
            cost = dict(flops=6 * shared * loads * unpack.shape[1], moved=2 * shared * unpack.shape[1])
            if last:
                outs = call(
                    rest_last_kernel,
                    ins,
                    [shape(order, loads)] * 2,
                    out_specs=[HBM] * 2,
                    scratch=[pltpu.VMEM((rest, loads), F32)] * 2 + [pltpu.SemaphoreType.DMA((2,))],
                    flops=3 * full * rest,
                    moved=4 * rest * order,
                    name="rest_last",
                )
                outs = call(
                    functools.partial(last_kernel, times),
                    (*shadow, *outs),
                    [shape(order, loads)] * 2,
                    in_specs=[SMEM] + [VMEM] * (len(shadow) - 1) + [HBM] * 2,
                    out_specs=[HBM] * 2,
                    scratch=[pltpu.VMEM((shared, loads), F32)] * 2 + [pltpu.SemaphoreType.DMA((2,))],
                    alias={len(shadow): 0, len(shadow) + 1: 1},
                    name="last",
                    **cost,
                )
                return tuple(out[None] for out in outs)
            mult_n, ahead = call(
                rest_kernel,
                (*ins, top_high, top_low, pack),
                [shape(rest, loads), shape(shared + padded, loads)],
                flops=3 * full * order,
                moved=4 * order * order,
                name="rest",
            )
            mult_s, *sends = call(
                functools.partial(sweep_kernel, times, cap),
                (*shadow, pack_high, pack_low, ahead),
                [shape(shared, loads)] + sent,
                name="sweep",
                **cost,
            )


def solution(mesh):
    wide = mesh.shape["wide"]
    narrow = mesh.shape["narrow"]

    def body(*args):
        return local(wide, narrow, *args)

    return jax.shard_map(
        body,
        mesh=mesh,
        in_specs=(
            P(("groups", "wide", "narrow"), None, None),
            P(("groups", "wide"), "narrow"),
            P(("groups", "wide", "narrow"), None, None),
            P(("groups", "wide", "narrow"), None, None),
            P(("groups", "wide", "narrow"), None, None),
            P(("groups", "wide", "narrow"), None, None),
            P(("groups", "wide", "narrow"), None),
            P(("groups", "wide", "narrow")),
            P(("groups", "wide", "narrow"), None),
        ),
        out_specs=(
            P(("groups", "wide", "narrow"), None, None),
            P(("groups", "wide", "narrow"), None, None),
        ),
        check_vma=False,
    )
```

```python
import functools

import jax
import jax.numpy as jnp
from jax import lax
from jax.experimental import pallas as pl
from jax.experimental.pallas import tpu as pltpu
from jax.sharding import PartitionSpec as P

OUTER = 2
INNER = 3
STEP = 0.3
F32 = jnp.float32
BF16 = jnp.bfloat16
PARAMS = pltpu.CompilerParams(vmem_limit_bytes=24 * 1024 * 1024)


def split(value):
    high = value.astype(BF16)
    return high, (value - high.astype(F32)).astype(BF16)


def mm(left, right):
    return jnp.dot(left, right, preferred_element_type=F32)


def product(left, right):
    (left_high, left_low), (right_high, right_low) = left, right
    width = right_high.shape[1]
    both = mm(left_high, jnp.concatenate([right_high, right_low], axis=1))
    return both[:, :width] + (both[:, width:] + mm(left_low, right_high))


def pick(chosen, value):
    width = value.shape[1]
    both = mm(chosen, jnp.concatenate(split(value), axis=1))
    return both[:, :width] + both[:, width:]


def live(size, start, rows, width):
    return lax.broadcasted_iota(jnp.int32, (rows, width), 0) + start < size


def call(body, ins, outs, in_specs=None, out_specs=None, scratch=(), grid=(), flops=0, moved=0, alias=None, name=None):
    if in_specs is None:
        in_specs = [SMEM if value.ndim == 1 else VMEM for value in ins]
    if out_specs is None:
        out_specs = [VMEM] * len(outs)
    return pl.pallas_call(
        body,
        out_shape=outs,
        grid=grid,
        in_specs=in_specs,
        out_specs=out_specs,
        scratch_shapes=list(scratch),
        compiler_params=PARAMS,
        cost_estimate=pl.CostEstimate(flops=flops, bytes_accessed=moved, transcendentals=0),
        input_output_aliases=alias or {},
        name=name,
    )(*ins)


def whole(shape):
    return pl.BlockSpec(shape, lambda *i: (0,) * len(shape))


def block(shape, at=0, across=False):
    if across:
        return pl.BlockSpec(shape, lambda i: (0, i + at))
    return pl.BlockSpec(shape, lambda i: (i + at, 0))


SMEM = pl.BlockSpec(memory_space=pltpu.SMEM)
HBM = pl.BlockSpec(memory_space=pltpu.HBM)
VMEM = pl.BlockSpec(memory_space=pltpu.VMEM)


def shape(rows, columns, dtype=F32):
    return jax.ShapeDtypeStruct((rows, columns), dtype)


def first_kernel(n, cap, peers_at, rows_at, operator_at, mult_at, *refs):
    unpack_own, unpack_all, unpack, high, low, image = refs[:6]
    sends, (peers, rows, operator, mult, done) = refs[6:6 + n], refs[6 + n:]
    shared, width = image.shape
    copies = [
        pltpu.make_async_copy(source, target, done.at[i])
        for i, (source, target) in enumerate(
            ((peers_at, peers), (rows_at, rows), (mult_at, mult), (operator_at.at[pl.ds(0, shared)], operator))
        )
    ]
    for copy in copies:
        copy.start()
    copies[0].wait()
    copies[1].wait()
    across = jnp.broadcast_to(peers[...], (shared, shared))
    down = across.T
    first = lax.broadcasted_iota(jnp.int32, (shared, shared), 0)
    second = lax.broadcasted_iota(jnp.int32, (shared, shared), 1)
    slot = jnp.sum(
        jnp.where((across == down) & (second < first), 1.0, 0.0), axis=1, keepdims=True
    ).astype(jnp.int32)
    wanted = jnp.broadcast_to(rows[...], (shared, shared)).T[:, :1]
    far = down[:, :1] ^ lax.axis_index("wide")

    def marks(key, columns):
        hit = key == lax.broadcasted_iota(jnp.int32, (shared, columns), 1)
        return jnp.where(hit, 1.0, 0.0).astype(BF16)

    unpack_own[...] = marks(jnp.where(far == 0, wanted, -1), shared)
    unpack_all[...] = marks(jnp.where(far == 0, -1, (far - 1) * shared + wanted), unpack_all.shape[1])
    unpack[...] = marks(jnp.where(far == 0, -1, (far - 1) * cap + slot), unpack.shape[1])
    lane = lax.broadcasted_iota(jnp.int32, (shared, width), 1)
    for d, out in enumerate(sends, 1):
        out[shared:, :] = jnp.zeros((out.shape[0] - shared, width), F32)
        for c in range(-(-cap // width)):
            hit = (far == d) & (slot == lane + c * width)
            out[shared + c:shared + c + 1, :] = jnp.sum(
                jnp.where(hit, wanted.astype(F32), 0.0), axis=0, keepdims=True
            )
    copies[2].wait()
    copies[3].wait()
    parts = split(operator[...])
    high[...], low[...] = parts
    value = product(parts, split(mult[...]))
    image[...] = value
    for out in sends:
        out[:shared, :] = value


def pack_kernel(times, cap, *refs):
    n = len(times)
    recvs, (high, low, pack, stack_high, stack_low) = refs[:n], refs[n:]
    shared = pack.shape[1]
    width = recvs[0].shape[1]
    column = lax.broadcasted_iota(jnp.int32, (width, shared), 1).astype(F32)
    if n * cap < pack.shape[0]:
        pack[n * cap:, :] = jnp.zeros((pack.shape[0] - n * cap, shared), BF16)
    for d, recv in zip(times, recvs):
        for c in range(-(-cap // width)):
            wanted = jnp.broadcast_to(recv[shared + c:shared + c + 1, :], (shared, width)).T
            chosen = jnp.where(wanted == column, 1.0, 0.0).astype(BF16)
            size = min(width, cap - c * width)
            at = (d - 1) * cap + c * width
            pack[at:at + size, :] = chosen[:size]
    for source, stack in ((high, stack_high), (low, stack_low)):
        square = source[:, :shared]
        stack[:shared, :] = square
        stack[shared:, :] = mm(pack[...], square).astype(BF16)


def prepare_kernel(contact, modes, tile, floor, basis, tile_high, tile_low):
    order, width = floor.shape
    for at in range(0, order, width):
        flag = jnp.broadcast_to(contact[:, at:at + width], (width, width)).T
        floor[at:at + width, :] = jnp.where(flag == 1, 0.0, -jnp.inf)
    high, low = [part.astype(F32) for part in split(modes[...])]
    basis[...] = jnp.concatenate([high, high, low], axis=0).T.astype(BF16)
    tile_high[...], tile_low[...] = split(tile[...])


def send(cap, chosen, image, sends):
    picked = pick(chosen, image)
    for d, out in enumerate(sends):
        out[...] = picked[d * cap:(d + 1) * cap]


def arrived(times, recvs, shared, unpack):
    blocks = [recvs[times.index(d)][...][:shared] for d in sorted(times)]
    rows = sum(b.shape[0] for b in blocks)
    if rows < unpack.shape[1]:
        blocks.append(jnp.zeros((unpack.shape[1] - rows, blocks[0].shape[1]), F32))
    return pick(unpack[...], jnp.concatenate(blocks, axis=0))


def base_kernel(image, unpack_own, gap, base):
    own = image[...]
    base[...] = gap[:own.shape[0], :] - own + pick(unpack_own[...], own)


def settle(trial, floor, alive):
    return jnp.where(alive, jnp.maximum(trial, floor), 0.0)


def shared_residual(times, recvs, base, unpack, size):
    known = base[...]
    alive = live(size[0], 0, *known.shape)
    return jnp.where(alive, known + arrived(times, recvs, known.shape[0], unpack), 0.0), alive


def rest_start_kernel(size, operator, mult, mult_block, gap, modes, trial, coarse, high, low, halves):
    step = pl.program_id(0)
    rows, width = gap.shape

    @pl.when(step == 0)
    def _():
        halves[:, :width], halves[:, width:] = split(mult[...])
        coarse[...] = jnp.zeros_like(coarse)

    parts = split(operator[...])
    high[...], low[...] = parts
    both = mm(parts[0], halves[...])
    image = both[:, :width] + (both[:, width:] + mm(parts[1], halves[:, :width]))
    alive = live(size[0], (step + 1) * rows, rows, width)
    residual = jnp.where(alive, gap[...] - image, 0.0)
    trial[...] = mult_block[...] + STEP * residual
    coarse[...] += product(split(modes[...]), split(residual))


def rest_residual(size, high, low, mult_s, mult_n, gap):
    shared, (rows, width) = mult_s.shape[0], mult_n.shape
    mult = jnp.concatenate([mult_s[...], mult_n[...]], axis=0)
    image = product((high[...], low[...]), split(mult))
    alive = live(size[0], shared, rows, width)
    return jnp.where(alive, gap[shared:, :] - image, 0.0), alive


def rest_first_kernel(size, high, low, mult_s, mult_n, gap, modes, trial, coarse):
    residual, _ = rest_residual(size, high, low, mult_s, mult_n, gap)
    trial[...] = mult_n[...] + STEP * residual
    coarse[...] = product(split(modes[:, mult_s.shape[0]:]), split(residual))


def rest_kernel(size, high, low, mult_s, mult_n, gap, floor, top_high, top_low, pack, mult_out, ahead):
    shared = mult_s.shape[0]
    residual, alive = rest_residual(size, high, low, mult_s, mult_n, gap)
    mult = settle(mult_n[...] + STEP * residual, floor[shared:, :], alive)
    mult_out[...] = mult
    value = product((top_high[:, shared:], top_low[:, shared:]), split(mult))
    ahead[:shared, :] = value
    ahead[shared:, :] = pick(pack[...], value)


def rest_last_kernel(size, high, low, mult_s, mult_n, gap, floor, mult_out, residual_out, settled, left, done):
    shared, rows = mult_s.shape[0], mult_n.shape[0]
    residual, alive = rest_residual(size, high, low, mult_s, mult_n, gap)
    left[...] = residual
    settled[...] = settle(mult_n[...] + STEP * residual, floor[shared:, :], alive)
    copies = [
        pltpu.make_async_copy(source, target.at[pl.ds(shared, rows)], done.at[i])
        for i, (source, target) in enumerate(((left, residual_out), (settled, mult_out)))
    ]
    for copy in copies:
        copy.start()
    for copy in copies:
        copy.wait()


def coarse_kernel(times, size, *refs):
    n = len(times)
    recvs = refs[:n]
    base, unpack, mult, modes, started, trial = refs[n:n + 6]
    shared = base.shape[0]
    residual, _ = shared_residual(times, recvs, base, unpack, size)
    coarse = started[...] + product(split(modes[:, :shared]), split(residual))
    for out in refs[n + 6:]:
        out[...] = coarse
    trial[...] = mult[:shared, :] + STEP * residual


def tile_kernel(wide_order, narrow_order, high, low, *refs):
    n, m = len(wide_order), len(narrow_order)
    blocks, outs, (gathered, parts) = refs[:n + 1], refs[n + 1:n + m + 2], refs[n + m + 2:]
    count = blocks[0].shape[0]
    for d, ref in zip((0, *wide_order), blocks):
        at = pl.multiple_of((lax.axis_index("wide") ^ d) * count, count)
        gathered[pl.ds(at, count), :] = ref[...]
    parts[...] = product((high[...], low[...]), split(gathered[...]))
    for d, out in zip((0, *narrow_order), outs):
        at = pl.multiple_of((lax.axis_index("narrow") ^ d) * count, count)
        out[...] = parts[pl.ds(at, count), :]


def lift_kernel(n, m, cap, size, *refs):
    parts = refs[:m + 1]
    ins, (mult_s, mult_n, image), sends = refs[m + 1:m + 8], refs[m + 8:m + 11], refs[m + 11:]
    basis, trial_s, trial_n, floor, high, low, pack = ins
    solved = parts[0][...]
    for part in parts[1:]:
        solved = solved + part[...]
    shared, width = trial_s.shape
    order = floor.shape[0]
    high_part, low_part = split(solved)
    lifted = mm(basis[...], jnp.concatenate([high_part, low_part, high_part], axis=0))
    alive = live(size[0], 0, order, width)
    first = settle(trial_s[...] + lifted[:shared], floor[:shared], alive[:shared])
    rest = settle(trial_n[...] + lifted[shared:], floor[shared:], alive[shared:])
    mult_s[...] = first
    mult_n[...] = rest
    value = product((high[...], low[...]), split(jnp.concatenate([first, rest], axis=0)))
    image[...] = value
    send(cap, pack[...], value, sends)


def sweep_kernel(times, cap, size, *refs):
    n = len(times)
    recvs = refs[:n]
    base, unpack, mult, floor, high, low, ahead, mult_out, image_out = refs[n:n + 9]
    shared = base.shape[0]
    residual, alive = shared_residual(times, recvs, base, unpack, size)
    value = settle(mult[...] + STEP * residual, floor[:shared, :], alive)
    mult_out[...] = value
    both = ahead[...] + product((high[...], low[...]), split(value))
    image_out[...] = both[:shared]
    for d, out in enumerate(refs[n + 9:]):
        out[...] = both[shared + d * cap:shared + (d + 1) * cap]


def last_kernel(times, size, *refs):
    n = len(times)
    recvs = refs[:n]
    base, unpack, mult, floor, _, _, mult_out, residual_out, settled, left, done = refs[n:]
    shared = base.shape[0]
    residual, alive = shared_residual(times, recvs, base, unpack, size)
    left[...] = residual
    first = pltpu.make_async_copy(left, residual_out.at[pl.ds(0, shared)], done.at[0])
    first.start()
    settled[...] = settle(mult[...] + STEP * residual, floor[:shared, :], alive)
    second = pltpu.make_async_copy(settled, mult_out.at[pl.ds(0, shared)], done.at[1])
    second.start()
    first.wait()
    second.wait()


def swap(block, axis, count, d):
    return lax.ppermute(block, axis, [(i, i ^ d) for i in range(count)])


def swap_all(blocks, axis, count, order):
    return [swap(block, axis, count, d) for block, d in zip(blocks, order)]


def swap_rows(blocks, axis, count, times):
    return [swap(blocks[d - 1], axis, count, d) for d in times]


def half_first(count, back):
    half = count // 2
    others = [d for d in range(1, count) if d != half]
    return (half, *(others[::-1] if back else others))


def middle_first(count):
    return (count - 1, *range(1, count - 1))


def far_first(count):
    return tuple(range(count - 1, 0, -1))


def local(
    wide,
    narrow,
    operators,
    coarse_inverse,
    modes,
    gap,
    start_mult,
    peer_list,
    partner_row,
    interface_size,
    contact_rows,
):
    operator = operators[0]
    modes = modes[0]
    gap = gap[0]
    mult = start_mult[0]
    order, loads = mult.shape
    shared = partner_row.shape[1]
    count = modes.shape[0]
    rest = order - shared
    steps = rest // shared
    n, m = wide - 1, narrow - 1
    cap = 2 * shared // wide
    listed = n * cap
    padded = -(-listed // 128) * 128
    size = interface_size
    coarse_order, part_order = half_first(wide, True), far_first(narrow)
    half, half_back, middle = half_first(wide, False), half_first(wide, True), middle_first(wide)
    orders = ((middle, half, half_back), (half_back, half, half_back))
    sent = [shape(cap, loads)] * n
    full = 2 * order * loads

    list_rows = -(-(-(-cap // loads)) // 8) * 8
    unpack_own, unpack_all, unpack, top_high, top_low, image, *sends = call(
        functools.partial(first_kernel, n, cap),
        tuple(
            pltpu.with_memory_space_constraint(value, pltpu.HBM)
            for value in (peer_list[0].reshape(1, shared), partner_row, operator, mult)
        ),
        [shape(shared, shared, BF16), shape(shared, n * shared, BF16), shape(shared, padded, BF16)]
        + [shape(shared, order, BF16)] * 2
        + [shape(shared, loads)]
        + [shape(shared + list_rows, loads)] * n,
        in_specs=[HBM] * 4,
        scratch=[
            pltpu.VMEM((1, shared), jnp.int32),
            pltpu.VMEM((1, shared), jnp.int32),
            pltpu.VMEM((shared, order), F32),
            pltpu.VMEM((order, loads), F32),
            pltpu.SemaphoreType.DMA((4,)),
        ],
        flops=3 * full * shared,
        moved=8 * shared * order,
        name="first",
    )
    floor, basis, tile_high, tile_low = call(
        prepare_kernel,
        (contact_rows, modes, coarse_inverse),
        [shape(order, loads)] + [shape(order, 3 * count, BF16)] + [shape(*coarse_inverse.shape, BF16)] * 2,
        flops=full * count,
        moved=8 * coarse_inverse.size + 4 * full,
        name="prepare",
    )
    mult_s = mult
    scratch = [pltpu.VMEM((order, 2 * loads), BF16)]
    for outer in range(OUTER):
        times = orders[outer][0]
        recvs = swap_rows(sends, "wide", wide, times)
        base = call(
            base_kernel,
            (image, unpack_own, gap),
            [shape(shared, loads)],
            flops=4 * shared * shared * loads,
            moved=8 * shared * loads,
            name="base",
        )[0]
        if outer == 0:
            row_block, load_block = block((shared, order)), block((shared, loads))
            next_loads = block((shared, loads), 1)
            trial_n, started, high, low = call(
                rest_start_kernel,
                (size, operator, mult, mult, gap, modes),
                [shape(rest, loads), shape(count, loads)] + [shape(rest, order, BF16)] * 2,
                [
                    SMEM,
                    block((shared, order), 1),
                    whole((order, loads)),
                    next_loads,
                    next_loads,
                    block((count, shared), 1, across=True),
                ],
                [load_block, whole((count, loads)), row_block, row_block],
                scratch=scratch,
                grid=(steps,),
                flops=3 * full * rest,
                moved=8 * rest * order,
                name="rest_start",
            )
            marks = unpack_all
            pack, stack_high, stack_low = call(
                functools.partial(pack_kernel, times, cap),
                (*recvs, top_high, top_low),
                [shape(padded, shared, BF16)] + [shape(shared + padded, shared, BF16)] * 2,
                flops=8 * padded * shared * shared,
                moved=8 * padded * shared,
                name="pack",
            )
        else:
            trial_n, started = call(
                rest_first_kernel,
                (size, high, low, mult_s, mult_n, gap, modes),
                [shape(rest, loads), shape(count, loads)],
                flops=3 * full * rest,
                moved=4 * rest * order,
                name="rest_first",
            )
            marks = unpack
        trial_s, own, *coarse = call(
            functools.partial(coarse_kernel, times),
            (size, *recvs, base, marks, mult_s, modes, started),
            [shape(shared, loads)] + [shape(count, loads)] * wide,
            flops=6 * shared * loads * unpack.shape[1],
            moved=2 * shared * unpack.shape[1],
            name="coarse",
        )
        blocks = [own] + swap_all(coarse, "wide", wide, coarse_order)
        own, *parts = call(
            functools.partial(tile_kernel, coarse_order, part_order),
            (tile_high, tile_low, *blocks),
            [shape(count, loads)] * narrow,
            scratch=[
                pltpu.VMEM((wide * count, loads), F32),
                pltpu.VMEM((narrow * count, loads), F32),
            ],
            flops=6 * coarse_inverse.size * loads,
            moved=4 * coarse_inverse.size,
            name="tile",
        )
        parts = [own] + swap_all(parts, "narrow", narrow, part_order)
        mult_s, mult_n, image, *sends = call(
            functools.partial(lift_kernel, n, m, cap),
            (size, *parts, basis, trial_s, trial_n, floor, top_high, top_low, pack),
            [shape(shared, loads), shape(rest, loads), shape(shared, loads)] + sent,
            flops=3 * full * shared,
            moved=4 * order * shared,
            name="lift",
        )
        for inner in range(1, INNER):
            last = outer == OUTER - 1 and inner == INNER - 1
            times = orders[outer][inner]
            recvs = swap_rows(sends, "wide", wide, times)
            base = call(
                base_kernel,
                (image, unpack_own, gap),
                [shape(shared, loads)],
                flops=4 * shared * shared * loads,
                moved=8 * shared * loads,
                name="base",
            )[0]
            ins = (size, high, low, mult_s, mult_n, gap, floor)
            shadow = (size, *recvs, base, unpack, mult_s, floor)
            cost = dict(flops=6 * shared * loads * unpack.shape[1], moved=2 * shared * unpack.shape[1])
            if last:
                outs = call(
                    rest_last_kernel,
                    ins,
                    [shape(order, loads)] * 2,
                    out_specs=[HBM] * 2,
                    scratch=[pltpu.VMEM((rest, loads), F32)] * 2 + [pltpu.SemaphoreType.DMA((2,))],
                    flops=3 * full * rest,
                    moved=4 * rest * order,
                    name="rest_last",
                )
                outs = call(
                    functools.partial(last_kernel, times),
                    (*shadow, *outs),
                    [shape(order, loads)] * 2,
                    in_specs=[SMEM] + [VMEM] * (len(shadow) - 1) + [HBM] * 2,
                    out_specs=[HBM] * 2,
                    scratch=[pltpu.VMEM((shared, loads), F32)] * 2 + [pltpu.SemaphoreType.DMA((2,))],
                    alias={len(shadow): 0, len(shadow) + 1: 1},
                    name="last",
                    **cost,
                )
                return tuple(out[None] for out in outs)
            mult_n, ahead = call(
                rest_kernel,
                (*ins, top_high, top_low, pack),
                [shape(rest, loads), shape(shared + padded, loads)],
                flops=3 * full * order,
                moved=4 * order * order,
                name="rest",
            )
            mult_s, image, *sends = call(
                functools.partial(sweep_kernel, times, cap),
                (*shadow, stack_high, stack_low, ahead),
                [shape(shared, loads)] * 2 + sent,
                name="sweep",
                **cost,
            )


def solution(mesh):
    wide = mesh.shape["wide"]
    narrow = mesh.shape["narrow"]

    def body(*args):
        return local(wide, narrow, *args)

    return jax.shard_map(
        body,
        mesh=mesh,
        in_specs=(
            P(("groups", "wide", "narrow"), None, None),
            P(("groups", "wide"), "narrow"),
            P(("groups", "wide", "narrow"), None, None),
            P(("groups", "wide", "narrow"), None, None),
            P(("groups", "wide", "narrow"), None, None),
            P(("groups", "wide", "narrow"), None, None),
            P(("groups", "wide", "narrow"), None),
            P(("groups", "wide", "narrow")),
            P(("groups", "wide", "narrow"), None),
        ),
        out_specs=(
            P(("groups", "wide", "narrow"), None, None),
            P(("groups", "wide", "narrow"), None, None),
        ),
        check_vma=False,
    )
```

```python
import functools

import jax
import jax.numpy as jnp
from jax import lax
from jax.experimental import pallas as pl
from jax.experimental.pallas import tpu as pltpu
from jax.sharding import PartitionSpec as P

OUTER = 2
INNER = 3
STEP = 0.3
F32 = jnp.float32
BF16 = jnp.bfloat16
PARAMS = pltpu.CompilerParams(vmem_limit_bytes=24 * 1024 * 1024)


def split(value):
    high = value.astype(BF16)
    return high, (value - high.astype(F32)).astype(BF16)


def mm(left, right):
    return jnp.dot(left, right, preferred_element_type=F32)


def product(left, right):
    (left_high, left_low), (right_high, right_low) = left, right
    width = right_high.shape[1]
    both = mm(left_high, jnp.concatenate([right_high, right_low], axis=1))
    return both[:, :width] + (both[:, width:] + mm(left_low, right_high))


def pick(chosen, value):
    width = value.shape[1]
    both = mm(chosen, jnp.concatenate(split(value), axis=1))
    return both[:, :width] + both[:, width:]


def live(size, start, rows, width):
    return lax.broadcasted_iota(jnp.int32, (rows, width), 0) + start < size


def call(body, ins, outs, in_specs=None, out_specs=None, scratch=(), grid=(), flops=0, moved=0, alias=None, name=None):
    if in_specs is None:
        in_specs = [SMEM if value.ndim == 1 else VMEM for value in ins]
    if out_specs is None:
        out_specs = [VMEM] * len(outs)
    return pl.pallas_call(
        body,
        out_shape=outs,
        grid=grid,
        in_specs=in_specs,
        out_specs=out_specs,
        scratch_shapes=list(scratch),
        compiler_params=PARAMS,
        cost_estimate=pl.CostEstimate(flops=flops, bytes_accessed=moved, transcendentals=0),
        input_output_aliases=alias or {},
        name=name,
    )(*ins)


def whole(shape):
    return pl.BlockSpec(shape, lambda *i: (0,) * len(shape))


def block(shape, at=0, across=False):
    if across:
        return pl.BlockSpec(shape, lambda i: (0, i + at))
    return pl.BlockSpec(shape, lambda i: (i + at, 0))


SMEM = pl.BlockSpec(memory_space=pltpu.SMEM)
HBM = pl.BlockSpec(memory_space=pltpu.HBM)
VMEM = pl.BlockSpec(memory_space=pltpu.VMEM)


def shape(rows, columns, dtype=F32):
    return jax.ShapeDtypeStruct((rows, columns), dtype)


def first_kernel(n, cap, peers_at, rows_at, operator_at, mult_at, *refs):
    unpack_own, unpack_all, unpack, high, low, image = refs[:6]
    message, peers, rows, operator, mult, done = refs[6:]
    shared, width = image.shape
    copies = [
        pltpu.make_async_copy(source, target, done.at[i])
        for i, (source, target) in enumerate(
            ((peers_at, peers), (rows_at, rows), (mult_at, mult), (operator_at.at[pl.ds(0, shared)], operator))
        )
    ]
    for copy in copies:
        copy.start()
    copies[0].wait()
    copies[1].wait()
    across = jnp.broadcast_to(peers[...], (shared, shared))
    down = across.T
    first = lax.broadcasted_iota(jnp.int32, (shared, shared), 0)
    second = lax.broadcasted_iota(jnp.int32, (shared, shared), 1)
    slot = jnp.sum(
        jnp.where((across == down) & (second < first), 1.0, 0.0), axis=1, keepdims=True
    ).astype(jnp.int32)
    wanted = jnp.broadcast_to(rows[...], (shared, shared)).T[:, :1]
    far = down[:, :1] ^ lax.axis_index("wide")

    def marks(key, columns):
        hit = key == lax.broadcasted_iota(jnp.int32, (shared, columns), 1)
        return jnp.where(hit, 1.0, 0.0).astype(BF16)

    unpack_own[...] = marks(jnp.where(far == 0, wanted, -1), shared)
    unpack_all[...] = marks(jnp.where(far == 0, -1, (far - 1) * shared + wanted), unpack_all.shape[1])
    unpack[...] = marks(jnp.where(far == 0, -1, (far - 1) * cap + slot), unpack.shape[1])
    lane = lax.broadcasted_iota(jnp.int32, (shared, width), 1)
    message[shared:, :] = jnp.zeros((message.shape[0] - shared, width), F32)
    chunks = -(-cap // width)
    for k in range(n * chunks):
        d, c = k // chunks + 1, k % chunks
        hit = (far == d) & (slot == lane + c * width)
        message[shared + k:shared + k + 1, :] = jnp.sum(
            jnp.where(hit, wanted.astype(F32), 0.0), axis=0, keepdims=True
        )
    copies[2].wait()
    copies[3].wait()
    parts = split(operator[...])
    high[...], low[...] = parts
    value = product(parts, split(mult[...]))
    image[...] = value
    message[:shared, :] = value


def pack_kernel(times, relayed, cap, *refs):
    n = len(times)
    recvs, refs = refs[:n + relayed], refs[n + relayed:]
    recvs, (high, low, pack, stack_high, stack_low) = merged(recvs, relayed), refs
    shared = pack.shape[1]
    width = recvs[0].shape[1]
    column = lax.broadcasted_iota(jnp.int32, (width, shared), 1).astype(F32)
    if n * cap < pack.shape[0]:
        pack[n * cap:, :] = jnp.zeros((pack.shape[0] - n * cap, shared), BF16)
    for d, recv in zip(times, recvs):
        for c in range(-(-cap // width)):
            k = shared + (d - 1) * -(-cap // width) + c
            wanted = jnp.broadcast_to(recv[k:k + 1, :], (shared, width)).T
            chosen = jnp.where(wanted == column, 1.0, 0.0).astype(BF16)
            size = min(width, cap - c * width)
            at = (d - 1) * cap + c * width
            pack[at:at + size, :] = chosen[:size]
    for source, stack in ((high, stack_high), (low, stack_low)):
        square = source[:, :shared]
        stack[:shared, :] = square
        stack[shared:, :] = mm(pack[...], square).astype(BF16)


def prepare_kernel(contact, modes, tile, floor, basis, tile_high, tile_low):
    order, width = floor.shape
    for at in range(0, order, width):
        flag = jnp.broadcast_to(contact[:, at:at + width], (width, width)).T
        floor[at:at + width, :] = jnp.where(flag == 1, 0.0, -jnp.inf)
    high, low = [part.astype(F32) for part in split(modes[...])]
    basis[...] = jnp.concatenate([high, high, low], axis=0).T.astype(BF16)
    tile_high[...], tile_low[...] = split(tile[...])


def send(cap, chosen, image, sends):
    picked = pick(chosen, image)
    for d, out in enumerate(sends):
        out[...] = picked[d * cap:(d + 1) * cap]


def merged(recvs, relayed):
    blocks = [recv[...] for recv in recvs]
    if relayed:
        place = lax.axis_index("wide")
        outer = (place == 0) | (place == lax.axis_size("wide") - 1)
        blocks[-2:] = [jnp.where(outer, blocks[-1], blocks[-2])]
    return blocks


def arrived(times, recvs, shared, unpack):
    blocks = [recvs[times.index(d)][:shared] for d in sorted(times)]
    rows = sum(b.shape[0] for b in blocks)
    if rows < unpack.shape[1]:
        blocks.append(jnp.zeros((unpack.shape[1] - rows, blocks[0].shape[1]), F32))
    return pick(unpack[...], jnp.concatenate(blocks, axis=0))


def base_of(image, unpack_own, gap):
    own = image[...]
    return gap[:own.shape[0], :] - own + pick(unpack_own[...], own)


def settle(trial, floor, alive):
    return jnp.where(alive, jnp.maximum(trial, floor), 0.0)


def shared_residual(times, recvs, base, unpack, size):
    known = base[...]
    alive = live(size[0], 0, *known.shape)
    return jnp.where(alive, known + arrived(times, recvs, known.shape[0], unpack), 0.0), alive


def rest_start_kernel(
    size, operator, mult, mult_block, gap, modes, image, unpack_own, top_gap, trial, coarse, high, low, base, halves
):
    step = pl.program_id(0)
    rows, width = gap.shape

    @pl.when(step == 0)
    def _():
        halves[:, :width], halves[:, width:] = split(mult[...])
        coarse[...] = jnp.zeros_like(coarse)
        base[...] = base_of(image, unpack_own, top_gap)

    parts = split(operator[...])
    high[...], low[...] = parts
    both = mm(parts[0], halves[...])
    image = both[:, :width] + (both[:, width:] + mm(parts[1], halves[:, :width]))
    alive = live(size[0], (step + 1) * rows, rows, width)
    residual = jnp.where(alive, gap[...] - image, 0.0)
    trial[...] = mult_block[...] + STEP * residual
    coarse[...] += product(split(modes[...]), split(residual))


def rest_residual(size, high, low, mult_s, mult_n, gap):
    shared, (rows, width) = mult_s.shape[0], mult_n.shape
    mult = jnp.concatenate([mult_s[...], mult_n[...]], axis=0)
    image = product((high[...], low[...]), split(mult))
    alive = live(size[0], shared, rows, width)
    return jnp.where(alive, gap[shared:, :] - image, 0.0), alive


def rest_first_kernel(size, high, low, mult_s, mult_n, gap, image, unpack_own, modes, trial, coarse, base):
    residual, _ = rest_residual(size, high, low, mult_s, mult_n, gap)
    base[...] = base_of(image, unpack_own, gap)
    trial[...] = mult_n[...] + STEP * residual
    coarse[...] = product(split(modes[:, mult_s.shape[0]:]), split(residual))


def rest_kernel(
    size, high, low, mult_s, mult_n, gap, image, unpack_own, floor, top_high, top_low, pack, mult_out, ahead, base
):
    shared = mult_s.shape[0]
    base[...] = base_of(image, unpack_own, gap)
    residual, alive = rest_residual(size, high, low, mult_s, mult_n, gap)
    mult = settle(mult_n[...] + STEP * residual, floor[shared:, :], alive)
    mult_out[...] = mult
    value = product((top_high[:, shared:], top_low[:, shared:]), split(mult))
    ahead[:shared, :] = value
    ahead[shared:, :] = pick(pack[...], value)


def rest_last_kernel(
    size, high, low, mult_s, mult_n, gap, image, unpack_own, floor, mult_out, residual_out, base, settled, left, done
):
    shared, rows = mult_s.shape[0], mult_n.shape[0]
    residual, alive = rest_residual(size, high, low, mult_s, mult_n, gap)
    left[...] = residual
    base[...] = base_of(image, unpack_own, gap)
    settled[...] = settle(mult_n[...] + STEP * residual, floor[shared:, :], alive)
    copies = [
        pltpu.make_async_copy(source, target.at[pl.ds(shared, rows)], done.at[i])
        for i, (source, target) in enumerate(((left, residual_out), (settled, mult_out)))
    ]
    for copy in copies:
        copy.start()
    for copy in copies:
        copy.wait()


def coarse_kernel(times, relayed, size, *refs):
    n = len(times) + relayed
    recvs = merged(refs[:n], relayed)
    base, unpack, mult, modes, started, trial = refs[n:n + 6]
    shared = base.shape[0]
    residual, _ = shared_residual(times, recvs, base, unpack, size)
    coarse = started[...] + product(split(modes[:, :shared]), split(residual))
    for out in refs[n + 6:]:
        out[...] = coarse
    trial[...] = mult[:shared, :] + STEP * residual


def tile_kernel(wide_order, narrow_order, high, low, *refs):
    n, m = len(wide_order), len(narrow_order)
    blocks, outs, (gathered, parts) = refs[:n + 1], refs[n + 1:n + m + 2], refs[n + m + 2:]
    count = blocks[0].shape[0]
    for d, ref in zip((0, *wide_order), blocks):
        at = pl.multiple_of((lax.axis_index("wide") ^ d) * count, count)
        gathered[pl.ds(at, count), :] = ref[...]
    parts[...] = product((high[...], low[...]), split(gathered[...]))
    for d, out in zip((0, *narrow_order), outs):
        at = pl.multiple_of((lax.axis_index("narrow") ^ d) * count, count)
        out[...] = parts[pl.ds(at, count), :]


def lift_kernel(n, m, cap, size, *refs):
    parts = refs[:m + 1]
    ins, (mult_s, mult_n, image), sends = refs[m + 1:m + 8], refs[m + 8:m + 11], refs[m + 11:]
    basis, trial_s, trial_n, floor, high, low, pack = ins
    solved = parts[0][...]
    for part in parts[1:]:
        solved = solved + part[...]
    shared, width = trial_s.shape
    order = floor.shape[0]
    high_part, low_part = split(solved)
    lifted = mm(basis[...], jnp.concatenate([high_part, low_part, high_part], axis=0))
    alive = live(size[0], 0, order, width)
    first = settle(trial_s[...] + lifted[:shared], floor[:shared], alive[:shared])
    rest = settle(trial_n[...] + lifted[shared:], floor[shared:], alive[shared:])
    mult_s[...] = first
    mult_n[...] = rest
    value = product((high[...], low[...]), split(jnp.concatenate([first, rest], axis=0)))
    image[...] = value
    send(cap, pack[...], value, sends)


def sweep_kernel(times, cap, size, *refs):
    n = len(times)
    recvs = merged(refs[:n], False)
    base, unpack, mult, floor, high, low, ahead, mult_out, image_out = refs[n:n + 9]
    shared = base.shape[0]
    residual, alive = shared_residual(times, recvs, base, unpack, size)
    value = settle(mult[...] + STEP * residual, floor[:shared, :], alive)
    mult_out[...] = value
    both = ahead[...] + product((high[...], low[...]), split(value))
    image_out[...] = both[:shared]
    for d, out in enumerate(refs[n + 9:]):
        out[...] = both[shared + d * cap:shared + (d + 1) * cap]


def last_kernel(times, size, *refs):
    n = len(times)
    recvs = merged(refs[:n], False)
    base, unpack, mult, floor, _, _, mult_out, residual_out, settled, left, done = refs[n:]
    shared = base.shape[0]
    residual, alive = shared_residual(times, recvs, base, unpack, size)
    left[...] = residual
    first = pltpu.make_async_copy(left, residual_out.at[pl.ds(0, shared)], done.at[0])
    first.start()
    settled[...] = settle(mult[...] + STEP * residual, floor[:shared, :], alive)
    second = pltpu.make_async_copy(settled, mult_out.at[pl.ds(0, shared)], done.at[1])
    second.start()
    first.wait()
    second.wait()


def swap(block, axis, count, d):
    return lax.ppermute(block, axis, [(i, i ^ d) for i in range(count)])


def swap_all(blocks, axis, count, order):
    return [swap(block, axis, count, d) for block, d in zip(blocks, order)]


def swap_rows(blocks, axis, count, times):
    return [swap(blocks[d - 1], axis, count, d) for d in times]


def swap_all_rows(block, axis):
    crossed = swap(block, axis, 4, 3)
    return [
        crossed,
        swap(block, axis, 4, 1),
        lax.ppermute(block, axis, [(0, 2), (3, 1)]),
        lax.ppermute(crossed, axis, [(2, 3), (1, 0)]),
    ]


def half_first(count, back):
    half = count // 2
    others = [d for d in range(1, count) if d != half]
    return (half, *(others[::-1] if back else others))


def middle_first(count):
    return (count - 1, *range(1, count - 1))


def far_first(count):
    return tuple(range(count - 1, 0, -1))


def local(
    wide,
    narrow,
    operators,
    coarse_inverse,
    modes,
    gap,
    start_mult,
    peer_list,
    partner_row,
    interface_size,
    contact_rows,
):
    operator = operators[0]
    modes = modes[0]
    gap = gap[0]
    mult = start_mult[0]
    order, loads = mult.shape
    shared = partner_row.shape[1]
    count = modes.shape[0]
    rest = order - shared
    steps = rest // shared
    n, m = wide - 1, narrow - 1
    cap = 2 * shared // wide
    listed = n * cap
    padded = -(-listed // 128) * 128
    size = interface_size
    coarse_order, part_order = half_first(wide, True), far_first(narrow)
    half, half_back, middle = half_first(wide, False), half_first(wide, True), middle_first(wide)
    orders = ((middle, half, half_back), (half_back, half, half_back))
    sent = [shape(cap, loads)] * n
    full = 2 * order * loads

    list_rows = -(-n * -(-cap // loads) // 8) * 8
    unpack_own, unpack_all, unpack, top_high, top_low, image, message = call(
        functools.partial(first_kernel, n, cap),
        tuple(
            pltpu.with_memory_space_constraint(value, pltpu.HBM)
            for value in (peer_list[0].reshape(1, shared), partner_row, operator, mult)
        ),
        [shape(shared, shared, BF16), shape(shared, n * shared, BF16), shape(shared, padded, BF16)]
        + [shape(shared, order, BF16)] * 2
        + [shape(shared, loads)]
        + [shape(shared + list_rows, loads)],
        in_specs=[HBM] * 4,
        scratch=[
            pltpu.VMEM((1, shared), jnp.int32),
            pltpu.VMEM((1, shared), jnp.int32),
            pltpu.VMEM((shared, order), F32),
            pltpu.VMEM((order, loads), F32),
            pltpu.SemaphoreType.DMA((4,)),
        ],
        flops=3 * full * shared,
        moved=8 * shared * order,
        name="first",
    )
    floor, basis, tile_high, tile_low = call(
        prepare_kernel,
        (contact_rows, modes, coarse_inverse),
        [shape(order, loads)] + [shape(order, 3 * count, BF16)] + [shape(*coarse_inverse.shape, BF16)] * 2,
        flops=full * count,
        moved=8 * coarse_inverse.size + 4 * full,
        name="prepare",
    )
    mult_s = mult
    scratch = [pltpu.VMEM((order, 2 * loads), BF16)]
    for outer in range(OUTER):
        times = orders[outer][0]
        relayed = outer == 0 and wide == 4
        if relayed:
            recvs = swap_all_rows(message, "wide")
        else:
            recvs = swap_rows([message] * n if outer == 0 else sends, "wide", wide, times)
        if outer == 0:
            row_block, load_block = block((shared, order)), block((shared, loads))
            next_loads = block((shared, loads), 1)
            trial_n, started, high, low, base = call(
                rest_start_kernel,
                (size, operator, mult, mult, gap, modes, image, unpack_own, gap),
                [shape(rest, loads), shape(count, loads)] + [shape(rest, order, BF16)] * 2 + [shape(shared, loads)],
                [
                    SMEM,
                    block((shared, order), 1),
                    whole((order, loads)),
                    next_loads,
                    next_loads,
                    block((count, shared), 1, across=True),
                    whole((shared, loads)),
                    whole((shared, shared)),
                    whole((shared, loads)),
                ],
                [load_block, whole((count, loads)), row_block, row_block, whole((shared, loads))],
                scratch=scratch,
                grid=(steps,),
                flops=3 * full * rest,
                moved=8 * rest * order,
                name="rest_start",
            )
            marks = unpack_all
            pack, stack_high, stack_low = call(
                functools.partial(pack_kernel, times, relayed, cap),
                (*recvs, top_high, top_low),
                [shape(padded, shared, BF16)] + [shape(shared + padded, shared, BF16)] * 2,
                flops=8 * padded * shared * shared,
                moved=8 * padded * shared,
                name="pack",
            )
        else:
            trial_n, started, base = call(
                rest_first_kernel,
                (size, high, low, mult_s, mult_n, gap, image, unpack_own, modes),
                [shape(rest, loads), shape(count, loads), shape(shared, loads)],
                flops=3 * full * rest,
                moved=4 * rest * order,
                name="rest_first",
            )
            marks = unpack
        trial_s, own, *coarse = call(
            functools.partial(coarse_kernel, times, relayed),
            (size, *recvs, base, marks, mult_s, modes, started),
            [shape(shared, loads)] + [shape(count, loads)] * wide,
            flops=6 * shared * loads * unpack.shape[1],
            moved=2 * shared * unpack.shape[1],
            name="coarse",
        )
        blocks = [own] + swap_all(coarse, "wide", wide, coarse_order)
        own, *parts = call(
            functools.partial(tile_kernel, coarse_order, part_order),
            (tile_high, tile_low, *blocks),
            [shape(count, loads)] * narrow,
            scratch=[
                pltpu.VMEM((wide * count, loads), F32),
                pltpu.VMEM((narrow * count, loads), F32),
            ],
            flops=6 * coarse_inverse.size * loads,
            moved=4 * coarse_inverse.size,
            name="tile",
        )
        parts = [own] + swap_all(parts, "narrow", narrow, part_order)
        mult_s, mult_n, image, *sends = call(
            functools.partial(lift_kernel, n, m, cap),
            (size, *parts, basis, trial_s, trial_n, floor, top_high, top_low, pack),
            [shape(shared, loads), shape(rest, loads), shape(shared, loads)] + sent,
            flops=3 * full * shared,
            moved=4 * order * shared,
            name="lift",
        )
        for inner in range(1, INNER):
            last = outer == OUTER - 1 and inner == INNER - 1
            times = orders[outer][inner]
            recvs = swap_rows(sends, "wide", wide, times)
            ins = (size, high, low, mult_s, mult_n, gap, image, unpack_own, floor)
            cost = dict(flops=6 * shared * loads * unpack.shape[1], moved=2 * shared * unpack.shape[1])
            if last:
                *outs, base = call(
                    rest_last_kernel,
                    ins,
                    [shape(order, loads)] * 2 + [shape(shared, loads)],
                    out_specs=[HBM] * 2 + [VMEM],
                    scratch=[pltpu.VMEM((rest, loads), F32)] * 2 + [pltpu.SemaphoreType.DMA((2,))],
                    flops=3 * full * rest,
                    moved=4 * rest * order,
                    name="rest_last",
                )
                shadow = (size, *recvs, base, unpack, mult_s, floor)
                outs = call(
                    functools.partial(last_kernel, times),
                    (*shadow, *outs),
                    [shape(order, loads)] * 2,
                    in_specs=[SMEM] + [VMEM] * (len(shadow) - 1) + [HBM] * 2,
                    out_specs=[HBM] * 2,
                    scratch=[pltpu.VMEM((shared, loads), F32)] * 2 + [pltpu.SemaphoreType.DMA((2,))],
                    alias={len(shadow): 0, len(shadow) + 1: 1},
                    name="last",
                    **cost,
                )
                return tuple(out[None] for out in outs)
            next_n, ahead, base = call(
                rest_kernel,
                (*ins, top_high, top_low, pack),
                [shape(rest, loads), shape(shared + padded, loads), shape(shared, loads)],
                flops=3 * full * order,
                moved=4 * order * order,
                name="rest",
            )
            mult_n = next_n
            shadow = (size, *recvs, base, unpack, mult_s, floor)
            mult_s, image, *sends = call(
                functools.partial(sweep_kernel, times, cap),
                (*shadow, stack_high, stack_low, ahead),
                [shape(shared, loads)] * 2 + sent,
                name="sweep",
                **cost,
            )


def solution(mesh):
    wide = mesh.shape["wide"]
    narrow = mesh.shape["narrow"]

    def body(*args):
        return local(wide, narrow, *args)

    return jax.shard_map(
        body,
        mesh=mesh,
        in_specs=(
            P(("groups", "wide", "narrow"), None, None),
            P(("groups", "wide"), "narrow"),
            P(("groups", "wide", "narrow"), None, None),
            P(("groups", "wide", "narrow"), None, None),
            P(("groups", "wide", "narrow"), None, None),
            P(("groups", "wide", "narrow"), None, None),
            P(("groups", "wide", "narrow"), None),
            P(("groups", "wide", "narrow")),
            P(("groups", "wide", "narrow"), None),
        ),
        out_specs=(
            P(("groups", "wide", "narrow"), None, None),
            P(("groups", "wide", "narrow"), None, None),
        ),
        check_vma=False,
    )
```

```python
import functools

import jax
import jax.numpy as jnp
from jax import lax
from jax.experimental import pallas as pl
from jax.experimental.pallas import tpu as pltpu
from jax.sharding import PartitionSpec as P

OUTER = 2
INNER = 3
STEP = 0.3
F32 = jnp.float32
BF16 = jnp.bfloat16
PARAMS = pltpu.CompilerParams(vmem_limit_bytes=24 * 1024 * 1024)


def split(value):
    high = value.astype(BF16)
    return high, (value - high.astype(F32)).astype(BF16)


def mm(left, right):
    return jnp.dot(left, right, preferred_element_type=F32)


def product(left, right):
    (left_high, left_low), (right_high, right_low) = left, right
    width = right_high.shape[1]
    both = mm(left_high, jnp.concatenate([right_high, right_low], axis=1))
    return both[:, :width] + (both[:, width:] + mm(left_low, right_high))


def pick(chosen, value):
    width = value.shape[1]
    both = mm(chosen, jnp.concatenate(split(value), axis=1))
    return both[:, :width] + both[:, width:]


def live(size, start, rows, width):
    return lax.broadcasted_iota(jnp.int32, (rows, width), 0) + start < size


def call(body, ins, outs, in_specs=None, out_specs=None, scratch=(), grid=(), flops=0, moved=0, alias=None, name=None):
    if in_specs is None:
        in_specs = [SMEM if value.ndim == 1 else VMEM for value in ins]
    if out_specs is None:
        out_specs = [VMEM] * len(outs)
    return pl.pallas_call(
        body,
        out_shape=outs,
        grid=grid,
        in_specs=in_specs,
        out_specs=out_specs,
        scratch_shapes=list(scratch),
        compiler_params=PARAMS,
        cost_estimate=pl.CostEstimate(flops=flops, bytes_accessed=moved, transcendentals=0),
        input_output_aliases=alias or {},
        name=name,
    )(*ins)


def whole(shape):
    return pl.BlockSpec(shape, lambda *i: (0,) * len(shape))


def block(shape, at=0, across=False):
    if across:
        return pl.BlockSpec(shape, lambda i: (0, i + at))
    return pl.BlockSpec(shape, lambda i: (i + at, 0))


SMEM = pl.BlockSpec(memory_space=pltpu.SMEM)
HBM = pl.BlockSpec(memory_space=pltpu.HBM)
VMEM = pl.BlockSpec(memory_space=pltpu.VMEM)


def shape(rows, columns, dtype=F32):
    return jax.ShapeDtypeStruct((rows, columns), dtype)


def first_kernel(n, cap, peers_at, rows_at, operator_at, mult_at, *refs):
    unpack_own, unpack_all, unpack, high, low, image = refs[:6]
    sends, (peers, rows, operator, mult, done) = refs[6:6 + n], refs[6 + n:]
    shared, width = image.shape
    pieces = [(peers_at, peers), (rows_at, rows)]
    for source, target, count in ((mult_at, mult, 2), (operator_at, operator, 4)):
        step = target.shape[0] // count
        pieces += [(source.at[pl.ds(k * step, step)], target.at[pl.ds(k * step, step)]) for k in range(count)]
    copies = [pltpu.make_async_copy(source, target, done.at[i]) for i, (source, target) in enumerate(pieces)]
    for copy in copies:
        copy.start()
    copies[0].wait()
    copies[1].wait()
    across = jnp.broadcast_to(peers[...], (shared, shared))
    down = across.T
    first = lax.broadcasted_iota(jnp.int32, (shared, shared), 0)
    second = lax.broadcasted_iota(jnp.int32, (shared, shared), 1)
    slot = jnp.sum(
        jnp.where((across == down) & (second < first), 1.0, 0.0), axis=1, keepdims=True
    ).astype(jnp.int32)
    wanted = jnp.broadcast_to(rows[...], (shared, shared)).T[:, :1]
    far = down[:, :1] ^ lax.axis_index("wide")

    def marks(key, columns):
        hit = key == lax.broadcasted_iota(jnp.int32, (shared, columns), 1)
        return jnp.where(hit, 1.0, 0.0).astype(BF16)

    unpack_own[...] = marks(jnp.where(far == 0, wanted, -1), shared)
    unpack_all[...] = marks(jnp.where(far == 0, -1, (far - 1) * shared + wanted), unpack_all.shape[1])
    unpack[...] = marks(jnp.where(far == 0, -1, (far - 1) * cap + slot), unpack.shape[1])
    lane = lax.broadcasted_iota(jnp.int32, (shared, width), 1)
    for d, out in enumerate(sends, 1):
        out[shared:, :] = jnp.zeros((out.shape[0] - shared, width), F32)
        for c in range(-(-cap // width)):
            hit = (far == d) & (slot == lane + c * width)
            out[shared + c:shared + c + 1, :] = jnp.sum(
                jnp.where(hit, wanted.astype(F32), 0.0), axis=0, keepdims=True
            )
    for copy in copies[2:]:
        copy.wait()
    parts = split(operator[...])
    high[...], low[...] = parts
    value = product(parts, split(mult[...]))
    image[...] = value
    for out in sends:
        out[:shared, :] = value


def pack_kernel(times, cap, *refs):
    n = len(times)
    recvs, (high, low, pack, stack_high, stack_low) = refs[:n], refs[n:]
    shared = pack.shape[1]
    width = recvs[0].shape[1]
    column = lax.broadcasted_iota(jnp.int32, (width, shared), 1).astype(F32)
    if n * cap < pack.shape[0]:
        pack[n * cap:, :] = jnp.zeros((pack.shape[0] - n * cap, shared), BF16)
    for d, recv in zip(times, recvs):
        for c in range(-(-cap // width)):
            wanted = jnp.broadcast_to(recv[shared + c:shared + c + 1, :], (shared, width)).T
            chosen = jnp.where(wanted == column, 1.0, 0.0).astype(BF16)
            size = min(width, cap - c * width)
            at = (d - 1) * cap + c * width
            pack[at:at + size, :] = chosen[:size]
    for source, stack in ((high, stack_high), (low, stack_low)):
        square = source[:, :shared]
        stack[:shared, :] = square
        stack[shared:, :] = mm(pack[...], square).astype(BF16)


def prepare_kernel(contact, modes, tile, floor, basis, tile_high, tile_low):
    order, width = floor.shape
    for at in range(0, order, width):
        flag = jnp.broadcast_to(contact[:, at:at + width], (width, width)).T
        floor[at:at + width, :] = jnp.where(flag == 1, 0.0, -jnp.inf)
    high, low = [part.astype(F32) for part in split(modes[...])]
    basis[...] = jnp.concatenate([high, high, low], axis=0).T.astype(BF16)
    tile_high[...], tile_low[...] = split(tile[...])


def send(cap, chosen, image, sends):
    picked = pick(chosen, image)
    for d, out in enumerate(sends):
        out[...] = picked[d * cap:(d + 1) * cap]


def arrived(times, recvs, shared, unpack):
    blocks = [recvs[times.index(d)][...][:shared] for d in sorted(times)]
    rows = sum(b.shape[0] for b in blocks)
    if rows < unpack.shape[1]:
        blocks.append(jnp.zeros((unpack.shape[1] - rows, blocks[0].shape[1]), F32))
    return pick(unpack[...], jnp.concatenate(blocks, axis=0))


def base_kernel(image, unpack_own, gap, base):
    own = image[...]
    base[...] = gap[:own.shape[0], :] - own + pick(unpack_own[...], own)


def settle(trial, floor, alive):
    return jnp.where(alive, jnp.maximum(trial, floor), 0.0)


def shared_residual(times, recvs, base, unpack, size):
    known = base[...]
    alive = live(size[0], 0, *known.shape)
    return jnp.where(alive, known + arrived(times, recvs, known.shape[0], unpack), 0.0), alive


def rest_start_kernel(size, operator, mult, mult_block, gap, modes, trial, coarse, high, low, halves):
    step = pl.program_id(0)
    rows, width = gap.shape

    @pl.when(step == 0)
    def _():
        halves[:, :width], halves[:, width:] = split(mult[...])
        coarse[...] = jnp.zeros_like(coarse)

    parts = split(operator[...])
    high[...], low[...] = parts
    both = mm(parts[0], halves[...])
    image = both[:, :width] + (both[:, width:] + mm(parts[1], halves[:, :width]))
    alive = live(size[0], (step + 1) * rows, rows, width)
    residual = jnp.where(alive, gap[...] - image, 0.0)
    trial[...] = mult_block[...] + STEP * residual
    coarse[...] += product(split(modes[...]), split(residual))


def rest_residual(size, high, low, mult_s, mult_n, gap):
    shared, (rows, width) = mult_s.shape[0], mult_n.shape
    mult = jnp.concatenate([mult_s[...], mult_n[...]], axis=0)
    image = product((high[...], low[...]), split(mult))
    alive = live(size[0], shared, rows, width)
    return jnp.where(alive, gap[shared:, :] - image, 0.0), alive


def rest_first_kernel(size, high, low, mult_s, mult_n, gap, modes, trial, coarse):
    residual, _ = rest_residual(size, high, low, mult_s, mult_n, gap)
    trial[...] = mult_n[...] + STEP * residual
    coarse[...] = product(split(modes[:, mult_s.shape[0]:]), split(residual))


def rest_kernel(size, high, low, mult_s, mult_n, gap, floor, top_high, top_low, pack, mult_out, ahead):
    shared = mult_s.shape[0]
    residual, alive = rest_residual(size, high, low, mult_s, mult_n, gap)
    mult = settle(mult_n[...] + STEP * residual, floor[shared:, :], alive)
    mult_out[...] = mult
    value = product((top_high[:, shared:], top_low[:, shared:]), split(mult))
    ahead[:shared, :] = value
    ahead[shared:, :] = pick(pack[...], value)


def rest_last_kernel(size, high, low, mult_s, mult_n, gap, floor, mult_out, residual_out, settled, left, done):
    shared, rows = mult_s.shape[0], mult_n.shape[0]
    residual, alive = rest_residual(size, high, low, mult_s, mult_n, gap)
    left[...] = residual
    settled[...] = settle(mult_n[...] + STEP * residual, floor[shared:, :], alive)
    copies = [
        pltpu.make_async_copy(source, target.at[pl.ds(shared, rows)], done.at[i])
        for i, (source, target) in enumerate(((left, residual_out), (settled, mult_out)))
    ]
    for copy in copies:
        copy.start()
    for copy in copies:
        copy.wait()


def coarse_kernel(times, size, *refs):
    n = len(times)
    recvs = refs[:n]
    base, unpack, mult, modes, started, trial = refs[n:n + 6]
    shared = base.shape[0]
    residual, _ = shared_residual(times, recvs, base, unpack, size)
    coarse = started[...] + product(split(modes[:, :shared]), split(residual))
    for out in refs[n + 6:]:
        out[...] = coarse
    trial[...] = mult[:shared, :] + STEP * residual


def tile_kernel(wide_order, narrow_order, high, low, *refs):
    n, m = len(wide_order), len(narrow_order)
    blocks, outs, (gathered, parts) = refs[:n + 1], refs[n + 1:n + m + 2], refs[n + m + 2:]
    count = blocks[0].shape[0]
    for d, ref in zip((0, *wide_order), blocks):
        at = pl.multiple_of((lax.axis_index("wide") ^ d) * count, count)
        gathered[pl.ds(at, count), :] = ref[...]
    parts[...] = product((high[...], low[...]), split(gathered[...]))
    for d, out in zip((0, *narrow_order), outs):
        at = pl.multiple_of((lax.axis_index("narrow") ^ d) * count, count)
        out[...] = parts[pl.ds(at, count), :]


def lift_kernel(n, m, cap, size, *refs):
    parts = refs[:m + 1]
    ins, (mult_s, mult_n, image), sends, halves = refs[m + 1:m + 8], refs[m + 8:m + 11], refs[m + 11:-1], refs[-1]
    basis, trial_s, trial_n, floor, high, low, pack = ins
    solved = parts[0][...]
    for part in parts[1:]:
        solved = solved + part[...]
    shared, width = trial_s.shape
    order = floor.shape[0]
    high_part, low_part = split(solved)
    solved = jnp.concatenate([high_part, low_part, high_part], axis=0)
    shared, width = trial_s.shape
    for at in range(0, floor.shape[0], shared):
        rows = slice(at, at + shared)
        trial = trial_s[...] if at == 0 else trial_n[at - shared:at, :]
        alive = live(size[0], at, shared, width)
        mult = settle(trial + mm(basis[rows, :], solved), floor[rows, :], alive)
        if at == 0:
            mult_s[...] = mult
        else:
            mult_n[at - shared:at, :] = mult
        halves[rows, :width], halves[rows, width:] = split(mult)
    both = mm(high[...], halves[...])
    value = both[:, :width] + (both[:, width:] + mm(low[...], halves[:, :width]))
    image[...] = value
    send(cap, pack[...], value, sends)


def sweep_kernel(times, cap, size, *refs):
    n = len(times)
    recvs = refs[:n]
    base, unpack, mult, floor, high, low, ahead, mult_out, image_out = refs[n:n + 9]
    shared = base.shape[0]
    residual, alive = shared_residual(times, recvs, base, unpack, size)
    value = settle(mult[...] + STEP * residual, floor[:shared, :], alive)
    mult_out[...] = value
    both = ahead[...] + product((high[...], low[...]), split(value))
    image_out[...] = both[:shared]
    for d, out in enumerate(refs[n + 9:]):
        out[...] = both[shared + d * cap:shared + (d + 1) * cap]


def last_kernel(times, size, *refs):
    n = len(times)
    recvs = refs[:n]
    base, unpack, mult, floor, _, _, mult_out, residual_out, settled, left, done = refs[n:]
    shared = base.shape[0]
    residual, alive = shared_residual(times, recvs, base, unpack, size)
    left[...] = residual
    first = pltpu.make_async_copy(left, residual_out.at[pl.ds(0, shared)], done.at[0])
    first.start()
    settled[...] = settle(mult[...] + STEP * residual, floor[:shared, :], alive)
    second = pltpu.make_async_copy(settled, mult_out.at[pl.ds(0, shared)], done.at[1])
    second.start()
    first.wait()
    second.wait()


def swap(block, axis, count, d):
    return lax.ppermute(block, axis, [(i, i ^ d) for i in range(count)])


def swap_all(blocks, axis, count, order):
    return [swap(block, axis, count, d) for block, d in zip(blocks, order)]


def swap_rows(blocks, axis, count, times):
    return [swap(blocks[d - 1], axis, count, d) for d in times]


def half_first(count, back):
    half = count // 2
    others = [d for d in range(1, count) if d != half]
    return (half, *(others[::-1] if back else others))


def middle_first(count):
    return (count - 1, *range(1, count - 1))


def far_first(count):
    return tuple(range(count - 1, 0, -1))


def local(
    wide,
    narrow,
    operators,
    coarse_inverse,
    modes,
    gap,
    start_mult,
    peer_list,
    partner_row,
    interface_size,
    contact_rows,
):
    operator = operators[0]
    modes = modes[0]
    gap = gap[0]
    mult = start_mult[0]
    order, loads = mult.shape
    shared = partner_row.shape[1]
    count = modes.shape[0]
    rest = order - shared
    steps = rest // shared
    n, m = wide - 1, narrow - 1
    cap = 2 * shared // wide
    listed = n * cap
    padded = -(-listed // 128) * 128
    size = interface_size
    coarse_order, part_order = half_first(wide, True), far_first(narrow)
    half, half_back, middle = half_first(wide, False), half_first(wide, True), middle_first(wide)
    orders = ((middle, half, half_back), (half_back, half, half_back))
    sent = [shape(cap, loads)] * n
    full = 2 * order * loads

    list_rows = -(-(-(-cap // loads)) // 8) * 8
    unpack_own, unpack_all, unpack, top_high, top_low, image, *sends = call(
        functools.partial(first_kernel, n, cap),
        tuple(
            pltpu.with_memory_space_constraint(value, pltpu.HBM)
            for value in (peer_list[0].reshape(1, shared), partner_row, operator, mult)
        ),
        [shape(shared, shared, BF16), shape(shared, n * shared, BF16), shape(shared, padded, BF16)]
        + [shape(shared, order, BF16)] * 2
        + [shape(shared, loads)]
        + [shape(shared + list_rows, loads)] * n,
        in_specs=[HBM] * 4,
        scratch=[
            pltpu.VMEM((1, shared), jnp.int32),
            pltpu.VMEM((1, shared), jnp.int32),
            pltpu.VMEM((shared, order), F32),
            pltpu.VMEM((order, loads), F32),
            pltpu.SemaphoreType.DMA((8,)),
        ],
        flops=3 * full * shared,
        moved=8 * shared * order,
        name="first",
    )
    floor, basis, tile_high, tile_low = call(
        prepare_kernel,
        (contact_rows, modes, coarse_inverse),
        [shape(order, loads)] + [shape(order, 3 * count, BF16)] + [shape(*coarse_inverse.shape, BF16)] * 2,
        flops=full * count,
        moved=8 * coarse_inverse.size + 4 * full,
        name="prepare",
    )
    mult_s = mult
    scratch = [pltpu.VMEM((order, 2 * loads), BF16)]
    for outer in range(OUTER):
        times = orders[outer][0]
        recvs = swap_rows(sends, "wide", wide, times)
        base = call(
            base_kernel,
            (image, unpack_own, gap),
            [shape(shared, loads)],
            flops=4 * shared * shared * loads,
            moved=8 * shared * loads,
            name="base",
        )[0]
        if outer == 0:
            row_block, load_block = block((shared, order)), block((shared, loads))
            next_loads = block((shared, loads), 1)
            trial_n, started, high, low = call(
                rest_start_kernel,
                (size, operator, mult, mult, gap, modes),
                [shape(rest, loads), shape(count, loads)] + [shape(rest, order, BF16)] * 2,
                [
                    SMEM,
                    block((shared, order), 1),
                    whole((order, loads)),
                    next_loads,
                    next_loads,
                    block((count, shared), 1, across=True),
                ],
                [load_block, whole((count, loads)), row_block, row_block],
                scratch=scratch,
                grid=(steps,),
                flops=3 * full * rest,
                moved=8 * rest * order,
                name="rest_start",
            )
            marks = unpack_all
            pack, stack_high, stack_low = call(
                functools.partial(pack_kernel, times, cap),
                (*recvs, top_high, top_low),
                [shape(padded, shared, BF16)] + [shape(shared + padded, shared, BF16)] * 2,
                flops=8 * padded * shared * shared,
                moved=8 * padded * shared,
                name="pack",
            )
        else:
            trial_n, started = call(
                rest_first_kernel,
                (size, high, low, mult_s, mult_n, gap, modes),
                [shape(rest, loads), shape(count, loads)],
                flops=3 * full * rest,
                moved=4 * rest * order,
                name="rest_first",
            )
            marks = unpack
        trial_s, own, *coarse = call(
            functools.partial(coarse_kernel, times),
            (size, *recvs, base, marks, mult_s, modes, started),
            [shape(shared, loads)] + [shape(count, loads)] * wide,
            flops=6 * shared * loads * unpack.shape[1],
            moved=2 * shared * unpack.shape[1],
            name="coarse",
        )
        blocks = [own] + swap_all(coarse, "wide", wide, coarse_order)
        own, *parts = call(
            functools.partial(tile_kernel, coarse_order, part_order),
            (tile_high, tile_low, *blocks),
            [shape(count, loads)] * narrow,
            scratch=[
                pltpu.VMEM((wide * count, loads), F32),
                pltpu.VMEM((narrow * count, loads), F32),
            ],
            flops=6 * coarse_inverse.size * loads,
            moved=4 * coarse_inverse.size,
            name="tile",
        )
        parts = [own] + swap_all(parts, "narrow", narrow, part_order)
        mult_s, mult_n, image, *sends = call(
            functools.partial(lift_kernel, n, m, cap),
            (size, *parts, basis, trial_s, trial_n, floor, top_high, top_low, pack),
            [shape(shared, loads), shape(rest, loads), shape(shared, loads)] + sent,
            flops=3 * full * shared,
            moved=4 * order * shared,
            scratch=scratch,
            name="lift",
        )
        for inner in range(1, INNER):
            last = outer == OUTER - 1 and inner == INNER - 1
            times = orders[outer][inner]
            recvs = swap_rows(sends, "wide", wide, times)
            base = call(
                base_kernel,
                (image, unpack_own, gap),
                [shape(shared, loads)],
                flops=4 * shared * shared * loads,
                moved=8 * shared * loads,
                name="base",
            )[0]
            ins = (size, high, low, mult_s, mult_n, gap, floor)
            shadow = (size, *recvs, base, unpack, mult_s, floor)
            cost = dict(flops=6 * shared * loads * unpack.shape[1], moved=2 * shared * unpack.shape[1])
            if last:
                outs = call(
                    rest_last_kernel,
                    ins,
                    [shape(order, loads)] * 2,
                    out_specs=[HBM] * 2,
                    scratch=[pltpu.VMEM((rest, loads), F32)] * 2 + [pltpu.SemaphoreType.DMA((2,))],
                    flops=3 * full * rest,
                    moved=4 * rest * order,
                    name="rest_last",
                )
                outs = call(
                    functools.partial(last_kernel, times),
                    (*shadow, *outs),
                    [shape(order, loads)] * 2,
                    in_specs=[SMEM] + [VMEM] * (len(shadow) - 1) + [HBM] * 2,
                    out_specs=[HBM] * 2,
                    scratch=[pltpu.VMEM((shared, loads), F32)] * 2 + [pltpu.SemaphoreType.DMA((2,))],
                    alias={len(shadow): 0, len(shadow) + 1: 1},
                    name="last",
                    **cost,
                )
                return tuple(out[None] for out in outs)
            mult_n, ahead = call(
                rest_kernel,
                (*ins, top_high, top_low, pack),
                [shape(rest, loads), shape(shared + padded, loads)],
                flops=3 * full * order,
                moved=4 * order * order,
                name="rest",
            )
            mult_s, image, *sends = call(
                functools.partial(sweep_kernel, times, cap),
                (*shadow, stack_high, stack_low, ahead),
                [shape(shared, loads)] * 2 + sent,
                name="sweep",
                **cost,
            )


def solution(mesh):
    wide = mesh.shape["wide"]
    narrow = mesh.shape["narrow"]

    def body(*args):
        return local(wide, narrow, *args)

    return jax.shard_map(
        body,
        mesh=mesh,
        in_specs=(
            P(("groups", "wide", "narrow"), None, None),
            P(("groups", "wide"), "narrow"),
            P(("groups", "wide", "narrow"), None, None),
            P(("groups", "wide", "narrow"), None, None),
            P(("groups", "wide", "narrow"), None, None),
            P(("groups", "wide", "narrow"), None, None),
            P(("groups", "wide", "narrow"), None),
            P(("groups", "wide", "narrow")),
            P(("groups", "wide", "narrow"), None),
        ),
        out_specs=(
            P(("groups", "wide", "narrow"), None, None),
            P(("groups", "wide", "narrow"), None, None),
        ),
        check_vma=False,
    )
```

```python
import functools

import jax
import jax.numpy as jnp
from jax import lax
from jax.experimental import pallas as pl
from jax.experimental.pallas import tpu as pltpu
from jax.sharding import PartitionSpec as P

OUTER = 2
INNER = 3
STEP = 0.3
F32 = jnp.float32
BF16 = jnp.bfloat16
PARAMS = pltpu.CompilerParams(vmem_limit_bytes=24 * 1024 * 1024)


def split(value):
    high = value.astype(BF16)
    return high, (value - high.astype(F32)).astype(BF16)


def mm(left, right):
    return jnp.dot(left, right, preferred_element_type=F32)


def product(left, right):
    (left_high, left_low), (right_high, right_low) = left, right
    width = right_high.shape[1]
    both = mm(left_high, jnp.concatenate([right_high, right_low], axis=1))
    return both[:, :width] + (both[:, width:] + mm(left_low, right_high))


def pick(chosen, value, start=0, stop=None):
    width = value.shape[1]
    halves = jnp.concatenate(split(value), axis=1)
    chunks = []
    for at in range(start, chosen.shape[0] if stop is None else stop, 128):
        both = mm(chosen[at:at + 128, :], halves)
        chunks.append(both[:, :width] + both[:, width:])
    return chunks[0] if len(chunks) == 1 else jnp.concatenate(chunks, axis=0)


def keep(halves, at, value):
    rows, width = value.shape
    halves[at:at + rows, :width], halves[at:at + rows, width:] = split(value)


def kept_product(high, low, rows, halves):
    width = halves.shape[1] // 2
    both = mm(high[rows, :], halves[...])
    return both[:, :width] + (both[:, width:] + mm(low[rows, :], halves[:, :width]))


def live(size, start, rows, width):
    return lax.broadcasted_iota(jnp.int32, (rows, width), 0) + start < size


def call(body, ins, outs, in_specs=None, out_specs=None, scratch=(), grid=(), flops=0, moved=0, alias=None, name=None):
    if in_specs is None:
        in_specs = [SMEM if value.ndim == 1 else VMEM for value in ins]
    if out_specs is None:
        out_specs = [VMEM] * len(outs)
    return pl.pallas_call(
        body,
        out_shape=outs,
        grid=grid,
        in_specs=in_specs,
        out_specs=out_specs,
        scratch_shapes=list(scratch),
        compiler_params=PARAMS,
        cost_estimate=pl.CostEstimate(flops=flops, bytes_accessed=moved, transcendentals=0),
        input_output_aliases=alias or {},
        name=name,
    )(*ins)


def whole(shape):
    return pl.BlockSpec(shape, lambda *i: (0,) * len(shape))


def block(shape, at=0, across=False):
    if across:
        return pl.BlockSpec(shape, lambda i: (0, i + at))
    return pl.BlockSpec(shape, lambda i: (i + at, 0))


SMEM = pl.BlockSpec(memory_space=pltpu.SMEM)
HBM = pl.BlockSpec(memory_space=pltpu.HBM)
VMEM = pl.BlockSpec(memory_space=pltpu.VMEM)


def shape(rows, columns, dtype=F32):
    return jax.ShapeDtypeStruct((rows, columns), dtype)


def first_kernel(n, cap, peers_at, rows_at, operator_at, mult_at, *refs):
    unpack_own, unpack_all, unpack, high, low, image = refs[:6]
    sends, (peers, rows, operator, mult, halves, done) = refs[6:6 + n], refs[6 + n:]
    shared, width = image.shape
    pieces = [(peers_at, peers), (rows_at, rows)]
    for source, target, count in ((mult_at, mult, 2), (operator_at, operator, 4)):
        step = target.shape[0] // count
        pieces += [(source.at[pl.ds(k * step, step)], target.at[pl.ds(k * step, step)]) for k in range(count)]
    copies = [pltpu.make_async_copy(source, target, done.at[i]) for i, (source, target) in enumerate(pieces)]
    for copy in copies:
        copy.start()
    copies[0].wait()
    copies[1].wait()
    across = jnp.broadcast_to(peers[...], (shared, shared))
    down = across.T
    first = lax.broadcasted_iota(jnp.int32, (shared, shared), 0)
    second = lax.broadcasted_iota(jnp.int32, (shared, shared), 1)
    slot = jnp.sum(
        jnp.where((across == down) & (second < first), 1.0, 0.0), axis=1, keepdims=True
    ).astype(jnp.int32)
    wanted = jnp.broadcast_to(rows[...], (shared, shared)).T[:, :1]
    far = down[:, :1] ^ lax.axis_index("wide")

    def marks(key, columns):
        hit = key == lax.broadcasted_iota(jnp.int32, (shared, columns), 1)
        return jnp.where(hit, 1.0, 0.0).astype(BF16)

    unpack_own[...] = marks(jnp.where(far == 0, wanted, -1), shared)
    unpack_all[...] = marks(jnp.where(far == 0, -1, (far - 1) * shared + wanted), unpack_all.shape[1])
    unpack[...] = marks(jnp.where(far == 0, -1, (far - 1) * cap + slot), unpack.shape[1])
    lane = lax.broadcasted_iota(jnp.int32, (shared, width), 1)
    for d, out in enumerate(sends, 1):
        out[shared:, :] = jnp.zeros((out.shape[0] - shared, width), F32)
        for c in range(-(-cap // width)):
            hit = (far == d) & (slot == lane + c * width)
            out[shared + c:shared + c + 1, :] = jnp.sum(
                jnp.where(hit, wanted.astype(F32), 0.0), axis=0, keepdims=True
            )
    for copy in copies[2:4]:
        copy.wait()
    for at in range(0, mult.shape[0], shared):
        keep(halves, at, mult[at:at + shared, :])
    step = shared // 4
    for at, copy in zip(range(0, shared, step), copies[4:]):
        copy.wait()
        high[at:at + step, :], low[at:at + step, :] = split(operator[at:at + step, :])
    value = kept_product(high, low, slice(None), halves)
    image[...] = value
    for out in sends:
        out[:shared, :] = value


def pack_kernel(times, cap, *refs):
    n = len(times)
    recvs, (high, low, pack, stack_high, stack_low) = refs[:n], refs[n:]
    shared = pack.shape[1]
    width = recvs[0].shape[1]
    column = lax.broadcasted_iota(jnp.int32, (width, shared), 1).astype(F32)
    if n * cap < pack.shape[0]:
        pack[n * cap:, :] = jnp.zeros((pack.shape[0] - n * cap, shared), BF16)
    for d, recv in zip(times, recvs):
        for c in range(-(-cap // width)):
            wanted = jnp.broadcast_to(recv[shared + c:shared + c + 1, :], (shared, width)).T
            chosen = jnp.where(wanted == column, 1.0, 0.0).astype(BF16)
            size = min(width, cap - c * width)
            at = (d - 1) * cap + c * width
            pack[at:at + size, :] = chosen[:size]
    for source, stack in ((high, stack_high), (low, stack_low)):
        square = source[:, :shared]
        stack[:shared, :] = square
        stack[shared:, :] = mm(pack[...], square).astype(BF16)


def prepare_kernel(contact, modes, tile, floor, basis, tile_high, tile_low):
    order, width = floor.shape
    for at in range(0, order, width):
        flag = jnp.broadcast_to(contact[:, at:at + width], (width, width)).T
        floor[at:at + width, :] = jnp.where(flag == 1, 0.0, -jnp.inf)
    high, low = [part.astype(F32) for part in split(modes[...])]
    basis[...] = jnp.concatenate([high, high, low], axis=0).T.astype(BF16)
    tile_high[...], tile_low[...] = split(tile[...])


def send(cap, chosen, image, sends):
    picked = pick(chosen, image)
    for d, out in enumerate(sends):
        out[...] = picked[d * cap:(d + 1) * cap]


def arrived(times, recvs, shared, unpack):
    blocks = [recvs[times.index(d)][...][:shared] for d in sorted(times)]
    rows = sum(b.shape[0] for b in blocks)
    if rows < unpack.shape[1]:
        blocks.append(jnp.zeros((unpack.shape[1] - rows, blocks[0].shape[1]), F32))
    return pick(unpack, jnp.concatenate(blocks, axis=0))


def base_kernel(image, unpack_own, gap, base):
    own = image[...]
    base[...] = gap[:own.shape[0], :] - own + pick(unpack_own, own)


def settle(trial, floor, alive):
    return jnp.where(alive, jnp.maximum(trial, floor), 0.0)


def shared_residual(times, recvs, base, unpack, size):
    known = base[...]
    alive = live(size[0], 0, *known.shape)
    return jnp.where(alive, known + arrived(times, recvs, known.shape[0], unpack), 0.0), alive


def rest_start_kernel(size, operator, mult, mult_block, gap, modes, trial, coarse, high, low, halves):
    step = pl.program_id(0)
    rows, width = gap.shape

    @pl.when(step == 0)
    def _():
        halves[:, :width], halves[:, width:] = split(mult[...])
        coarse[...] = jnp.zeros_like(coarse)

    parts = split(operator[...])
    high[...], low[...] = parts
    both = mm(parts[0], halves[...])
    image = both[:, :width] + (both[:, width:] + mm(parts[1], halves[:, :width]))
    alive = live(size[0], (step + 1) * rows, rows, width)
    residual = jnp.where(alive, gap[...] - image, 0.0)
    trial[...] = mult_block[...] + STEP * residual
    coarse[...] += product(split(modes[...]), split(residual))


def rest_residual(size, high, low, mult_s, mult_n, gap):
    shared, (rows, width) = mult_s.shape[0], mult_n.shape
    mult = jnp.concatenate([mult_s[...], mult_n[...]], axis=0)
    image = product((high[...], low[...]), split(mult))
    alive = live(size[0], shared, rows, width)
    return jnp.where(alive, gap[shared:, :] - image, 0.0), alive


def rest_first_kernel(size, high, low, mult_s, mult_n, gap, modes, trial, coarse):
    residual, _ = rest_residual(size, high, low, mult_s, mult_n, gap)
    trial[...] = mult_n[...] + STEP * residual
    coarse[...] = product(split(modes[:, mult_s.shape[0]:]), split(residual))


def rest_kernel(size, high, low, mult_s, mult_n, gap, floor, top_high, top_low, pack, mult_out, ahead):
    shared = mult_s.shape[0]
    residual, alive = rest_residual(size, high, low, mult_s, mult_n, gap)
    mult = settle(mult_n[...] + STEP * residual, floor[shared:, :], alive)
    mult_out[...] = mult
    value = product((top_high[:, shared:], top_low[:, shared:]), split(mult))
    ahead[:shared, :] = value
    ahead[shared:, :] = pick(pack, value)


def rest_last_kernel(size, high, low, mult_s, mult_n, gap, floor, mult_out, residual_out, settled, left, done):
    shared, rows = mult_s.shape[0], mult_n.shape[0]
    residual, alive = rest_residual(size, high, low, mult_s, mult_n, gap)
    left[...] = residual
    settled[...] = settle(mult_n[...] + STEP * residual, floor[shared:, :], alive)
    copies = [
        pltpu.make_async_copy(source, target.at[pl.ds(shared, rows)], done.at[i])
        for i, (source, target) in enumerate(((left, residual_out), (settled, mult_out)))
    ]
    for copy in copies:
        copy.start()
    for copy in copies:
        copy.wait()


def coarse_kernel(times, size, *refs):
    n = len(times)
    recvs = refs[:n]
    base, unpack, mult, modes, started, trial = refs[n:n + 6]
    shared = base.shape[0]
    residual, _ = shared_residual(times, recvs, base, unpack, size)
    coarse = started[...] + product(split(modes[:, :shared]), split(residual))
    for out in refs[n + 6:]:
        out[...] = coarse
    trial[...] = mult[:shared, :] + STEP * residual


def tile_kernel(wide_order, narrow_order, high, low, *refs):
    n, m = len(wide_order), len(narrow_order)
    blocks, outs, (gathered, parts) = refs[:n + 1], refs[n + 1:n + m + 2], refs[n + m + 2:]
    count = blocks[0].shape[0]
    for d, ref in zip((0, *wide_order), blocks):
        at = pl.multiple_of((lax.axis_index("wide") ^ d) * count, count)
        gathered[pl.ds(at, count), :] = ref[...]
    parts[...] = product((high[...], low[...]), split(gathered[...]))
    for d, out in zip((0, *narrow_order), outs):
        at = pl.multiple_of((lax.axis_index("narrow") ^ d) * count, count)
        out[...] = parts[pl.ds(at, count), :]


def lift_kernel(n, m, cap, size, *refs):
    parts = refs[:m + 1]
    ins, (mult_s, mult_n, image), sends, halves = refs[m + 1:m + 8], refs[m + 8:m + 11], refs[m + 11:-1], refs[-1]
    basis, trial_s, trial_n, floor, high, low, pack = ins
    solved = parts[0][...]
    for part in parts[1:]:
        solved = solved + part[...]
    shared, width = trial_s.shape
    order = floor.shape[0]
    high_part, low_part = split(solved)
    solved = jnp.concatenate([high_part, low_part, high_part], axis=0)
    shared, width = trial_s.shape
    for at in range(0, floor.shape[0], shared):
        rows = slice(at, at + shared)
        trial = trial_s[...] if at == 0 else trial_n[at - shared:at, :]
        alive = live(size[0], at, shared, width)
        mult = settle(trial + mm(basis[rows, :], solved), floor[rows, :], alive)
        if at == 0:
            mult_s[...] = mult
        else:
            mult_n[at - shared:at, :] = mult
        keep(halves, at, mult)
    value = kept_product(high, low, slice(None), halves)
    image[...] = value
    send(cap, pack, value, sends)


def sweep_kernel(times, cap, size, *refs):
    n = len(times)
    recvs = refs[:n]
    base, unpack, mult, floor, high, low, ahead, mult_out, image_out = refs[n:n + 9]
    sends, halves = refs[n + 9:-1], refs[-1]
    shared = base.shape[0]
    residual, alive = shared_residual(times, recvs, base, unpack, size)
    value = settle(mult[...] + STEP * residual, floor[:shared, :], alive)
    mult_out[...] = value
    keep(halves, 0, value)
    for out, at in [(out, shared + d * cap) for d, out in enumerate(sends)] + [(image_out, 0)]:
        rows = slice(at, at + out.shape[0])
        out[...] = ahead[rows, :] + kept_product(high, low, rows, halves)


def last_kernel(times, size, *refs):
    n = len(times)
    recvs = refs[:n]
    base, unpack, mult, floor, _, _, mult_out, residual_out, settled, left, done = refs[n:]
    shared = base.shape[0]
    residual, alive = shared_residual(times, recvs, base, unpack, size)
    left[...] = residual
    first = pltpu.make_async_copy(left, residual_out.at[pl.ds(0, shared)], done.at[0])
    first.start()
    settled[...] = settle(mult[...] + STEP * residual, floor[:shared, :], alive)
    second = pltpu.make_async_copy(settled, mult_out.at[pl.ds(0, shared)], done.at[1])
    second.start()
    first.wait()
    second.wait()


def swap(block, axis, count, d):
    return lax.ppermute(block, axis, [(i, i ^ d) for i in range(count)])


def swap_all(blocks, axis, count, order):
    return [swap(block, axis, count, d) for block, d in zip(blocks, order)]


def swap_rows(blocks, axis, count, times):
    return [swap(blocks[d - 1], axis, count, d) for d in times]


def half_first(count, back):
    half = count // 2
    others = [d for d in range(1, count) if d != half]
    return (half, *(others[::-1] if back else others))


def middle_first(count):
    return (count - 1, *range(1, count - 1))


def far_first(count):
    return tuple(range(count - 1, 0, -1))


def local(
    wide,
    narrow,
    operators,
    coarse_inverse,
    modes,
    gap,
    start_mult,
    peer_list,
    partner_row,
    interface_size,
    contact_rows,
):
    operator = operators[0]
    modes = modes[0]
    gap = gap[0]
    mult = start_mult[0]
    order, loads = mult.shape
    shared = partner_row.shape[1]
    count = modes.shape[0]
    rest = order - shared
    steps = rest // shared
    n, m = wide - 1, narrow - 1
    cap = 2 * shared // wide
    listed = n * cap
    padded = -(-listed // 128) * 128
    size = interface_size
    coarse_order, part_order = half_first(wide, True), far_first(narrow)
    half, half_back, middle = half_first(wide, False), half_first(wide, True), middle_first(wide)
    orders = ((middle, half, half_back), (half_back, half, half_back))
    sent = [shape(cap, loads)] * n
    full = 2 * order * loads

    list_rows = -(-(-(-cap // loads)) // 8) * 8
    unpack_own, unpack_all, unpack, top_high, top_low, image, *sends = call(
        functools.partial(first_kernel, n, cap),
        tuple(
            pltpu.with_memory_space_constraint(value, pltpu.HBM)
            for value in (peer_list[0].reshape(1, shared), partner_row, operator, mult)
        ),
        [shape(shared, shared, BF16), shape(shared, n * shared, BF16), shape(shared, padded, BF16)]
        + [shape(shared, order, BF16)] * 2
        + [shape(shared, loads)]
        + [shape(shared + list_rows, loads)] * n,
        in_specs=[HBM] * 4,
        scratch=[
            pltpu.VMEM((1, shared), jnp.int32),
            pltpu.VMEM((1, shared), jnp.int32),
            pltpu.VMEM((shared, order), F32),
            pltpu.VMEM((order, loads), F32),
            pltpu.VMEM((order, 2 * loads), BF16),
            pltpu.SemaphoreType.DMA((8,)),
        ],
        flops=3 * full * shared,
        moved=8 * shared * order,
        name="first",
    )
    floor, basis, tile_high, tile_low = call(
        prepare_kernel,
        (contact_rows, modes, coarse_inverse),
        [shape(order, loads)] + [shape(order, 3 * count, BF16)] + [shape(*coarse_inverse.shape, BF16)] * 2,
        flops=full * count,
        moved=8 * coarse_inverse.size + 4 * full,
        name="prepare",
    )
    mult_s = mult
    scratch = [pltpu.VMEM((order, 2 * loads), BF16)]
    for outer in range(OUTER):
        times = orders[outer][0]
        recvs = swap_rows(sends, "wide", wide, times)
        base = call(
            base_kernel,
            (image, unpack_own, gap),
            [shape(shared, loads)],
            flops=4 * shared * shared * loads,
            moved=8 * shared * loads,
            name="base",
        )[0]
        if outer == 0:
            row_block, load_block = block((shared, order)), block((shared, loads))
            next_loads = block((shared, loads), 1)
            trial_n, started, high, low = call(
                rest_start_kernel,
                (size, operator, mult, mult, gap, modes),
                [shape(rest, loads), shape(count, loads)] + [shape(rest, order, BF16)] * 2,
                [
                    SMEM,
                    block((shared, order), 1),
                    whole((order, loads)),
                    next_loads,
                    next_loads,
                    block((count, shared), 1, across=True),
                ],
                [load_block, whole((count, loads)), row_block, row_block],
                scratch=scratch,
                grid=(steps,),
                flops=3 * full * rest,
                moved=8 * rest * order,
                name="rest_start",
            )
            marks = unpack_all
            pack, stack_high, stack_low = call(
                functools.partial(pack_kernel, times, cap),
                (*recvs, top_high, top_low),
                [shape(padded, shared, BF16)] + [shape(shared + padded, shared, BF16)] * 2,
                flops=8 * padded * shared * shared,
                moved=8 * padded * shared,
                name="pack",
            )
        else:
            trial_n, started = call(
                rest_first_kernel,
                (size, high, low, mult_s, mult_n, gap, modes),
                [shape(rest, loads), shape(count, loads)],
                flops=3 * full * rest,
                moved=4 * rest * order,
                name="rest_first",
            )
            marks = unpack
        trial_s, own, *coarse = call(
            functools.partial(coarse_kernel, times),
            (size, *recvs, base, marks, mult_s, modes, started),
            [shape(shared, loads)] + [shape(count, loads)] * wide,
            flops=6 * shared * loads * unpack.shape[1],
            moved=2 * shared * unpack.shape[1],
            name="coarse",
        )
        blocks = [own] + swap_all(coarse, "wide", wide, coarse_order)
        own, *parts = call(
            functools.partial(tile_kernel, coarse_order, part_order),
            (tile_high, tile_low, *blocks),
            [shape(count, loads)] * narrow,
            scratch=[
                pltpu.VMEM((wide * count, loads), F32),
                pltpu.VMEM((narrow * count, loads), F32),
            ],
            flops=6 * coarse_inverse.size * loads,
            moved=4 * coarse_inverse.size,
            name="tile",
        )
        parts = [own] + swap_all(parts, "narrow", narrow, part_order)
        mult_s, mult_n, image, *sends = call(
            functools.partial(lift_kernel, n, m, cap),
            (size, *parts, basis, trial_s, trial_n, floor, top_high, top_low, pack),
            [shape(shared, loads), shape(rest, loads), shape(shared, loads)] + sent,
            flops=3 * full * shared,
            moved=4 * order * shared,
            scratch=scratch,
            name="lift",
        )
        for inner in range(1, INNER):
            last = outer == OUTER - 1 and inner == INNER - 1
            times = orders[outer][inner]
            recvs = swap_rows(sends, "wide", wide, times)
            base = call(
                base_kernel,
                (image, unpack_own, gap),
                [shape(shared, loads)],
                flops=4 * shared * shared * loads,
                moved=8 * shared * loads,
                name="base",
            )[0]
            ins = (size, high, low, mult_s, mult_n, gap, floor)
            shadow = (size, *recvs, base, unpack, mult_s, floor)
            cost = dict(flops=6 * shared * loads * unpack.shape[1], moved=2 * shared * unpack.shape[1])
            if last:
                outs = call(
                    rest_last_kernel,
                    ins,
                    [shape(order, loads)] * 2,
                    out_specs=[HBM] * 2,
                    scratch=[pltpu.VMEM((rest, loads), F32)] * 2 + [pltpu.SemaphoreType.DMA((2,))],
                    flops=3 * full * rest,
                    moved=4 * rest * order,
                    name="rest_last",
                )
                outs = call(
                    functools.partial(last_kernel, times),
                    (*shadow, *outs),
                    [shape(order, loads)] * 2,
                    in_specs=[SMEM] + [VMEM] * (len(shadow) - 1) + [HBM] * 2,
                    out_specs=[HBM] * 2,
                    scratch=[pltpu.VMEM((shared, loads), F32)] * 2 + [pltpu.SemaphoreType.DMA((2,))],
                    alias={len(shadow): 0, len(shadow) + 1: 1},
                    name="last",
                    **cost,
                )
                return tuple(out[None] for out in outs)
            mult_n, ahead = call(
                rest_kernel,
                (*ins, top_high, top_low, pack),
                [shape(rest, loads), shape(shared + padded, loads)],
                flops=3 * full * order,
                moved=4 * order * order,
                name="rest",
            )
            mult_s, image, *sends = call(
                functools.partial(sweep_kernel, times, cap),
                (*shadow, stack_high, stack_low, ahead),
                [shape(shared, loads)] * 2 + sent,
                scratch=[pltpu.VMEM((shared, 2 * loads), BF16)],
                name="sweep",
                **cost,
            )


def solution(mesh):
    wide = mesh.shape["wide"]
    narrow = mesh.shape["narrow"]

    def body(*args):
        return local(wide, narrow, *args)

    return jax.shard_map(
        body,
        mesh=mesh,
        in_specs=(
            P(("groups", "wide", "narrow"), None, None),
            P(("groups", "wide"), "narrow"),
            P(("groups", "wide", "narrow"), None, None),
            P(("groups", "wide", "narrow"), None, None),
            P(("groups", "wide", "narrow"), None, None),
            P(("groups", "wide", "narrow"), None, None),
            P(("groups", "wide", "narrow"), None),
            P(("groups", "wide", "narrow")),
            P(("groups", "wide", "narrow"), None),
        ),
        out_specs=(
            P(("groups", "wide", "narrow"), None, None),
            P(("groups", "wide", "narrow"), None, None),
        ),
        check_vma=False,
    )
```

```python
import functools

import jax
import jax.numpy as jnp
from jax import lax
from jax.experimental import pallas as pl
from jax.experimental.pallas import tpu as pltpu
from jax.sharding import PartitionSpec as P

OUTER = 2
INNER = 3
STEP = 0.3
F32 = jnp.float32
BF16 = jnp.bfloat16
PARAMS = pltpu.CompilerParams(vmem_limit_bytes=24 * 1024 * 1024)


def split(value):
    high = value.astype(BF16)
    return high, (value - high.astype(F32)).astype(BF16)


def mm(left, right):
    return jnp.dot(left, right, preferred_element_type=F32)


def product(left, right):
    (left_high, left_low), (right_high, right_low) = left, right
    width = right_high.shape[1]
    both = mm(left_high, jnp.concatenate([right_high, right_low], axis=1))
    return both[:, :width] + (both[:, width:] + mm(left_low, right_high))


def pick(chosen, value):
    width = value.shape[1]
    both = mm(chosen, jnp.concatenate(split(value), axis=1))
    return both[:, :width] + both[:, width:]


def live(size, start, rows, width):
    return lax.broadcasted_iota(jnp.int32, (rows, width), 0) + start < size


def call(body, ins, outs, in_specs=None, out_specs=None, scratch=(), grid=(), flops=0, moved=0, alias=None, name=None):
    if in_specs is None:
        in_specs = [SMEM if value.ndim == 1 else VMEM for value in ins]
    if out_specs is None:
        out_specs = [VMEM] * len(outs)
    return pl.pallas_call(
        body,
        out_shape=outs,
        grid=grid,
        in_specs=in_specs,
        out_specs=out_specs,
        scratch_shapes=list(scratch),
        compiler_params=PARAMS,
        cost_estimate=pl.CostEstimate(flops=flops, bytes_accessed=moved, transcendentals=0),
        input_output_aliases=alias or {},
        name=name,
    )(*ins)


def whole(shape):
    return pl.BlockSpec(shape, lambda *i: (0,) * len(shape))


def block(shape, at=0, across=False):
    if across:
        return pl.BlockSpec(shape, lambda i: (0, i + at))
    return pl.BlockSpec(shape, lambda i: (i + at, 0))


SMEM = pl.BlockSpec(memory_space=pltpu.SMEM)
HBM = pl.BlockSpec(memory_space=pltpu.HBM)
VMEM = pl.BlockSpec(memory_space=pltpu.VMEM)


def shape(rows, columns, dtype=F32):
    return jax.ShapeDtypeStruct((rows, columns), dtype)


def first_kernel(n, cap, peers_at, rows_at, operator_at, mult_at, *refs):
    unpack_own, unpack_all, unpack, high, low, image = refs[:6]
    sends, (peers, rows, operator, mult, done) = refs[6:6 + n], refs[6 + n:]
    shared, width = image.shape
    pieces = [(peers_at, peers), (rows_at, rows)]
    for source, target, count in ((mult_at, mult, 2), (operator_at, operator, 4)):
        step = target.shape[0] // count
        pieces += [(source.at[pl.ds(k * step, step)], target.at[pl.ds(k * step, step)]) for k in range(count)]
    copies = [pltpu.make_async_copy(source, target, done.at[i]) for i, (source, target) in enumerate(pieces)]
    for copy in copies:
        copy.start()
    copies[0].wait()
    copies[1].wait()
    across = jnp.broadcast_to(peers[...], (shared, shared))
    down = across.T
    first = lax.broadcasted_iota(jnp.int32, (shared, shared), 0)
    second = lax.broadcasted_iota(jnp.int32, (shared, shared), 1)
    slot = jnp.sum(
        jnp.where((across == down) & (second < first), 1.0, 0.0), axis=1, keepdims=True
    ).astype(jnp.int32)
    wanted = jnp.broadcast_to(rows[...], (shared, shared)).T[:, :1]
    far = down[:, :1] ^ lax.axis_index("wide")

    def marks(key, columns):
        hit = key == lax.broadcasted_iota(jnp.int32, (shared, columns), 1)
        return jnp.where(hit, 1.0, 0.0).astype(BF16)

    unpack_own[...] = marks(jnp.where(far == 0, wanted, -1), shared)
    unpack_all[...] = marks(jnp.where(far == 0, -1, (far - 1) * shared + wanted), unpack_all.shape[1])
    unpack[...] = marks(jnp.where(far == 0, -1, (far - 1) * cap + slot), unpack.shape[1])
    lane = lax.broadcasted_iota(jnp.int32, (shared, width), 1)
    for d, out in enumerate(sends, 1):
        out[shared:, :] = jnp.zeros((out.shape[0] - shared, width), F32)
        for c in range(-(-cap // width)):
            hit = (far == d) & (slot == lane + c * width)
            out[shared + c:shared + c + 1, :] = jnp.sum(
                jnp.where(hit, wanted.astype(F32), 0.0), axis=0, keepdims=True
            )
    for copy in copies[2:]:
        copy.wait()
    parts = split(operator[...])
    high[...], low[...] = parts
    value = product(parts, split(mult[...]))
    image[...] = value
    for out in sends:
        out[:shared, :] = value


def pack_kernel(times, cap, *refs):
    n = len(times)
    recvs, (high, low, pack, stack_high, stack_low) = refs[:n], refs[n:]
    shared = pack.shape[1]
    width = recvs[0].shape[1]
    column = lax.broadcasted_iota(jnp.int32, (width, shared), 1).astype(F32)
    if n * cap < pack.shape[0]:
        pack[n * cap:, :] = jnp.zeros((pack.shape[0] - n * cap, shared), BF16)
    for d, recv in zip(times, recvs):
        for c in range(-(-cap // width)):
            wanted = jnp.broadcast_to(recv[shared + c:shared + c + 1, :], (shared, width)).T
            chosen = jnp.where(wanted == column, 1.0, 0.0).astype(BF16)
            size = min(width, cap - c * width)
            at = (d - 1) * cap + c * width
            pack[at:at + size, :] = chosen[:size]
    for source, stack in ((high, stack_high), (low, stack_low)):
        square = source[:, :shared]
        stack[:shared, :] = square
        stack[shared:, :] = mm(pack[...], square).astype(BF16)


def prepare_kernel(contact, modes, tile, floor, basis, tile_high, tile_low):
    order, width = floor.shape
    for at in range(0, order, width):
        flag = jnp.broadcast_to(contact[:, at:at + width], (width, width)).T
        floor[at:at + width, :] = jnp.where(flag == 1, 0.0, -jnp.inf)
    high, low = [part.astype(F32) for part in split(modes[...])]
    basis[...] = jnp.concatenate([high, high, low], axis=0).T.astype(BF16)
    tile_high[...], tile_low[...] = split(tile[...])


def send(cap, chosen, image, sends):
    picked = pick(chosen, image)
    for d, out in enumerate(sends):
        out[...] = picked[d * cap:(d + 1) * cap]


def arrived(times, recvs, shared, unpack):
    blocks = [recvs[times.index(d)][...][:shared] for d in sorted(times)]
    rows = sum(b.shape[0] for b in blocks)
    if rows < unpack.shape[1]:
        blocks.append(jnp.zeros((unpack.shape[1] - rows, blocks[0].shape[1]), F32))
    halves = jnp.concatenate(split(jnp.concatenate(blocks, axis=0)), axis=1)
    width = blocks[0].shape[1]
    chunks = []
    for at in range(0, shared, 128):
        both = mm(unpack[at:at + 128, :], halves)
        chunks.append(both[:, :width] + both[:, width:])
    return jnp.concatenate(chunks, axis=0)


def base_kernel(image, unpack_own, gap, base):
    own = image[...]
    base[...] = gap[:own.shape[0], :] - own + pick(unpack_own[...], own)


def settle(trial, floor, alive):
    return jnp.where(alive, jnp.maximum(trial, floor), 0.0)


def shared_residual(times, recvs, base, unpack, size):
    known = base[...]
    alive = live(size[0], 0, *known.shape)
    return jnp.where(alive, known + arrived(times, recvs, known.shape[0], unpack), 0.0), alive


def rest_start_kernel(size, operator, mult, mult_block, gap, modes, trial, coarse, high, low, halves):
    step = pl.program_id(0)
    rows, width = gap.shape

    @pl.when(step == 0)
    def _():
        halves[:, :width], halves[:, width:] = split(mult[...])
        coarse[...] = jnp.zeros_like(coarse)

    parts = split(operator[...])
    high[...], low[...] = parts
    both = mm(parts[0], halves[...])
    image = both[:, :width] + (both[:, width:] + mm(parts[1], halves[:, :width]))
    alive = live(size[0], (step + 1) * rows, rows, width)
    residual = jnp.where(alive, gap[...] - image, 0.0)
    trial[...] = mult_block[...] + STEP * residual
    coarse[...] += product(split(modes[...]), split(residual))


def rest_residual(size, high, low, mult_s, mult_n, gap):
    shared, (rows, width) = mult_s.shape[0], mult_n.shape
    mult = jnp.concatenate([mult_s[...], mult_n[...]], axis=0)
    image = product((high[...], low[...]), split(mult))
    alive = live(size[0], shared, rows, width)
    return jnp.where(alive, gap[shared:, :] - image, 0.0), alive


def rest_first_kernel(size, high, low, mult_s, mult_n, gap, modes, trial, coarse):
    residual, _ = rest_residual(size, high, low, mult_s, mult_n, gap)
    trial[...] = mult_n[...] + STEP * residual
    coarse[...] = product(split(modes[:, mult_s.shape[0]:]), split(residual))


def rest_kernel(size, high, low, mult_s, mult_n, gap, floor, top_high, top_low, pack, mult_out, ahead):
    shared = mult_s.shape[0]
    residual, alive = rest_residual(size, high, low, mult_s, mult_n, gap)
    mult = settle(mult_n[...] + STEP * residual, floor[shared:, :], alive)
    mult_out[...] = mult
    value = product((top_high[:, shared:], top_low[:, shared:]), split(mult))
    ahead[:shared, :] = value
    ahead[shared:, :] = pick(pack[...], value)


def rest_last_kernel(size, high, low, mult_s, mult_n, gap, floor, mult_out, residual_out, settled, left, done):
    shared, rows = mult_s.shape[0], mult_n.shape[0]
    residual, alive = rest_residual(size, high, low, mult_s, mult_n, gap)
    left[...] = residual
    settled[...] = settle(mult_n[...] + STEP * residual, floor[shared:, :], alive)
    copies = [
        pltpu.make_async_copy(source, target.at[pl.ds(shared, rows)], done.at[i])
        for i, (source, target) in enumerate(((left, residual_out), (settled, mult_out)))
    ]
    for copy in copies:
        copy.start()
    for copy in copies:
        copy.wait()


def coarse_kernel(times, size, *refs):
    n = len(times)
    recvs = refs[:n]
    base, unpack, mult, modes, started, trial = refs[n:n + 6]
    shared = base.shape[0]
    residual, _ = shared_residual(times, recvs, base, unpack, size)
    coarse = started[...] + product(split(modes[:, :shared]), split(residual))
    for out in refs[n + 6:]:
        out[...] = coarse
    trial[...] = mult[:shared, :] + STEP * residual


def tile_kernel(wide_order, narrow_order, high, low, *refs):
    n, m = len(wide_order), len(narrow_order)
    blocks, outs, (gathered, parts) = refs[:n + 1], refs[n + 1:n + m + 2], refs[n + m + 2:]
    count = blocks[0].shape[0]
    for d, ref in zip((0, *wide_order), blocks):
        at = pl.multiple_of((lax.axis_index("wide") ^ d) * count, count)
        gathered[pl.ds(at, count), :] = ref[...]
    parts[...] = product((high[...], low[...]), split(gathered[...]))
    for d, out in zip((0, *narrow_order), outs):
        at = pl.multiple_of((lax.axis_index("narrow") ^ d) * count, count)
        out[...] = parts[pl.ds(at, count), :]


def lift_kernel(n, m, cap, size, *refs):
    parts = refs[:m + 1]
    ins, (mult_s, mult_n, image), sends, halves = refs[m + 1:m + 8], refs[m + 8:m + 11], refs[m + 11:-1], refs[-1]
    basis, trial_s, trial_n, floor, high, low, pack = ins
    solved = parts[0][...]
    for part in parts[1:]:
        solved = solved + part[...]
    shared, width = trial_s.shape
    order = floor.shape[0]
    high_part, low_part = split(solved)
    solved = jnp.concatenate([high_part, low_part, high_part], axis=0)
    shared, width = trial_s.shape
    for at in range(0, floor.shape[0], shared):
        rows = slice(at, at + shared)
        trial = trial_s[...] if at == 0 else trial_n[at - shared:at, :]
        alive = live(size[0], at, shared, width)
        mult = settle(trial + mm(basis[rows, :], solved), floor[rows, :], alive)
        if at == 0:
            mult_s[...] = mult
        else:
            mult_n[at - shared:at, :] = mult
        halves[rows, :width], halves[rows, width:] = split(mult)
    both = mm(high[...], halves[...])
    value = both[:, :width] + (both[:, width:] + mm(low[...], halves[:, :width]))
    image[...] = value
    send(cap, pack[...], value, sends)


def sweep_kernel(times, cap, size, *refs):
    n = len(times)
    recvs = refs[:n]
    base, unpack, mult, floor, high, low, ahead, mult_out, image_out = refs[n:n + 9]
    shared = base.shape[0]
    residual, alive = shared_residual(times, recvs, base, unpack, size)
    value = settle(mult[...] + STEP * residual, floor[:shared, :], alive)
    mult_out[...] = value
    both = ahead[...] + product((high[...], low[...]), split(value))
    image_out[...] = both[:shared]
    for d, out in enumerate(refs[n + 9:]):
        out[...] = both[shared + d * cap:shared + (d + 1) * cap]


def last_kernel(times, size, *refs):
    n = len(times)
    recvs = refs[:n]
    base, unpack, mult, floor, _, _, mult_out, residual_out, settled, left, done = refs[n:]
    shared = base.shape[0]
    residual, alive = shared_residual(times, recvs, base, unpack, size)
    left[...] = residual
    first = pltpu.make_async_copy(left, residual_out.at[pl.ds(0, shared)], done.at[0])
    first.start()
    settled[...] = settle(mult[...] + STEP * residual, floor[:shared, :], alive)
    second = pltpu.make_async_copy(settled, mult_out.at[pl.ds(0, shared)], done.at[1])
    second.start()
    first.wait()
    second.wait()


def swap(block, axis, count, d):
    return lax.ppermute(block, axis, [(i, i ^ d) for i in range(count)])


def swap_all(blocks, axis, count, order):
    return [swap(block, axis, count, d) for block, d in zip(blocks, order)]


def swap_rows(blocks, axis, count, times):
    return [swap(blocks[d - 1], axis, count, d) for d in times]


def half_first(count, back):
    half = count // 2
    others = [d for d in range(1, count) if d != half]
    return (half, *(others[::-1] if back else others))


def middle_first(count):
    return (count - 1, *range(1, count - 1))


def far_first(count):
    return tuple(range(count - 1, 0, -1))


def local(
    wide,
    narrow,
    operators,
    coarse_inverse,
    modes,
    gap,
    start_mult,
    peer_list,
    partner_row,
    interface_size,
    contact_rows,
):
    operator = operators[0]
    modes = modes[0]
    gap = gap[0]
    mult = start_mult[0]
    order, loads = mult.shape
    shared = partner_row.shape[1]
    count = modes.shape[0]
    rest = order - shared
    steps = rest // shared
    n, m = wide - 1, narrow - 1
    cap = 2 * shared // wide
    listed = n * cap
    padded = -(-listed // 128) * 128
    size = interface_size
    coarse_order, part_order = half_first(wide, True), far_first(narrow)
    half, half_back, middle = half_first(wide, False), half_first(wide, True), middle_first(wide)
    orders = ((middle, half, half_back), (half_back, half, half_back))
    sent = [shape(cap, loads)] * n
    full = 2 * order * loads

    list_rows = -(-(-(-cap // loads)) // 8) * 8
    unpack_own, unpack_all, unpack, top_high, top_low, image, *sends = call(
        functools.partial(first_kernel, n, cap),
        tuple(
            pltpu.with_memory_space_constraint(value, pltpu.HBM)
            for value in (peer_list[0].reshape(1, shared), partner_row, operator, mult)
        ),
        [shape(shared, shared, BF16), shape(shared, n * shared, BF16), shape(shared, padded, BF16)]
        + [shape(shared, order, BF16)] * 2
        + [shape(shared, loads)]
        + [shape(shared + list_rows, loads)] * n,
        in_specs=[HBM] * 4,
        scratch=[
            pltpu.VMEM((1, shared), jnp.int32),
            pltpu.VMEM((1, shared), jnp.int32),
            pltpu.VMEM((shared, order), F32),
            pltpu.VMEM((order, loads), F32),
            pltpu.SemaphoreType.DMA((8,)),
        ],
        flops=3 * full * shared,
        moved=8 * shared * order,
        name="first",
    )
    floor, basis, tile_high, tile_low = call(
        prepare_kernel,
        (contact_rows, modes, coarse_inverse),
        [shape(order, loads)] + [shape(order, 3 * count, BF16)] + [shape(*coarse_inverse.shape, BF16)] * 2,
        flops=full * count,
        moved=8 * coarse_inverse.size + 4 * full,
        name="prepare",
    )
    mult_s = mult
    scratch = [pltpu.VMEM((order, 2 * loads), BF16)]
    for outer in range(OUTER):
        times = orders[outer][0]
        recvs = swap_rows(sends, "wide", wide, times)
        base = call(
            base_kernel,
            (image, unpack_own, gap),
            [shape(shared, loads)],
            flops=4 * shared * shared * loads,
            moved=8 * shared * loads,
            name="base",
        )[0]
        if outer == 0:
            row_block, load_block = block((shared, order)), block((shared, loads))
            next_loads = block((shared, loads), 1)
            trial_n, started, high, low = call(
                rest_start_kernel,
                (
                    size,
                    *(
                        pltpu.with_memory_space_constraint(value, pltpu.HBM)
                        for value in (operator, mult, mult, gap, modes)
                    ),
                ),
                [shape(rest, loads), shape(count, loads)] + [shape(rest, order, BF16)] * 2,
                [
                    SMEM,
                    block((shared, order), 1),
                    whole((order, loads)),
                    next_loads,
                    next_loads,
                    block((count, shared), 1, across=True),
                ],
                [load_block, whole((count, loads)), row_block, row_block],
                scratch=scratch,
                grid=(steps,),
                flops=3 * full * rest,
                moved=8 * rest * order,
                name="rest_start",
            )
            marks = unpack_all
            pack, stack_high, stack_low = call(
                functools.partial(pack_kernel, times, cap),
                (*recvs, top_high, top_low),
                [shape(padded, shared, BF16)] + [shape(shared + padded, shared, BF16)] * 2,
                flops=8 * padded * shared * shared,
                moved=8 * padded * shared,
                name="pack",
            )
        else:
            trial_n, started = call(
                rest_first_kernel,
                (size, high, low, mult_s, mult_n, gap, modes),
                [shape(rest, loads), shape(count, loads)],
                flops=3 * full * rest,
                moved=4 * rest * order,
                name="rest_first",
            )
            marks = unpack
        trial_s, own, *coarse = call(
            functools.partial(coarse_kernel, times),
            (size, *recvs, base, marks, mult_s, modes, started),
            [shape(shared, loads)] + [shape(count, loads)] * wide,
            flops=6 * shared * loads * unpack.shape[1],
            moved=2 * shared * unpack.shape[1],
            name="coarse",
        )
        blocks = [own] + swap_all(coarse, "wide", wide, coarse_order)
        own, *parts = call(
            functools.partial(tile_kernel, coarse_order, part_order),
            (tile_high, tile_low, *blocks),
            [shape(count, loads)] * narrow,
            scratch=[
                pltpu.VMEM((wide * count, loads), F32),
                pltpu.VMEM((narrow * count, loads), F32),
            ],
            flops=6 * coarse_inverse.size * loads,
            moved=4 * coarse_inverse.size,
            name="tile",
        )
        parts = [own] + swap_all(parts, "narrow", narrow, part_order)
        mult_s, mult_n, image, *sends = call(
            functools.partial(lift_kernel, n, m, cap),
            (size, *parts, basis, trial_s, trial_n, floor, top_high, top_low, pack),
            [shape(shared, loads), shape(rest, loads), shape(shared, loads)] + sent,
            flops=3 * full * shared,
            moved=4 * order * shared,
            scratch=scratch,
            name="lift",
        )
        for inner in range(1, INNER):
            last = outer == OUTER - 1 and inner == INNER - 1
            times = orders[outer][inner]
            recvs = swap_rows(sends, "wide", wide, times)
            base = call(
                base_kernel,
                (image, unpack_own, gap),
                [shape(shared, loads)],
                flops=4 * shared * shared * loads,
                moved=8 * shared * loads,
                name="base",
            )[0]
            ins = (size, high, low, mult_s, mult_n, gap, floor)
            shadow = (size, *recvs, base, unpack, mult_s, floor)
            cost = dict(flops=6 * shared * loads * unpack.shape[1], moved=2 * shared * unpack.shape[1])
            if last:
                outs = call(
                    rest_last_kernel,
                    ins,
                    [shape(order, loads)] * 2,
                    out_specs=[HBM] * 2,
                    scratch=[pltpu.VMEM((rest, loads), F32)] * 2 + [pltpu.SemaphoreType.DMA((2,))],
                    flops=3 * full * rest,
                    moved=4 * rest * order,
                    name="rest_last",
                )
                outs = call(
                    functools.partial(last_kernel, times),
                    (*shadow, *outs),
                    [shape(order, loads)] * 2,
                    in_specs=[SMEM] + [VMEM] * (len(shadow) - 1) + [HBM] * 2,
                    out_specs=[HBM] * 2,
                    scratch=[pltpu.VMEM((shared, loads), F32)] * 2 + [pltpu.SemaphoreType.DMA((2,))],
                    alias={len(shadow): 0, len(shadow) + 1: 1},
                    name="last",
                    **cost,
                )
                return tuple(out[None] for out in outs)
            mult_n, ahead = call(
                rest_kernel,
                (*ins, top_high, top_low, pack),
                [shape(rest, loads), shape(shared + padded, loads)],
                flops=3 * full * order,
                moved=4 * order * order,
                name="rest",
            )
            mult_s, image, *sends = call(
                functools.partial(sweep_kernel, times, cap),
                (*shadow, stack_high, stack_low, ahead),
                [shape(shared, loads)] * 2 + sent,
                name="sweep",
                **cost,
            )


def solution(mesh):
    wide = mesh.shape["wide"]
    narrow = mesh.shape["narrow"]

    def body(*args):
        return local(wide, narrow, *args)

    return jax.shard_map(
        body,
        mesh=mesh,
        in_specs=(
            P(("groups", "wide", "narrow"), None, None),
            P(("groups", "wide"), "narrow"),
            P(("groups", "wide", "narrow"), None, None),
            P(("groups", "wide", "narrow"), None, None),
            P(("groups", "wide", "narrow"), None, None),
            P(("groups", "wide", "narrow"), None, None),
            P(("groups", "wide", "narrow"), None),
            P(("groups", "wide", "narrow")),
            P(("groups", "wide", "narrow"), None),
        ),
        out_specs=(
            P(("groups", "wide", "narrow"), None, None),
            P(("groups", "wide", "narrow"), None, None),
        ),
        check_vma=False,
    )
```

```python
import functools

import jax
import jax.numpy as jnp
from jax import lax
from jax.experimental import pallas as pl
from jax.experimental.pallas import tpu as pltpu
from jax.sharding import PartitionSpec as P

OUTER = 2
INNER = 3
STEP = 0.3
F32 = jnp.float32
BF16 = jnp.bfloat16
PARAMS = pltpu.CompilerParams(vmem_limit_bytes=24 * 1024 * 1024)


def split(value):
    high = value.astype(BF16)
    return high, (value - high.astype(F32)).astype(BF16)


def mm(left, right):
    return jnp.dot(left, right, preferred_element_type=F32)


def product(left, right):
    (left_high, left_low), (right_high, right_low) = left, right
    width = right_high.shape[1]
    both = mm(left_high, jnp.concatenate([right_high, right_low], axis=1))
    return both[:, :width] + (both[:, width:] + mm(left_low, right_high))


def pick(chosen, value):
    width = value.shape[1]
    both = mm(chosen, jnp.concatenate(split(value), axis=1))
    return both[:, :width] + both[:, width:]


def live(size, start, rows, width):
    return lax.broadcasted_iota(jnp.int32, (rows, width), 0) + start < size


def call(body, ins, outs, in_specs=None, out_specs=None, scratch=(), grid=(), flops=0, moved=0, alias=None, name=None):
    if in_specs is None:
        in_specs = [SMEM if value.ndim == 1 else VMEM for value in ins]
    if out_specs is None:
        out_specs = [VMEM] * len(outs)
    return pl.pallas_call(
        body,
        out_shape=outs,
        grid=grid,
        in_specs=in_specs,
        out_specs=out_specs,
        scratch_shapes=list(scratch),
        compiler_params=PARAMS,
        cost_estimate=pl.CostEstimate(flops=flops, bytes_accessed=moved, transcendentals=0),
        input_output_aliases=alias or {},
        name=name,
    )(*ins)


def whole(shape):
    return pl.BlockSpec(shape, lambda *i: (0,) * len(shape))


def block(shape, at=0, across=False):
    if across:
        return pl.BlockSpec(shape, lambda i: (0, i + at))
    return pl.BlockSpec(shape, lambda i: (i + at, 0))


SMEM = pl.BlockSpec(memory_space=pltpu.SMEM)
HBM = pl.BlockSpec(memory_space=pltpu.HBM)
VMEM = pl.BlockSpec(memory_space=pltpu.VMEM)


def shape(rows, columns, dtype=F32):
    return jax.ShapeDtypeStruct((rows, columns), dtype)


def first_kernel(n, cap, peers_at, rows_at, operator_at, mult_at, *refs):
    unpack_own, unpack_all, unpack, high, low, image = refs[:6]
    sends, (peers, rows, operator, mult, done) = refs[6:6 + n], refs[6 + n:]
    shared, width = image.shape
    pieces = [(peers_at, peers), (rows_at, rows)]
    for source, target, count in ((mult_at, mult, 2), (operator_at, operator, 4)):
        step = target.shape[0] // count
        pieces += [(source.at[pl.ds(k * step, step)], target.at[pl.ds(k * step, step)]) for k in range(count)]
    copies = [pltpu.make_async_copy(source, target, done.at[i]) for i, (source, target) in enumerate(pieces)]
    for copy in copies:
        copy.start()
    copies[0].wait()
    copies[1].wait()
    across = jnp.broadcast_to(peers[...], (shared, shared))
    down = across.T
    first = lax.broadcasted_iota(jnp.int32, (shared, shared), 0)
    second = lax.broadcasted_iota(jnp.int32, (shared, shared), 1)
    slot = jnp.sum(
        jnp.where((across == down) & (second < first), 1.0, 0.0), axis=1, keepdims=True
    ).astype(jnp.int32)
    wanted = jnp.broadcast_to(rows[...], (shared, shared)).T[:, :1]
    far = down[:, :1] ^ lax.axis_index("wide")

    def marks(key, columns):
        hit = key == lax.broadcasted_iota(jnp.int32, (shared, columns), 1)
        return jnp.where(hit, 1.0, 0.0).astype(BF16)

    unpack_own[...] = marks(jnp.where(far == 0, wanted, -1), shared)
    unpack_all[...] = marks(jnp.where(far == 0, -1, (far - 1) * shared + wanted), unpack_all.shape[1])
    unpack[...] = marks(jnp.where(far == 0, -1, (far - 1) * cap + slot), unpack.shape[1])
    lane = lax.broadcasted_iota(jnp.int32, (shared, width), 1)
    for d, out in enumerate(sends, 1):
        out[shared:, :] = jnp.zeros((out.shape[0] - shared, width), F32)
        for c in range(-(-cap // width)):
            hit = (far == d) & (slot == lane + c * width)
            out[shared + c:shared + c + 1, :] = jnp.sum(
                jnp.where(hit, wanted.astype(F32), 0.0), axis=0, keepdims=True
            )
    for copy in copies[2:]:
        copy.wait()
    parts = split(operator[...])
    high[...], low[...] = parts
    value = product(parts, split(mult[...]))
    image[...] = value
    for out in sends:
        out[:shared, :] = value


def pack_kernel(times, cap, *refs):
    n = len(times)
    recvs, (high, low, pack, stack_high, stack_low) = refs[:n], refs[n:]
    shared = pack.shape[1]
    width = recvs[0].shape[1]
    column = lax.broadcasted_iota(jnp.int32, (width, shared), 1).astype(F32)
    if n * cap < pack.shape[0]:
        pack[n * cap:, :] = jnp.zeros((pack.shape[0] - n * cap, shared), BF16)
    for d, recv in zip(times, recvs):
        for c in range(-(-cap // width)):
            wanted = jnp.broadcast_to(recv[shared + c:shared + c + 1, :], (shared, width)).T
            chosen = jnp.where(wanted == column, 1.0, 0.0).astype(BF16)
            size = min(width, cap - c * width)
            at = (d - 1) * cap + c * width
            pack[at:at + size, :] = chosen[:size]
    for source, stack in ((high, stack_high), (low, stack_low)):
        square = source[:, :shared]
        stack[:shared, :] = square
        stack[shared:, :] = mm(pack[...], square).astype(BF16)


def prepare_kernel(contact, modes, tile, floor, basis, tile_high, tile_low):
    order, width = floor.shape
    for at in range(0, order, width):
        flag = jnp.broadcast_to(contact[:, at:at + width], (width, width)).T
        floor[at:at + width, :] = jnp.where(flag == 1, 0.0, -jnp.inf)
    high, low = [part.astype(F32) for part in split(modes[...])]
    basis[...] = jnp.concatenate([high, high, low], axis=0).T.astype(BF16)
    tile_high[...], tile_low[...] = split(tile[...])


def send(cap, chosen, image, sends):
    picked = pick(chosen, image)
    for d, out in enumerate(sends):
        out[...] = picked[d * cap:(d + 1) * cap]


def arrived(times, recvs, shared, unpack, chunk):
    blocks = [recvs[times.index(d)][...][:shared] for d in sorted(times)]
    rows = sum(b.shape[0] for b in blocks)
    if rows < unpack.shape[1]:
        blocks.append(jnp.zeros((unpack.shape[1] - rows, blocks[0].shape[1]), F32))
    halves = jnp.concatenate(split(jnp.concatenate(blocks, axis=0)), axis=1)
    width = blocks[0].shape[1]
    for at in range(0, shared, chunk):
        both = mm(unpack[at:at + chunk, :], halves)
        yield both[:, :width] + both[:, width:]


def base_kernel(image, unpack_own, gap, base):
    own = image[...]
    base[...] = gap[:own.shape[0], :] - own + pick(unpack_own[...], own)


def settle(trial, floor, alive):
    return jnp.where(alive, jnp.maximum(trial, floor), 0.0)


def shared_residual(times, recvs, base, unpack, size, chunk):
    known = base[...]
    shared = known.shape[0]
    across = jnp.concatenate(list(arrived(times, recvs, shared, unpack, chunk)), axis=0)
    alive = live(size[0], 0, *known.shape)
    return jnp.where(alive, known + across, 0.0), alive


def rest_start_kernel(size, operator, mult, mult_block, gap, modes, trial, coarse, high, low, halves):
    step = pl.program_id(0)
    rows, width = gap.shape

    @pl.when(step == 0)
    def _():
        halves[:, :width], halves[:, width:] = split(mult[...])
        coarse[...] = jnp.zeros_like(coarse)

    parts = split(operator[...])
    high[...], low[...] = parts
    both = mm(parts[0], halves[...])
    image = both[:, :width] + (both[:, width:] + mm(parts[1], halves[:, :width]))
    alive = live(size[0], (step + 1) * rows, rows, width)
    residual = jnp.where(alive, gap[...] - image, 0.0)
    trial[...] = mult_block[...] + STEP * residual
    coarse[...] += product(split(modes[...]), split(residual))


def rest_residual(size, high, low, mult_s, mult_n, gap):
    shared, (rows, width) = mult_s.shape[0], mult_n.shape
    mult = jnp.concatenate([mult_s[...], mult_n[...]], axis=0)
    image = product((high[...], low[...]), split(mult))
    alive = live(size[0], shared, rows, width)
    return jnp.where(alive, gap[shared:, :] - image, 0.0), alive


def rest_first_kernel(size, high, low, mult_s, mult_n, gap, modes, trial, coarse):
    residual, _ = rest_residual(size, high, low, mult_s, mult_n, gap)
    trial[...] = mult_n[...] + STEP * residual
    coarse[...] = product(split(modes[:, mult_s.shape[0]:]), split(residual))


def rest_kernel(size, high, low, mult_s, mult_n, gap, floor, top_high, top_low, pack, mult_out, ahead):
    shared = mult_s.shape[0]
    residual, alive = rest_residual(size, high, low, mult_s, mult_n, gap)
    mult = settle(mult_n[...] + STEP * residual, floor[shared:, :], alive)
    mult_out[...] = mult
    value = product((top_high[:, shared:], top_low[:, shared:]), split(mult))
    ahead[:shared, :] = value
    ahead[shared:, :] = pick(pack[...], value)


def rest_last_kernel(size, high, low, mult_s, mult_n, gap, floor, mult_out, residual_out, settled, left, done):
    shared, rows = mult_s.shape[0], mult_n.shape[0]
    residual, alive = rest_residual(size, high, low, mult_s, mult_n, gap)
    left[...] = residual
    settled[...] = settle(mult_n[...] + STEP * residual, floor[shared:, :], alive)
    copies = [
        pltpu.make_async_copy(source, target.at[pl.ds(shared, rows)], done.at[i])
        for i, (source, target) in enumerate(((left, residual_out), (settled, mult_out)))
    ]
    for copy in copies:
        copy.start()
    for copy in copies:
        copy.wait()


def coarse_kernel(times, size, *refs):
    n = len(times)
    recvs = refs[:n]
    base, unpack, mult, modes, started, trial = refs[n:n + 6]
    shared = base.shape[0]
    residual, _ = shared_residual(times, recvs, base, unpack, size, 128)
    coarse = started[...] + product(split(modes[:, :shared]), split(residual))
    for out in refs[n + 6:]:
        out[...] = coarse
    trial[...] = mult[:shared, :] + STEP * residual


def tile_kernel(wide_order, narrow_order, high, low, *refs):
    n, m = len(wide_order), len(narrow_order)
    blocks, outs, (gathered, parts) = refs[:n + 1], refs[n + 1:n + m + 2], refs[n + m + 2:]
    count = blocks[0].shape[0]
    for d, ref in zip((0, *wide_order), blocks):
        at = pl.multiple_of((lax.axis_index("wide") ^ d) * count, count)
        gathered[pl.ds(at, count), :] = ref[...]
    parts[...] = product((high[...], low[...]), split(gathered[...]))
    for d, out in zip((0, *narrow_order), outs):
        at = pl.multiple_of((lax.axis_index("narrow") ^ d) * count, count)
        out[...] = parts[pl.ds(at, count), :]


def lift_kernel(n, m, cap, size, *refs):
    parts = refs[:m + 1]
    ins, (mult_s, mult_n, image), sends, halves = refs[m + 1:m + 8], refs[m + 8:m + 11], refs[m + 11:-1], refs[-1]
    basis, trial_s, trial_n, floor, high, low, pack = ins
    solved = parts[0][...]
    for part in parts[1:]:
        solved = solved + part[...]
    shared, width = trial_s.shape
    order = floor.shape[0]
    high_part, low_part = split(solved)
    solved = jnp.concatenate([high_part, low_part, high_part], axis=0)
    shared, width = trial_s.shape
    for at in range(0, floor.shape[0], shared):
        rows = slice(at, at + shared)
        trial = trial_s[...] if at == 0 else trial_n[at - shared:at, :]
        alive = live(size[0], at, shared, width)
        mult = settle(trial + mm(basis[rows, :], solved), floor[rows, :], alive)
        if at == 0:
            mult_s[...] = mult
        else:
            mult_n[at - shared:at, :] = mult
        halves[rows, :width], halves[rows, width:] = split(mult)
    both = mm(high[...], halves[...])
    value = both[:, :width] + (both[:, width:] + mm(low[...], halves[:, :width]))
    image[...] = value
    send(cap, pack[...], value, sends)


def sweep_kernel(times, cap, size, *refs):
    n = len(times)
    recvs = refs[:n]
    base, unpack, mult, floor, high, low, ahead, mult_out, image_out = refs[n:n + 9]
    shared = base.shape[0]
    residual, alive = shared_residual(times, recvs, base, unpack, size, shared)
    value = settle(mult[...] + STEP * residual, floor[:shared, :], alive)
    mult_out[...] = value
    both = ahead[...] + product((high[...], low[...]), split(value))
    image_out[...] = both[:shared]
    for d, out in enumerate(refs[n + 9:]):
        out[...] = both[shared + d * cap:shared + (d + 1) * cap]


def last_kernel(times, size, *refs):
    n = len(times)
    recvs = refs[:n]
    base, unpack, mult, floor, _, _, mult_out, residual_out, settled, left, done = refs[n:]
    shared = base.shape[0]
    copies = []
    for k, across in enumerate(arrived(times, recvs, shared, unpack, 128)):
        rows, at = slice(k * 128, (k + 1) * 128), pl.ds(k * 128, 128)
        alive = live(size[0], k * 128, *across.shape)
        residual = jnp.where(alive, base[rows, :] + across, 0.0)
        left[rows, :] = residual
        settled[rows, :] = settle(mult[rows, :] + STEP * residual, floor[rows, :], alive)
        copies += [
            pltpu.make_async_copy(left.at[at], residual_out.at[at], done.at[2 * k]),
            pltpu.make_async_copy(settled.at[at], mult_out.at[at], done.at[2 * k + 1]),
        ]
        for copy in copies[-2:]:
            copy.start()
    for copy in copies:
        copy.wait()


def swap(block, axis, count, d):
    return lax.ppermute(block, axis, [(i, i ^ d) for i in range(count)])


def swap_all(blocks, axis, count, order):
    return [swap(block, axis, count, d) for block, d in zip(blocks, order)]


def swap_rows(blocks, axis, count, times):
    return [swap(blocks[d - 1], axis, count, d) for d in times]


def half_first(count, back):
    half = count // 2
    others = [d for d in range(1, count) if d != half]
    return (half, *(others[::-1] if back else others))


def middle_first(count):
    return (count - 1, *range(1, count - 1))


def far_first(count):
    return tuple(range(count - 1, 0, -1))


def local(
    wide,
    narrow,
    operators,
    coarse_inverse,
    modes,
    gap,
    start_mult,
    peer_list,
    partner_row,
    interface_size,
    contact_rows,
):
    operator = operators[0]
    modes = modes[0]
    gap = gap[0]
    mult = start_mult[0]
    order, loads = mult.shape
    shared = partner_row.shape[1]
    count = modes.shape[0]
    rest = order - shared
    steps = rest // shared
    n, m = wide - 1, narrow - 1
    cap = 2 * shared // wide
    listed = n * cap
    padded = -(-listed // 128) * 128
    size = interface_size
    coarse_order, part_order = half_first(wide, True), far_first(narrow)
    half, half_back, middle = half_first(wide, False), half_first(wide, True), middle_first(wide)
    orders = ((middle, half, half_back), (half_back, half, half_back))
    sent = [shape(cap, loads)] * n
    full = 2 * order * loads

    list_rows = -(-(-(-cap // loads)) // 8) * 8
    unpack_own, unpack_all, unpack, top_high, top_low, image, *sends = call(
        functools.partial(first_kernel, n, cap),
        tuple(
            pltpu.with_memory_space_constraint(value, pltpu.HBM)
            for value in (peer_list[0].reshape(1, shared), partner_row, operator, mult)
        ),
        [shape(shared, shared, BF16), shape(shared, n * shared, BF16), shape(shared, padded, BF16)]
        + [shape(shared, order, BF16)] * 2
        + [shape(shared, loads)]
        + [shape(shared + list_rows, loads)] * n,
        in_specs=[HBM] * 4,
        scratch=[
            pltpu.VMEM((1, shared), jnp.int32),
            pltpu.VMEM((1, shared), jnp.int32),
            pltpu.VMEM((shared, order), F32),
            pltpu.VMEM((order, loads), F32),
            pltpu.SemaphoreType.DMA((8,)),
        ],
        flops=3 * full * shared,
        moved=8 * shared * order,
        name="first",
    )
    floor, basis, tile_high, tile_low = call(
        prepare_kernel,
        (contact_rows, modes, coarse_inverse),
        [shape(order, loads)] + [shape(order, 3 * count, BF16)] + [shape(*coarse_inverse.shape, BF16)] * 2,
        flops=full * count,
        moved=8 * coarse_inverse.size + 4 * full,
        name="prepare",
    )
    mult_s = mult
    scratch = [pltpu.VMEM((order, 2 * loads), BF16)]
    for outer in range(OUTER):
        times = orders[outer][0]
        recvs = swap_rows(sends, "wide", wide, times)
        base = call(
            base_kernel,
            (image, unpack_own, gap),
            [shape(shared, loads)],
            flops=4 * shared * shared * loads,
            moved=8 * shared * loads,
            name="base",
        )[0]
        if outer == 0:
            row_block, load_block = block((shared, order)), block((shared, loads))
            next_loads = block((shared, loads), 1)
            trial_n, started, high, low = call(
                rest_start_kernel,
                (
                    size,
                    *(
                        pltpu.with_memory_space_constraint(value, pltpu.HBM)
                        for value in (operator, mult, mult, gap, modes)
                    ),
                ),
                [shape(rest, loads), shape(count, loads)] + [shape(rest, order, BF16)] * 2,
                [
                    SMEM,
                    block((shared, order), 1),
                    whole((order, loads)),
                    next_loads,
                    next_loads,
                    block((count, shared), 1, across=True),
                ],
                [load_block, whole((count, loads)), row_block, row_block],
                scratch=scratch,
                grid=(steps,),
                flops=3 * full * rest,
                moved=8 * rest * order,
                name="rest_start",
            )
            marks = unpack_all
            pack, stack_high, stack_low = call(
                functools.partial(pack_kernel, times, cap),
                (*recvs, top_high, top_low),
                [shape(padded, shared, BF16)] + [shape(shared + padded, shared, BF16)] * 2,
                flops=8 * padded * shared * shared,
                moved=8 * padded * shared,
                name="pack",
            )
        else:
            trial_n, started = call(
                rest_first_kernel,
                (size, high, low, mult_s, mult_n, gap, modes),
                [shape(rest, loads), shape(count, loads)],
                flops=3 * full * rest,
                moved=4 * rest * order,
                name="rest_first",
            )
            marks = unpack
        trial_s, own, *coarse = call(
            functools.partial(coarse_kernel, times),
            (size, *recvs, base, marks, mult_s, modes, started),
            [shape(shared, loads)] + [shape(count, loads)] * wide,
            flops=6 * shared * loads * unpack.shape[1],
            moved=2 * shared * unpack.shape[1],
            name="coarse",
        )
        blocks = [own] + swap_all(coarse, "wide", wide, coarse_order)
        own, *parts = call(
            functools.partial(tile_kernel, coarse_order, part_order),
            (tile_high, tile_low, *blocks),
            [shape(count, loads)] * narrow,
            scratch=[
                pltpu.VMEM((wide * count, loads), F32),
                pltpu.VMEM((narrow * count, loads), F32),
            ],
            flops=6 * coarse_inverse.size * loads,
            moved=4 * coarse_inverse.size,
            name="tile",
        )
        parts = [own] + swap_all(parts, "narrow", narrow, part_order)
        mult_s, mult_n, image, *sends = call(
            functools.partial(lift_kernel, n, m, cap),
            (size, *parts, basis, trial_s, trial_n, floor, top_high, top_low, pack),
            [shape(shared, loads), shape(rest, loads), shape(shared, loads)] + sent,
            flops=3 * full * shared,
            moved=4 * order * shared,
            scratch=scratch,
            name="lift",
        )
        for inner in range(1, INNER):
            last = outer == OUTER - 1 and inner == INNER - 1
            times = orders[outer][inner]
            recvs = swap_rows(sends, "wide", wide, times)
            base = call(
                base_kernel,
                (image, unpack_own, gap),
                [shape(shared, loads)],
                flops=4 * shared * shared * loads,
                moved=8 * shared * loads,
                name="base",
            )[0]
            ins = (size, high, low, mult_s, mult_n, gap, floor)
            shadow = (size, *recvs, base, unpack, mult_s, floor)
            cost = dict(flops=6 * shared * loads * unpack.shape[1], moved=2 * shared * unpack.shape[1])
            if last:
                outs = call(
                    rest_last_kernel,
                    ins,
                    [shape(order, loads)] * 2,
                    out_specs=[HBM] * 2,
                    scratch=[pltpu.VMEM((rest, loads), F32)] * 2 + [pltpu.SemaphoreType.DMA((2,))],
                    flops=3 * full * rest,
                    moved=4 * rest * order,
                    name="rest_last",
                )
                outs = call(
                    functools.partial(last_kernel, times),
                    (*shadow, *outs),
                    [shape(order, loads)] * 2,
                    in_specs=[SMEM] + [VMEM] * (len(shadow) - 1) + [HBM] * 2,
                    out_specs=[HBM] * 2,
                    scratch=[pltpu.VMEM((shared, loads), F32)] * 2 + [pltpu.SemaphoreType.DMA((2 * (shared // 128),))],
                    alias={len(shadow): 0, len(shadow) + 1: 1},
                    name="last",
                    **cost,
                )
                return tuple(out[None] for out in outs)
            mult_n, ahead = call(
                rest_kernel,
                (*ins, top_high, top_low, pack),
                [shape(rest, loads), shape(shared + padded, loads)],
                flops=3 * full * order,
                moved=4 * order * order,
                name="rest",
            )
            mult_s, image, *sends = call(
                functools.partial(sweep_kernel, times, cap),
                (*shadow, stack_high, stack_low, ahead),
                [shape(shared, loads)] * 2 + sent,
                name="sweep",
                **cost,
            )


def solution(mesh):
    wide = mesh.shape["wide"]
    narrow = mesh.shape["narrow"]

    def body(*args):
        return local(wide, narrow, *args)

    return jax.shard_map(
        body,
        mesh=mesh,
        in_specs=(
            P(("groups", "wide", "narrow"), None, None),
            P(("groups", "wide"), "narrow"),
            P(("groups", "wide", "narrow"), None, None),
            P(("groups", "wide", "narrow"), None, None),
            P(("groups", "wide", "narrow"), None, None),
            P(("groups", "wide", "narrow"), None, None),
            P(("groups", "wide", "narrow"), None),
            P(("groups", "wide", "narrow")),
            P(("groups", "wide", "narrow"), None),
        ),
        out_specs=(
            P(("groups", "wide", "narrow"), None, None),
            P(("groups", "wide", "narrow"), None, None),
        ),
        check_vma=False,
    )
```

```python
import functools

import jax
import jax.numpy as jnp
from jax import lax
from jax.experimental import pallas as pl
from jax.experimental.pallas import tpu as pltpu
from jax.sharding import PartitionSpec as P

OUTER = 2
INNER = 3
STEP = 0.3
F32 = jnp.float32
BF16 = jnp.bfloat16
PARAMS = pltpu.CompilerParams(vmem_limit_bytes=24 * 1024 * 1024)


def split(value):
    high = value.astype(BF16)
    return high, (value - high.astype(F32)).astype(BF16)


def mm(left, right):
    return jnp.dot(left, right, preferred_element_type=F32)


def product(left, right):
    (left_high, left_low), (right_high, right_low) = left, right
    width = right_high.shape[1]
    both = mm(left_high, jnp.concatenate([right_high, right_low], axis=1))
    return both[:, :width] + (both[:, width:] + mm(left_low, right_high))


def pick(chosen, value):
    width = value.shape[1]
    both = mm(chosen, jnp.concatenate(split(value), axis=1))
    return both[:, :width] + both[:, width:]


def live(size, start, rows, width):
    return lax.broadcasted_iota(jnp.int32, (rows, width), 0) + start < size


def call(body, ins, outs, in_specs=None, out_specs=None, scratch=(), grid=(), flops=0, moved=0, alias=None, name=None):
    if in_specs is None:
        in_specs = [SMEM if value.ndim == 1 else VMEM for value in ins]
    if out_specs is None:
        out_specs = [VMEM] * len(outs)
    return pl.pallas_call(
        body,
        out_shape=outs,
        grid=grid,
        in_specs=in_specs,
        out_specs=out_specs,
        scratch_shapes=list(scratch),
        compiler_params=PARAMS,
        cost_estimate=pl.CostEstimate(flops=flops, bytes_accessed=moved, transcendentals=0),
        input_output_aliases=alias or {},
        name=name,
    )(*ins)


def whole(shape):
    return pl.BlockSpec(shape, lambda *i: (0,) * len(shape))


def block(shape, at=0, across=False):
    if across:
        return pl.BlockSpec(shape, lambda i: (0, i + at))
    return pl.BlockSpec(shape, lambda i: (i + at, 0))


SMEM = pl.BlockSpec(memory_space=pltpu.SMEM)
HBM = pl.BlockSpec(memory_space=pltpu.HBM)
VMEM = pl.BlockSpec(memory_space=pltpu.VMEM)


def shape(rows, columns, dtype=F32):
    return jax.ShapeDtypeStruct((rows, columns), dtype)


def lines_of(times):
    return times if isinstance(times[0], tuple) else (times, times)


def by_line(even, odd):
    return even if odd is even else jnp.where(lax.axis_index("narrow") % 2 == 1, odd, even)


def first_kernel(n, cap, peers_at, rows_at, operator_at, mult_at, *refs):
    unpack_own, unpack_all, unpack, high, low, image = refs[:6]
    sends, (peers, rows, operator, mult, done) = refs[6:6 + n], refs[6 + n:]
    shared, width = image.shape
    pieces = [(peers_at, peers), (rows_at, rows)]
    for source, target, count in ((mult_at, mult, 2), (operator_at, operator, 4)):
        step = target.shape[0] // count
        pieces += [(source.at[pl.ds(k * step, step)], target.at[pl.ds(k * step, step)]) for k in range(count)]
    copies = [pltpu.make_async_copy(source, target, done.at[i]) for i, (source, target) in enumerate(pieces)]
    for copy in copies:
        copy.start()
    copies[0].wait()
    copies[1].wait()
    across = jnp.broadcast_to(peers[...], (shared, shared))
    down = across.T
    first = lax.broadcasted_iota(jnp.int32, (shared, shared), 0)
    second = lax.broadcasted_iota(jnp.int32, (shared, shared), 1)
    slot = jnp.sum(
        jnp.where((across == down) & (second < first), 1.0, 0.0), axis=1, keepdims=True
    ).astype(jnp.int32)
    wanted = jnp.broadcast_to(rows[...], (shared, shared)).T[:, :1]
    far = down[:, :1] ^ lax.axis_index("wide")

    def marks(key, columns):
        hit = key == lax.broadcasted_iota(jnp.int32, (shared, columns), 1)
        return jnp.where(hit, 1.0, 0.0).astype(BF16)

    unpack_own[...] = marks(jnp.where(far == 0, wanted, -1), shared)
    unpack_all[...] = marks(jnp.where(far == 0, -1, (far - 1) * shared + wanted), unpack_all.shape[1])
    unpack[...] = marks(jnp.where(far == 0, -1, (far - 1) * cap + slot), unpack.shape[1])
    lane = lax.broadcasted_iota(jnp.int32, (shared, width), 1)
    for d, out in enumerate(sends, 1):
        out[shared:, :] = jnp.zeros((out.shape[0] - shared, width), F32)
        for c in range(-(-cap // width)):
            hit = (far == d) & (slot == lane + c * width)
            out[shared + c:shared + c + 1, :] = jnp.sum(
                jnp.where(hit, wanted.astype(F32), 0.0), axis=0, keepdims=True
            )
    for copy in copies[2:]:
        copy.wait()
    parts = split(operator[...])
    high[...], low[...] = parts
    value = product(parts, split(mult[...]))
    image[...] = value
    for out in sends:
        out[:shared, :] = value


def pack_kernel(times, cap, *refs):
    n = len(times)
    recvs, (high, low, pack, stack_high, stack_low) = refs[:n], refs[n:]
    shared = pack.shape[1]
    width = recvs[0].shape[1]
    column = lax.broadcasted_iota(jnp.int32, (width, shared), 1).astype(F32)
    if n * cap < pack.shape[0]:
        pack[n * cap:, :] = jnp.zeros((pack.shape[0] - n * cap, shared), BF16)
    for d, recv in zip(times, recvs):
        for c in range(-(-cap // width)):
            wanted = jnp.broadcast_to(recv[shared + c:shared + c + 1, :], (shared, width)).T
            chosen = jnp.where(wanted == column, 1.0, 0.0).astype(BF16)
            size = min(width, cap - c * width)
            at = (d - 1) * cap + c * width
            pack[at:at + size, :] = chosen[:size]
    for source, stack in ((high, stack_high), (low, stack_low)):
        square = source[:, :shared]
        stack[:shared, :] = square
        stack[shared:, :] = mm(pack[...], square).astype(BF16)


def prepare_kernel(contact, modes, tile, floor, basis, tile_high, tile_low):
    order, width = floor.shape
    for at in range(0, order, width):
        flag = jnp.broadcast_to(contact[:, at:at + width], (width, width)).T
        floor[at:at + width, :] = jnp.where(flag == 1, 0.0, -jnp.inf)
    high, low = [part.astype(F32) for part in split(modes[...])]
    basis[...] = jnp.concatenate([high, high, low], axis=0).T.astype(BF16)
    tile_high[...], tile_low[...] = split(tile[...])


def send(times, cap, chosen, image, sends):
    picked = pick(chosen, image)
    rows = [picked[at:at + cap] for at in range(0, len(sends) * cap, cap)]
    for out, (even, odd) in zip(sends, zip(*lines_of(times))):
        out[...] = by_line(rows[even - 1], rows[odd - 1])


def arrived(times, recvs, shared, unpack, chunk):
    lines = lines_of(times)
    got = [recv[...][:shared] for recv in recvs]
    blocks = [by_line(*(got[line.index(d)] for line in lines)) for d in sorted(lines[0])]
    rows = sum(b.shape[0] for b in blocks)
    if rows < unpack.shape[1]:
        blocks.append(jnp.zeros((unpack.shape[1] - rows, blocks[0].shape[1]), F32))
    halves = jnp.concatenate(split(jnp.concatenate(blocks, axis=0)), axis=1)
    width = blocks[0].shape[1]
    for at in range(0, shared, chunk):
        both = mm(unpack[at:at + chunk, :], halves)
        yield both[:, :width] + both[:, width:]


def base_kernel(image, unpack_own, gap, base):
    own = image[...]
    base[...] = gap[:own.shape[0], :] - own + pick(unpack_own[...], own)


def settle(trial, floor, alive):
    return jnp.where(alive, jnp.maximum(trial, floor), 0.0)


def shared_residual(times, recvs, base, unpack, size, chunk):
    known = base[...]
    shared = known.shape[0]
    across = jnp.concatenate(list(arrived(times, recvs, shared, unpack, chunk)), axis=0)
    alive = live(size[0], 0, *known.shape)
    return jnp.where(alive, known + across, 0.0), alive


def rest_start_kernel(size, operator, mult, mult_block, gap, modes, trial, coarse, high, low, halves):
    step = pl.program_id(0)
    rows, width = gap.shape

    @pl.when(step == 0)
    def _():
        halves[:, :width], halves[:, width:] = split(mult[...])
        coarse[...] = jnp.zeros_like(coarse)

    parts = split(operator[...])
    high[...], low[...] = parts
    both = mm(parts[0], halves[...])
    image = both[:, :width] + (both[:, width:] + mm(parts[1], halves[:, :width]))
    alive = live(size[0], (step + 1) * rows, rows, width)
    residual = jnp.where(alive, gap[...] - image, 0.0)
    trial[...] = mult_block[...] + STEP * residual
    coarse[...] += product(split(modes[...]), split(residual))


def rest_residual(size, high, low, mult_s, mult_n, gap):
    shared, (rows, width) = mult_s.shape[0], mult_n.shape
    mult = jnp.concatenate([mult_s[...], mult_n[...]], axis=0)
    image = product((high[...], low[...]), split(mult))
    alive = live(size[0], shared, rows, width)
    return jnp.where(alive, gap[shared:, :] - image, 0.0), alive


def rest_first_kernel(size, high, low, mult_s, mult_n, gap, modes, trial, coarse):
    residual, _ = rest_residual(size, high, low, mult_s, mult_n, gap)
    trial[...] = mult_n[...] + STEP * residual
    coarse[...] = product(split(modes[:, mult_s.shape[0]:]), split(residual))


def rest_kernel(size, high, low, mult_s, mult_n, gap, floor, top_high, top_low, pack, mult_out, ahead):
    shared = mult_s.shape[0]
    residual, alive = rest_residual(size, high, low, mult_s, mult_n, gap)
    mult = settle(mult_n[...] + STEP * residual, floor[shared:, :], alive)
    mult_out[...] = mult
    value = product((top_high[:, shared:], top_low[:, shared:]), split(mult))
    ahead[:shared, :] = value
    ahead[shared:, :] = pick(pack[...], value)


def rest_last_kernel(size, high, low, mult_s, mult_n, gap, floor, mult_out, residual_out, settled, left, done):
    shared, rows = mult_s.shape[0], mult_n.shape[0]
    residual, alive = rest_residual(size, high, low, mult_s, mult_n, gap)
    left[...] = residual
    settled[...] = settle(mult_n[...] + STEP * residual, floor[shared:, :], alive)
    copies = [
        pltpu.make_async_copy(source, target.at[pl.ds(shared, rows)], done.at[i])
        for i, (source, target) in enumerate(((left, residual_out), (settled, mult_out)))
    ]
    for copy in copies:
        copy.start()
    for copy in copies:
        copy.wait()


def coarse_kernel(times, size, *refs):
    n = len(times)
    recvs = refs[:n]
    base, unpack, mult, modes, started, trial = refs[n:n + 6]
    shared = base.shape[0]
    residual, _ = shared_residual(times, recvs, base, unpack, size, 128)
    coarse = started[...] + product(split(modes[:, :shared]), split(residual))
    for out in refs[n + 6:]:
        out[...] = coarse
    trial[...] = mult[:shared, :] + STEP * residual


def tile_kernel(wide_order, narrow_order, high, low, *refs):
    n, m = len(wide_order), len(narrow_order)
    blocks, outs, (gathered, parts) = refs[:n + 1], refs[n + 1:n + m + 2], refs[n + m + 2:]
    count = blocks[0].shape[0]
    for d, ref in zip((0, *wide_order), blocks):
        at = pl.multiple_of((lax.axis_index("wide") ^ d) * count, count)
        gathered[pl.ds(at, count), :] = ref[...]
    parts[...] = product((high[...], low[...]), split(gathered[...]))
    for d, out in zip((0, *narrow_order), outs):
        at = pl.multiple_of((lax.axis_index("narrow") ^ d) * count, count)
        out[...] = parts[pl.ds(at, count), :]


def lift_kernel(times, m, cap, size, *refs):
    parts = refs[:m + 1]
    ins, (mult_s, mult_n, image), sends, halves = refs[m + 1:m + 8], refs[m + 8:m + 11], refs[m + 11:-1], refs[-1]
    basis, trial_s, trial_n, floor, high, low, pack = ins
    solved = parts[0][...]
    for part in parts[1:]:
        solved = solved + part[...]
    shared, width = trial_s.shape
    order = floor.shape[0]
    high_part, low_part = split(solved)
    solved = jnp.concatenate([high_part, low_part, high_part], axis=0)
    shared, width = trial_s.shape
    for at in range(0, floor.shape[0], shared):
        rows = slice(at, at + shared)
        trial = trial_s[...] if at == 0 else trial_n[at - shared:at, :]
        alive = live(size[0], at, shared, width)
        mult = settle(trial + mm(basis[rows, :], solved), floor[rows, :], alive)
        if at == 0:
            mult_s[...] = mult
        else:
            mult_n[at - shared:at, :] = mult
        halves[rows, :width], halves[rows, width:] = split(mult)
    both = mm(high[...], halves[...])
    value = both[:, :width] + (both[:, width:] + mm(low[...], halves[:, :width]))
    image[...] = value
    send(times, cap, pack[...], value, sends)


def sweep_kernel(times, cap, size, *refs):
    n = len(lines_of(times)[0])
    recvs = refs[:n]
    base, unpack, mult, floor, high, low, ahead, mult_out, image_out = refs[n:n + 9]
    shared = base.shape[0]
    residual, alive = shared_residual(times, recvs, base, unpack, size, shared)
    value = settle(mult[...] + STEP * residual, floor[:shared, :], alive)
    mult_out[...] = value
    both = ahead[...] + product((high[...], low[...]), split(value))
    image_out[...] = both[:shared]
    for d, out in enumerate(refs[n + 9:]):
        out[...] = both[shared + d * cap:shared + (d + 1) * cap]


def last_kernel(times, size, *refs):
    n = len(times)
    recvs = refs[:n]
    base, unpack, mult, floor, _, _, mult_out, residual_out, settled, left, done = refs[n:]
    shared = base.shape[0]
    copies = []
    for k, across in enumerate(arrived(times, recvs, shared, unpack, 128)):
        rows, at = slice(k * 128, (k + 1) * 128), pl.ds(k * 128, 128)
        alive = live(size[0], k * 128, *across.shape)
        residual = jnp.where(alive, base[rows, :] + across, 0.0)
        left[rows, :] = residual
        settled[rows, :] = settle(mult[rows, :] + STEP * residual, floor[rows, :], alive)
        copies += [
            pltpu.make_async_copy(left.at[at], residual_out.at[at], done.at[2 * k]),
            pltpu.make_async_copy(settled.at[at], mult_out.at[at], done.at[2 * k + 1]),
        ]
        for copy in copies[-2:]:
            copy.start()
    for copy in copies:
        copy.wait()


def swap(block, axis, count, d):
    return lax.ppermute(block, axis, [(i, i ^ d) for i in range(count)])


def swap_all(blocks, axis, count, order):
    return [swap(block, axis, count, d) for block, d in zip(blocks, order)]


def swap_lines(blocks, wide, narrow, times):
    return [
        lax.ppermute(
            block,
            ("wide", "narrow"),
            [(w * narrow + i, (w ^ ds[i % 2]) * narrow + i) for w in range(wide) for i in range(narrow)],
        )
        for block, ds in zip(blocks, zip(*times))
    ]


def swap_rows(blocks, axis, count, times):
    return [swap(blocks[d - 1], axis, count, d) for d in times]


def half_first(count, back):
    half = count // 2
    others = [d for d in range(1, count) if d != half]
    return (half, *(others[::-1] if back else others))


def middle_first(count):
    return (count - 1, *range(1, count - 1))


def far_first(count):
    return tuple(range(count - 1, 0, -1))


def local(
    wide,
    narrow,
    operators,
    coarse_inverse,
    modes,
    gap,
    start_mult,
    peer_list,
    partner_row,
    interface_size,
    contact_rows,
):
    operator = operators[0]
    modes = modes[0]
    gap = gap[0]
    mult = start_mult[0]
    order, loads = mult.shape
    shared = partner_row.shape[1]
    count = modes.shape[0]
    rest = order - shared
    steps = rest // shared
    n, m = wide - 1, narrow - 1
    cap = 2 * shared // wide
    listed = n * cap
    padded = -(-listed // 128) * 128
    size = interface_size
    coarse_order, part_order = half_first(wide, True), far_first(narrow)
    half_back, middle = half_first(wide, True), middle_first(wide)
    apart = tuple(range(1, wide)), half_back
    orders = ((middle, apart, half_back), (half_back, apart, half_back))
    sent = [shape(cap, loads)] * n
    full = 2 * order * loads

    list_rows = -(-(-(-cap // loads)) // 8) * 8
    unpack_own, unpack_all, unpack, top_high, top_low, image, *sends = call(
        functools.partial(first_kernel, n, cap),
        tuple(
            pltpu.with_memory_space_constraint(value, pltpu.HBM)
            for value in (peer_list[0].reshape(1, shared), partner_row, operator, mult)
        ),
        [shape(shared, shared, BF16), shape(shared, n * shared, BF16), shape(shared, padded, BF16)]
        + [shape(shared, order, BF16)] * 2
        + [shape(shared, loads)]
        + [shape(shared + list_rows, loads)] * n,
        in_specs=[HBM] * 4,
        scratch=[
            pltpu.VMEM((1, shared), jnp.int32),
            pltpu.VMEM((1, shared), jnp.int32),
            pltpu.VMEM((shared, order), F32),
            pltpu.VMEM((order, loads), F32),
            pltpu.SemaphoreType.DMA((8,)),
        ],
        flops=3 * full * shared,
        moved=8 * shared * order,
        name="first",
    )
    floor, basis, tile_high, tile_low = call(
        prepare_kernel,
        (contact_rows, modes, coarse_inverse),
        [shape(order, loads)] + [shape(order, 3 * count, BF16)] + [shape(*coarse_inverse.shape, BF16)] * 2,
        flops=full * count,
        moved=8 * coarse_inverse.size + 4 * full,
        name="prepare",
    )
    mult_s = mult
    scratch = [pltpu.VMEM((order, 2 * loads), BF16)]
    for outer in range(OUTER):
        times = orders[outer][0]
        recvs = swap_rows(sends, "wide", wide, times)
        base = call(
            base_kernel,
            (image, unpack_own, gap),
            [shape(shared, loads)],
            flops=4 * shared * shared * loads,
            moved=8 * shared * loads,
            name="base",
        )[0]
        if outer == 0:
            row_block, load_block = block((shared, order)), block((shared, loads))
            next_loads = block((shared, loads), 1)
            trial_n, started, high, low = call(
                rest_start_kernel,
                (
                    size,
                    *(
                        pltpu.with_memory_space_constraint(value, pltpu.HBM)
                        for value in (operator, mult, mult, gap, modes)
                    ),
                ),
                [shape(rest, loads), shape(count, loads)] + [shape(rest, order, BF16)] * 2,
                [
                    SMEM,
                    block((shared, order), 1),
                    whole((order, loads)),
                    next_loads,
                    next_loads,
                    block((count, shared), 1, across=True),
                ],
                [load_block, whole((count, loads)), row_block, row_block],
                scratch=scratch,
                grid=(steps,),
                flops=3 * full * rest,
                moved=8 * rest * order,
                name="rest_start",
            )
            marks = unpack_all
            pack, stack_high, stack_low = call(
                functools.partial(pack_kernel, times, cap),
                (*recvs, top_high, top_low),
                [shape(padded, shared, BF16)] + [shape(shared + padded, shared, BF16)] * 2,
                flops=8 * padded * shared * shared,
                moved=8 * padded * shared,
                name="pack",
            )
        else:
            trial_n, started = call(
                rest_first_kernel,
                (size, high, low, mult_s, mult_n, gap, modes),
                [shape(rest, loads), shape(count, loads)],
                flops=3 * full * rest,
                moved=4 * rest * order,
                name="rest_first",
            )
            marks = unpack
        trial_s, own, *coarse = call(
            functools.partial(coarse_kernel, times),
            (size, *recvs, base, marks, mult_s, modes, started),
            [shape(shared, loads)] + [shape(count, loads)] * wide,
            flops=6 * shared * loads * unpack.shape[1],
            moved=2 * shared * unpack.shape[1],
            name="coarse",
        )
        blocks = [own] + swap_all(coarse, "wide", wide, coarse_order)
        own, *parts = call(
            functools.partial(tile_kernel, coarse_order, part_order),
            (tile_high, tile_low, *blocks),
            [shape(count, loads)] * narrow,
            scratch=[
                pltpu.VMEM((wide * count, loads), F32),
                pltpu.VMEM((narrow * count, loads), F32),
            ],
            flops=6 * coarse_inverse.size * loads,
            moved=4 * coarse_inverse.size,
            name="tile",
        )
        parts = [own] + swap_all(parts, "narrow", narrow, part_order)
        mult_s, mult_n, image, *sends = call(
            functools.partial(lift_kernel, orders[outer][1], m, cap),
            (size, *parts, basis, trial_s, trial_n, floor, top_high, top_low, pack),
            [shape(shared, loads), shape(rest, loads), shape(shared, loads)] + sent,
            flops=3 * full * shared,
            moved=4 * order * shared,
            scratch=scratch,
            name="lift",
        )
        for inner in range(1, INNER):
            last = outer == OUTER - 1 and inner == INNER - 1
            times = orders[outer][inner]
            if inner == 1:
                recvs = swap_lines(sends, wide, narrow, times)
            else:
                recvs = swap_rows(sends, "wide", wide, times)
            base = call(
                base_kernel,
                (image, unpack_own, gap),
                [shape(shared, loads)],
                flops=4 * shared * shared * loads,
                moved=8 * shared * loads,
                name="base",
            )[0]
            ins = (size, high, low, mult_s, mult_n, gap, floor)
            shadow = (size, *recvs, base, unpack, mult_s, floor)
            cost = dict(flops=6 * shared * loads * unpack.shape[1], moved=2 * shared * unpack.shape[1])
            if last:
                outs = call(
                    rest_last_kernel,
                    ins,
                    [shape(order, loads)] * 2,
                    out_specs=[HBM] * 2,
                    scratch=[pltpu.VMEM((rest, loads), F32)] * 2 + [pltpu.SemaphoreType.DMA((2,))],
                    flops=3 * full * rest,
                    moved=4 * rest * order,
                    name="rest_last",
                )
                outs = call(
                    functools.partial(last_kernel, times),
                    (*shadow, *outs),
                    [shape(order, loads)] * 2,
                    in_specs=[SMEM] + [VMEM] * (len(shadow) - 1) + [HBM] * 2,
                    out_specs=[HBM] * 2,
                    scratch=[pltpu.VMEM((shared, loads), F32)] * 2 + [pltpu.SemaphoreType.DMA((2 * (shared // 128),))],
                    alias={len(shadow): 0, len(shadow) + 1: 1},
                    name="last",
                    **cost,
                )
                return tuple(out[None] for out in outs)
            mult_n, ahead = call(
                rest_kernel,
                (*ins, top_high, top_low, pack),
                [shape(rest, loads), shape(shared + padded, loads)],
                flops=3 * full * order,
                moved=4 * order * order,
                name="rest",
            )
            mult_s, image, *sends = call(
                functools.partial(sweep_kernel, times, cap),
                (*shadow, stack_high, stack_low, ahead),
                [shape(shared, loads)] * 2 + sent,
                name="sweep",
                **cost,
            )


def solution(mesh):
    wide = mesh.shape["wide"]
    narrow = mesh.shape["narrow"]

    def body(*args):
        return local(wide, narrow, *args)

    return jax.shard_map(
        body,
        mesh=mesh,
        in_specs=(
            P(("groups", "wide", "narrow"), None, None),
            P(("groups", "wide"), "narrow"),
            P(("groups", "wide", "narrow"), None, None),
            P(("groups", "wide", "narrow"), None, None),
            P(("groups", "wide", "narrow"), None, None),
            P(("groups", "wide", "narrow"), None, None),
            P(("groups", "wide", "narrow"), None),
            P(("groups", "wide", "narrow")),
            P(("groups", "wide", "narrow"), None),
        ),
        out_specs=(
            P(("groups", "wide", "narrow"), None, None),
            P(("groups", "wide", "narrow"), None, None),
        ),
        check_vma=False,
    )
```

```python
import functools

import jax
import jax.numpy as jnp
from jax import lax
from jax.experimental import pallas as pl
from jax.experimental.pallas import tpu as pltpu
from jax.sharding import PartitionSpec as P

OUTER = 2
INNER = 3
STEP = 0.3
F32 = jnp.float32
BF16 = jnp.bfloat16
PARAMS = pltpu.CompilerParams(vmem_limit_bytes=24 * 1024 * 1024)


def split(value):
    high = value.astype(BF16)
    return high, (value - high.astype(F32)).astype(BF16)


def mm(left, right):
    return jnp.dot(left, right, preferred_element_type=F32)


def product(left, right):
    (left_high, left_low), (right_high, right_low) = left, right
    width = right_high.shape[1]
    both = mm(left_high, jnp.concatenate([right_high, right_low], axis=1))
    return both[:, :width] + (both[:, width:] + mm(left_low, right_high))


def pick(chosen, value):
    width = value.shape[1]
    both = mm(chosen, jnp.concatenate(split(value), axis=1))
    return both[:, :width] + both[:, width:]


def live(size, start, rows, width):
    return lax.broadcasted_iota(jnp.int32, (rows, width), 0) + start < size


def call(body, ins, outs, in_specs=None, out_specs=None, scratch=(), grid=(), flops=0, moved=0, alias=None, name=None):
    if in_specs is None:
        in_specs = [SMEM if value.ndim == 1 else VMEM for value in ins]
    if out_specs is None:
        out_specs = [VMEM] * len(outs)
    return pl.pallas_call(
        body,
        out_shape=outs,
        grid=grid,
        in_specs=in_specs,
        out_specs=out_specs,
        scratch_shapes=list(scratch),
        compiler_params=PARAMS,
        cost_estimate=pl.CostEstimate(flops=flops, bytes_accessed=moved, transcendentals=0),
        input_output_aliases=alias or {},
        name=name,
    )(*ins)


def whole(shape):
    return pl.BlockSpec(shape, lambda *i: (0,) * len(shape))


def block(shape, at=0, across=False):
    if across:
        return pl.BlockSpec(shape, lambda i: (0, i + at))
    return pl.BlockSpec(shape, lambda i: (i + at, 0))


SMEM = pl.BlockSpec(memory_space=pltpu.SMEM)
HBM = pl.BlockSpec(memory_space=pltpu.HBM)
VMEM = pl.BlockSpec(memory_space=pltpu.VMEM)


def shape(rows, columns, dtype=F32):
    return jax.ShapeDtypeStruct((rows, columns), dtype)


def places(peers, rows):
    shared = peers.shape[1]
    across = jnp.broadcast_to(peers[...], (shared, shared))
    down = across.T
    first = lax.broadcasted_iota(jnp.int32, (shared, shared), 0)
    second = lax.broadcasted_iota(jnp.int32, (shared, shared), 1)
    slot = jnp.sum(
        jnp.where((across == down) & (second < first), 1.0, 0.0), axis=1, keepdims=True
    ).astype(jnp.int32)
    wanted = jnp.broadcast_to(rows[...], (shared, shared)).T[:, :1]
    return down[:, :1] ^ lax.axis_index("wide"), slot, wanted


def marks_kernel(cap, peers, rows, unpack_own, unpack_all, unpack):
    far, slot, wanted = places(peers, rows)
    shared = peers.shape[1]
    for key, out in (
        (jnp.where(far == 0, wanted, -1), unpack_own),
        (jnp.where(far == 0, -1, (far - 1) * shared + wanted), unpack_all),
        (jnp.where(far == 0, -1, (far - 1) * cap + slot), unpack),
    ):
        hit = key == lax.broadcasted_iota(jnp.int32, out.shape, 1)
        out[...] = jnp.where(hit, 1.0, 0.0).astype(BF16)


def first_kernel(n, cap, peers_at, rows_at, operator_at, mult_at, *refs):
    high, low, image = refs[:3]
    sends, (peers, rows, operator, mult, done) = refs[3:3 + n], refs[3 + n:]
    shared, width = image.shape
    pieces = [(peers_at, peers), (rows_at, rows)]
    for source, target, count in ((mult_at, mult, 2), (operator_at, operator, 4)):
        step = target.shape[0] // count
        pieces += [(source.at[pl.ds(k * step, step)], target.at[pl.ds(k * step, step)]) for k in range(count)]
    copies = [pltpu.make_async_copy(source, target, done.at[i]) for i, (source, target) in enumerate(pieces)]
    for copy in copies:
        copy.start()
    copies[0].wait()
    copies[1].wait()
    far, slot, wanted = places(peers, rows)
    lane = lax.broadcasted_iota(jnp.int32, (shared, width), 1)
    for d, out in enumerate(sends, 1):
        out[shared:, :] = jnp.zeros((out.shape[0] - shared, width), F32)
        for c in range(-(-cap // width)):
            hit = (far == d) & (slot == lane + c * width)
            out[shared + c:shared + c + 1, :] = jnp.sum(
                jnp.where(hit, wanted.astype(F32), 0.0), axis=0, keepdims=True
            )
    for copy in copies[2:]:
        copy.wait()
    parts = split(operator[...])
    high[...], low[...] = parts
    value = product(parts, split(mult[...]))
    image[...] = value
    for out in sends:
        out[:shared, :] = value


def pack_kernel(times, cap, *refs):
    n = len(times)
    recvs, (high, low, pack, stack_high, stack_low) = refs[:n], refs[n:]
    shared = pack.shape[1]
    width = recvs[0].shape[1]
    column = lax.broadcasted_iota(jnp.int32, (width, shared), 1).astype(F32)
    if n * cap < pack.shape[0]:
        pack[n * cap:, :] = jnp.zeros((pack.shape[0] - n * cap, shared), BF16)
    for d, recv in zip(times, recvs):
        for c in range(-(-cap // width)):
            wanted = jnp.broadcast_to(recv[shared + c:shared + c + 1, :], (shared, width)).T
            chosen = jnp.where(wanted == column, 1.0, 0.0).astype(BF16)
            size = min(width, cap - c * width)
            at = (d - 1) * cap + c * width
            pack[at:at + size, :] = chosen[:size]
    for source, stack in ((high, stack_high), (low, stack_low)):
        square = source[:, :shared]
        stack[:shared, :] = square
        stack[shared:, :] = mm(pack[...], square).astype(BF16)


def prepare_kernel(contact, modes, tile, floor, basis, tile_high, tile_low):
    order, width = floor.shape
    for at in range(0, order, width):
        flag = jnp.broadcast_to(contact[:, at:at + width], (width, width)).T
        floor[at:at + width, :] = jnp.where(flag == 1, 0.0, -jnp.inf)
    high, low = [part.astype(F32) for part in split(modes[...])]
    basis[...] = jnp.concatenate([high, high, low], axis=0).T.astype(BF16)
    tile_high[...], tile_low[...] = split(tile[...])


def send(cap, chosen, image, sends):
    picked = pick(chosen, image)
    for d, out in enumerate(sends):
        out[...] = picked[d * cap:(d + 1) * cap]


def arrived(times, recvs, shared, unpack, chunk):
    blocks = [recvs[times.index(d)][...][:shared] for d in sorted(times)]
    rows = sum(b.shape[0] for b in blocks)
    if rows < unpack.shape[1]:
        blocks.append(jnp.zeros((unpack.shape[1] - rows, blocks[0].shape[1]), F32))
    halves = jnp.concatenate(split(jnp.concatenate(blocks, axis=0)), axis=1)
    width = blocks[0].shape[1]
    for at in range(0, shared, chunk):
        both = mm(unpack[at:at + chunk, :], halves)
        yield both[:, :width] + both[:, width:]


def base_kernel(image, unpack_own, gap, base):
    own = image[...]
    base[...] = gap[:own.shape[0], :] - own + pick(unpack_own[...], own)


def settle(trial, floor, alive):
    return jnp.where(alive, jnp.maximum(trial, floor), 0.0)


def shared_residual(times, recvs, base, unpack, size, chunk):
    known = base[...]
    shared = known.shape[0]
    across = jnp.concatenate(list(arrived(times, recvs, shared, unpack, chunk)), axis=0)
    alive = live(size[0], 0, *known.shape)
    return jnp.where(alive, known + across, 0.0), alive


def rest_start_kernel(size, operator, mult, mult_block, gap, modes, trial, coarse, high, low, halves):
    step = pl.program_id(0)
    rows, width = gap.shape

    @pl.when(step == 0)
    def _():
        halves[:, :width], halves[:, width:] = split(mult[...])
        coarse[...] = jnp.zeros_like(coarse)

    parts = split(operator[...])
    high[...], low[...] = parts
    both = mm(parts[0], halves[...])
    image = both[:, :width] + (both[:, width:] + mm(parts[1], halves[:, :width]))
    alive = live(size[0], (step + 1) * rows, rows, width)
    residual = jnp.where(alive, gap[...] - image, 0.0)
    trial[...] = mult_block[...] + STEP * residual
    coarse[...] += product(split(modes[...]), split(residual))


def rest_residual(size, high, low, mult_s, mult_n, gap):
    shared, (rows, width) = mult_s.shape[0], mult_n.shape
    mult = jnp.concatenate([mult_s[...], mult_n[...]], axis=0)
    image = product((high[...], low[...]), split(mult))
    alive = live(size[0], shared, rows, width)
    return jnp.where(alive, gap[shared:, :] - image, 0.0), alive


def rest_first_kernel(size, high, low, mult_s, mult_n, gap, modes, trial, coarse):
    residual, _ = rest_residual(size, high, low, mult_s, mult_n, gap)
    trial[...] = mult_n[...] + STEP * residual
    coarse[...] = product(split(modes[:, mult_s.shape[0]:]), split(residual))


def rest_kernel(size, high, low, mult_s, mult_n, gap, floor, top_high, top_low, pack, mult_out, ahead):
    shared = mult_s.shape[0]
    residual, alive = rest_residual(size, high, low, mult_s, mult_n, gap)
    mult = settle(mult_n[...] + STEP * residual, floor[shared:, :], alive)
    mult_out[...] = mult
    value = product((top_high[:, shared:], top_low[:, shared:]), split(mult))
    ahead[:shared, :] = value
    ahead[shared:, :] = pick(pack[...], value)


def rest_last_kernel(size, high, low, mult_s, mult_n, gap, floor, mult_out, residual_out, settled, left, done):
    shared, rows = mult_s.shape[0], mult_n.shape[0]
    residual, alive = rest_residual(size, high, low, mult_s, mult_n, gap)
    left[...] = residual
    settled[...] = settle(mult_n[...] + STEP * residual, floor[shared:, :], alive)
    copies = [
        pltpu.make_async_copy(source, target.at[pl.ds(shared, rows)], done.at[i])
        for i, (source, target) in enumerate(((left, residual_out), (settled, mult_out)))
    ]
    for copy in copies:
        copy.start()
    for copy in copies:
        copy.wait()


def coarse_kernel(times, size, *refs):
    n = len(times)
    recvs = refs[:n]
    base, unpack, mult, modes, started, trial = refs[n:n + 6]
    shared = base.shape[0]
    residual, _ = shared_residual(times, recvs, base, unpack, size, 128)
    coarse = started[...] + product(split(modes[:, :shared]), split(residual))
    for out in refs[n + 6:]:
        out[...] = coarse
    trial[...] = mult[:shared, :] + STEP * residual


def tile_kernel(wide_order, narrow_order, high, low, *refs):
    n, m = len(wide_order), len(narrow_order)
    blocks, outs, (gathered, parts) = refs[:n + 1], refs[n + 1:n + m + 2], refs[n + m + 2:]
    count = blocks[0].shape[0]
    for d, ref in zip((0, *wide_order), blocks):
        at = pl.multiple_of((lax.axis_index("wide") ^ d) * count, count)
        gathered[pl.ds(at, count), :] = ref[...]
    parts[...] = product((high[...], low[...]), split(gathered[...]))
    for d, out in zip((0, *narrow_order), outs):
        at = pl.multiple_of((lax.axis_index("narrow") ^ d) * count, count)
        out[...] = parts[pl.ds(at, count), :]


def lift_kernel(n, m, cap, size, *refs):
    parts = refs[:m + 1]
    ins, (mult_s, mult_n, image), sends, halves = refs[m + 1:m + 8], refs[m + 8:m + 11], refs[m + 11:-1], refs[-1]
    basis, trial_s, trial_n, floor, high, low, pack = ins
    solved = parts[0][...]
    for part in parts[1:]:
        solved = solved + part[...]
    shared, width = trial_s.shape
    order = floor.shape[0]
    high_part, low_part = split(solved)
    solved = jnp.concatenate([high_part, low_part, high_part], axis=0)
    shared, width = trial_s.shape
    for at in range(0, floor.shape[0], shared):
        rows = slice(at, at + shared)
        trial = trial_s[...] if at == 0 else trial_n[at - shared:at, :]
        alive = live(size[0], at, shared, width)
        mult = settle(trial + mm(basis[rows, :], solved), floor[rows, :], alive)
        if at == 0:
            mult_s[...] = mult
        else:
            mult_n[at - shared:at, :] = mult
        halves[rows, :width], halves[rows, width:] = split(mult)
    both = mm(high[...], halves[...])
    value = both[:, :width] + (both[:, width:] + mm(low[...], halves[:, :width]))
    image[...] = value
    send(cap, pack[...], value, sends)


def sweep_kernel(times, cap, size, *refs):
    n = len(times)
    recvs = refs[:n]
    base, unpack, mult, floor, high, low, ahead, mult_out, image_out = refs[n:n + 9]
    shared = base.shape[0]
    residual, alive = shared_residual(times, recvs, base, unpack, size, shared)
    value = settle(mult[...] + STEP * residual, floor[:shared, :], alive)
    mult_out[...] = value
    both = ahead[...] + product((high[...], low[...]), split(value))
    image_out[...] = both[:shared]
    for d, out in enumerate(refs[n + 9:]):
        out[...] = both[shared + d * cap:shared + (d + 1) * cap]


def last_kernel(times, size, *refs):
    n = len(times)
    recvs = refs[:n]
    base, unpack, mult, floor, _, _, mult_out, residual_out, settled, left, done = refs[n:]
    shared = base.shape[0]
    copies = []
    for k, across in enumerate(arrived(times, recvs, shared, unpack, 128)):
        rows, at = slice(k * 128, (k + 1) * 128), pl.ds(k * 128, 128)
        alive = live(size[0], k * 128, *across.shape)
        residual = jnp.where(alive, base[rows, :] + across, 0.0)
        left[rows, :] = residual
        settled[rows, :] = settle(mult[rows, :] + STEP * residual, floor[rows, :], alive)
        copies += [
            pltpu.make_async_copy(left.at[at], residual_out.at[at], done.at[2 * k]),
            pltpu.make_async_copy(settled.at[at], mult_out.at[at], done.at[2 * k + 1]),
        ]
        for copy in copies[-2:]:
            copy.start()
    for copy in copies:
        copy.wait()


def swap(block, axis, count, d):
    return lax.ppermute(block, axis, [(i, i ^ d) for i in range(count)])


def swap_all(blocks, axis, count, order):
    return [swap(block, axis, count, d) for block, d in zip(blocks, order)]


def swap_rows(blocks, axis, count, times):
    return [swap(blocks[d - 1], axis, count, d) for d in times]


def half_first(count, back):
    half = count // 2
    others = [d for d in range(1, count) if d != half]
    return (half, *(others[::-1] if back else others))


def middle_first(count):
    return (count - 1, *range(1, count - 1))


def far_first(count):
    return tuple(range(count - 1, 0, -1))


def local(
    wide,
    narrow,
    operators,
    coarse_inverse,
    modes,
    gap,
    start_mult,
    peer_list,
    partner_row,
    interface_size,
    contact_rows,
):
    operator = operators[0]
    modes = modes[0]
    gap = gap[0]
    mult = start_mult[0]
    order, loads = mult.shape
    shared = partner_row.shape[1]
    count = modes.shape[0]
    rest = order - shared
    steps = rest // shared
    n, m = wide - 1, narrow - 1
    cap = 2 * shared // wide
    listed = n * cap
    padded = -(-listed // 128) * 128
    size = interface_size
    coarse_order, part_order = half_first(wide, True), far_first(narrow)
    half, half_back, middle = half_first(wide, False), half_first(wide, True), middle_first(wide)
    orders = ((middle, half, half_back), (half_back, half, half_back))
    sent = [shape(cap, loads)] * n
    full = 2 * order * loads

    list_rows = -(-(-(-cap // loads)) // 8) * 8
    pairs = peer_list[0].reshape(1, shared), partner_row
    top_high, top_low, image, *sends = call(
        functools.partial(first_kernel, n, cap),
        tuple(
            pltpu.with_memory_space_constraint(value, pltpu.HBM)
            for value in (*pairs, operator, mult)
        ),
        [shape(shared, order, BF16)] * 2
        + [shape(shared, loads)]
        + [shape(shared + list_rows, loads)] * n,
        in_specs=[HBM] * 4,
        scratch=[
            pltpu.VMEM((1, shared), jnp.int32),
            pltpu.VMEM((1, shared), jnp.int32),
            pltpu.VMEM((shared, order), F32),
            pltpu.VMEM((order, loads), F32),
            pltpu.SemaphoreType.DMA((8,)),
        ],
        flops=3 * full * shared,
        moved=8 * shared * order,
        name="first",
    )
    unpack_own, unpack_all, unpack = call(
        functools.partial(marks_kernel, cap),
        pairs,
        [shape(shared, shared, BF16), shape(shared, n * shared, BF16), shape(shared, padded, BF16)],
        flops=8 * shared * shared * wide,
        moved=2 * shared * shared * wide,
        name="marks",
    )
    floor, basis, tile_high, tile_low = call(
        prepare_kernel,
        (contact_rows, modes, coarse_inverse),
        [shape(order, loads)] + [shape(order, 3 * count, BF16)] + [shape(*coarse_inverse.shape, BF16)] * 2,
        flops=full * count,
        moved=8 * coarse_inverse.size + 4 * full,
        name="prepare",
    )
    mult_s = mult
    scratch = [pltpu.VMEM((order, 2 * loads), BF16)]
    for outer in range(OUTER):
        times = orders[outer][0]
        recvs = swap_rows(sends, "wide", wide, times)
        base = call(
            base_kernel,
            (image, unpack_own, gap),
            [shape(shared, loads)],
            flops=4 * shared * shared * loads,
            moved=8 * shared * loads,
            name="base",
        )[0]
        if outer == 0:
            row_block, load_block = block((shared, order)), block((shared, loads))
            next_loads = block((shared, loads), 1)
            trial_n, started, high, low = call(
                rest_start_kernel,
                (
                    size,
                    *(
                        pltpu.with_memory_space_constraint(value, pltpu.HBM)
                        for value in (operator, mult, mult, gap, modes)
                    ),
                ),
                [shape(rest, loads), shape(count, loads)] + [shape(rest, order, BF16)] * 2,
                [
                    SMEM,
                    block((shared, order), 1),
                    whole((order, loads)),
                    next_loads,
                    next_loads,
                    block((count, shared), 1, across=True),
                ],
                [load_block, whole((count, loads)), row_block, row_block],
                scratch=scratch,
                grid=(steps,),
                flops=3 * full * rest,
                moved=8 * rest * order,
                name="rest_start",
            )
            marks = unpack_all
            pack, stack_high, stack_low = call(
                functools.partial(pack_kernel, times, cap),
                (*recvs, top_high, top_low),
                [shape(padded, shared, BF16)] + [shape(shared + padded, shared, BF16)] * 2,
                flops=8 * padded * shared * shared,
                moved=8 * padded * shared,
                name="pack",
            )
        else:
            trial_n, started = call(
                rest_first_kernel,
                (size, high, low, mult_s, mult_n, gap, modes),
                [shape(rest, loads), shape(count, loads)],
                flops=3 * full * rest,
                moved=4 * rest * order,
                name="rest_first",
            )
            marks = unpack
        trial_s, own, *coarse = call(
            functools.partial(coarse_kernel, times),
            (size, *recvs, base, marks, mult_s, modes, started),
            [shape(shared, loads)] + [shape(count, loads)] * wide,
            flops=6 * shared * loads * unpack.shape[1],
            moved=2 * shared * unpack.shape[1],
            name="coarse",
        )
        blocks = [own] + swap_all(coarse, "wide", wide, coarse_order)
        own, *parts = call(
            functools.partial(tile_kernel, coarse_order, part_order),
            (tile_high, tile_low, *blocks),
            [shape(count, loads)] * narrow,
            scratch=[
                pltpu.VMEM((wide * count, loads), F32),
                pltpu.VMEM((narrow * count, loads), F32),
            ],
            flops=6 * coarse_inverse.size * loads,
            moved=4 * coarse_inverse.size,
            name="tile",
        )
        parts = [own] + swap_all(parts, "narrow", narrow, part_order)
        mult_s, mult_n, image, *sends = call(
            functools.partial(lift_kernel, n, m, cap),
            (size, *parts, basis, trial_s, trial_n, floor, top_high, top_low, pack),
            [shape(shared, loads), shape(rest, loads), shape(shared, loads)] + sent,
            flops=3 * full * shared,
            moved=4 * order * shared,
            scratch=scratch,
            name="lift",
        )
        for inner in range(1, INNER):
            last = outer == OUTER - 1 and inner == INNER - 1
            times = orders[outer][inner]
            recvs = swap_rows(sends, "wide", wide, times)
            base = call(
                base_kernel,
                (image, unpack_own, gap),
                [shape(shared, loads)],
                flops=4 * shared * shared * loads,
                moved=8 * shared * loads,
                name="base",
            )[0]
            ins = (size, high, low, mult_s, mult_n, gap, floor)
            shadow = (size, *recvs, base, unpack, mult_s, floor)
            cost = dict(flops=6 * shared * loads * unpack.shape[1], moved=2 * shared * unpack.shape[1])
            if last:
                outs = call(
                    rest_last_kernel,
                    ins,
                    [shape(order, loads)] * 2,
                    out_specs=[HBM] * 2,
                    scratch=[pltpu.VMEM((rest, loads), F32)] * 2 + [pltpu.SemaphoreType.DMA((2,))],
                    flops=3 * full * rest,
                    moved=4 * rest * order,
                    name="rest_last",
                )
                outs = call(
                    functools.partial(last_kernel, times),
                    (*shadow, *outs),
                    [shape(order, loads)] * 2,
                    in_specs=[SMEM] + [VMEM] * (len(shadow) - 1) + [HBM] * 2,
                    out_specs=[HBM] * 2,
                    scratch=[pltpu.VMEM((shared, loads), F32)] * 2 + [pltpu.SemaphoreType.DMA((2 * (shared // 128),))],
                    alias={len(shadow): 0, len(shadow) + 1: 1},
                    name="last",
                    **cost,
                )
                return tuple(out[None] for out in outs)
            mult_n, ahead = call(
                rest_kernel,
                (*ins, top_high, top_low, pack),
                [shape(rest, loads), shape(shared + padded, loads)],
                flops=3 * full * order,
                moved=4 * order * order,
                name="rest",
            )
            mult_s, image, *sends = call(
                functools.partial(sweep_kernel, times, cap),
                (*shadow, stack_high, stack_low, ahead),
                [shape(shared, loads)] * 2 + sent,
                name="sweep",
                **cost,
            )


def solution(mesh):
    wide = mesh.shape["wide"]
    narrow = mesh.shape["narrow"]

    def body(*args):
        return local(wide, narrow, *args)

    return jax.shard_map(
        body,
        mesh=mesh,
        in_specs=(
            P(("groups", "wide", "narrow"), None, None),
            P(("groups", "wide"), "narrow"),
            P(("groups", "wide", "narrow"), None, None),
            P(("groups", "wide", "narrow"), None, None),
            P(("groups", "wide", "narrow"), None, None),
            P(("groups", "wide", "narrow"), None, None),
            P(("groups", "wide", "narrow"), None),
            P(("groups", "wide", "narrow")),
            P(("groups", "wide", "narrow"), None),
        ),
        out_specs=(
            P(("groups", "wide", "narrow"), None, None),
            P(("groups", "wide", "narrow"), None, None),
        ),
        check_vma=False,
    )
```
